32 devices in a mesh: pipe: 4 (over x, core), ctx: 2 (over y), tp: 4 (over z).
Axes of the slice: x: 2, y: 2, z: 4, core: 2. Of those that a mesh axis runs over, the one named last changes fastest.
Arguments:
- segment_inputs: bfloat16 [4, 2, 256, 4096], P('pipe', None, ('ctx', 'tp')), may hold values from -128 to 128
- keys: bfloat16 [4, 2, 256, 512], P('pipe', None, 'ctx', 'tp'), may hold values from -64 to 64
- values: bfloat16 [4, 2, 256, 512], P('pipe', None, 'ctx', 'tp'), may hold values from -6 to 6
- norm_gain: float32 [4, 4096], P('pipe'), may hold values from 0.1 to 1.9
- waiting_grads: bfloat16 [4, 256, 4096], P('pipe', ('ctx', 'tp')), may hold values from -32 to 32
- output_grads: bfloat16 [1, 256, 4096], P(None, ('ctx', 'tp')), may hold values from -32 to 32
- doc_lengths: int32 [5, 8], replicated, may hold values from 1 to 128, as said below
Outputs:
- input_grads: bfloat16 [4, 2, 256, 4096], P('pipe', None, ('ctx', 'tp'))
- key_grads: float32 [4, 2, 256, 512], P('pipe', None, 'ctx', 'tp')
- value_grads: float32 [4, 2, 256, 512], P('pipe', None, 'ctx', 'tp')
- gain_grads: float32 [4, 4096], P('pipe')
The draws below stay inside these ranges and needn't reach their ends.
Inputs may be any that keep to these rules, and one draw needn't show every extreme that they name: `doc_lengths`: row m lists in order of position the lengths of the 8 documents packed into microbatch m's sequence; each row sums to 256; the last document is exactly 128 long.
All inputs are finite; a program needn't handle non-finite values.
Results may differ from the reference program's by a relative error of at most 0.009.
The reference program's roundings to bfloat16 on the way (of `queries`, `arriving`, `dscore`, `probs_low` and `query_grad`) count: a program that leaves them out, or rounds other values in their place, can miss the bound.
Values may be sent and summed in bfloat16 or wider, within the bound.
No kernel may reach another device: no remote copies, remote signals or barrier semaphores. Data moves between devices by JAX's collectives and lax.ppermute only.
A program may use at most 64 MiB of HBM per device.

```python
import jax
import jax.numpy as jnp
from jax import lax

QH = 32
KVH = 4
HD = 128
S_DEV = 128
TICKS = 2
DOCS = 8
SEGMENTS = 4
MICRO = 5
SEQ = 256
QW = 4096
KVW = 512
DOC_MOST = 128
N_CTX = 2


def input_field(key):
    full_shape = (SEGMENTS, TICKS, SEQ, QW)
    key_core, key_cols, key_rows = jax.random.split(jax.random.fold_in(key, 101), 3)
    col_scale = 10.0 ** jax.random.uniform(key_cols, (SEGMENTS, 1, 1, QW), jnp.float32)
    row_scale = 10.0 ** (jax.random.uniform(key_rows, (SEGMENTS, TICKS, SEQ, 1), jnp.float32) - 0.5)
    core_draw = jnp.clip(jax.random.normal(key_core, full_shape, jnp.float32), -4.0, 4.0)
    return core_draw * col_scale * row_scale


def draw_segment_inputs(key, part):
    return input_field(key).astype(jnp.bfloat16)


def draw_keys(key, part):
    full_shape = (SEGMENTS, TICKS, SEQ, KVW)
    key_base = jax.random.fold_in(jax.random.fold_in(key, 202), 0)
    base_draw = jnp.clip(jax.random.normal(key_base, full_shape, jnp.float32), -4.0, 4.0)
    return base_draw.astype(jnp.bfloat16)


def grad_field(key, lead_count, salt_value):
    full_shape = (lead_count, SEQ, QW)
    key_core, key_rows = jax.random.split(jax.random.fold_in(key, salt_value), 2)
    position = jnp.arange(SEQ, dtype=jnp.float32) / SEQ - 0.5
    growth = 3.0
    row_trend = (growth ** position)[None, :, None]
    spread = 10.0 ** (jax.random.uniform(key_rows, (lead_count, SEQ, 1), jnp.float32) - 0.5)
    core_draw = jnp.clip(jax.random.normal(key_core, full_shape, jnp.float32), -4.0, 4.0)
    return core_draw * row_trend * spread


def draw_waiting_grads(key, part):
    return grad_field(key, SEGMENTS, 303).astype(jnp.bfloat16)


def draw_output_grads(key, part):
    return grad_field(key, TICKS - 1, 404).astype(jnp.bfloat16)


def draw_doc_lengths(key, part):
    remaining = SEQ - DOC_MOST

    def one_row(row_key):
        picked = jax.random.permutation(row_key, remaining - 1)[:DOCS - 2] + 1
        cuts = jnp.sort(picked.astype(jnp.int32))
        edges = jnp.concatenate([jnp.zeros((1,), jnp.int32), cuts, jnp.full((1,), remaining, jnp.int32)])
        return jnp.concatenate([edges[1:] - edges[:-1], jnp.full((1,), DOC_MOST, jnp.int32)])
    return jax.vmap(one_row)(jax.random.split(jax.random.fold_in(key, 505), MICRO))


def shard_levels(stream_key, shape, cuts, low, high):
    level, own = 1.0, jax.random.fold_in(stream_key, 6)
    for dim, parts in cuts:
        draws = jnp.exp(jax.random.uniform(jax.random.fold_in(own, dim), (parts,), jnp.float32, low / len(cuts), high / len(cuts)))
        level = level * jnp.repeat(draws, shape[dim] // parts).reshape([-1 if axis == dim else 1 for axis in range(len(shape))])
    return level


def centred(rng, shape, scale, limit, pieces=(), kind=jnp.bfloat16):
    array = scale * jax.random.normal(rng, shape, jnp.float32)
    if pieces:
        array = array * shard_levels(rng, shape, pieces, -0.22, 0.18)
    return jnp.clip(array, -limit, limit).astype(kind)


def setup_inputs(seed: int = 0) -> dict:
    splits = jax.random.split(jax.random.key(seed), 8)
    segment_inputs = draw_segment_inputs(jax.random.fold_in(splits[7], 71), 0)
    keys = draw_keys(jax.random.fold_in(splits[7], 71), 0)
    values = centred(splits[2], (SEGMENTS, TICKS, SEQ, KVW), 1.0, 6.0, ((0, 4), (2, 2), (3, 4)))
    norm_gain = jnp.clip(1.0 + 0.18 * jax.random.normal(splits[3], (SEGMENTS, QW), jnp.float32), 0.1, 1.9)
    waiting_grads = draw_waiting_grads(jax.random.fold_in(splits[7], 71), 0)
    output_grads = draw_output_grads(jax.random.fold_in(splits[7], 71), 0)
    doc_lengths = draw_doc_lengths(jax.random.fold_in(splits[7], 71), 0)
    return dict(segment_inputs=segment_inputs, keys=keys, values=values, norm_gain=norm_gain, waiting_grads=waiting_grads, output_grads=output_grads, doc_lengths=doc_lengths)


epsilon = 1e-05
masked_fill = -1e+30

def row_positions(rows, half_rows, cycle_count):
    section = rows // half_rows
    offset = rows % half_rows
    owner = section // 2
    placed = jnp.where(section % 2 == 0, owner, 2 * cycle_count - 1 - owner)
    return (placed * half_rows + offset).astype(jnp.int32)

def document_starts(lengths_row, positions):
    closing = jnp.cumsum(lengths_row)
    passed = closing[None, :] <= positions[:, None]
    return lax.optimization_barrier(jnp.sum(jnp.where(passed, lengths_row[None, :], 0), axis=1)).astype(jnp.int32)

def segment_tick(inputs, key_rows, value_rows, gain_row, arriving, lengths_row):
    scale_factor = HD ** (-0.5)
    group_size = QH // KVH
    widened = inputs.astype(jnp.float32)
    inverse = lax.rsqrt(lax.optimization_barrier(jnp.mean(widened * widened, axis=-1, keepdims=True)) + epsilon)
    normed = widened * inverse
    queries = (normed * gain_row[None, :]).astype(jnp.bfloat16)
    positions = row_positions(jnp.arange(SEQ, dtype=jnp.int32), S_DEV // 2, N_CTX)
    starts = document_starts(lengths_row, positions)
    visible = (positions[None, :] <= positions[:, None]) & (positions[None, :] >= starts[:, None])

    def one_head(head_index):
        shared = head_index // group_size
        query_head = lax.dynamic_slice_in_dim(queries, head_index * HD, HD, 1)
        grad_head = lax.dynamic_slice_in_dim(arriving, head_index * HD, HD, 1)
        key_head = lax.dynamic_slice_in_dim(key_rows, shared * HD, HD, 1)
        value_head = lax.dynamic_slice_in_dim(value_rows, shared * HD, HD, 1)
        scores = scale_factor * jnp.dot(query_head, key_head.T, preferred_element_type=jnp.float32)
        filled = jnp.where(visible, scores, masked_fill)
        row_peak = lax.optimization_barrier(jnp.max(filled, axis=-1, keepdims=True))
        row_total = lax.optimization_barrier(jnp.sum(jnp.where(visible, jnp.exp(scores - row_peak), 0.0), axis=-1, keepdims=True))
        logsum = row_peak + jnp.log(row_total)
        prob_weights = jnp.where(visible, jnp.exp(scores - logsum), 0.0)
        prob_grad = jnp.dot(grad_head, value_head.T, preferred_element_type=jnp.float32)
        row_term = lax.optimization_barrier(jnp.sum(prob_weights * prob_grad, axis=-1, keepdims=True))
        dscore = (prob_weights * (prob_grad - row_term)).astype(jnp.bfloat16)
        probs_low = prob_weights.astype(jnp.bfloat16)
        dquery = scale_factor * jnp.dot(dscore, key_head, preferred_element_type=jnp.float32)
        key_grad = scale_factor * jnp.dot(dscore.T, query_head, preferred_element_type=jnp.float32)
        dvalue = jnp.dot(probs_low.T, grad_head, preferred_element_type=jnp.float32)
        return (dquery, key_grad, dvalue)
    dquery, key_grad, dvalue = lax.map(one_head, jnp.arange(QH, dtype=jnp.int32))
    query_grad = jnp.transpose(dquery, (1, 0, 2)).reshape(SEQ, QW)
    key_sum = lax.optimization_barrier(jnp.sum(key_grad.reshape(KVH, group_size, SEQ, HD), axis=1))
    value_sum = lax.optimization_barrier(jnp.sum(dvalue.reshape(KVH, group_size, SEQ, HD), axis=1))
    key_out = jnp.transpose(key_sum, (1, 0, 2)).reshape(SEQ, KVW)
    value_out = jnp.transpose(value_sum, (1, 0, 2)).reshape(SEQ, KVW)
    rounded = lax.optimization_barrier(query_grad.astype(jnp.bfloat16)).astype(jnp.float32)
    scaled = rounded * gain_row[None, :]
    coupling = lax.optimization_barrier(jnp.mean(scaled * normed, axis=-1, keepdims=True))
    input_grad = (arriving.astype(jnp.float32) + inverse * (scaled - normed * coupling)).astype(jnp.bfloat16)
    gain_part = lax.optimization_barrier(jnp.sum(rounded * normed, axis=0))
    return (input_grad, key_out, value_out, gain_part)

def reference(segment_inputs, keys, values, norm_gain, waiting_grads, output_grads, doc_lengths):
    results = {}
    for tick_index in range(TICKS):
        for segment_index in range(SEGMENTS):
            if tick_index == 0:
                arriving = waiting_grads[segment_index]
            elif segment_index == SEGMENTS - 1:
                arriving = output_grads[tick_index - 1]
            else:
                arriving = results[segment_index + 1, tick_index - 1][0]
            lengths_row = doc_lengths[segment_index + tick_index]
            results[segment_index, tick_index] = segment_tick(segment_inputs[segment_index, tick_index], keys[segment_index, tick_index], values[segment_index, tick_index], norm_gain[segment_index], arriving, lengths_row)
    input_grads = jnp.stack([jnp.stack([results[segment_index, tick_index][0] for tick_index in range(TICKS)]) for segment_index in range(SEGMENTS)])
    key_grads = jnp.stack([jnp.stack([results[segment_index, tick_index][1] for tick_index in range(TICKS)]) for segment_index in range(SEGMENTS)])
    value_grads = jnp.stack([jnp.stack([results[segment_index, tick_index][2] for tick_index in range(TICKS)]) for segment_index in range(SEGMENTS)])
    gain_rows = []
    for segment_index in range(SEGMENTS):
        running = jnp.zeros((QW,), jnp.float32)
        for tick_index in range(TICKS):
            running = running + results[segment_index, tick_index][3]
        gain_rows.append(running)
    gain_grads = jnp.stack(gain_rows)
    return (input_grads, key_grads, value_grads, gain_grads)
```

```python
import functools

import jax
import jax.numpy as jnp
from jax import lax
from jax.experimental import pallas as pl
from jax.experimental.pallas import tpu as pltpu
from jax.sharding import PartitionSpec as P

HD = 128
EPSILON = 1e-05
FILL = -1e30
SCALE = HD ** (-0.5)
F32 = jnp.float32
BF16 = jnp.bfloat16

NT = (((1,), (1,)), ((), ()))
NN = (((1,), (0,)), ((), ()))
TN = (((0,), (0,)), ((), ()))


def dot(a, b, dims):
    return lax.dot_general(a, b, dims, preferred_element_type=F32)


def split_two(value):
    high = value.astype(BF16)
    low = (value - high.astype(F32)).astype(BF16)
    return high, low


def joined(high, low):
    return high.astype(F32) + low.astype(F32)


def in_order(values, owners):
    total = None
    for owner in range(len(values)):
        term = jnp.where(owners[0] == owner, values[0], 0.0)
        for value, whose in zip(values[1:], owners[1:]):
            term = jnp.where(whose == owner, value, term)
        total = term if total is None else total + term
    return total


def pack_kernel(tp_count, half, keys_ref, values_ref, own_ref, other_ref):
    parity = lax.axis_index("tp") // (tp_count // 2)
    for tick in range(keys_ref.shape[1]):
        for kind, ref in enumerate((keys_ref, values_ref)):
            own_ref[tick, kind] = ref[0, tick, pl.ds(parity * half, half), :]
            other_ref[tick, kind] = ref[0, tick, pl.ds((1 - parity) * half, half), :]


def attention_kernel(sizes, tick, n_arrive, *refs):
    rows, half, cycle, tp_count, group, columns = sizes
    refs = list(refs)
    doc_ref, x_ref, gain_ref = refs[:3]
    arrive_refs = refs[3 : 3 + n_arrive]
    kv_refs = refs[3 + n_arrive : 3 + n_arrive + cycle]
    rest = refs[3 + n_arrive + cycle :]
    if tick:
        before_gain_ref, before_ref = rest[:2]
        rest = rest[2:]
    input_grad_ref = rest[0]
    gain_part_ref, own_ref = rest[1:3]
    send_refs = rest[3 : 3 + cycle - 1]
    query_grad_ref, gain_rows_ref = rest[3 + cycle - 1 :]

    pipe_place = lax.axis_index("pipe")
    cycle_place = lax.axis_index("ctx")
    tp_place = lax.axis_index("tp")
    parity = tp_place // (tp_count // 2)
    key_count = cycle * half
    stacked = group * rows
    width = group * HD

    def section_first(owner):
        return half * jnp.where(parity == 0, owner, 2 * cycle - 1 - owner)

    row_first = section_first(cycle_place) + (tp_place % (tp_count // 2)) * rows
    query_pos = row_first + (lax.broadcasted_iota(jnp.int32, (1, stacked), 1) & (rows - 1))
    key_place = lax.broadcasted_iota(jnp.int32, (key_count, 1), 0)
    key_pos = key_place + section_first(cycle_place)
    for turn in range(1, cycle):
        owner = (cycle_place - turn + cycle) % cycle
        key_pos = jnp.where(
            key_place >= turn * half, key_place - turn * half + section_first(owner), key_pos
        )
    micro = pipe_place + tick
    closing = jnp.int32(0)
    query_start = jnp.zeros((1, stacked), jnp.int32)
    for doc in range(doc_ref.shape[1]):
        length = doc_ref[micro, doc]
        closing = closing + length
        query_start = query_start + jnp.where(closing <= query_pos, length, 0)
    visible = (key_pos <= query_pos) & (key_pos >= query_start)

    squares = jnp.zeros((rows, HD), F32)
    for first in range(0, columns, HD):
        part = x_ref[0, tick, :, first : first + HD].astype(F32)
        squares = squares + part * part
    mean = jnp.sum(squares, axis=1, keepdims=True) * (1.0 / columns)
    inverse = lax.rsqrt(mean + EPSILON)

    def arriving(first, count):
        where = pl.ds(first, count)
        if n_arrive == 1:
            return arrive_refs[0][:, where]
        last = pipe_place == lax.axis_size("pipe") - 1
        return jnp.where(last, arrive_refs[1][:, where], arrive_refs[0][:, where])

    def one_group(turn, coupled):
        head_group = tp_place ^ turn
        first = pl.multiple_of(head_group * width, width)
        normed, gains, queries, grads = [], [], [], []
        for head in range(group):
            begin = first + head * HD
            normed.append(x_ref[0, tick, :, pl.ds(begin, HD)].astype(F32) * inverse)
            gains.append(gain_ref[:, pl.ds(begin, HD)])
            queries.append((normed[-1] * gains[-1]).astype(BF16))
            grads.append(arriving(begin, HD))
        query = jnp.concatenate(queries, axis=0)
        grad = jnp.concatenate(grads, axis=0)
        key = jnp.concatenate([ref[turn, 0] for ref in kv_refs], axis=0)
        value = jnp.concatenate([ref[turn, 1] for ref in kv_refs], axis=0)

        scores = jnp.where(visible, SCALE * dot(key, query, NT), FILL)
        weights = jnp.exp(scores - jnp.max(scores, axis=0, keepdims=True))
        probs = weights * (1.0 / jnp.sum(weights, axis=0, keepdims=True))
        prob_grad = dot(value, grad, NT)
        row_term = jnp.sum(probs * prob_grad, axis=0, keepdims=True)
        dscore = (probs * (prob_grad - row_term)).astype(BF16)
        probs_low = probs.astype(BF16)
        query_grad = (SCALE * dot(dscore, key, TN)).astype(BF16)
        key_grad = SCALE * dot(dscore, query, NN)
        value_grad = dot(probs_low, grad, NN)

        for kind, part in enumerate((key_grad, value_grad)):
            begin = pl.multiple_of((turn * 2 + kind) * half, half)
            own_ref[pl.ds(begin, half), :] = part[:half]
            for step, ref in enumerate(send_refs, 1):
                ref[pl.ds(begin, half), :] = part[step * half : (step + 1) * half].astype(BF16)

        gain_rows = []
        for head in range(group):
            low = query_grad[head * rows : (head + 1) * rows]
            query_grad_ref[:, pl.ds(first + head * HD, HD)] = low
            term = low.astype(F32) * normed[head]
            coupled = coupled + term * gains[head]
            gain_rows.append(jnp.sum(term, axis=0, keepdims=True))
        gain_rows_ref[pl.ds(pl.multiple_of(head_group * group, group), group), :] = (
            jnp.concatenate(gain_rows, axis=0)
        )
        return coupled

    coupled = jnp.zeros((rows, HD), F32)
    if key_count * stacked <= 65536:
        for turn in range(tp_count):
            coupled = one_group(turn, coupled)
    else:
        coupled = lax.fori_loop(0, tp_count, one_group, coupled)
    coupling = jnp.sum(coupled, axis=1, keepdims=True) * (1.0 / columns)

    for first in range(0, columns, HD):
        here = slice(first, first + HD)
        scaled = query_grad_ref[:, here].astype(F32) * gain_ref[:, here]
        normed_part = x_ref[0, tick, :, here].astype(F32) * inverse
        result = arriving(first, HD).astype(F32) + inverse * (scaled - normed_part * coupling)
        if tick:
            input_grad_ref[0, tick, :, here] = result.astype(BF16)
            input_grad_ref[0, 0, :, here] = before_ref[:, here]
        else:
            input_grad_ref[:, here] = result.astype(BF16)

    gain_rows = gain_rows_ref[...]
    if tick:
        gain_rows = gain_rows + before_gain_ref[...]
    gain_part_ref[...] = gain_rows
    if tick and send_refs:
        high, low = split_two(gain_rows)
        count = high.shape[0]
        begin = tp_count * 2 * half
        for ref in send_refs:
            ref[begin : begin + count, :] = high
            ref[begin + count : begin + 2 * count, :] = low


def cycle_sum_kernel(sizes, ticks, *refs):
    rows, half, cycle, tp_count, group, columns = sizes
    gain_ref = refs[0]
    per_tick = [refs[1 + tick * cycle : 1 + (tick + 1) * cycle] for tick in range(ticks)]
    keep_ref, gain_sum_ref = refs[1 + ticks * cycle :][:2]
    send_refs = refs[1 + ticks * cycle :][2:]
    block = 2 * half
    for tick in range(ticks):
        for turn in range(tp_count):
            here = slice(turn * block, (turn + 1) * block)
            total = per_tick[tick][0][here, :]
            for ref in per_tick[tick][1:]:
                total = total + ref[here, :].astype(F32)
            if turn == 0:
                keep_ref[tick * block : (tick + 1) * block, :] = total
            else:
                send_refs[turn - 1][tick * block : (tick + 1) * block, :] = total.astype(BF16)
    count = gain_ref.shape[0]
    begin = tp_count * block
    cycle_place = lax.axis_index("ctx")
    values = [joined(*split_two(gain_ref[...]))]
    owners = [cycle_place]
    for step, ref in enumerate(per_tick[ticks - 1][1:], 1):
        values.append(
            joined(ref[begin : begin + count, :], ref[begin + count : begin + 2 * count, :])
        )
        owners.append((cycle_place + step) % cycle)
    gain = in_order(values, owners)
    gain_sum_ref[...] = gain
    high, low = split_two(gain)
    for ref in send_refs:
        ref[ticks * block : ticks * block + count, :] = high
        ref[ticks * block + count : ticks * block + 2 * count, :] = low


def finish_kernel(sizes, ticks, *refs):
    rows, half, cycle, tp_count, group, columns = sizes
    keep_ref, gain_ref = refs[:2]
    receive_refs = refs[2 : 2 + tp_count - 1]
    key_ref, value_ref, gain_out_ref = refs[2 + tp_count - 1 :]
    block = 2 * half
    tp_place = lax.axis_index("tp")
    parity = tp_place // (tp_count // 2)
    for tick in range(ticks):
        for kind, out in enumerate((key_ref, value_ref)):
            begin = tick * block + kind * half
            own = keep_ref[begin : begin + half, :]
            other = None
            for turn in range(1, tp_count):
                part = receive_refs[turn - 1][begin : begin + half, :].astype(F32)
                if turn < tp_count // 2:
                    own = own + part
                else:
                    other = part if other is None else other + part
            out[0, tick, pl.ds(pl.multiple_of(parity * half, half), half), :] = own
            out[0, tick, pl.ds(pl.multiple_of((1 - parity) * half, half), half), :] = other
    count = gain_ref.shape[0]
    begin = ticks * block
    values = [joined(*split_two(gain_ref[...]))]
    owners = [tp_place]
    for turn, ref in enumerate(receive_refs, 1):
        values.append(
            joined(ref[begin : begin + count, :], ref[begin + count : begin + 2 * count, :])
        )
        owners.append(tp_place ^ turn)
    gain_out_ref[...] = in_order(values, owners)


def whole(ref_count):
    return [pl.BlockSpec(memory_space=pltpu.VMEM)] * ref_count


def shape(dims, dtype):
    return jax.ShapeDtypeStruct(dims, dtype)


def on_device(segment_inputs, keys, values, norm_gain, waiting_grads, output_grads, doc_lengths):
    cycle = lax.axis_size("ctx")
    tp_count = lax.axis_size("tp")
    pipe_count = lax.axis_size("pipe")
    _, ticks, rows, columns = segment_inputs.shape
    half = keys.shape[2] // 2
    group = columns // (tp_count * HD)
    gain_count = columns // HD
    sizes = (rows, half, cycle, tp_count, group, columns)
    block = 2 * half
    score_bytes = cycle * half * group * rows * 4
    params = pltpu.CompilerParams(vmem_limit_bytes=min(56 << 20, (12 << 20) + 14 * score_bytes))

    def to_partner(value, turn):
        return lax.ppermute(value, "tp", [(i, i ^ turn) for i in range(tp_count)])

    def to_block(value, step):
        return lax.ppermute(value, "ctx", [(i, (i + step) % cycle) for i in range(cycle)])

    packed = shape((ticks, 2, half, HD), BF16)
    own_kv, other_kv = pl.pallas_call(
        functools.partial(pack_kernel, tp_count, half),
        out_shape=(packed, packed),
        in_specs=whole(2),
        out_specs=whole(2),
        compiler_params=params,
        name="pack_kv",
    )(keys, values)

    def gathered(tick):
        parts = [own_kv[tick]]
        for turn in range(1, tp_count):
            parts.append(to_partner((own_kv if turn < tp_count // 2 else other_kv)[tick], turn))
        near = jnp.stack(parts)
        return [near] + [to_block(near, step) for step in range(1, cycle)]

    def attention(tick, arrive, kv, before):
        n_arrive = len(arrive)
        in_specs = [pl.BlockSpec(memory_space=pltpu.SMEM)]
        in_specs += whole(2 + n_arrive + cycle + len(before))
        extra = 2 * gain_count if tick else 0
        out_shape = [
            shape((1, ticks, rows, columns) if tick else (rows, columns), BF16),
            shape((gain_count, HD), F32),
            shape((tp_count * block, HD), F32),
        ]
        out_shape += [shape((tp_count * block + extra, HD), BF16)] * (cycle - 1)
        return pl.pallas_call(
            functools.partial(attention_kernel, sizes, tick, n_arrive),
            out_shape=out_shape,
            in_specs=in_specs,
            out_specs=whole(len(out_shape)),
            scratch_shapes=[
                pltpu.VMEM((rows, columns), BF16),
                pltpu.VMEM((gain_count, HD), F32),
            ],
            compiler_params=params,
            name=f"attention_{tick}",
        )(doc_lengths, segment_inputs, norm_gain, *arrive, *kv, *before)

    kv_first = gathered(0)
    kv_second = gathered(1)
    first = attention(0, [waiting_grads[0]], kv_first, [])
    input_grad_first, gain_first = first[:2]
    arrived = lax.ppermute(
        input_grad_first, "pipe", [(i, (i - 1) % pipe_count) for i in range(pipe_count)]
    )

    def turned(own, sends):
        return [own] + [to_block(value, -step) for step, value in enumerate(sends, 1)]

    sums_first = turned(first[2], first[3:])
    second = attention(
        1, [arrived, output_grads[0]], kv_second, [gain_first, input_grad_first]
    )
    input_grads, gain_rows = second[:2]
    sums_second = turned(second[2], second[3:])

    message = shape((ticks * block + 2 * gain_count, HD), BF16)
    keep, gain_sum, *sends = pl.pallas_call(
        functools.partial(cycle_sum_kernel, sizes, ticks),
        out_shape=[shape((ticks * block, HD), F32), shape((gain_count, HD), F32)]
        + [message] * (tp_count - 1),
        in_specs=whole(1 + ticks * cycle),
        out_specs=whole(2 + tp_count - 1),
        compiler_params=params,
        name="cycle_sum",
    )(gain_rows, *sums_first, *sums_second)
    received = [to_partner(value, turn) for turn, value in enumerate(sends, 1)]
    grads_shape = shape((1, ticks, block, HD), F32)
    key_grads, value_grads, gain_grads = pl.pallas_call(
        functools.partial(finish_kernel, sizes, ticks),
        out_shape=[grads_shape, grads_shape, shape((gain_count, HD), F32)],
        in_specs=whole(2 + tp_count - 1),
        out_specs=whole(3),
        compiler_params=params,
        name="finish",
    )(keep, gain_sum, *received)
    return input_grads, key_grads, value_grads, gain_grads.reshape(1, columns)


def solution(mesh):
    in_specs = (
        P("pipe", None, ("ctx", "tp"), None),
        P("pipe", None, "ctx", "tp"),
        P("pipe", None, "ctx", "tp"),
        P("pipe", None),
        P("pipe", ("ctx", "tp"), None),
        P(None, ("ctx", "tp"), None),
        P(),
    )
    out_specs = (
        P("pipe", None, ("ctx", "tp"), None),
        P("pipe", None, "ctx", "tp"),
        P("pipe", None, "ctx", "tp"),
        P("pipe", None),
    )
    return jax.shard_map(
        on_device, mesh=mesh, in_specs=in_specs, out_specs=out_specs, check_vma=False
    )
```

```python
import functools

import jax
import jax.numpy as jnp
from jax import lax
from jax.experimental import pallas as pl
from jax.experimental.pallas import tpu as pltpu
from jax.sharding import PartitionSpec as P

HD = 128
EPSILON = 1e-05
FILL = -1e30
SCALE = HD ** (-0.5)
F32 = jnp.float32
BF16 = jnp.bfloat16

NT = (((1,), (1,)), ((), ()))
NN = (((1,), (0,)), ((), ()))
TN = (((0,), (0,)), ((), ()))


def dot(a, b, dims):
    return lax.dot_general(a, b, dims, preferred_element_type=F32)


def split_two(value):
    high = value.astype(BF16)
    low = (value - high.astype(F32)).astype(BF16)
    return high, low


def joined(high, low):
    return high.astype(F32) + low.astype(F32)


def in_order(values, owners):
    total = None
    for owner in range(len(values)):
        term = jnp.where(owners[0] == owner, values[0], 0.0)
        for value, whose in zip(values[1:], owners[1:]):
            term = jnp.where(whose == owner, value, term)
        total = term if total is None else total + term
    return total


def pack_kernel(tp_count, half, keys_ref, values_ref, own_ref, other_ref, later_ref, sems):
    parity = lax.axis_index("tp") // (tp_count // 2)
    own_first = pl.multiple_of(parity * half, half)
    other_first = pl.multiple_of((1 - parity) * half, half)
    copies = []
    for kind, ref in enumerate((keys_ref, values_ref)):
        moves = (
            (ref.at[0, 0, pl.ds(own_first, half), :], own_ref.at[kind]),
            (ref.at[0, 0, pl.ds(other_first, half), :], other_ref.at[kind]),
            (ref.at[0, 1], later_ref.at[kind]),
        )
        for place, (source, target) in enumerate(moves):
            copies.append(pltpu.make_async_copy(source, target, sems.at[kind, place]))
    for copy in copies:
        copy.start()
    for copy in copies:
        copy.wait()


def section_kernel(tp_count, half, cycle, *refs):
    blocks, (own_ref, other_ref) = refs[:cycle], refs[cycle:]
    parity = lax.axis_index("tp") // (tp_count // 2)
    for turn, ref in enumerate(blocks):
        own_ref[turn] = ref[:, pl.ds(pl.multiple_of(parity * half, half), half), :]
        other_ref[turn] = ref[:, pl.ds(pl.multiple_of((1 - parity) * half, half), half), :]


def norm_kernel(x_ref, gain_ref, query_ref, inverse_ref):
    _, ticks, rows, columns = x_ref.shape
    for tick in range(ticks):
        squares = jnp.zeros((rows, HD), F32)
        for first in range(0, columns, HD):
            part = x_ref[0, tick, :, first : first + HD].astype(F32)
            squares = squares + part * part
        mean = jnp.sum(squares, axis=1, keepdims=True) * (1.0 / columns)
        inverse = jnp.broadcast_to(lax.rsqrt(mean + EPSILON), (rows, HD))
        inverse_ref[tick] = inverse
        for first in range(0, columns, HD):
            here = slice(first, first + HD)
            normed = x_ref[0, tick, :, here].astype(F32) * inverse
            query_ref[tick, :, here] = (normed * gain_ref[:, here]).astype(BF16)


class Group:
    def __init__(self, sizes, turn):
        self.rows, self.group = sizes[0], sizes[4]
        width = self.group * HD
        self.head_group = lax.axis_index("tp") ^ turn
        self.first = pl.multiple_of(self.head_group * width, width)

    def head(self, index):
        return pl.ds(self.first + index * HD, HD)

    def stacked(self, load):
        return jnp.concatenate([load(self.head(index)) for index in range(self.group)], axis=0)

    def unstacked(self, value):
        return [value[index * self.rows : (index + 1) * self.rows] for index in range(self.group)]


def arriving_from(refs):
    if len(refs) == 1:
        return lambda where: refs[0][0, :, where]
    last = lax.axis_index("pipe") == lax.axis_size("pipe") - 1
    return lambda where: jnp.where(last, refs[1][0, :, where], refs[0][:, where])


def visible_keys(sizes, tick, doc_ref):
    rows, half, cycle, tp_count, group, columns = sizes
    cycle_place = lax.axis_index("ctx")
    tp_place = lax.axis_index("tp")
    parity = tp_place // (tp_count // 2)
    stacked = group * rows

    def section_first(owner):
        return half * jnp.where(parity == 0, owner, 2 * cycle - 1 - owner)

    row_first = section_first(cycle_place) + (tp_place % (tp_count // 2)) * rows
    query_pos = row_first + (lax.broadcasted_iota(jnp.int32, (1, stacked), 1) & (rows - 1))
    key_place = lax.broadcasted_iota(jnp.int32, (cycle * half, 1), 0)
    key_pos = key_place + section_first(cycle_place)
    for turn in range(1, cycle):
        first = section_first((cycle_place - turn + cycle) % cycle)
        key_pos = jnp.where(key_place >= turn * half, key_place - turn * half + first, key_pos)
    micro = lax.axis_index("pipe") + tick
    closing = jnp.int32(0)
    query_start = jnp.zeros((1, stacked), jnp.int32)
    for doc in range(doc_ref.shape[1]):
        length = doc_ref[micro, doc]
        closing = closing + length
        query_start = query_start + jnp.where(closing <= query_pos, length, 0)
    return (key_pos <= query_pos) & (key_pos >= query_start)


def probabilities(visible, key, query):
    scores = jnp.where(visible, SCALE * dot(key, query, NT), FILL)
    weights = jnp.exp(scores - jnp.max(scores, axis=0, keepdims=True))
    return weights * (1.0 / jnp.sum(weights, axis=0, keepdims=True))


def score_grads(probs, value, grad):
    prob_grad = dot(value, grad, NT)
    row_term = jnp.sum(probs * prob_grad, axis=0, keepdims=True)
    return (probs * (prob_grad - row_term)).astype(BF16)


def by_block(refs, turn, kind):
    return jnp.concatenate([ref[turn, kind] for ref in refs], axis=0)


def by_head(refs, turn, kind):
    parts = refs[turn]
    return jnp.concatenate([parts[block, kind] for block in range(parts.shape[0])], axis=0)


def put_key_grads(sizes, turn, key_grad, value_grad, own_ref, send_refs):
    half = sizes[1]
    for kind, part in enumerate((key_grad, value_grad)):
        here = slice((turn * 2 + kind) * half, (turn * 2 + kind + 1) * half)
        own_ref[here, :] = part[:half]
        for step, ref in enumerate(send_refs, 1):
            ref[here, :] = part[step * half : (step + 1) * half].astype(BF16)


def gain_terms(columns_of, low_parts, normed_of, gain_rows_ref):
    rows = []
    for index, low in enumerate(low_parts):
        term = low.astype(F32) * normed_of(columns_of.head(index))
        rows.append(jnp.sum(term, axis=0, keepdims=True))
    group = columns_of.group
    place = pl.ds(pl.multiple_of(columns_of.head_group * group, group), group)
    gain_rows_ref[place, :] = jnp.concatenate(rows, axis=0)


def write_input_grads(sizes, tick, x_ref, gain_ref, inverse, query_grad_ref, arriving, write):
    rows, columns = sizes[0], sizes[5]
    coupled = jnp.zeros((rows, HD), F32)
    for first in range(0, columns, HD):
        here = slice(first, first + HD)
        scaled = query_grad_ref[:, here].astype(F32) * gain_ref[:, here]
        coupled = coupled + scaled * (x_ref[0, tick, :, here].astype(F32) * inverse)
    coupling = jnp.sum(coupled, axis=1, keepdims=True) * (1.0 / columns)
    for first in range(0, columns, HD):
        here = slice(first, first + HD)
        scaled = query_grad_ref[:, here].astype(F32) * gain_ref[:, here]
        normed = x_ref[0, tick, :, here].astype(F32) * inverse
        result = arriving(here).astype(F32) + inverse * (scaled - normed * coupling)
        write(here, result.astype(BF16))


def first_rows_kernel(sizes, *refs):
    cycle, tp_count = sizes[2:4]
    doc_ref, x_ref, gain_ref, query_ref, inverse_ref, waiting_ref = refs[:6]
    kv_refs = refs[6 : 6 + cycle]
    input_grad_ref, query_grad_ref, dscore_ref, probs_ref = refs[6 + cycle :]
    visible = visible_keys(sizes, 0, doc_ref)
    arriving = arriving_from([waiting_ref])
    for turn in range(tp_count):
        columns_of = Group(sizes, turn)
        query = columns_of.stacked(lambda where: query_ref[0, :, where])
        grad = columns_of.stacked(arriving)
        key, value = by_block(kv_refs, turn, 0), by_block(kv_refs, turn, 1)
        probs = probabilities(visible, key, query)
        dscore = score_grads(probs, value, grad)
        dscore_ref[turn] = dscore
        probs_ref[turn] = probs.astype(BF16)
        query_grad = (SCALE * dot(dscore, key, TN)).astype(BF16)
        for index, low in enumerate(columns_of.unstacked(query_grad)):
            query_grad_ref[:, columns_of.head(index)] = low

    def write(here, result):
        input_grad_ref[:, here] = result

    write_input_grads(
        sizes, 0, x_ref, gain_ref, inverse_ref[0], query_grad_ref, arriving, write
    )


def first_keys_kernel(sizes, *refs):
    tp_count = sizes[3]
    x_ref, query_ref, inverse_ref, waiting_ref, query_grad_ref, dscore_ref, probs_ref = refs[:7]
    gain_rows_ref, own_ref = refs[7:9]
    send_refs = refs[9:]
    arriving = arriving_from([waiting_ref])
    inverse = inverse_ref[0]
    for turn in range(tp_count):
        columns_of = Group(sizes, turn)
        query = columns_of.stacked(lambda where: query_ref[0, :, where])
        grad = columns_of.stacked(arriving)
        key_grad = SCALE * dot(dscore_ref[turn], query, NN)
        value_grad = dot(probs_ref[turn], grad, NN)
        put_key_grads(sizes, turn, key_grad, value_grad, own_ref, send_refs)
        gain_terms(
            columns_of,
            [query_grad_ref[:, columns_of.head(index)] for index in range(columns_of.group)],
            lambda where: x_ref[0, 0, :, where].astype(F32) * inverse,
            gain_rows_ref,
        )


def second_probs_kernel(sizes, *refs):
    tp_count = sizes[3]
    doc_ref, query_ref = refs[:2]
    kv_refs, probs_ref = refs[2 : 2 + tp_count], refs[2 + tp_count]
    visible = visible_keys(sizes, 1, doc_ref)
    for turn in range(tp_count):
        query = Group(sizes, turn).stacked(lambda where: query_ref[1, :, where])
        probs_ref[turn] = probabilities(visible, by_head(kv_refs, turn, 0), query)


def second_keys_kernel(sizes, *refs):
    tp_count = sizes[3]
    x_ref, query_ref, inverse_ref, arrived_ref, output_ref, probs_ref, before_ref = refs[:7]
    kv_refs = refs[7 : 7 + tp_count]
    query_grad_ref, gain_rows_ref, own_ref = refs[7 + tp_count :][:3]
    send_refs, (gain_scratch,) = refs[7 + tp_count :][3:-1], refs[-1:]
    arriving = arriving_from([arrived_ref, output_ref])
    inverse = inverse_ref[1]
    for turn in range(tp_count):
        columns_of = Group(sizes, turn)
        query = columns_of.stacked(lambda where: query_ref[1, :, where])
        grad = columns_of.stacked(arriving)
        key, value = by_head(kv_refs, turn, 0), by_head(kv_refs, turn, 1)
        probs = probs_ref[turn]
        dscore = score_grads(probs, value, grad)
        key_grad = SCALE * dot(dscore, query, NN)
        value_grad = dot(probs.astype(BF16), grad, NN)
        put_key_grads(sizes, turn, key_grad, value_grad, own_ref, send_refs)
        query_grad = (SCALE * dot(dscore, key, TN)).astype(BF16)
        low_parts = columns_of.unstacked(query_grad)
        for index, low in enumerate(low_parts):
            query_grad_ref[:, columns_of.head(index)] = low
        gain_terms(
            columns_of,
            low_parts,
            lambda where: x_ref[0, 1, :, where].astype(F32) * inverse,
            gain_scratch,
        )
    gain_rows = gain_scratch[...] + before_ref[...]
    gain_rows_ref[...] = gain_rows
    high, low = split_two(gain_rows)
    count = high.shape[0]
    begin = own_ref.shape[0]
    for ref in send_refs:
        ref[begin : begin + count, :] = high
        ref[begin + count : begin + 2 * count, :] = low


def second_rows_kernel(sizes, *refs):
    x_ref, gain_ref, inverse_ref, arrived_ref, output_ref, query_grad_ref, first_ref = refs[:7]
    input_grads_ref = refs[7]
    input_grads_ref[0, 0] = first_ref[...]

    def write(here, result):
        input_grads_ref[0, 1, :, here] = result

    arriving = arriving_from([arrived_ref, output_ref])
    write_input_grads(
        sizes, 1, x_ref, gain_ref, inverse_ref[1], query_grad_ref, arriving, write
    )


def cycle_sum_kernel(sizes, with_gain, *refs):
    rows, half, cycle, tp_count, group, columns = sizes
    parts, refs = refs[:cycle], refs[cycle:]
    if with_gain:
        gain_ref, refs = refs[0], refs[1:]
        gain_sum_ref, refs = refs[0], refs[1:]
    keep_ref, send_refs = refs[0], refs[1:]
    block = 2 * half
    for turn in range(tp_count):
        here = slice(turn * block, (turn + 1) * block)
        total = parts[0][here, :]
        for ref in parts[1:]:
            total = total + ref[here, :].astype(F32)
        if turn == 0:
            keep_ref[...] = total
        else:
            send_refs[turn - 1][:block, :] = total.astype(BF16)
    if not with_gain:
        return
    count = gain_ref.shape[0]
    begin = tp_count * block
    cycle_place = lax.axis_index("ctx")
    values = [joined(*split_two(gain_ref[...]))]
    owners = [cycle_place]
    for step, ref in enumerate(parts[1:], 1):
        values.append(
            joined(ref[begin : begin + count, :], ref[begin + count : begin + 2 * count, :])
        )
        owners.append((cycle_place + step) % cycle)
    gain = in_order(values, owners)
    gain_sum_ref[...] = gain
    high, low = split_two(gain)
    for ref in send_refs:
        ref[block : block + count, :] = high
        ref[block + count : block + 2 * count, :] = low


def finish_kernel(sizes, ticks, *refs):
    rows, half, cycle, tp_count, group, columns = sizes
    gain_ref, refs = refs[0], refs[1:]
    per_tick = [refs[tick * tp_count : (tick + 1) * tp_count] for tick in range(ticks)]
    key_ref, value_ref, gain_out_ref = refs[ticks * tp_count :]
    block = 2 * half
    tp_place = lax.axis_index("tp")
    parity = tp_place // (tp_count // 2)
    for tick in range(ticks):
        keep_ref, receive_refs = per_tick[tick][0], per_tick[tick][1:]
        for kind, out in enumerate((key_ref, value_ref)):
            here = slice(kind * half, (kind + 1) * half)
            own = keep_ref[here, :]
            other = None
            for turn, ref in enumerate(receive_refs, 1):
                part = ref[here, :].astype(F32)
                if turn < tp_count // 2:
                    own = own + part
                else:
                    other = part if other is None else other + part
            out[0, tick, pl.ds(pl.multiple_of(parity * half, half), half), :] = own
            out[0, tick, pl.ds(pl.multiple_of((1 - parity) * half, half), half), :] = other
    count = gain_ref.shape[0]
    values = [joined(*split_two(gain_ref[...]))]
    owners = [tp_place]
    for turn, ref in enumerate(per_tick[ticks - 1][1:], 1):
        values.append(
            joined(ref[block : block + count, :], ref[block + count : block + 2 * count, :])
        )
        owners.append(tp_place ^ turn)
    gain_out_ref[...] = in_order(values, owners)


def shape(dims, dtype):
    return jax.ShapeDtypeStruct(dims, dtype)


def on_device(segment_inputs, keys, values, norm_gain, waiting_grads, output_grads, doc_lengths):
    cycle = lax.axis_size("ctx")
    tp_count = lax.axis_size("tp")
    pipe_count = lax.axis_size("pipe")
    _, ticks, rows, columns = segment_inputs.shape
    half = keys.shape[2] // 2
    group = columns // (tp_count * HD)
    gain_count = columns // HD
    sizes = (rows, half, cycle, tp_count, group, columns)
    block = 2 * half
    key_count = cycle * half
    stacked = group * rows
    score_bytes = key_count * stacked * 4
    params = pltpu.CompilerParams(vmem_limit_bytes=min(56 << 20, (12 << 20) + 16 * score_bytes))

    def call(kernel, name, operands, out_shape, memory=pltpu.VMEM, scratch=(), scalars=0):
        in_specs = [pl.BlockSpec(memory_space=pltpu.SMEM)] * scalars
        in_specs += [pl.BlockSpec(memory_space=memory)] * (len(operands) - scalars)
        return pl.pallas_call(
            kernel,
            out_shape=out_shape,
            in_specs=in_specs,
            out_specs=[pl.BlockSpec(memory_space=pltpu.VMEM)] * len(out_shape),
            scratch_shapes=scratch,
            compiler_params=params,
            name=name,
        )(*operands)

    def to_partner(value, turn):
        return lax.ppermute(value, "tp", [(i, i ^ turn) for i in range(tp_count)])

    def to_block(value, step):
        return lax.ppermute(value, "ctx", [(i, (i + step) % cycle) for i in range(cycle)])

    def from_partners(own, other):
        return [to_partner(own if d < tp_count // 2 else other, d) for d in range(1, tp_count)]

    section = shape((2, half, HD), BF16)
    own_kv, other_kv, later_kv = call(
        functools.partial(pack_kernel, tp_count, half),
        "pack_kv",
        (keys, values),
        [section, section, shape((2, block, HD), BF16)],
        memory=pl.ANY,
        scratch=[pltpu.SemaphoreType.DMA((2, 3))],
    )
    heads_first = from_partners(own_kv, other_kv)
    blocks_second = [to_block(later_kv, step) for step in range(1, cycle)]
    queries, inverse = call(
        norm_kernel,
        "norm",
        (segment_inputs, norm_gain),
        [shape((ticks, rows, columns), BF16), shape((ticks, rows, HD), F32)],
    )
    near = jnp.stack([own_kv] + heads_first)
    kv_first = [near] + [to_block(near, step) for step in range(1, cycle)]
    sections = shape((cycle, 2, half, HD), BF16)
    own_second, other_second = call(
        functools.partial(section_kernel, tp_count, half, cycle),
        "sections",
        (later_kv, *blocks_second),
        [sections, sections],
    )
    kv_second = [own_second] + from_partners(own_second, other_second)

    low_rows = shape((rows, columns), BF16)
    low_scores = shape((tp_count, key_count, stacked), BF16)
    input_grad_first, query_grad_first, dscore_first, probs_first = call(
        functools.partial(first_rows_kernel, sizes),
        "first_rows",
        (doc_lengths, segment_inputs, norm_gain, queries, inverse, waiting_grads, *kv_first),
        [low_rows, low_rows, low_scores, low_scores],
        scalars=1,
    )
    arrived = lax.ppermute(
        input_grad_first, "pipe", [(i, (i - 1) % pipe_count) for i in range(pipe_count)]
    )
    gain_shape = shape((gain_count, HD), F32)
    own_shape = shape((tp_count * block, HD), F32)

    def send_shapes(extra):
        return [shape((tp_count * block + extra, HD), BF16)] * (cycle - 1)

    def turned(sends):
        return [to_block(value, -step) for step, value in enumerate(sends, 1)]

    gain_first, own_first, *sends_first = call(
        functools.partial(first_keys_kernel, sizes),
        "first_keys",
        (
            segment_inputs,
            queries,
            inverse,
            waiting_grads,
            query_grad_first,
            dscore_first,
            probs_first,
        ),
        [gain_shape, own_shape] + send_shapes(0),
    )
    turned_first = turned(sends_first)
    (probs_second,) = call(
        functools.partial(second_probs_kernel, sizes),
        "second_probs",
        (doc_lengths, queries, *kv_second),
        [shape((tp_count, key_count, stacked), F32)],
        scalars=1,
    )
    query_grad_second, gain_rows, own_second_sum, *sends_second = call(
        functools.partial(second_keys_kernel, sizes),
        "second_keys",
        (
            segment_inputs,
            queries,
            inverse,
            arrived,
            output_grads,
            probs_second,
            gain_first,
            *kv_second,
        ),
        [low_rows, gain_shape, own_shape] + send_shapes(2 * gain_count),
        scratch=[pltpu.VMEM((gain_count, HD), F32)],
    )
    turned_second = turned(sends_second)
    (input_grads,) = call(
        functools.partial(second_rows_kernel, sizes),
        "second_rows",
        (
            segment_inputs,
            norm_gain,
            inverse,
            arrived,
            output_grads,
            query_grad_second,
            input_grad_first,
        ),
        [shape((1, ticks, rows, columns), BF16)],
    )
    keep_shape = shape((block, HD), F32)
    keep_first, *heads_sums_first = call(
        functools.partial(cycle_sum_kernel, sizes, False),
        "first_sum",
        (own_first, *turned_first),
        [keep_shape] + [shape((block, HD), BF16)] * (tp_count - 1),
    )
    received_first = [to_partner(value, d) for d, value in enumerate(heads_sums_first, 1)]
    gain_sum, keep_second, *heads_sums_second = call(
        functools.partial(cycle_sum_kernel, sizes, True),
        "second_sum",
        (own_second_sum, *turned_second, gain_rows),
        [gain_shape, keep_shape]
        + [shape((block + 2 * gain_count, HD), BF16)] * (tp_count - 1),
    )
    received_second = [to_partner(value, d) for d, value in enumerate(heads_sums_second, 1)]
    grads_shape = shape((1, ticks, block, HD), F32)
    key_grads, value_grads, gain_grads = call(
        functools.partial(finish_kernel, sizes, ticks),
        "finish",
        (gain_sum, keep_first, *received_first, keep_second, *received_second),
        [grads_shape, grads_shape, gain_shape],
    )
    return input_grads, key_grads, value_grads, gain_grads.reshape(1, columns)


def solution(mesh):
    in_specs = (
        P("pipe", None, ("ctx", "tp"), None),
        P("pipe", None, "ctx", "tp"),
        P("pipe", None, "ctx", "tp"),
        P("pipe", None),
        P("pipe", ("ctx", "tp"), None),
        P(None, ("ctx", "tp"), None),
        P(),
    )
    out_specs = (
        P("pipe", None, ("ctx", "tp"), None),
        P("pipe", None, "ctx", "tp"),
        P("pipe", None, "ctx", "tp"),
        P("pipe", None),
    )
    return jax.shard_map(
        on_device, mesh=mesh, in_specs=in_specs, out_specs=out_specs, check_vma=False
    )
```

```python
import functools

import jax
import jax.numpy as jnp
from jax import lax
from jax.experimental import pallas as pl
from jax.experimental.pallas import tpu as pltpu
from jax.sharding import PartitionSpec as P

HD = 128
EPSILON = 1e-05
FILL = -1e30
SCALE = HD ** (-0.5)
F32 = jnp.float32
BF16 = jnp.bfloat16

NT = (((1,), (1,)), ((), ()))
NN = (((1,), (0,)), ((), ()))
TN = (((0,), (0,)), ((), ()))


def dot(a, b, dims):
    return lax.dot_general(a, b, dims, preferred_element_type=F32)


def split_two(value):
    high = value.astype(BF16)
    low = (value - high.astype(F32)).astype(BF16)
    return high, low


def joined(high, low):
    return high.astype(F32) + low.astype(F32)


def in_order(values, owners):
    total = None
    for owner in range(len(values)):
        term = jnp.where(owners[0] == owner, values[0], 0.0)
        for value, whose in zip(values[1:], owners[1:]):
            term = jnp.where(whose == owner, value, term)
        total = term if total is None else total + term
    return total


def pack_kernel(tp_count, half, keys_ref, values_ref, own_ref, other_ref, sems):
    parity = lax.axis_index("tp") // (tp_count // 2)
    own_first = pl.multiple_of(parity * half, half)
    other_first = pl.multiple_of((1 - parity) * half, half)
    copies = []
    for kind, ref in enumerate((keys_ref, values_ref)):
        for tick in range(keys_ref.shape[1]):
            for place, (first, target) in enumerate(
                ((own_first, own_ref), (other_first, other_ref))
            ):
                source = ref.at[0, tick, pl.ds(first, half), :]
                copies.append(
                    pltpu.make_async_copy(
                        source, target.at[tick, kind], sems.at[kind, tick, place]
                    )
                )
    for copy in copies:
        copy.start()
    for copy in copies:
        copy.wait()


def norm_kernel(x_ref, gain_ref, query_ref, inverse_ref):
    _, ticks, rows, columns = x_ref.shape
    for tick in range(ticks):
        squares = jnp.zeros((rows, HD), F32)
        for first in range(0, columns, HD):
            part = x_ref[0, tick, :, first : first + HD].astype(F32)
            squares = squares + part * part
        mean = jnp.sum(squares, axis=1, keepdims=True) * (1.0 / columns)
        inverse = jnp.broadcast_to(lax.rsqrt(mean + EPSILON), (rows, HD))
        inverse_ref[tick] = inverse
        for first in range(0, columns, HD):
            here = slice(first, first + HD)
            normed = x_ref[0, tick, :, here].astype(F32) * inverse
            query_ref[tick, :, here] = (normed * gain_ref[:, here]).astype(BF16)


class Group:
    def __init__(self, sizes, turn):
        self.rows, self.group = sizes[0], sizes[4]
        width = self.group * HD
        self.head_group = lax.axis_index("tp") ^ turn
        self.first = pl.multiple_of(self.head_group * width, width)

    def head(self, index):
        return pl.ds(self.first + index * HD, HD)

    def stacked(self, load):
        return jnp.concatenate([load(self.head(index)) for index in range(self.group)], axis=0)

    def unstacked(self, value):
        return [value[index * self.rows : (index + 1) * self.rows] for index in range(self.group)]


def arriving_from(refs):
    if len(refs) == 1:
        return lambda where: refs[0][0, :, where]
    last = lax.axis_index("pipe") == lax.axis_size("pipe") - 1
    return lambda where: jnp.where(last, refs[1][0, :, where], refs[0][:, where])


def visible_keys(sizes, tick, doc_ref):
    rows, half, cycle, tp_count, group, columns = sizes
    cycle_place = lax.axis_index("ctx")
    tp_place = lax.axis_index("tp")
    parity = tp_place // (tp_count // 2)
    stacked = group * rows

    def section_first(owner):
        return half * jnp.where(parity == 0, owner, 2 * cycle - 1 - owner)

    row_first = section_first(cycle_place) + (tp_place % (tp_count // 2)) * rows
    query_pos = row_first + (lax.broadcasted_iota(jnp.int32, (1, stacked), 1) & (rows - 1))
    key_place = lax.broadcasted_iota(jnp.int32, (cycle * half, 1), 0)
    key_pos = key_place + section_first(cycle_place)
    for turn in range(1, cycle):
        first = section_first((cycle_place - turn + cycle) % cycle)
        key_pos = jnp.where(key_place >= turn * half, key_place - turn * half + first, key_pos)
    micro = lax.axis_index("pipe") + tick
    closing = jnp.int32(0)
    query_start = jnp.zeros((1, stacked), jnp.int32)
    for doc in range(doc_ref.shape[1]):
        length = doc_ref[micro, doc]
        closing = closing + length
        query_start = query_start + jnp.where(closing <= query_pos, length, 0)
    return (key_pos <= query_pos) & (key_pos >= query_start)


def probabilities(visible, products):
    scores = jnp.where(visible, SCALE * products, FILL)
    weights = jnp.exp(scores - jnp.max(scores, axis=0, keepdims=True))
    return weights * (1.0 / jnp.sum(weights, axis=0, keepdims=True))


def score_grads(probs, prob_grad):
    row_term = jnp.sum(probs * prob_grad, axis=0, keepdims=True)
    return (probs * (prob_grad - row_term)).astype(BF16)


class Keys:
    def __init__(self, sizes, tick, refs):
        self.near_count = sizes[3] // 2
        self.cycle = sizes[2]
        self.tick = tick
        self.refs = refs

    def __call__(self, turn, kind):
        near, far = turn % self.near_count, turn // self.near_count
        parts = [self.refs[near][self.tick, far, kind]]
        for step in range(1, self.cycle):
            if self.tick:
                parts.append(self.refs[self.near_count + step - 1][near, far, kind])
            else:
                parts.append(self.refs[step * self.near_count + near][far, kind])
        return jnp.concatenate(parts, axis=0)


def place_of(sizes, far, kind):
    half = sizes[1]
    return slice((far * 2 + kind) * half, (far * 2 + kind + 1) * half)


def gain_terms(columns_of, low_parts, normed_of, gain_rows_ref):
    rows = []
    for index, low in enumerate(low_parts):
        term = low.astype(F32) * normed_of(columns_of.head(index))
        rows.append(jnp.sum(term, axis=0, keepdims=True))
    group = columns_of.group
    place = pl.ds(pl.multiple_of(columns_of.head_group * group, group), group)
    gain_rows_ref[place, :] = jnp.concatenate(rows, axis=0)


def write_input_grads(sizes, tick, x_ref, gain_ref, inverse, query_grad_ref, arriving, write):
    rows, columns = sizes[0], sizes[5]
    coupled = jnp.zeros((rows, HD), F32)
    for first in range(0, columns, HD):
        here = slice(first, first + HD)
        scaled = query_grad_ref[:, here].astype(F32) * gain_ref[:, here]
        coupled = coupled + scaled * (x_ref[0, tick, :, here].astype(F32) * inverse)
    coupling = jnp.sum(coupled, axis=1, keepdims=True) * (1.0 / columns)
    for first in range(0, columns, HD):
        here = slice(first, first + HD)
        scaled = query_grad_ref[:, here].astype(F32) * gain_ref[:, here]
        normed = x_ref[0, tick, :, here].astype(F32) * inverse
        result = arriving(here).astype(F32) + inverse * (scaled - normed * coupling)
        write(here, result.astype(BF16))


def first_rows_kernel(sizes, kv_count, *refs):
    tp_count = sizes[3]
    turns = range(tp_count)
    doc_ref, x_ref, gain_ref, query_ref, inverse_ref, waiting_ref = refs[:6]
    keys = Keys(sizes, 0, refs[6 : 6 + kv_count])
    input_grad_ref, query_grad_ref, dscore_ref, probs_ref = refs[6 + kv_count :]
    visible = visible_keys(sizes, 0, doc_ref)
    arriving = arriving_from([waiting_ref])
    columns_of = [Group(sizes, turn) for turn in turns]
    scores, prob_grads = [], []
    for turn in turns:
        query = columns_of[turn].stacked(lambda where: query_ref[0, :, where])
        scores.append(dot(keys(turn, 0), query, NT))
        grad = columns_of[turn].stacked(arriving)
        prob_grads.append(dot(keys(turn, 1), grad, NT))
    dscores = []
    for turn in turns:
        probs = probabilities(visible, scores[turn])
        dscores.append(score_grads(probs, prob_grads[turn]))
        dscore_ref[turn] = dscores[turn]
        probs_ref[turn] = probs.astype(BF16)
    for turn in turns:
        query_grad = (SCALE * dot(dscores[turn], keys(turn, 0), TN)).astype(BF16)
        for index, low in enumerate(columns_of[turn].unstacked(query_grad)):
            query_grad_ref[:, columns_of[turn].head(index)] = low

    def write(here, result):
        input_grad_ref[:, here] = result

    write_input_grads(
        sizes, 0, x_ref, gain_ref, inverse_ref[0], query_grad_ref, arriving, write
    )


def first_keys_kernel(sizes, *refs):
    half, cycle, tp_count = sizes[1:4]
    x_ref, query_ref, inverse_ref, waiting_ref, query_grad_ref, dscore_ref, probs_ref = refs[:7]
    gain_rows_ref, own_ref = refs[7:9]
    send_refs = refs[9:]
    arriving = arriving_from([waiting_ref])
    inverse = inverse_ref[0]
    for turn in range(tp_count):
        columns_of = Group(sizes, turn)
        query = columns_of.stacked(lambda where: query_ref[0, :, where])
        grad = columns_of.stacked(arriving)
        near, far = turn % (tp_count // 2), turn // (tp_count // 2)
        for kind, part in enumerate(
            (SCALE * dot(dscore_ref[turn], query, NN), dot(probs_ref[turn], grad, NN))
        ):
            here = place_of(sizes, far, kind)
            own_ref[near, here, :] = part[:half]
            for step, ref in enumerate(send_refs, 1):
                ref[near, here, :] = part[step * half : (step + 1) * half].astype(BF16)
        gain_terms(
            columns_of,
            [query_grad_ref[:, columns_of.head(index)] for index in range(columns_of.group)],
            lambda where: x_ref[0, 0, :, where].astype(F32) * inverse,
            gain_rows_ref,
        )


def second_probs_kernel(sizes, kv_count, *refs):
    turns = range(sizes[3])
    doc_ref, query_ref = refs[:2]
    keys, probs_ref = Keys(sizes, 1, refs[2 : 2 + kv_count]), refs[2 + kv_count]
    visible = visible_keys(sizes, 1, doc_ref)
    scores = []
    for turn in turns:
        query = Group(sizes, turn).stacked(lambda where: query_ref[1, :, where])
        scores.append(dot(keys(turn, 0), query, NT))
    for turn in turns:
        probs_ref[turn] = probabilities(visible, scores[turn])


def second_keys_kernel(sizes, kv_count, *refs):
    half, cycle, tp_count = sizes[1:4]
    turns = range(tp_count)
    near_count = tp_count // 2
    x_ref, query_ref, inverse_ref, arrived_ref, output_ref, probs_ref, before_ref = refs[:7]
    keys, refs = Keys(sizes, 1, refs[7 : 7 + kv_count]), refs[7 + kv_count :]
    first_refs, refs = refs[:cycle], refs[cycle:]
    query_grad_ref, gain_rows_ref, own_ref, own_first_ref = refs[:4]
    message_refs, gain_scratch = refs[4:-1], refs[-1]
    arriving = arriving_from([arrived_ref, output_ref])
    inverse = inverse_ref[1]
    columns_of = [Group(sizes, turn) for turn in turns]
    grads = [columns_of[turn].stacked(arriving) for turn in turns]
    prob_grads = [dot(keys(turn, 1), grads[turn], NT) for turn in turns]
    value_grads = [dot(probs_ref[turn].astype(BF16), grads[turn], NN) for turn in turns]
    dscores = [score_grads(probs_ref[turn], prob_grads[turn]) for turn in turns]
    query_grads = [
        (SCALE * dot(dscores[turn], keys(turn, 0), TN)).astype(BF16) for turn in turns
    ]
    for turn in turns:
        query = columns_of[turn].stacked(lambda where: query_ref[1, :, where])
        key_grad = SCALE * dot(dscores[turn], query, NN)
        near, far = turn % near_count, turn // near_count
        for kind, part in enumerate((key_grad, value_grads[turn])):
            here = place_of(sizes, far, kind)
            for step in range(cycle):
                piece = part[step * half : (step + 1) * half]
                if step == 0 and near == 0:
                    own_ref[here, :] = piece
                else:
                    message_refs[step * near_count + near - 1][here, :] = piece.astype(BF16)
    for turn in turns:
        low_parts = columns_of[turn].unstacked(query_grads[turn])
        for index, low in enumerate(low_parts):
            query_grad_ref[:, columns_of[turn].head(index)] = low
        gain_terms(
            columns_of[turn],
            low_parts,
            lambda where: x_ref[0, 1, :, where].astype(F32) * inverse,
            gain_scratch,
        )
    gain_rows = gain_scratch[...] + before_ref[...]
    gain_rows_ref[...] = gain_rows
    high, low = split_two(gain_rows)
    count = high.shape[0]
    begin = own_ref.shape[0]
    for ref in message_refs:
        ref[begin : begin + count, :] = high
        ref[begin + count : begin + 2 * count, :] = low
    begin += 2 * count
    for near in range(near_count):
        total = first_refs[0][near]
        for ref in first_refs[1:]:
            total = total + ref[near].astype(F32)
        if near == 0:
            own_first_ref[...] = total
        else:
            message_refs[near - 1][begin : begin + total.shape[0], :] = total.astype(BF16)


def second_rows_kernel(sizes, *refs):
    x_ref, gain_ref, inverse_ref, arrived_ref, output_ref, query_grad_ref, first_ref = refs[:7]
    input_grads_ref = refs[7]
    input_grads_ref[0, 0] = first_ref[...]

    def write(here, result):
        input_grads_ref[0, 1, :, here] = result

    arriving = arriving_from([arrived_ref, output_ref])
    write_input_grads(
        sizes, 1, x_ref, gain_ref, inverse_ref[1], query_grad_ref, arriving, write
    )


def near_sum_kernel(sizes, *refs):
    rows, half, cycle, tp_count, group, columns = sizes
    near_count = tp_count // 2
    members = cycle * near_count
    own_ref, own_first_ref, gain_ref = refs[:3]
    message_refs = refs[3 : 3 + members - 1]
    keep_ref, gain_sum_ref, send_ref = refs[3 + members - 1 :]
    block = 2 * half
    size = 2 * block
    count = gain_ref.shape[0]
    begin = size + 2 * count
    for tick in range(2):
        for far in range(2):
            here = slice(far * block, (far + 1) * block)
            if tick:
                total = own_ref[here, :]
                for ref in message_refs:
                    total = total + ref[here, :].astype(F32)
            else:
                total = own_first_ref[here, :]
                for ref in message_refs[: near_count - 1]:
                    total = total + ref[begin + far * block : begin + (far + 1) * block, :].astype(F32)
            target = slice(tick * block, (tick + 1) * block)
            if far:
                send_ref[target, :] = total.astype(BF16)
            else:
                keep_ref[target, :] = total
    cycle_place = lax.axis_index("ctx")
    near_place = lax.axis_index("tp") % near_count
    values = [joined(*split_two(gain_ref[...]))]
    owners = [cycle_place * near_count + near_place]
    for place, ref in enumerate(message_refs, 1):
        step, near = place // near_count, place % near_count
        values.append(joined(ref[size : size + count, :], ref[size + count : size + 2 * count, :]))
        owners.append(((cycle_place + step) % cycle) * near_count + (near_place ^ near))
    gain = in_order(values, owners)
    gain_sum_ref[...] = gain
    high, low = split_two(gain)
    send_ref[size : size + count, :] = high
    send_ref[size + count : size + 2 * count, :] = low


def finish_kernel(sizes, keep_ref, gain_ref, receive_ref, key_ref, value_ref, gain_out_ref):
    rows, half, cycle, tp_count, group, columns = sizes
    parity = lax.axis_index("tp") // (tp_count // 2)
    block = 2 * half
    for tick in range(2):
        for kind, out in enumerate((key_ref, value_ref)):
            here = slice(tick * block + kind * half, tick * block + (kind + 1) * half)
            own_first = pl.multiple_of(parity * half, half)
            other_first = pl.multiple_of((1 - parity) * half, half)
            out[0, tick, pl.ds(own_first, half), :] = keep_ref[here, :]
            out[0, tick, pl.ds(other_first, half), :] = receive_ref[here, :].astype(F32)
    count = gain_ref.shape[0]
    size = 2 * block
    own = joined(*split_two(gain_ref[...]))
    other = joined(receive_ref[size : size + count, :], receive_ref[size + count :, :])
    gain_out_ref[...] = own + other


def shape(dims, dtype):
    return jax.ShapeDtypeStruct(dims, dtype)


def on_device(segment_inputs, keys, values, norm_gain, waiting_grads, output_grads, doc_lengths):
    cycle = lax.axis_size("ctx")
    tp_count = lax.axis_size("tp")
    pipe_count = lax.axis_size("pipe")
    _, ticks, rows, columns = segment_inputs.shape
    half = keys.shape[2] // 2
    group = columns // (tp_count * HD)
    gain_count = columns // HD
    sizes = (rows, half, cycle, tp_count, group, columns)
    block = 2 * half
    key_count = cycle * half
    stacked = group * rows
    score_bytes = key_count * stacked * 4
    usual_limit = min(56 << 20, (12 << 20) + 20 * score_bytes)

    def call(
        kernel, name, operands, out_shape, memory=pltpu.VMEM, scratch=(), scalars=0, limit=None
    ):
        in_specs = [pl.BlockSpec(memory_space=pltpu.SMEM)] * scalars
        in_specs += [pl.BlockSpec(memory_space=memory)] * (len(operands) - scalars)
        return pl.pallas_call(
            kernel,
            out_shape=out_shape,
            in_specs=in_specs,
            out_specs=[pl.BlockSpec(memory_space=pltpu.VMEM)] * len(out_shape),
            scratch_shapes=scratch,
            compiler_params=pltpu.CompilerParams(vmem_limit_bytes=limit or usual_limit),
            name=name,
        )(*operands)

    near_count = tp_count // 2

    def to_near(value, step, near):
        if step == 0:
            return lax.ppermute(value, "tp", [(i, i ^ near) for i in range(tp_count)])
        if near == 0:
            return lax.ppermute(value, "ctx", [(i, (i + step) % cycle) for i in range(cycle)])
        pairs = [
            (c * tp_count + t, ((c + step) % cycle) * tp_count + (t ^ near))
            for c in range(cycle)
            for t in range(tp_count)
        ]
        return lax.ppermute(value, ("ctx", "tp"), pairs)

    def to_far(value):
        return lax.ppermute(value, "tp", [(i, i ^ near_count) for i in range(tp_count)])

    sections = shape((ticks, 2, half, HD), BF16)
    own_kv, other_kv = call(
        functools.partial(pack_kernel, tp_count, half),
        "pack_kv",
        (keys, values),
        [sections, sections],
        memory=pl.ANY,
        scratch=[pltpu.SemaphoreType.DMA((2, ticks, 2))],
        limit=60 << 20,
    )
    pair = jnp.stack([own_kv, to_far(other_kv)], axis=1)
    near_kv = [pair] + [to_near(pair, 0, near) for near in range(1, near_count)]
    kv_first = near_kv + [
        to_near(pair[0], step, near) for step in range(1, cycle) for near in range(near_count)
    ]
    later = jnp.stack([part[1] for part in near_kv])
    kv_second = near_kv + [to_near(later, step, 0) for step in range(1, cycle)]
    queries, inverse = call(
        norm_kernel,
        "norm",
        (segment_inputs, norm_gain),
        [shape((ticks, rows, columns), BF16), shape((ticks, rows, HD), F32)],
    )

    low_rows = shape((rows, columns), BF16)
    low_scores = shape((tp_count, key_count, stacked), BF16)
    input_grad_first, query_grad_first, dscore_first, probs_first = call(
        functools.partial(first_rows_kernel, sizes, len(kv_first)),
        "first_rows",
        (doc_lengths, segment_inputs, norm_gain, queries, inverse, waiting_grads, *kv_first),
        [low_rows, low_rows, low_scores, low_scores],
        scalars=1,
    )
    arrived = lax.ppermute(
        input_grad_first, "pipe", [(i, (i - 1) % pipe_count) for i in range(pipe_count)]
    )
    gain_shape = shape((gain_count, HD), F32)
    first_sums = (near_count, 2 * block, HD)
    gain_first, *sums_first = call(
        functools.partial(first_keys_kernel, sizes),
        "first_keys",
        (
            segment_inputs,
            queries,
            inverse,
            waiting_grads,
            query_grad_first,
            dscore_first,
            probs_first,
        ),
        [gain_shape, shape(first_sums, F32)] + [shape(first_sums, BF16)] * (cycle - 1),
    )
    sums_first = sums_first[:1] + [
        to_near(value, -step, 0) for step, value in enumerate(sums_first[1:], 1)
    ]
    (probs_second,) = call(
        functools.partial(second_probs_kernel, sizes, len(kv_second)),
        "second_probs",
        (doc_lengths, queries, *kv_second),
        [shape((tp_count, key_count, stacked), F32)],
        scalars=1,
    )
    places = [(step, near) for step in range(cycle) for near in range(near_count)][1:]
    pair_rows = 2 * block
    own_shape = shape((pair_rows, HD), F32)
    messages = [
        shape((pair_rows * (2 if step == 0 else 1) + 2 * gain_count, HD), BF16)
        for step, near in places
    ]
    query_grad_second, gain_rows, own_second, own_first, *sends = call(
        functools.partial(second_keys_kernel, sizes, len(kv_second)),
        "second_keys",
        (
            segment_inputs,
            queries,
            inverse,
            arrived,
            output_grads,
            probs_second,
            gain_first,
            *kv_second,
            *sums_first,
        ),
        [low_rows, gain_shape, own_shape, own_shape] + messages,
        scratch=[pltpu.VMEM((gain_count, HD), F32)],
    )
    received = [to_near(value, -step, near) for value, (step, near) in zip(sends, places)]
    (input_grads,) = call(
        functools.partial(second_rows_kernel, sizes),
        "second_rows",
        (
            segment_inputs,
            norm_gain,
            inverse,
            arrived,
            output_grads,
            query_grad_second,
            input_grad_first,
        ),
        [shape((1, ticks, rows, columns), BF16)],
    )
    keep, gain_sum, send = call(
        functools.partial(near_sum_kernel, sizes),
        "near_sum",
        (own_second, own_first, gain_rows, *received),
        [own_shape, gain_shape, shape((pair_rows + 2 * gain_count, HD), BF16)],
    )
    grads_shape = shape((1, ticks, block, HD), F32)
    key_grads, value_grads, gain_grads = call(
        functools.partial(finish_kernel, sizes),
        "finish",
        (keep, gain_sum, to_far(send)),
        [grads_shape, grads_shape, gain_shape],
    )
    return input_grads, key_grads, value_grads, gain_grads.reshape(1, columns)


def solution(mesh):
    in_specs = (
        P("pipe", None, ("ctx", "tp"), None),
        P("pipe", None, "ctx", "tp"),
        P("pipe", None, "ctx", "tp"),
        P("pipe", None),
        P("pipe", ("ctx", "tp"), None),
        P(None, ("ctx", "tp"), None),
        P(),
    )
    out_specs = (
        P("pipe", None, ("ctx", "tp"), None),
        P("pipe", None, "ctx", "tp"),
        P("pipe", None, "ctx", "tp"),
        P("pipe", None),
    )
    return jax.shard_map(
        on_device, mesh=mesh, in_specs=in_specs, out_specs=out_specs, check_vma=False
    )
```

```python
import functools

import jax
import jax.numpy as jnp
from jax import lax
from jax.experimental import pallas as pl
from jax.experimental.pallas import tpu as pltpu
from jax.sharding import PartitionSpec as P

HD = 128
EPSILON = 1e-05
FILL = -1e30
SCALE = HD ** (-0.5)
TICKS = 2
F32 = jnp.float32
BF16 = jnp.bfloat16

NT = (((1,), (1,)), ((), ()))
NN = (((1,), (0,)), ((), ()))
TN = (((0,), (0,)), ((), ()))


def dot(a, b, dims):
    return lax.dot_general(a, b, dims, preferred_element_type=F32)


def split_two(value):
    high = value.astype(BF16)
    low = (value - high.astype(F32)).astype(BF16)
    return high, low


def joined(high, low):
    return high.astype(F32) + low.astype(F32)


def in_order(values, owners):
    total = None
    for owner in range(len(values)):
        term = jnp.where(owners[0] == owner, values[0], 0.0)
        for value, whose in zip(values[1:], owners[1:]):
            term = jnp.where(whose == owner, value, term)
        total = term if total is None else total + term
    return total


def pack_kernel(tp_count, half, both_ref, own_ref, other_ref):
    parity = lax.axis_index("tp") // (tp_count // 2)
    own_first = pl.multiple_of(parity * half, half)
    other_first = pl.multiple_of((1 - parity) * half, half)
    for kind in range(2):
        for tick in range(TICKS):
            own_ref[tick, kind] = both_ref[kind, tick, pl.ds(own_first, half), :]
            other_ref[tick, kind] = both_ref[kind, tick, pl.ds(other_first, half), :]


def norm_kernel(x_ref, gain_ref, query_ref, inverse_ref):
    _, ticks, rows, columns = x_ref.shape
    for tick in range(ticks):
        squares = jnp.zeros((rows, HD), F32)
        for first in range(0, columns, HD):
            part = x_ref[0, tick, :, first : first + HD].astype(F32)
            squares = squares + part * part
        mean = jnp.sum(squares, axis=1, keepdims=True) * (1.0 / columns)
        inverse = jnp.broadcast_to(lax.rsqrt(mean + EPSILON), (rows, HD))
        inverse_ref[tick] = inverse
        for first in range(0, columns, HD):
            here = slice(first, first + HD)
            normed = x_ref[0, tick, :, here].astype(F32) * inverse
            query_ref[tick, :, here] = (normed * gain_ref[:, here]).astype(BF16)


class Group:
    def __init__(self, sizes, turn):
        self.rows, self.group = sizes[0], sizes[4]
        width = self.group * HD
        self.head_group = lax.axis_index("tp") ^ turn
        self.first = pl.multiple_of(self.head_group * width, width)

    def head(self, index):
        return pl.ds(self.first + index * HD, HD)

    def stacked(self, load):
        return jnp.concatenate([load(self.head(index)) for index in range(self.group)], axis=0)

    def unstacked(self, value):
        return [value[index * self.rows : (index + 1) * self.rows] for index in range(self.group)]


def arriving_from(refs):
    if len(refs) == 1:
        return lambda where: refs[0][0, :, where]
    last = lax.axis_index("pipe") == lax.axis_size("pipe") - 1
    return lambda where: jnp.where(last, refs[1][0, :, where], refs[0][:, where])


def visible_keys(sizes, tick, doc_ref):
    rows, half, cycle, tp_count, group, columns = sizes
    cycle_place = lax.axis_index("ctx")
    tp_place = lax.axis_index("tp")
    parity = tp_place // (tp_count // 2)
    stacked = group * rows

    def section_first(owner):
        return half * jnp.where(parity == 0, owner, 2 * cycle - 1 - owner)

    row_first = section_first(cycle_place) + (tp_place % (tp_count // 2)) * rows
    query_pos = row_first + (lax.broadcasted_iota(jnp.int32, (1, stacked), 1) & (rows - 1))
    key_place = lax.broadcasted_iota(jnp.int32, (cycle * half, 1), 0)
    key_pos = key_place + section_first(cycle_place)
    for turn in range(1, cycle):
        first = section_first((cycle_place - turn + cycle) % cycle)
        key_pos = jnp.where(key_place >= turn * half, key_place - turn * half + first, key_pos)
    micro = lax.axis_index("pipe") + tick
    closing = jnp.int32(0)
    query_start = jnp.zeros((1, stacked), jnp.int32)
    for doc in range(doc_ref.shape[1]):
        length = doc_ref[micro, doc]
        closing = closing + length
        query_start = query_start + jnp.where(closing <= query_pos, length, 0)
    return (key_pos <= query_pos) & (key_pos >= query_start)


def probabilities(visible, products):
    scores = jnp.where(visible, SCALE * products, FILL)
    weights = jnp.exp(scores - jnp.max(scores, axis=0, keepdims=True))
    return weights * (1.0 / jnp.sum(weights, axis=0, keepdims=True))


def score_grads(probs, prob_grad):
    row_term = jnp.sum(probs * prob_grad, axis=0, keepdims=True)
    return (probs * (prob_grad - row_term)).astype(BF16)


class Keys:
    def __init__(self, sizes, tick, refs):
        self.near_count = sizes[3] // 2
        self.tick = tick
        self.refs = refs

    def __call__(self, turn, kind):
        near, far = turn % self.near_count, turn // self.near_count
        parts = [ref[self.tick, far, kind] for ref in self.refs[near :: self.near_count]]
        return jnp.concatenate(parts, axis=0)


def place_of(sizes, far, kind):
    half = sizes[1]
    return slice((far * 2 + kind) * half, (far * 2 + kind + 1) * half)


def put_key_grads(sizes, turn, parts, own_ref, message_refs):
    half, cycle, tp_count = sizes[1:4]
    near_count = tp_count // 2
    near, far = turn % near_count, turn // near_count
    for kind, part in enumerate(parts):
        here = place_of(sizes, far, kind)
        for step in range(cycle):
            piece = part[step * half : (step + 1) * half]
            if step == 0 and near == 0:
                own_ref[here, :] = piece
            else:
                message_refs[step * near_count + near - 1][here, :] = piece.astype(BF16)


def gain_terms(columns_of, low_parts, normed_of, gain_rows_ref):
    rows = []
    for index, low in enumerate(low_parts):
        term = low.astype(F32) * normed_of(columns_of.head(index))
        rows.append(jnp.sum(term, axis=0, keepdims=True))
    group = columns_of.group
    place = pl.ds(pl.multiple_of(columns_of.head_group * group, group), group)
    gain_rows_ref[place, :] = jnp.concatenate(rows, axis=0)


def write_input_grads(sizes, tick, x_ref, gain_ref, inverse, query_grad_ref, arriving, write):
    rows, columns = sizes[0], sizes[5]
    coupled = jnp.zeros((rows, HD), F32)
    for first in range(0, columns, HD):
        here = slice(first, first + HD)
        scaled = query_grad_ref[:, here].astype(F32) * gain_ref[:, here]
        coupled = coupled + scaled * (x_ref[0, tick, :, here].astype(F32) * inverse)
    coupling = jnp.sum(coupled, axis=1, keepdims=True) * (1.0 / columns)
    for first in range(0, columns, HD):
        here = slice(first, first + HD)
        scaled = query_grad_ref[:, here].astype(F32) * gain_ref[:, here]
        normed = x_ref[0, tick, :, here].astype(F32) * inverse
        result = arriving(here).astype(F32) + inverse * (scaled - normed * coupling)
        write(here, result.astype(BF16))


def first_rows_kernel(sizes, kv_count, *refs):
    tp_count = sizes[3]
    turns = range(tp_count)
    doc_ref, x_ref, gain_ref, query_ref, inverse_ref, waiting_ref = refs[:6]
    keys = Keys(sizes, 0, refs[6 : 6 + kv_count])
    input_grad_ref, query_grad_ref, dscore_ref, probs_ref = refs[6 + kv_count :]
    visible = visible_keys(sizes, 0, doc_ref)
    arriving = arriving_from([waiting_ref])
    columns_of = [Group(sizes, turn) for turn in turns]
    scores, prob_grads = [], []
    for turn in turns:
        query = columns_of[turn].stacked(lambda where: query_ref[0, :, where])
        scores.append(dot(keys(turn, 0), query, NT))
        grad = columns_of[turn].stacked(arriving)
        prob_grads.append(dot(keys(turn, 1), grad, NT))
    dscores = []
    for turn in turns:
        probs = probabilities(visible, scores[turn])
        dscores.append(score_grads(probs, prob_grads[turn]))
        dscore_ref[turn] = dscores[turn]
        probs_ref[turn] = probs.astype(BF16)
    for turn in turns:
        query_grad = (SCALE * dot(dscores[turn], keys(turn, 0), TN)).astype(BF16)
        for index, low in enumerate(columns_of[turn].unstacked(query_grad)):
            query_grad_ref[:, columns_of[turn].head(index)] = low

    def write(here, result):
        input_grad_ref[:, here] = result

    write_input_grads(
        sizes, 0, x_ref, gain_ref, inverse_ref[0], query_grad_ref, arriving, write
    )


def first_keys_kernel(sizes, *refs):
    half, cycle, tp_count = sizes[1:4]
    x_ref, query_ref, inverse_ref, waiting_ref, query_grad_ref, dscore_ref, probs_ref = refs[:7]
    gain_rows_ref, own_ref = refs[7:9]
    send_refs = refs[9:]
    arriving = arriving_from([waiting_ref])
    inverse = inverse_ref[0]
    for turn in range(tp_count):
        columns_of = Group(sizes, turn)
        query = columns_of.stacked(lambda where: query_ref[0, :, where])
        grad = columns_of.stacked(arriving)
        parts = (SCALE * dot(dscore_ref[turn], query, NN), dot(probs_ref[turn], grad, NN))
        near, far = turn % (tp_count // 2), turn // (tp_count // 2)
        for kind, part in enumerate(parts):
            here = place_of(sizes, far, kind)
            own_ref[near, here, :] = part[:half]
            for step, ref in enumerate(send_refs, 1):
                ref[near, here, :] = part[step * half : (step + 1) * half].astype(BF16)
        gain_terms(
            columns_of,
            [query_grad_ref[:, columns_of.head(index)] for index in range(columns_of.group)],
            lambda where: x_ref[0, 0, :, where].astype(F32) * inverse,
            gain_rows_ref,
        )


def second_probs_kernel(sizes, kv_count, *refs):
    turns = range(sizes[3])
    doc_ref, query_ref = refs[:2]
    keys, probs_ref = Keys(sizes, 1, refs[2 : 2 + kv_count]), refs[2 + kv_count]
    visible = visible_keys(sizes, 1, doc_ref)
    scores = []
    for turn in turns:
        query = Group(sizes, turn).stacked(lambda where: query_ref[1, :, where])
        scores.append(dot(keys(turn, 0), query, NT))
    for turn in turns:
        probs_ref[turn] = probabilities(visible, scores[turn])


def second_keys_kernel(sizes, *refs):
    cycle, tp_count = sizes[2:4]
    turns = range(tp_count)
    members = cycle * (tp_count // 2)
    x_ref, query_ref, inverse_ref, arrived_ref, output_ref, probs_ref, before_ref = refs[:7]
    keys, refs = Keys(sizes, 1, refs[7 : 7 + members]), refs[7 + members :]
    first_refs, refs = refs[:cycle], refs[cycle:]
    query_grad_ref, gain_rows_ref, own_ref, own_first_ref = refs[:4]
    message_refs, gain_scratch = refs[4:-1], refs[-1]
    arriving = arriving_from([arrived_ref, output_ref])
    inverse = inverse_ref[1]
    columns_of = [Group(sizes, turn) for turn in turns]
    grads = [columns_of[turn].stacked(arriving) for turn in turns]
    prob_grads = [dot(keys(turn, 1), grads[turn], NT) for turn in turns]
    value_grads = [dot(probs_ref[turn].astype(BF16), grads[turn], NN) for turn in turns]
    dscores = [score_grads(probs_ref[turn], prob_grads[turn]) for turn in turns]
    query_grads = [
        (SCALE * dot(dscores[turn], keys(turn, 0), TN)).astype(BF16) for turn in turns
    ]
    for turn in turns:
        query = columns_of[turn].stacked(lambda where: query_ref[1, :, where])
        key_grad = SCALE * dot(dscores[turn], query, NN)
        put_key_grads(sizes, turn, (key_grad, value_grads[turn]), own_ref, message_refs)
    for turn in turns:
        low_parts = columns_of[turn].unstacked(query_grads[turn])
        for index, low in enumerate(low_parts):
            query_grad_ref[:, columns_of[turn].head(index)] = low
        gain_terms(
            columns_of[turn],
            low_parts,
            lambda where: x_ref[0, 1, :, where].astype(F32) * inverse,
            gain_scratch,
        )
    gain_rows = gain_scratch[...] + before_ref[...]
    gain_rows_ref[...] = gain_rows
    high, low = split_two(gain_rows)
    count = high.shape[0]
    begin = own_ref.shape[0]
    for ref in message_refs:
        ref[begin : begin + count, :] = high
        ref[begin + count : begin + 2 * count, :] = low
    begin += 2 * count
    for near in range(tp_count // 2):
        total = first_refs[0][near]
        for ref in first_refs[1:]:
            total = total + ref[near].astype(F32)
        if near == 0:
            own_first_ref[...] = total
        else:
            message_refs[near - 1][begin:, :] = total.astype(BF16)


def second_rows_kernel(sizes, *refs):
    x_ref, gain_ref, inverse_ref, arrived_ref, output_ref, query_grad_ref, first_ref = refs[:7]
    input_grads_ref = refs[7]
    input_grads_ref[0, 0] = first_ref[...]

    def write(here, result):
        input_grads_ref[0, 1, :, here] = result

    arriving = arriving_from([arrived_ref, output_ref])
    write_input_grads(
        sizes, 1, x_ref, gain_ref, inverse_ref[1], query_grad_ref, arriving, write
    )


def near_sum_kernel(sizes, *refs):
    rows, half, cycle, tp_count, group, columns = sizes
    near_count = tp_count // 2
    members = cycle * near_count
    own_refs, gain_ref = refs[:TICKS], refs[TICKS]
    message_refs = refs[TICKS + 1 : TICKS + members]
    keep_ref, gain_sum_ref, send_ref = refs[TICKS + members :]
    block = 2 * half
    size = TICKS * block
    count = gain_ref.shape[0]
    after = 2 * block + 2 * count
    for tick in range(TICKS):
        for far in range(2):
            here = slice(far * block, (far + 1) * block)
            there = here if tick else slice(after + here.start, after + here.stop)
            total = own_refs[tick][here, :]
            for ref in message_refs if tick else message_refs[: near_count - 1]:
                total = total + ref[there, :].astype(F32)
            target = slice(tick * block, (tick + 1) * block)
            if far:
                send_ref[target, :] = total.astype(BF16)
            else:
                keep_ref[target, :] = total
    cycle_place = lax.axis_index("ctx")
    near_place = lax.axis_index("tp") % near_count
    values = [joined(*split_two(gain_ref[...]))]
    owners = [cycle_place * near_count + near_place]
    for place, ref in enumerate(message_refs, 1):
        step, near = place // near_count, place % near_count
        begin = 2 * block
        values.append(
            joined(ref[begin : begin + count, :], ref[begin + count : begin + 2 * count, :])
        )
        owners.append(((cycle_place + step) % cycle) * near_count + (near_place ^ near))
    gain = in_order(values, owners)
    gain_sum_ref[...] = gain
    high, low = split_two(gain)
    send_ref[size : size + count, :] = high
    send_ref[size + count : size + 2 * count, :] = low


def finish_kernel(sizes, keep_ref, gain_ref, receive_ref, key_ref, value_ref, gain_out_ref):
    rows, half, cycle, tp_count, group, columns = sizes
    parity = lax.axis_index("tp") // (tp_count // 2)
    block = 2 * half
    for tick in range(TICKS):
        for kind, out in enumerate((key_ref, value_ref)):
            here = slice(tick * block + kind * half, tick * block + (kind + 1) * half)
            own_first = pl.multiple_of(parity * half, half)
            other_first = pl.multiple_of((1 - parity) * half, half)
            out[0, tick, pl.ds(own_first, half), :] = keep_ref[here, :]
            out[0, tick, pl.ds(other_first, half), :] = receive_ref[here, :].astype(F32)
    count = gain_ref.shape[0]
    size = 2 * block
    own = joined(*split_two(gain_ref[...]))
    other = joined(receive_ref[size : size + count, :], receive_ref[size + count :, :])
    gain_out_ref[...] = own + other


def shape(dims, dtype):
    return jax.ShapeDtypeStruct(dims, dtype)


def on_device(segment_inputs, keys, values, norm_gain, waiting_grads, output_grads, doc_lengths):
    cycle = lax.axis_size("ctx")
    tp_count = lax.axis_size("tp")
    pipe_count = lax.axis_size("pipe")
    _, ticks, rows, columns = segment_inputs.shape
    half = keys.shape[2] // 2
    group = columns // (tp_count * HD)
    gain_count = columns // HD
    sizes = (rows, half, cycle, tp_count, group, columns)
    block = 2 * half
    key_count = cycle * half
    stacked = group * rows
    score_bytes = key_count * stacked * 4
    usual_limit = min(56 << 20, (12 << 20) + 20 * score_bytes)

    def call(kernel, name, operands, out_shape, scratch=(), scalars=0):
        in_specs = [pl.BlockSpec(memory_space=pltpu.SMEM)] * scalars
        in_specs += [pl.BlockSpec(memory_space=pltpu.VMEM)] * (len(operands) - scalars)
        return pl.pallas_call(
            kernel,
            out_shape=out_shape,
            in_specs=in_specs,
            out_specs=[pl.BlockSpec(memory_space=pltpu.VMEM)] * len(out_shape),
            scratch_shapes=scratch,
            compiler_params=pltpu.CompilerParams(vmem_limit_bytes=usual_limit),
            name=name,
        )(*operands)

    near_count = tp_count // 2

    def to_near(value, step, near):
        if step == 0:
            return lax.ppermute(value, "tp", [(i, i ^ near) for i in range(tp_count)])
        if near == 0:
            return lax.ppermute(value, "ctx", [(i, (i + step) % cycle) for i in range(cycle)])
        pairs = [
            (c * tp_count + t, ((c + step) % cycle) * tp_count + (t ^ near))
            for c in range(cycle)
            for t in range(tp_count)
        ]
        return lax.ppermute(value, ("ctx", "tp"), pairs)

    def to_far(value):
        return lax.ppermute(value, "tp", [(i, i ^ near_count) for i in range(tp_count)])

    sections = shape((ticks, 2, half, HD), BF16)
    own_kv, other_kv = call(
        functools.partial(pack_kernel, tp_count, half),
        "pack_kv",
        (jnp.stack([keys[0], values[0]]),),
        [sections, sections],
    )
    pair = jnp.stack([own_kv, to_far(other_kv)], axis=1)
    places = [(step, near) for step in range(cycle) for near in range(near_count)][1:]
    kv = [pair] + [to_near(pair, step, near) for step, near in places]
    queries, inverse = call(
        norm_kernel,
        "norm",
        (segment_inputs, norm_gain),
        [shape((ticks, rows, columns), BF16), shape((ticks, rows, HD), F32)],
    )

    low_rows = shape((rows, columns), BF16)
    low_scores = shape((tp_count, key_count, stacked), BF16)
    input_grad_first, query_grad_first, dscore_first, probs_first = call(
        functools.partial(first_rows_kernel, sizes, len(kv)),
        "first_rows",
        (doc_lengths, segment_inputs, norm_gain, queries, inverse, waiting_grads, *kv),
        [low_rows, low_rows, low_scores, low_scores],
        scalars=1,
    )
    arrived = lax.ppermute(
        input_grad_first, "pipe", [(i, (i - 1) % pipe_count) for i in range(pipe_count)]
    )
    gain_shape = shape((gain_count, HD), F32)
    pair_rows = 2 * block
    own_shape = shape((pair_rows, HD), F32)
    first_sums = (near_count, pair_rows, HD)
    gain_first, *sums_first = call(
        functools.partial(first_keys_kernel, sizes),
        "first_keys",
        (
            segment_inputs,
            queries,
            inverse,
            waiting_grads,
            query_grad_first,
            dscore_first,
            probs_first,
        ),
        [gain_shape, shape(first_sums, F32)] + [shape(first_sums, BF16)] * (cycle - 1),
    )
    sums_first = sums_first[:1] + [
        to_near(value, -step, 0) for step, value in enumerate(sums_first[1:], 1)
    ]
    (probs_second,) = call(
        functools.partial(second_probs_kernel, sizes, len(kv)),
        "second_probs",
        (doc_lengths, queries, *kv),
        [shape((tp_count, key_count, stacked), F32)],
        scalars=1,
    )
    messages = [
        shape((pair_rows * (2 if step == 0 else 1) + 2 * gain_count, HD), BF16)
        for step, near in places
    ]
    query_grad_second, gain_rows, own_second, own_first, *sends = call(
        functools.partial(second_keys_kernel, sizes),
        "second_keys",
        (
            segment_inputs,
            queries,
            inverse,
            arrived,
            output_grads,
            probs_second,
            gain_first,
            *kv,
            *sums_first,
        ),
        [low_rows, gain_shape, own_shape, own_shape] + messages,
        scratch=[pltpu.VMEM((gain_count, HD), F32)],
    )
    received = [to_near(value, -step, near) for value, (step, near) in zip(sends, places)]
    (input_grads,) = call(
        functools.partial(second_rows_kernel, sizes),
        "second_rows",
        (
            segment_inputs,
            norm_gain,
            inverse,
            arrived,
            output_grads,
            query_grad_second,
            input_grad_first,
        ),
        [shape((1, ticks, rows, columns), BF16)],
    )
    keep, gain_sum, send = call(
        functools.partial(near_sum_kernel, sizes),
        "near_sum",
        (own_first, own_second, gain_rows, *received),
        [own_shape, gain_shape, shape((pair_rows + 2 * gain_count, HD), BF16)],
    )
    grads_shape = shape((1, ticks, block, HD), F32)
    key_grads, value_grads, gain_grads = call(
        functools.partial(finish_kernel, sizes),
        "finish",
        (keep, gain_sum, to_far(send)),
        [grads_shape, grads_shape, gain_shape],
    )
    return input_grads, key_grads, value_grads, gain_grads.reshape(1, columns)


def solution(mesh):
    in_specs = (
        P("pipe", None, ("ctx", "tp"), None),
        P("pipe", None, "ctx", "tp"),
        P("pipe", None, "ctx", "tp"),
        P("pipe", None),
        P("pipe", ("ctx", "tp"), None),
        P(None, ("ctx", "tp"), None),
        P(),
    )
    out_specs = (
        P("pipe", None, ("ctx", "tp"), None),
        P("pipe", None, "ctx", "tp"),
        P("pipe", None, "ctx", "tp"),
        P("pipe", None),
    )
    return jax.shard_map(
        on_device, mesh=mesh, in_specs=in_specs, out_specs=out_specs, check_vma=False
    )
```

```python
import functools

import jax
import jax.numpy as jnp
from jax import lax
from jax.experimental import pallas as pl
from jax.experimental.pallas import tpu as pltpu
from jax.sharding import PartitionSpec as P

HD = 128
EPSILON = 1e-05
FILL = -1e30
SCALE = HD ** (-0.5)
TICKS = 2
F32 = jnp.float32
BF16 = jnp.bfloat16

NT = (((1,), (1,)), ((), ()))
NN = (((1,), (0,)), ((), ()))
TN = (((0,), (0,)), ((), ()))


def dot(a, b, dims):
    return lax.dot_general(a, b, dims, preferred_element_type=F32)


def split_two(value):
    high = value.astype(BF16)
    low = (value - high.astype(F32)).astype(BF16)
    return high, low


def joined(high, low):
    return high.astype(F32) + low.astype(F32)


def in_order(values, owners):
    total = None
    for owner in range(len(values)):
        term = jnp.where(owners[0] == owner, values[0], 0.0)
        for value, whose in zip(values[1:], owners[1:]):
            term = jnp.where(whose == owner, value, term)
        total = term if total is None else total + term
    return total


def pack_kernel(tp_count, half, both_ref, own_ref, other_ref):
    parity = lax.axis_index("tp") // (tp_count // 2)
    own_first = pl.multiple_of(parity * half, half)
    other_first = pl.multiple_of((1 - parity) * half, half)
    for kind in range(2):
        for tick in range(TICKS):
            own_ref[tick, kind] = both_ref[kind, tick, pl.ds(own_first, half), :]
            other_ref[tick, kind] = both_ref[kind, tick, pl.ds(other_first, half), :]


def norm_kernel(x_ref, gain_ref, query_ref, inverse_ref):
    _, ticks, rows, columns = x_ref.shape
    for tick in range(ticks):
        squares = jnp.zeros((rows, HD), F32)
        for first in range(0, columns, HD):
            part = x_ref[0, tick, :, first : first + HD].astype(F32)
            squares = squares + part * part
        mean = jnp.sum(squares, axis=1, keepdims=True) * (1.0 / columns)
        inverse = jnp.broadcast_to(lax.rsqrt(mean + EPSILON), (rows, HD))
        inverse_ref[tick] = inverse
        for first in range(0, columns, HD):
            here = slice(first, first + HD)
            normed = x_ref[0, tick, :, here].astype(F32) * inverse
            query_ref[tick, :, here] = (normed * gain_ref[:, here]).astype(BF16)


class Group:
    def __init__(self, sizes, turn):
        self.rows, self.group = sizes[0], sizes[4]
        width = self.group * HD
        self.head_group = lax.axis_index("tp") ^ turn
        self.first = pl.multiple_of(self.head_group * width, width)

    def head(self, index):
        return pl.ds(self.first + index * HD, HD)

    def stacked(self, load):
        return jnp.concatenate([load(self.head(index)) for index in range(self.group)], axis=0)

    def unstacked(self, value):
        return [value[index * self.rows : (index + 1) * self.rows] for index in range(self.group)]


def arriving_from(refs):
    if len(refs) == 1:
        return lambda where: refs[0][0, :, where]
    last = lax.axis_index("pipe") == lax.axis_size("pipe") - 1
    return lambda where: jnp.where(last, refs[1][0, :, where], refs[0][:, where])


def visible_keys(sizes, tick, doc_ref):
    rows, half, cycle, tp_count, group, columns = sizes
    cycle_place = lax.axis_index("ctx")
    tp_place = lax.axis_index("tp")
    parity = tp_place // (tp_count // 2)
    stacked = group * rows

    def section_first(owner):
        return half * jnp.where(parity == 0, owner, 2 * cycle - 1 - owner)

    row_first = section_first(cycle_place) + (tp_place % (tp_count // 2)) * rows
    query_pos = row_first + (lax.broadcasted_iota(jnp.int32, (1, stacked), 1) & (rows - 1))
    key_place = lax.broadcasted_iota(jnp.int32, (cycle * half, 1), 0)
    key_pos = key_place + section_first(cycle_place)
    for turn in range(1, cycle):
        first = section_first((cycle_place - turn + cycle) % cycle)
        key_pos = jnp.where(key_place >= turn * half, key_place - turn * half + first, key_pos)
    micro = lax.axis_index("pipe") + tick
    closing = jnp.int32(0)
    query_start = jnp.zeros((1, stacked), jnp.int32)
    for doc in range(doc_ref.shape[1]):
        length = doc_ref[micro, doc]
        closing = closing + length
        query_start = query_start + jnp.where(closing <= query_pos, length, 0)
    return (key_pos <= query_pos) & (key_pos >= query_start)


def probabilities(visible, products):
    scores = jnp.where(visible, SCALE * products, FILL)
    weights = jnp.exp(scores - jnp.max(scores, axis=0, keepdims=True))
    return weights * (1.0 / jnp.sum(weights, axis=0, keepdims=True))


def score_grads(probs, prob_grad):
    row_term = jnp.sum(probs * prob_grad, axis=0, keepdims=True)
    return (probs * (prob_grad - row_term)).astype(BF16)


class Keys:
    def __init__(self, sizes, tick, refs):
        self.near_count = sizes[3] // 2
        self.tick = tick
        self.refs = refs

    def __call__(self, turn, kind):
        near, far = turn % self.near_count, turn // self.near_count
        count = len(self.refs) // 2
        refs = self.refs[far * count : (far + 1) * count]
        parts = [ref[self.tick, kind] for ref in refs[near :: self.near_count]]
        return jnp.concatenate(parts, axis=0)


def place_of(sizes, far, kind):
    half = sizes[1]
    return slice((far * 2 + kind) * half, (far * 2 + kind + 1) * half)


def put_key_grads(sizes, turn, parts, own_ref, message_refs):
    half, cycle, tp_count = sizes[1:4]
    near_count = tp_count // 2
    near, far = turn % near_count, turn // near_count
    for kind, part in enumerate(parts):
        here = place_of(sizes, far, kind)
        for step in range(cycle):
            piece = part[step * half : (step + 1) * half]
            if step == 0 and near == 0:
                own_ref[here, :] = piece
            else:
                message_refs[step * near_count + near - 1][here, :] = piece.astype(BF16)


def gain_terms(columns_of, low_parts, normed_of, gain_rows_ref):
    rows = []
    for index, low in enumerate(low_parts):
        term = low.astype(F32) * normed_of(columns_of.head(index))
        rows.append(jnp.sum(term, axis=0, keepdims=True))
    group = columns_of.group
    place = pl.ds(pl.multiple_of(columns_of.head_group * group, group), group)
    gain_rows_ref[place, :] = jnp.concatenate(rows, axis=0)


def write_input_grads(sizes, tick, x_ref, gain_ref, inverse, query_grad_ref, arriving, write):
    rows, columns = sizes[0], sizes[5]
    coupled = jnp.zeros((rows, HD), F32)
    for first in range(0, columns, HD):
        here = slice(first, first + HD)
        scaled = query_grad_ref[:, here].astype(F32) * gain_ref[:, here]
        coupled = coupled + scaled * (x_ref[0, tick, :, here].astype(F32) * inverse)
    coupling = jnp.sum(coupled, axis=1, keepdims=True) * (1.0 / columns)
    for first in range(0, columns, HD):
        here = slice(first, first + HD)
        scaled = query_grad_ref[:, here].astype(F32) * gain_ref[:, here]
        normed = x_ref[0, tick, :, here].astype(F32) * inverse
        result = arriving(here).astype(F32) + inverse * (scaled - normed * coupling)
        write(here, result.astype(BF16))


def first_rows_kernel(sizes, kv_count, *refs):
    tp_count = sizes[3]
    turns = range(tp_count)
    doc_ref, x_ref, gain_ref, query_ref, inverse_ref, waiting_ref = refs[:6]
    keys = Keys(sizes, 0, refs[6 : 6 + kv_count])
    input_grad_ref, query_grad_ref, dscore_ref, probs_ref = refs[6 + kv_count :]
    visible = visible_keys(sizes, 0, doc_ref)
    arriving = arriving_from([waiting_ref])
    columns_of = [Group(sizes, turn) for turn in turns]
    scores, prob_grads = [], []
    for turn in turns:
        query = columns_of[turn].stacked(lambda where: query_ref[0, :, where])
        scores.append(dot(keys(turn, 0), query, NT))
        grad = columns_of[turn].stacked(arriving)
        prob_grads.append(dot(keys(turn, 1), grad, NT))
    dscores = []
    for turn in turns:
        probs = probabilities(visible, scores[turn])
        dscores.append(score_grads(probs, prob_grads[turn]))
        dscore_ref[turn] = dscores[turn]
        probs_ref[turn] = probs.astype(BF16)
    for turn in turns:
        query_grad = (SCALE * dot(dscores[turn], keys(turn, 0), TN)).astype(BF16)
        for index, low in enumerate(columns_of[turn].unstacked(query_grad)):
            query_grad_ref[:, columns_of[turn].head(index)] = low

    def write(here, result):
        input_grad_ref[:, here] = result

    write_input_grads(
        sizes, 0, x_ref, gain_ref, inverse_ref[0], query_grad_ref, arriving, write
    )


def first_keys_kernel(sizes, *refs):
    half, cycle, tp_count = sizes[1:4]
    x_ref, query_ref, inverse_ref, waiting_ref, query_grad_ref, dscore_ref, probs_ref = refs[:7]
    gain_rows_ref, own_ref = refs[7:9]
    send_refs = refs[9:]
    arriving = arriving_from([waiting_ref])
    inverse = inverse_ref[0]
    for turn in range(tp_count):
        columns_of = Group(sizes, turn)
        query = columns_of.stacked(lambda where: query_ref[0, :, where])
        grad = columns_of.stacked(arriving)
        parts = (SCALE * dot(dscore_ref[turn], query, NN), dot(probs_ref[turn], grad, NN))
        near, far = turn % (tp_count // 2), turn // (tp_count // 2)
        for kind, part in enumerate(parts):
            here = place_of(sizes, far, kind)
            own_ref[near, here, :] = part[:half]
            for step, ref in enumerate(send_refs, 1):
                ref[near, here, :] = part[step * half : (step + 1) * half].astype(BF16)
        gain_terms(
            columns_of,
            [query_grad_ref[:, columns_of.head(index)] for index in range(columns_of.group)],
            lambda where: x_ref[0, 0, :, where].astype(F32) * inverse,
            gain_rows_ref,
        )


def second_probs_kernel(sizes, kv_count, *refs):
    turns = range(sizes[3])
    doc_ref, query_ref = refs[:2]
    keys, probs_ref = Keys(sizes, 1, refs[2 : 2 + kv_count]), refs[2 + kv_count]
    visible = visible_keys(sizes, 1, doc_ref)
    scores = []
    for turn in turns:
        query = Group(sizes, turn).stacked(lambda where: query_ref[1, :, where])
        scores.append(dot(keys(turn, 0), query, NT))
    for turn in turns:
        probs_ref[turn] = probabilities(visible, scores[turn])


def second_keys_kernel(sizes, *refs):
    cycle, tp_count = sizes[2:4]
    turns = range(tp_count)
    members = cycle * (tp_count // 2)
    x_ref, query_ref, inverse_ref, arrived_ref, output_ref, probs_ref, before_ref = refs[:7]
    keys, refs = Keys(sizes, 1, refs[7 : 7 + 2 * members]), refs[7 + 2 * members :]
    query_grad_ref, gain_rows_ref, own_ref = refs[:3]
    message_refs, gain_scratch = refs[3:-1], refs[-1]
    arriving = arriving_from([arrived_ref, output_ref])
    inverse = inverse_ref[1]
    columns_of = [Group(sizes, turn) for turn in turns]
    grads = [columns_of[turn].stacked(arriving) for turn in turns]
    prob_grads = [dot(keys(turn, 1), grads[turn], NT) for turn in turns]
    value_grads = [dot(probs_ref[turn].astype(BF16), grads[turn], NN) for turn in turns]
    dscores = [score_grads(probs_ref[turn], prob_grads[turn]) for turn in turns]
    query_grads = [
        (SCALE * dot(dscores[turn], keys(turn, 0), TN)).astype(BF16) for turn in turns
    ]
    for turn in turns:
        query = columns_of[turn].stacked(lambda where: query_ref[1, :, where])
        key_grad = SCALE * dot(dscores[turn], query, NN)
        put_key_grads(sizes, turn, (key_grad, value_grads[turn]), own_ref, message_refs)
    for turn in turns:
        low_parts = columns_of[turn].unstacked(query_grads[turn])
        for index, low in enumerate(low_parts):
            query_grad_ref[:, columns_of[turn].head(index)] = low
        gain_terms(
            columns_of[turn],
            low_parts,
            lambda where: x_ref[0, 1, :, where].astype(F32) * inverse,
            gain_scratch,
        )
    gain_rows = gain_scratch[...] + before_ref[...]
    gain_rows_ref[...] = gain_rows
    high, low = split_two(gain_rows)
    count = high.shape[0]
    begin = own_ref.shape[0]
    for ref in message_refs:
        ref[begin : begin + count, :] = high
        ref[begin + count : begin + 2 * count, :] = low


def first_sum_kernel(sizes, *refs):
    cycle = sizes[2]
    parts, own_ref, message_refs = refs[:cycle], refs[cycle], refs[cycle + 1 :]
    for near in range(sizes[3] // 2):
        total = parts[0][near]
        for ref in parts[1:]:
            total = total + ref[near].astype(F32)
        if near == 0:
            own_ref[...] = total
        else:
            message_refs[near - 1][...] = total.astype(BF16)


def second_rows_kernel(sizes, *refs):
    x_ref, gain_ref, inverse_ref, arrived_ref, output_ref, query_grad_ref, first_ref = refs[:7]
    input_grads_ref = refs[7]
    input_grads_ref[0, 0] = first_ref[...]

    def write(here, result):
        input_grads_ref[0, 1, :, here] = result

    arriving = arriving_from([arrived_ref, output_ref])
    write_input_grads(
        sizes, 1, x_ref, gain_ref, inverse_ref[1], query_grad_ref, arriving, write
    )


def first_near_kernel(sizes, own_ref, *refs):
    block = 2 * sizes[1]
    keep_ref, send_ref = refs[-2:]
    total = own_ref[...]
    for ref in refs[:-2]:
        total = total + ref[...].astype(F32)
    keep_ref[...] = total[:block]
    send_ref[...] = total[block:].astype(BF16)


def second_near_kernel(sizes, *refs):
    rows, half, cycle, tp_count, group, columns = sizes
    near_count = tp_count // 2
    members = cycle * near_count
    own_ref, gain_ref = refs[:2]
    message_refs = refs[2 : 1 + members]
    keep_ref, gain_sum_ref, send_ref = refs[1 + members :]
    block = 2 * half
    count = gain_ref.shape[0]
    total = own_ref[...]
    for ref in message_refs:
        total = total + ref[: 2 * block, :].astype(F32)
    keep_ref[...] = total[:block]
    send_ref[:block, :] = total[block:].astype(BF16)
    cycle_place = lax.axis_index("ctx")
    near_place = lax.axis_index("tp") % near_count
    values = [joined(*split_two(gain_ref[...]))]
    owners = [cycle_place * near_count + near_place]
    begin = 2 * block
    for place, ref in enumerate(message_refs, 1):
        step, near = place // near_count, place % near_count
        values.append(
            joined(ref[begin : begin + count, :], ref[begin + count : begin + 2 * count, :])
        )
        owners.append(((cycle_place + step) % cycle) * near_count + (near_place ^ near))
    gain = in_order(values, owners)
    gain_sum_ref[...] = gain
    high, low = split_two(gain)
    send_ref[block : block + count, :] = high
    send_ref[block + count : block + 2 * count, :] = low


def finish_kernel(sizes, *refs):
    half = sizes[1]
    keep_refs, receive_refs, gain_ref = refs[:TICKS], refs[TICKS : 2 * TICKS], refs[2 * TICKS]
    key_ref, value_ref, gain_out_ref = refs[2 * TICKS + 1 :]
    parity = lax.axis_index("tp") // (sizes[3] // 2)
    block = 2 * half
    own_first = pl.multiple_of(parity * half, half)
    other_first = pl.multiple_of((1 - parity) * half, half)
    for tick in range(TICKS):
        for kind, out in enumerate((key_ref, value_ref)):
            here = slice(kind * half, (kind + 1) * half)
            out[0, tick, pl.ds(own_first, half), :] = keep_refs[tick][here, :]
            out[0, tick, pl.ds(other_first, half), :] = receive_refs[tick][here, :].astype(F32)
    count = gain_ref.shape[0]
    last = receive_refs[TICKS - 1]
    own = joined(*split_two(gain_ref[...]))
    gain_out_ref[...] = own + joined(last[block : block + count, :], last[block + count :, :])


def shape(dims, dtype):
    return jax.ShapeDtypeStruct(dims, dtype)


def on_device(segment_inputs, keys, values, norm_gain, waiting_grads, output_grads, doc_lengths):
    cycle = lax.axis_size("ctx")
    tp_count = lax.axis_size("tp")
    pipe_count = lax.axis_size("pipe")
    _, ticks, rows, columns = segment_inputs.shape
    half = keys.shape[2] // 2
    group = columns // (tp_count * HD)
    gain_count = columns // HD
    sizes = (rows, half, cycle, tp_count, group, columns)
    block = 2 * half
    key_count = cycle * half
    stacked = group * rows
    score_bytes = key_count * stacked * 4
    usual_limit = min(56 << 20, (12 << 20) + 20 * score_bytes)

    def call(kernel, name, operands, out_shape, scratch=(), scalars=0):
        in_specs = [pl.BlockSpec(memory_space=pltpu.SMEM)] * scalars
        in_specs += [pl.BlockSpec(memory_space=pltpu.VMEM)] * (len(operands) - scalars)
        return pl.pallas_call(
            kernel,
            out_shape=out_shape,
            in_specs=in_specs,
            out_specs=[pl.BlockSpec(memory_space=pltpu.VMEM)] * len(out_shape),
            scratch_shapes=scratch,
            compiler_params=pltpu.CompilerParams(vmem_limit_bytes=usual_limit),
            name=name,
        )(*operands)

    near_count = tp_count // 2

    def to_near(value, step, near):
        if step == 0:
            return lax.ppermute(value, "tp", [(i, i ^ near) for i in range(tp_count)])
        if near == 0:
            return lax.ppermute(value, "ctx", [(i, (i + step) % cycle) for i in range(cycle)])
        pairs = [
            (c * tp_count + t, ((c + step) % cycle) * tp_count + (t ^ near))
            for c in range(cycle)
            for t in range(tp_count)
        ]
        return lax.ppermute(value, ("ctx", "tp"), pairs)

    def to_far(value):
        return lax.ppermute(value, "tp", [(i, i ^ near_count) for i in range(tp_count)])

    sections = shape((ticks, 2, half, HD), BF16)
    own_kv, other_kv = call(
        functools.partial(pack_kernel, tp_count, half),
        "pack_kv",
        (jnp.stack([keys[0], values[0]]),),
        [sections, sections],
    )
    far_kv = to_far(other_kv)
    places = [(step, near) for step in range(cycle) for near in range(near_count)][1:]
    kv = [
        block if place == (0, 0) else to_near(block, *place)
        for block in (own_kv, far_kv)
        for place in [(0, 0)] + places
    ]
    queries, inverse = call(
        norm_kernel,
        "norm",
        (segment_inputs, norm_gain),
        [shape((ticks, rows, columns), BF16), shape((ticks, rows, HD), F32)],
    )

    low_rows = shape((rows, columns), BF16)
    low_scores = shape((tp_count, key_count, stacked), BF16)
    input_grad_first, query_grad_first, dscore_first, probs_first = call(
        functools.partial(first_rows_kernel, sizes, len(kv)),
        "first_rows",
        (doc_lengths, segment_inputs, norm_gain, queries, inverse, waiting_grads, *kv),
        [low_rows, low_rows, low_scores, low_scores],
        scalars=1,
    )
    arrived = lax.ppermute(
        input_grad_first, "pipe", [(i, (i - 1) % pipe_count) for i in range(pipe_count)]
    )
    gain_shape = shape((gain_count, HD), F32)
    pair_rows = 2 * block
    own_shape = shape((pair_rows, HD), F32)
    first_sums = (near_count, pair_rows, HD)
    gain_first, *sums_first = call(
        functools.partial(first_keys_kernel, sizes),
        "first_keys",
        (
            segment_inputs,
            queries,
            inverse,
            waiting_grads,
            query_grad_first,
            dscore_first,
            probs_first,
        ),
        [gain_shape, shape(first_sums, F32)] + [shape(first_sums, BF16)] * (cycle - 1),
    )
    sums_first = sums_first[:1] + [
        to_near(value, -step, 0) for step, value in enumerate(sums_first[1:], 1)
    ]
    (probs_second,) = call(
        functools.partial(second_probs_kernel, sizes, len(kv)),
        "second_probs",
        (doc_lengths, queries, *kv),
        [shape((tp_count, key_count, stacked), F32)],
        scalars=1,
    )
    message = shape((pair_rows + 2 * gain_count, HD), BF16)
    query_grad_second, gain_rows, own_second, *sends = call(
        functools.partial(second_keys_kernel, sizes),
        "second_keys",
        (
            segment_inputs,
            queries,
            inverse,
            arrived,
            output_grads,
            probs_second,
            gain_first,
            *kv,
        ),
        [low_rows, gain_shape, own_shape] + [message] * len(places),
        scratch=[pltpu.VMEM((gain_count, HD), F32)],
    )
    received = [to_near(value, -step, near) for value, (step, near) in zip(sends, places)]
    own_first, *sends_first = call(
        functools.partial(first_sum_kernel, sizes),
        "first_sum",
        sums_first,
        [own_shape] + [shape((pair_rows, HD), BF16)] * (near_count - 1),
    )
    received_first = [to_near(value, 0, near) for near, value in enumerate(sends_first, 1)]
    (input_grads,) = call(
        functools.partial(second_rows_kernel, sizes),
        "second_rows",
        (
            segment_inputs,
            norm_gain,
            inverse,
            arrived,
            output_grads,
            query_grad_second,
            input_grad_first,
        ),
        [shape((1, ticks, rows, columns), BF16)],
    )
    keep_shape = shape((block, HD), F32)
    keep_first, send_first = call(
        functools.partial(first_near_kernel, sizes),
        "first_near",
        (own_first, *received_first),
        [keep_shape, shape((block, HD), BF16)],
    )
    keep_second, gain_sum, send_second = call(
        functools.partial(second_near_kernel, sizes),
        "second_near",
        (own_second, gain_rows, *received),
        [keep_shape, gain_shape, shape((block + 2 * gain_count, HD), BF16)],
    )
    grads_shape = shape((1, ticks, block, HD), F32)
    key_grads, value_grads, gain_grads = call(
        functools.partial(finish_kernel, sizes),
        "finish",
        (keep_first, keep_second, to_far(send_first), to_far(send_second), gain_sum),
        [grads_shape, grads_shape, gain_shape],
    )
    return input_grads, key_grads, value_grads, gain_grads.reshape(1, columns)


def solution(mesh):
    in_specs = (
        P("pipe", None, ("ctx", "tp"), None),
        P("pipe", None, "ctx", "tp"),
        P("pipe", None, "ctx", "tp"),
        P("pipe", None),
        P("pipe", ("ctx", "tp"), None),
        P(None, ("ctx", "tp"), None),
        P(),
    )
    out_specs = (
        P("pipe", None, ("ctx", "tp"), None),
        P("pipe", None, "ctx", "tp"),
        P("pipe", None, "ctx", "tp"),
        P("pipe", None),
    )
    return jax.shard_map(
        on_device, mesh=mesh, in_specs=in_specs, out_specs=out_specs, check_vma=False
    )
```

```python
import functools

import jax
import jax.numpy as jnp
from jax import lax
from jax.experimental import pallas as pl
from jax.experimental.pallas import tpu as pltpu
from jax.sharding import PartitionSpec as P

HD = 128
EPSILON = 1e-05
FILL = -1e30
SCALE = HD ** (-0.5)
TICKS = 2
F32 = jnp.float32
BF16 = jnp.bfloat16

NT = (((1,), (1,)), ((), ()))
NN = (((1,), (0,)), ((), ()))
TN = (((0,), (0,)), ((), ()))


def dot(a, b, dims):
    return lax.dot_general(a, b, dims, preferred_element_type=F32)


def in_order(values, owners):
    total = None
    for owner in range(len(values)):
        term = jnp.where(owners[0] == owner, values[0], 0.0)
        for value, whose in zip(values[1:], owners[1:]):
            term = jnp.where(whose == owner, value, term)
        total = term if total is None else total + term
    return total


def pack_kernel(tp_count, half, both_ref, own_ref, other_ref):
    parity = lax.axis_index("tp") // (tp_count // 2)
    own_first = pl.multiple_of(parity * half, half)
    other_first = pl.multiple_of((1 - parity) * half, half)
    for kind in range(2):
        for tick in range(TICKS):
            own_ref[tick, kind] = both_ref[kind, tick, pl.ds(own_first, half), :]
            other_ref[tick, kind] = both_ref[kind, tick, pl.ds(other_first, half), :]


def norm_kernel(x_ref, gain_ref, query_ref, inverse_ref):
    _, ticks, rows, columns = x_ref.shape
    for tick in range(ticks):
        squares = jnp.zeros((rows, HD), F32)
        for first in range(0, columns, HD):
            part = x_ref[0, tick, :, first : first + HD].astype(F32)
            squares = squares + part * part
        mean = jnp.sum(squares, axis=1, keepdims=True) * (1.0 / columns)
        inverse = jnp.broadcast_to(lax.rsqrt(mean + EPSILON), (rows, HD))
        inverse_ref[tick] = inverse
        for first in range(0, columns, HD):
            here = slice(first, first + HD)
            normed = x_ref[0, tick, :, here].astype(F32) * inverse
            query_ref[tick, :, here] = (normed * gain_ref[:, here]).astype(BF16)


class Group:
    def __init__(self, sizes, turn):
        self.rows, self.group = sizes[0], sizes[4]
        width = self.group * HD
        self.head_group = lax.axis_index("tp") ^ turn
        self.first = pl.multiple_of(self.head_group * width, width)

    def head(self, index):
        return pl.ds(self.first + index * HD, HD)

    def stacked(self, load):
        return jnp.concatenate([load(self.head(index)) for index in range(self.group)], axis=0)

    def unstacked(self, value):
        return [value[index * self.rows : (index + 1) * self.rows] for index in range(self.group)]


def arriving_from(refs):
    if len(refs) == 1:
        return lambda where: refs[0][0, :, where]
    last = lax.axis_index("pipe") == lax.axis_size("pipe") - 1
    return lambda where: jnp.where(last, refs[1][0, :, where], refs[0][:, where])


def visible_keys(sizes, tick, doc_ref):
    rows, half, cycle, tp_count, group, columns = sizes
    cycle_place = lax.axis_index("ctx")
    tp_place = lax.axis_index("tp")
    parity = tp_place // (tp_count // 2)
    stacked = group * rows

    def section_first(owner):
        return half * jnp.where(parity == 0, owner, 2 * cycle - 1 - owner)

    row_first = section_first(cycle_place) + (tp_place % (tp_count // 2)) * rows
    query_pos = row_first + (lax.broadcasted_iota(jnp.int32, (1, stacked), 1) & (rows - 1))
    key_place = lax.broadcasted_iota(jnp.int32, (cycle * half, 1), 0)
    key_pos = key_place + section_first(cycle_place)
    for turn in range(1, cycle):
        first = section_first((cycle_place - turn + cycle) % cycle)
        key_pos = jnp.where(key_place >= turn * half, key_place - turn * half + first, key_pos)
    micro = lax.axis_index("pipe") + tick
    closing = jnp.int32(0)
    query_start = jnp.zeros((1, stacked), jnp.int32)
    for doc in range(doc_ref.shape[1]):
        length = doc_ref[micro, doc]
        closing = closing + length
        query_start = query_start + jnp.where(closing <= query_pos, length, 0)
    return (key_pos <= query_pos) & (key_pos >= query_start)


def probabilities(visible, products):
    scores = jnp.where(visible, SCALE * products, FILL)
    weights = jnp.exp(scores - jnp.max(scores, axis=0, keepdims=True))
    return weights * (1.0 / jnp.sum(weights, axis=0, keepdims=True))


def score_grads(probs, prob_grad):
    row_term = jnp.sum(probs * prob_grad, axis=0, keepdims=True)
    return (probs * (prob_grad - row_term)).astype(BF16)


class Keys:
    def __init__(self, sizes, tick, refs):
        self.near_count = sizes[3] // 2
        self.tick = tick
        self.refs = refs

    def __call__(self, turn, kind):
        near, far = turn % self.near_count, turn // self.near_count
        count = len(self.refs) // 2
        refs = self.refs[far * count : (far + 1) * count]
        parts = [ref[self.tick, kind] for ref in refs[near :: self.near_count]]
        return jnp.concatenate(parts, axis=0)


def place_of(sizes, far, kind):
    half = sizes[1]
    return slice((far * 2 + kind) * half, (far * 2 + kind + 1) * half)


def put_key_grads(sizes, turn, parts, own_ref, message_refs):
    half, cycle, tp_count = sizes[1:4]
    near_count = tp_count // 2
    near, far = turn % near_count, turn // near_count
    for kind, part in enumerate(parts):
        here = place_of(sizes, far, kind)
        for step in range(cycle):
            piece = part[step * half : (step + 1) * half]
            if step == 0 and near == 0:
                own_ref[here, :] = piece
            else:
                message_refs[step * near_count + near - 1][here, :] = piece.astype(BF16)


def gain_terms(columns_of, low_parts, normed_of, gain_rows_ref):
    rows = []
    for index, low in enumerate(low_parts):
        term = low.astype(F32) * normed_of(columns_of.head(index))
        rows.append(jnp.sum(term, axis=0, keepdims=True))
    group = columns_of.group
    place = pl.ds(pl.multiple_of(columns_of.head_group * group, group), group)
    gain_rows_ref[place, :] = jnp.concatenate(rows, axis=0)


def write_input_grads(sizes, tick, x_ref, gain_ref, inverse, query_grad_ref, arriving, write):
    rows, columns = sizes[0], sizes[5]
    coupled = jnp.zeros((rows, HD), F32)
    for first in range(0, columns, HD):
        here = slice(first, first + HD)
        scaled = query_grad_ref[:, here].astype(F32) * gain_ref[:, here]
        coupled = coupled + scaled * (x_ref[0, tick, :, here].astype(F32) * inverse)
    coupling = jnp.sum(coupled, axis=1, keepdims=True) * (1.0 / columns)
    for first in range(0, columns, HD):
        here = slice(first, first + HD)
        scaled = query_grad_ref[:, here].astype(F32) * gain_ref[:, here]
        normed = x_ref[0, tick, :, here].astype(F32) * inverse
        result = arriving(here).astype(F32) + inverse * (scaled - normed * coupling)
        write(here, result.astype(BF16))


def first_rows_kernel(sizes, kv_count, *refs):
    tp_count = sizes[3]
    turns = range(tp_count)
    doc_ref, x_ref, gain_ref, query_ref, inverse_ref, waiting_ref = refs[:6]
    keys = Keys(sizes, 0, refs[6 : 6 + kv_count])
    input_grad_ref, query_grad_ref, dscore_ref, probs_ref = refs[6 + kv_count :]
    visible = visible_keys(sizes, 0, doc_ref)
    arriving = arriving_from([waiting_ref])
    columns_of = [Group(sizes, turn) for turn in turns]
    scores, prob_grads = [], []
    for turn in turns:
        query = columns_of[turn].stacked(lambda where: query_ref[0, :, where])
        scores.append(dot(keys(turn, 0), query, NT))
        grad = columns_of[turn].stacked(arriving)
        prob_grads.append(dot(keys(turn, 1), grad, NT))
    dscores = []
    for turn in turns:
        probs = probabilities(visible, scores[turn])
        dscores.append(score_grads(probs, prob_grads[turn]))
        dscore_ref[turn] = dscores[turn]
        probs_ref[turn] = probs.astype(BF16)
    for turn in turns:
        query_grad = (SCALE * dot(dscores[turn], keys(turn, 0), TN)).astype(BF16)
        for index, low in enumerate(columns_of[turn].unstacked(query_grad)):
            query_grad_ref[:, columns_of[turn].head(index)] = low

    def write(here, result):
        input_grad_ref[:, here] = result

    write_input_grads(
        sizes, 0, x_ref, gain_ref, inverse_ref[0], query_grad_ref, arriving, write
    )


def first_keys_kernel(sizes, *refs):
    half, cycle, tp_count = sizes[1:4]
    x_ref, query_ref, inverse_ref, waiting_ref, query_grad_ref, dscore_ref, probs_ref = refs[:7]
    gain_rows_ref, own_ref = refs[7:9]
    send_refs = refs[9:]
    arriving = arriving_from([waiting_ref])
    inverse = inverse_ref[0]
    for turn in range(tp_count):
        columns_of = Group(sizes, turn)
        query = columns_of.stacked(lambda where: query_ref[0, :, where])
        grad = columns_of.stacked(arriving)
        parts = (SCALE * dot(dscore_ref[turn], query, NN), dot(probs_ref[turn], grad, NN))
        near, far = turn % (tp_count // 2), turn // (tp_count // 2)
        for kind, part in enumerate(parts):
            here = place_of(sizes, far, kind)
            own_ref[near, here, :] = part[:half]
            for step, ref in enumerate(send_refs, 1):
                ref[near, here, :] = part[step * half : (step + 1) * half].astype(BF16)
        gain_terms(
            columns_of,
            [query_grad_ref[:, columns_of.head(index)] for index in range(columns_of.group)],
            lambda where: x_ref[0, 0, :, where].astype(F32) * inverse,
            gain_rows_ref,
        )


def second_probs_kernel(sizes, kv_count, *refs):
    turns = range(sizes[3])
    doc_ref, query_ref = refs[:2]
    keys, probs_ref = Keys(sizes, 1, refs[2 : 2 + kv_count]), refs[2 + kv_count]
    visible = visible_keys(sizes, 1, doc_ref)
    scores = []
    for turn in turns:
        query = Group(sizes, turn).stacked(lambda where: query_ref[1, :, where])
        scores.append(dot(keys(turn, 0), query, NT))
    for turn in turns:
        probs_ref[turn] = probabilities(visible, scores[turn])


def second_keys_kernel(sizes, *refs):
    cycle, tp_count = sizes[2:4]
    turns = range(tp_count)
    members = cycle * (tp_count // 2)
    x_ref, query_ref, inverse_ref, arrived_ref, output_ref, probs_ref, before_ref = refs[:7]
    keys, refs = Keys(sizes, 1, refs[7 : 7 + 2 * members]), refs[7 + 2 * members :]
    query_grad_ref, gain_rows_ref, own_ref = refs[:3]
    message_refs, gain_scratch = refs[3:-1], refs[-1]
    arriving = arriving_from([arrived_ref, output_ref])
    inverse = inverse_ref[1]
    columns_of = [Group(sizes, turn) for turn in turns]
    grads = [columns_of[turn].stacked(arriving) for turn in turns]
    prob_grads = [dot(keys(turn, 1), grads[turn], NT) for turn in turns]
    value_grads = [dot(probs_ref[turn].astype(BF16), grads[turn], NN) for turn in turns]
    dscores = [score_grads(probs_ref[turn], prob_grads[turn]) for turn in turns]
    query_grads = [
        (SCALE * dot(dscores[turn], keys(turn, 0), TN)).astype(BF16) for turn in turns
    ]
    for turn in turns:
        query = columns_of[turn].stacked(lambda where: query_ref[1, :, where])
        key_grad = SCALE * dot(dscores[turn], query, NN)
        put_key_grads(sizes, turn, (key_grad, value_grads[turn]), own_ref, message_refs)
    for turn in turns:
        low_parts = columns_of[turn].unstacked(query_grads[turn])
        for index, low in enumerate(low_parts):
            query_grad_ref[:, columns_of[turn].head(index)] = low
        gain_terms(
            columns_of[turn],
            low_parts,
            lambda where: x_ref[0, 1, :, where].astype(F32) * inverse,
            gain_scratch,
        )
    gain_rows = gain_scratch[...] + before_ref[...]
    gain_rows_ref[...] = gain_rows
    gain_low = gain_rows.astype(BF16)
    for ref in message_refs:
        ref[own_ref.shape[0] :, :] = gain_low


def first_sum_kernel(sizes, *refs):
    cycle = sizes[2]
    parts, own_ref, message_refs = refs[:cycle], refs[cycle], refs[cycle + 1 :]
    for near in range(sizes[3] // 2):
        total = parts[0][near]
        for ref in parts[1:]:
            total = total + ref[near].astype(F32)
        if near == 0:
            own_ref[...] = total
        else:
            message_refs[near - 1][...] = total.astype(BF16)


def second_rows_kernel(sizes, *refs):
    x_ref, gain_ref, inverse_ref, arrived_ref, output_ref, query_grad_ref, first_ref = refs[:7]
    input_grads_ref = refs[7]
    input_grads_ref[0, 0] = first_ref[...]

    def write(here, result):
        input_grads_ref[0, 1, :, here] = result

    arriving = arriving_from([arrived_ref, output_ref])
    write_input_grads(
        sizes, 1, x_ref, gain_ref, inverse_ref[1], query_grad_ref, arriving, write
    )


def first_near_kernel(sizes, own_ref, *refs):
    block = 2 * sizes[1]
    keep_ref, send_ref = refs[-2:]
    total = own_ref[...]
    for ref in refs[:-2]:
        total = total + ref[...].astype(F32)
    keep_ref[...] = total[:block]
    send_ref[...] = total[block:].astype(BF16)


def second_near_kernel(sizes, *refs):
    rows, half, cycle, tp_count, group, columns = sizes
    near_count = tp_count // 2
    members = cycle * near_count
    own_ref, gain_ref = refs[:2]
    message_refs = refs[2 : 1 + members]
    keep_ref, gain_sum_ref, send_ref = refs[1 + members :]
    block = 2 * half
    total = own_ref[...]
    for ref in message_refs:
        total = total + ref[: 2 * block, :].astype(F32)
    keep_ref[...] = total[:block]
    send_ref[:block, :] = total[block:].astype(BF16)
    cycle_place = lax.axis_index("ctx")
    near_place = lax.axis_index("tp") % near_count
    values = [gain_ref[...].astype(BF16).astype(F32)]
    owners = [cycle_place * near_count + near_place]
    for place, ref in enumerate(message_refs, 1):
        step, near = place // near_count, place % near_count
        values.append(ref[2 * block :, :].astype(F32))
        owners.append(((cycle_place + step) % cycle) * near_count + (near_place ^ near))
    gain = in_order(values, owners)
    gain_sum_ref[...] = gain
    send_ref[block:, :] = gain.astype(BF16)


def finish_kernel(sizes, *refs):
    half = sizes[1]
    keep_refs, receive_refs, gain_ref = refs[:TICKS], refs[TICKS : 2 * TICKS], refs[2 * TICKS]
    key_ref, value_ref, gain_out_ref = refs[2 * TICKS + 1 :]
    parity = lax.axis_index("tp") // (sizes[3] // 2)
    block = 2 * half
    own_first = pl.multiple_of(parity * half, half)
    other_first = pl.multiple_of((1 - parity) * half, half)
    for tick in range(TICKS):
        for kind, out in enumerate((key_ref, value_ref)):
            here = slice(kind * half, (kind + 1) * half)
            out[0, tick, pl.ds(own_first, half), :] = keep_refs[tick][here, :]
            out[0, tick, pl.ds(other_first, half), :] = receive_refs[tick][here, :].astype(F32)
    own = gain_ref[...].astype(BF16).astype(F32)
    gain_out_ref[...] = own + receive_refs[TICKS - 1][block:, :].astype(F32)


def shape(dims, dtype):
    return jax.ShapeDtypeStruct(dims, dtype)


def on_device(segment_inputs, keys, values, norm_gain, waiting_grads, output_grads, doc_lengths):
    cycle = lax.axis_size("ctx")
    tp_count = lax.axis_size("tp")
    pipe_count = lax.axis_size("pipe")
    _, ticks, rows, columns = segment_inputs.shape
    half = keys.shape[2] // 2
    group = columns // (tp_count * HD)
    gain_count = columns // HD
    sizes = (rows, half, cycle, tp_count, group, columns)
    block = 2 * half
    key_count = cycle * half
    stacked = group * rows
    score_bytes = key_count * stacked * 4
    usual_limit = min(56 << 20, (12 << 20) + 20 * score_bytes)

    def call(kernel, name, operands, out_shape, scratch=(), scalars=0):
        in_specs = [pl.BlockSpec(memory_space=pltpu.SMEM)] * scalars
        in_specs += [pl.BlockSpec(memory_space=pltpu.VMEM)] * (len(operands) - scalars)
        return pl.pallas_call(
            kernel,
            out_shape=out_shape,
            in_specs=in_specs,
            out_specs=[pl.BlockSpec(memory_space=pltpu.VMEM)] * len(out_shape),
            scratch_shapes=scratch,
            compiler_params=pltpu.CompilerParams(vmem_limit_bytes=usual_limit),
            name=name,
        )(*operands)

    near_count = tp_count // 2

    def to_near(value, step, near):
        if step == 0:
            return lax.ppermute(value, "tp", [(i, i ^ near) for i in range(tp_count)])
        if near == 0:
            return lax.ppermute(value, "ctx", [(i, (i + step) % cycle) for i in range(cycle)])
        pairs = [
            (c * tp_count + t, ((c + step) % cycle) * tp_count + (t ^ near))
            for c in range(cycle)
            for t in range(tp_count)
        ]
        return lax.ppermute(value, ("ctx", "tp"), pairs)

    def to_far(value):
        return lax.ppermute(value, "tp", [(i, i ^ near_count) for i in range(tp_count)])

    sections = shape((ticks, 2, half, HD), BF16)
    own_kv, other_kv = call(
        functools.partial(pack_kernel, tp_count, half),
        "pack_kv",
        (jnp.stack([keys[0], values[0]]),),
        [sections, sections],
    )
    far_kv = to_far(other_kv)
    places = [(step, near) for step in range(cycle) for near in range(near_count)][1:]
    kv = [
        block if place == (0, 0) else to_near(block, *place)
        for block in (own_kv, far_kv)
        for place in [(0, 0)] + places
    ]
    queries, inverse = call(
        norm_kernel,
        "norm",
        (segment_inputs, norm_gain),
        [shape((ticks, rows, columns), BF16), shape((ticks, rows, HD), F32)],
    )

    low_rows = shape((rows, columns), BF16)
    low_scores = shape((tp_count, key_count, stacked), BF16)
    input_grad_first, query_grad_first, dscore_first, probs_first = call(
        functools.partial(first_rows_kernel, sizes, len(kv)),
        "first_rows",
        (doc_lengths, segment_inputs, norm_gain, queries, inverse, waiting_grads, *kv),
        [low_rows, low_rows, low_scores, low_scores],
        scalars=1,
    )
    arrived = lax.ppermute(
        input_grad_first, "pipe", [(i, (i - 1) % pipe_count) for i in range(pipe_count)]
    )
    gain_shape = shape((gain_count, HD), F32)
    pair_rows = 2 * block
    own_shape = shape((pair_rows, HD), F32)
    first_sums = (near_count, pair_rows, HD)
    gain_first, *sums_first = call(
        functools.partial(first_keys_kernel, sizes),
        "first_keys",
        (
            segment_inputs,
            queries,
            inverse,
            waiting_grads,
            query_grad_first,
            dscore_first,
            probs_first,
        ),
        [gain_shape, shape(first_sums, F32)] + [shape(first_sums, BF16)] * (cycle - 1),
    )
    sums_first = sums_first[:1] + [
        to_near(value, -step, 0) for step, value in enumerate(sums_first[1:], 1)
    ]
    (probs_second,) = call(
        functools.partial(second_probs_kernel, sizes, len(kv)),
        "second_probs",
        (doc_lengths, queries, *kv),
        [shape((tp_count, key_count, stacked), F32)],
        scalars=1,
    )
    message = shape((pair_rows + gain_count, HD), BF16)
    query_grad_second, gain_rows, own_second, *sends = call(
        functools.partial(second_keys_kernel, sizes),
        "second_keys",
        (
            segment_inputs,
            queries,
            inverse,
            arrived,
            output_grads,
            probs_second,
            gain_first,
            *kv,
        ),
        [low_rows, gain_shape, own_shape] + [message] * len(places),
        scratch=[pltpu.VMEM((gain_count, HD), F32)],
    )
    received = [to_near(value, -step, near) for value, (step, near) in zip(sends, places)]
    own_first, *sends_first = call(
        functools.partial(first_sum_kernel, sizes),
        "first_sum",
        sums_first,
        [own_shape] + [shape((pair_rows, HD), BF16)] * (near_count - 1),
    )
    received_first = [to_near(value, 0, near) for near, value in enumerate(sends_first, 1)]
    (input_grads,) = call(
        functools.partial(second_rows_kernel, sizes),
        "second_rows",
        (
            segment_inputs,
            norm_gain,
            inverse,
            arrived,
            output_grads,
            query_grad_second,
            input_grad_first,
        ),
        [shape((1, ticks, rows, columns), BF16)],
    )
    keep_shape = shape((block, HD), F32)
    keep_first, send_first = call(
        functools.partial(first_near_kernel, sizes),
        "first_near",
        (own_first, *received_first),
        [keep_shape, shape((block, HD), BF16)],
    )
    keep_second, gain_sum, send_second = call(
        functools.partial(second_near_kernel, sizes),
        "second_near",
        (own_second, gain_rows, *received),
        [keep_shape, gain_shape, shape((block + gain_count, HD), BF16)],
    )
    grads_shape = shape((1, ticks, block, HD), F32)
    key_grads, value_grads, gain_grads = call(
        functools.partial(finish_kernel, sizes),
        "finish",
        (keep_first, keep_second, to_far(send_first), to_far(send_second), gain_sum),
        [grads_shape, grads_shape, gain_shape],
    )
    return input_grads, key_grads, value_grads, gain_grads.reshape(1, columns)


def solution(mesh):
    in_specs = (
        P("pipe", None, ("ctx", "tp"), None),
        P("pipe", None, "ctx", "tp"),
        P("pipe", None, "ctx", "tp"),
        P("pipe", None),
        P("pipe", ("ctx", "tp"), None),
        P(None, ("ctx", "tp"), None),
        P(),
    )
    out_specs = (
        P("pipe", None, ("ctx", "tp"), None),
        P("pipe", None, "ctx", "tp"),
        P("pipe", None, "ctx", "tp"),
        P("pipe", None),
    )
    return jax.shard_map(
        on_device, mesh=mesh, in_specs=in_specs, out_specs=out_specs, check_vma=False
    )
```

```python
import functools

import jax
import jax.numpy as jnp
from jax import lax
from jax.experimental import pallas as pl
from jax.experimental.pallas import tpu as pltpu
from jax.sharding import PartitionSpec as P

HD = 128
EPSILON = 1e-05
FILL = -1e30
SCALE = HD ** (-0.5)
TICKS = 2
F32 = jnp.float32
BF16 = jnp.bfloat16

NT = (((1,), (1,)), ((), ()))
NN = (((1,), (0,)), ((), ()))
TN = (((0,), (0,)), ((), ()))


def dot(a, b, dims):
    return lax.dot_general(a, b, dims, preferred_element_type=F32)


def in_order(values, owners):
    total = None
    for owner in range(len(values)):
        term = jnp.where(owners[0] == owner, values[0], 0.0)
        for value, whose in zip(values[1:], owners[1:]):
            term = jnp.where(whose == owner, value, term)
        total = term if total is None else total + term
    return total


def pack_kernel(tp_count, half, both_ref, own_ref, other_ref):
    parity = lax.axis_index("tp") // (tp_count // 2)
    own_first = pl.multiple_of(parity * half, half)
    other_first = pl.multiple_of((1 - parity) * half, half)
    for kind in range(2):
        for tick in range(TICKS):
            own_ref[tick, kind] = both_ref[kind, tick, pl.ds(own_first, half), :]
            other_ref[tick, kind] = both_ref[kind, tick, pl.ds(other_first, half), :]


def norm_kernel(sizes, doc_ref, x_ref, gain_ref, query_ref, inverse_ref, mask_ref):
    rows, columns = sizes[0], sizes[5]
    for tick in range(TICKS):
        squares = jnp.zeros((rows, HD), F32)
        for first in range(0, columns, HD):
            part = x_ref[0, tick, :, first : first + HD].astype(F32)
            squares = squares + part * part
        mean = jnp.sum(squares, axis=1, keepdims=True) * (1.0 / columns)
        inverse = jnp.broadcast_to(lax.rsqrt(mean + EPSILON), (rows, HD))
        inverse_ref[tick] = inverse
        for first in range(0, columns, HD):
            here = slice(first, first + HD)
            normed = x_ref[0, tick, :, here].astype(F32) * inverse
            query_ref[tick, :, here] = (normed * gain_ref[:, here]).astype(BF16)
        mask_ref[tick] = jnp.where(visible_keys(sizes, tick, doc_ref), 0.0, FILL)


class Group:
    def __init__(self, sizes, turn):
        self.rows, self.group = sizes[0], sizes[4]
        width = self.group * HD
        self.head_group = lax.axis_index("tp") ^ turn
        self.first = pl.multiple_of(self.head_group * width, width)

    def head(self, index):
        return pl.ds(self.first + index * HD, HD)

    def stacked(self, load):
        return jnp.concatenate([load(self.head(index)) for index in range(self.group)], axis=0)

    def unstacked(self, value):
        return [value[index * self.rows : (index + 1) * self.rows] for index in range(self.group)]


def arriving_from(refs):
    if len(refs) == 1:
        return lambda where: refs[0][0, :, where]
    last = lax.axis_index("pipe") == lax.axis_size("pipe") - 1
    return lambda where: jnp.where(last, refs[1][0, :, where], refs[0][:, where])


def visible_keys(sizes, tick, doc_ref):
    rows, half, cycle, tp_count, group, columns = sizes
    cycle_place = lax.axis_index("ctx")
    tp_place = lax.axis_index("tp")
    parity = tp_place // (tp_count // 2)
    stacked = group * rows

    def section_first(owner):
        return half * jnp.where(parity == 0, owner, 2 * cycle - 1 - owner)

    row_first = section_first(cycle_place) + (tp_place % (tp_count // 2)) * rows
    query_pos = row_first + (lax.broadcasted_iota(jnp.int32, (1, stacked), 1) & (rows - 1))
    key_place = lax.broadcasted_iota(jnp.int32, (cycle * half, 1), 0)
    key_pos = key_place + section_first(cycle_place)
    for turn in range(1, cycle):
        first = section_first((cycle_place - turn + cycle) % cycle)
        key_pos = jnp.where(key_place >= turn * half, key_place - turn * half + first, key_pos)
    micro = lax.axis_index("pipe") + tick
    closing = jnp.int32(0)
    query_start = jnp.zeros((1, stacked), jnp.int32)
    for doc in range(doc_ref.shape[1]):
        length = doc_ref[micro, doc]
        closing = closing + length
        query_start = query_start + jnp.where(closing <= query_pos, length, 0)
    return (key_pos <= query_pos) & (key_pos >= query_start)


def probabilities(mask, products):
    scores = SCALE * products + mask
    weights = jnp.exp(scores - jnp.max(scores, axis=0, keepdims=True))
    return weights * (1.0 / jnp.sum(weights, axis=0, keepdims=True))


def score_grads(probs, prob_grad):
    row_term = jnp.sum(probs * prob_grad, axis=0, keepdims=True)
    return (probs * (prob_grad - row_term)).astype(BF16)


class Keys:
    def __init__(self, sizes, tick, refs):
        self.near_count = sizes[3] // 2
        self.tick = tick
        self.refs = refs

    def __call__(self, near, kind):
        parts = [ref[self.tick, kind] for ref in self.refs[near :: self.near_count]]
        return jnp.concatenate(parts, axis=0)


def place_of(sizes, far, kind):
    half = sizes[1]
    return slice((far * 2 + kind) * half, (far * 2 + kind + 1) * half)


def put_key_grads(sizes, turn, parts, own_ref, message_refs):
    half, cycle, tp_count = sizes[1:4]
    near_count = tp_count // 2
    near, far = turn % near_count, turn // near_count
    for kind, part in enumerate(parts):
        here = place_of(sizes, far, kind)
        for step in range(cycle):
            piece = part[step * half : (step + 1) * half]
            if step == 0 and near == 0:
                own_ref[here, :] = piece
            else:
                message_refs[step * near_count + near - 1][here, :] = piece.astype(BF16)


def gain_terms(columns_of, query_grad, normed_of, gain_rows_ref):
    rows = []
    for index, low in enumerate(columns_of.unstacked(query_grad)):
        term = low.astype(F32) * normed_of(columns_of.head(index))
        rows.append(jnp.sum(term, axis=0, keepdims=True))
    group = columns_of.group
    place = pl.ds(pl.multiple_of(columns_of.head_group * group, group), group)
    gain_rows_ref[place, :] = jnp.concatenate(rows, axis=0)


def coupled_terms(columns_of, query_grad, normed_of, gain_ref, coupled):
    for index, low in enumerate(columns_of.unstacked(query_grad)):
        where = columns_of.head(index)
        coupled = coupled + low.astype(F32) * gain_ref[:, where] * normed_of(where)
    return coupled


def write_input_grads(sizes, coupled, query_grad_of, normed_of, gain_ref, inverse, arriving, write):
    coupling = jnp.sum(coupled, axis=1, keepdims=True) * (1.0 / sizes[5])
    for turn in range(sizes[3]):
        columns_of = Group(sizes, turn)
        for index, low in enumerate(columns_of.unstacked(query_grad_of(turn))):
            where = columns_of.head(index)
            scaled = low.astype(F32) * gain_ref[:, where]
            result = arriving(where).astype(F32) + inverse * (scaled - normed_of(where) * coupling)
            write(where, result.astype(BF16))


def normed_from(x_ref, tick, inverse):
    return lambda where: x_ref[0, tick, :, where].astype(F32) * inverse


def first_half(sizes, far, keys, mask, query_ref, arriving, dscore_ref, probs_ref):
    near_count = sizes[3] // 2
    nears = range(near_count)
    columns_of = [Group(sizes, far * near_count + near) for near in nears]
    scores, prob_grads = [], []
    for near in nears:
        query = columns_of[near].stacked(lambda where: query_ref[0, :, where])
        scores.append(dot(keys(near, 0), query, NT))
        prob_grads.append(dot(keys(near, 1), columns_of[near].stacked(arriving), NT))
    dscores = []
    for near in nears:
        probs = probabilities(mask, scores[near])
        dscores.append(score_grads(probs, prob_grads[near]))
        dscore_ref[near] = dscores[near]
        probs_ref[near] = probs.astype(BF16)
    return [(SCALE * dot(dscores[near], keys(near, 0), TN)).astype(BF16) for near in nears]


def first_near_rows_kernel(sizes, *refs):
    members = sizes[2] * sizes[3] // 2
    x_ref, gain_ref, query_ref, inverse_ref, mask_ref, waiting_ref = refs[:6]
    keys = Keys(sizes, 0, refs[6 : 6 + members])
    query_grad_ref, dscore_ref, probs_ref, coupled_ref = refs[6 + members :]
    query_grads = first_half(
        sizes,
        0,
        keys,
        mask_ref[0],
        query_ref,
        arriving_from([waiting_ref]),
        dscore_ref,
        probs_ref,
    )
    normed_of = normed_from(x_ref, 0, inverse_ref[0])
    coupled = jnp.zeros((sizes[0], HD), F32)
    for near, query_grad in enumerate(query_grads):
        query_grad_ref[near] = query_grad
        coupled = coupled_terms(Group(sizes, near), query_grad, normed_of, gain_ref, coupled)
    coupled_ref[...] = coupled


def first_far_rows_kernel(sizes, *refs):
    near_count = sizes[3] // 2
    members = sizes[2] * near_count
    x_ref, gain_ref, query_ref, inverse_ref, mask_ref, waiting_ref = refs[:6]
    keys = Keys(sizes, 0, refs[6 : 6 + members])
    near_grad_ref, coupled_ref = refs[6 + members : 8 + members]
    input_grad_ref, query_grad_ref, dscore_ref, probs_ref = refs[8 + members :]
    arriving = arriving_from([waiting_ref])
    query_grads = first_half(
        sizes, 1, keys, mask_ref[0], query_ref, arriving, dscore_ref, probs_ref
    )
    normed_of = normed_from(x_ref, 0, inverse_ref[0])
    coupled = coupled_ref[...]
    for near, query_grad in enumerate(query_grads):
        query_grad_ref[near] = query_grad
        coupled = coupled_terms(
            Group(sizes, near_count + near), query_grad, normed_of, gain_ref, coupled
        )

    def query_grad_of(turn):
        return near_grad_ref[turn] if turn < near_count else query_grads[turn - near_count]

    def write(where, result):
        input_grad_ref[:, where] = result

    write_input_grads(
        sizes, coupled, query_grad_of, normed_of, gain_ref, inverse_ref[0], arriving, write
    )


def first_keys_kernel(sizes, *refs):
    half, cycle, tp_count = sizes[1:4]
    near_count = tp_count // 2
    x_ref, query_ref, inverse_ref, waiting_ref = refs[:4]
    query_grad_refs, dscore_refs, probs_refs = refs[4:6], refs[6:8], refs[8:10]
    gain_rows_ref, own_ref = refs[10:12]
    send_refs = refs[12:]
    arriving = arriving_from([waiting_ref])
    normed_of = normed_from(x_ref, 0, inverse_ref[0])
    for turn in range(tp_count):
        near, far = turn % near_count, turn // near_count
        columns_of = Group(sizes, turn)
        query = columns_of.stacked(lambda where: query_ref[0, :, where])
        grad = columns_of.stacked(arriving)
        parts = (
            SCALE * dot(dscore_refs[far][near], query, NN),
            dot(probs_refs[far][near], grad, NN),
        )
        for kind, part in enumerate(parts):
            here = place_of(sizes, far, kind)
            own_ref[near, here, :] = part[:half]
            for step, ref in enumerate(send_refs, 1):
                ref[near, here, :] = part[step * half : (step + 1) * half].astype(BF16)
        gain_terms(columns_of, query_grad_refs[far][near], normed_of, gain_rows_ref)


def both_sets(sizes, refs):
    near_count = sizes[3] // 2
    members = sizes[2] * near_count
    sets = [Keys(sizes, 1, refs[:members]), Keys(sizes, 1, refs[members:])]
    return lambda turn, kind: sets[turn // near_count](turn % near_count, kind)


def second_probs_kernel(sizes, *refs):
    turns = range(sizes[3])
    mask_ref, query_ref = refs[:2]
    keys, probs_ref = both_sets(sizes, refs[2:-1]), refs[-1]
    mask = mask_ref[1]
    scores = []
    for turn in turns:
        query = Group(sizes, turn).stacked(lambda where: query_ref[1, :, where])
        scores.append(dot(keys(turn, 0), query, NT))
    for turn in turns:
        probs_ref[turn] = probabilities(mask, scores[turn])


def second_keys_kernel(sizes, *refs):
    cycle, tp_count = sizes[2:4]
    turns = range(tp_count)
    kv_count = cycle * tp_count
    x_ref, query_ref, inverse_ref, arrived_ref, output_ref, probs_ref, before_ref = refs[:7]
    keys, refs = both_sets(sizes, refs[7 : 7 + kv_count]), refs[7 + kv_count :]
    query_grad_ref, gain_rows_ref, own_ref = refs[:3]
    message_refs, gain_scratch = refs[3:-1], refs[-1]
    arriving = arriving_from([arrived_ref, output_ref])
    normed_of = normed_from(x_ref, 1, inverse_ref[1])
    columns_of = [Group(sizes, turn) for turn in turns]
    grads = [columns_of[turn].stacked(arriving) for turn in turns]
    prob_grads = [dot(keys(turn, 1), grads[turn], NT) for turn in turns]
    value_grads = [dot(probs_ref[turn].astype(BF16), grads[turn], NN) for turn in turns]
    dscores = [score_grads(probs_ref[turn], prob_grads[turn]) for turn in turns]
    query_grads = [
        (SCALE * dot(dscores[turn], keys(turn, 0), TN)).astype(BF16) for turn in turns
    ]
    for turn in turns:
        query = columns_of[turn].stacked(lambda where: query_ref[1, :, where])
        key_grad = SCALE * dot(dscores[turn], query, NN)
        put_key_grads(sizes, turn, (key_grad, value_grads[turn]), own_ref, message_refs)
    for turn in turns:
        query_grad_ref[turn] = query_grads[turn]
        gain_terms(columns_of[turn], query_grads[turn], normed_of, gain_scratch)
    gain_rows = gain_scratch[...] + before_ref[...]
    gain_rows_ref[...] = gain_rows
    gain_low = gain_rows.astype(BF16)
    for ref in message_refs:
        ref[own_ref.shape[0] :, :] = gain_low


def first_sum_kernel(sizes, *refs):
    cycle = sizes[2]
    parts, own_ref, message_refs = refs[:cycle], refs[cycle], refs[cycle + 1 :]
    for near in range(sizes[3] // 2):
        total = parts[0][near]
        for ref in parts[1:]:
            total = total + ref[near].astype(F32)
        if near == 0:
            own_ref[...] = total
        else:
            message_refs[near - 1][...] = total.astype(BF16)


def second_rows_kernel(sizes, *refs):
    x_ref, gain_ref, inverse_ref, arrived_ref, output_ref, query_grad_ref, first_ref = refs[:7]
    input_grads_ref = refs[7]
    input_grads_ref[0, 0] = first_ref[...]
    inverse = inverse_ref[1]
    normed_of = normed_from(x_ref, 1, inverse)
    coupled = jnp.zeros((sizes[0], HD), F32)
    for turn in range(sizes[3]):
        coupled = coupled_terms(
            Group(sizes, turn), query_grad_ref[turn], normed_of, gain_ref, coupled
        )

    def write(where, result):
        input_grads_ref[0, 1, :, where] = result

    write_input_grads(
        sizes,
        coupled,
        lambda turn: query_grad_ref[turn],
        normed_of,
        gain_ref,
        inverse,
        arriving_from([arrived_ref, output_ref]),
        write,
    )


def first_near_kernel(sizes, own_ref, *refs):
    block = 2 * sizes[1]
    keep_ref, send_ref = refs[-2:]
    total = own_ref[...]
    for ref in refs[:-2]:
        total = total + ref[...].astype(F32)
    keep_ref[...] = total[:block]
    send_ref[...] = total[block:].astype(BF16)


def second_near_kernel(sizes, *refs):
    rows, half, cycle, tp_count, group, columns = sizes
    near_count = tp_count // 2
    members = cycle * near_count
    own_ref, gain_ref = refs[:2]
    message_refs = refs[2 : 1 + members]
    keep_ref, gain_sum_ref, send_ref = refs[1 + members :]
    block = 2 * half
    total = own_ref[...]
    for ref in message_refs:
        total = total + ref[: 2 * block, :].astype(F32)
    keep_ref[...] = total[:block]
    send_ref[:block, :] = total[block:].astype(BF16)
    cycle_place = lax.axis_index("ctx")
    near_place = lax.axis_index("tp") % near_count
    values = [gain_ref[...].astype(BF16).astype(F32)]
    owners = [cycle_place * near_count + near_place]
    for place, ref in enumerate(message_refs, 1):
        step, near = place // near_count, place % near_count
        values.append(ref[2 * block :, :].astype(F32))
        owners.append(((cycle_place + step) % cycle) * near_count + (near_place ^ near))
    gain = in_order(values, owners)
    gain_sum_ref[...] = gain
    send_ref[block:, :] = gain.astype(BF16)


def finish_kernel(sizes, *refs):
    half = sizes[1]
    keep_refs, receive_refs, gain_ref = refs[:TICKS], refs[TICKS : 2 * TICKS], refs[2 * TICKS]
    key_ref, value_ref, gain_out_ref = refs[2 * TICKS + 1 :]
    parity = lax.axis_index("tp") // (sizes[3] // 2)
    block = 2 * half
    own_first = pl.multiple_of(parity * half, half)
    other_first = pl.multiple_of((1 - parity) * half, half)
    for tick in range(TICKS):
        for kind, out in enumerate((key_ref, value_ref)):
            here = slice(kind * half, (kind + 1) * half)
            out[0, tick, pl.ds(own_first, half), :] = keep_refs[tick][here, :]
            out[0, tick, pl.ds(other_first, half), :] = receive_refs[tick][here, :].astype(F32)
    own = gain_ref[...].astype(BF16).astype(F32)
    gain_out_ref[...] = own + receive_refs[TICKS - 1][block:, :].astype(F32)


def shape(dims, dtype):
    return jax.ShapeDtypeStruct(dims, dtype)


def on_device(segment_inputs, keys, values, norm_gain, waiting_grads, output_grads, doc_lengths):
    cycle = lax.axis_size("ctx")
    tp_count = lax.axis_size("tp")
    pipe_count = lax.axis_size("pipe")
    _, ticks, rows, columns = segment_inputs.shape
    half = keys.shape[2] // 2
    group = columns // (tp_count * HD)
    gain_count = columns // HD
    sizes = (rows, half, cycle, tp_count, group, columns)
    block = 2 * half
    key_count = cycle * half
    stacked = group * rows
    score_bytes = key_count * stacked * 4
    usual_limit = min(56 << 20, (12 << 20) + 20 * score_bytes)

    def call(kernel, name, operands, out_shape, scratch=(), scalars=0):
        in_specs = [pl.BlockSpec(memory_space=pltpu.SMEM)] * scalars
        in_specs += [pl.BlockSpec(memory_space=pltpu.VMEM)] * (len(operands) - scalars)
        return pl.pallas_call(
            kernel,
            out_shape=out_shape,
            in_specs=in_specs,
            out_specs=[pl.BlockSpec(memory_space=pltpu.VMEM)] * len(out_shape),
            scratch_shapes=scratch,
            compiler_params=pltpu.CompilerParams(vmem_limit_bytes=usual_limit),
            name=name,
        )(*operands)

    near_count = tp_count // 2

    def to_near(value, step, near):
        if step == 0:
            return lax.ppermute(value, "tp", [(i, i ^ near) for i in range(tp_count)])
        if near == 0:
            return lax.ppermute(value, "ctx", [(i, (i + step) % cycle) for i in range(cycle)])
        pairs = [
            (c * tp_count + t, ((c + step) % cycle) * tp_count + (t ^ near))
            for c in range(cycle)
            for t in range(tp_count)
        ]
        return lax.ppermute(value, ("ctx", "tp"), pairs)

    def to_far(value):
        return lax.ppermute(value, "tp", [(i, i ^ near_count) for i in range(tp_count)])

    sections = shape((ticks, 2, half, HD), BF16)
    own_kv, other_kv = call(
        functools.partial(pack_kernel, tp_count, half),
        "pack_kv",
        (jnp.stack([keys[0], values[0]]),),
        [sections, sections],
    )
    far_kv = to_far(other_kv)
    places = [(step, near) for step in range(cycle) for near in range(near_count)][1:]
    kv = [
        block if place == (0, 0) else to_near(block, *place)
        for block in (own_kv, far_kv)
        for place in [(0, 0)] + places
    ]
    own_set, far_set = kv[: len(kv) // 2], kv[len(kv) // 2 :]
    queries, inverse, masks = call(
        functools.partial(norm_kernel, sizes),
        "norm",
        (doc_lengths, segment_inputs, norm_gain),
        [
            shape((ticks, rows, columns), BF16),
            shape((ticks, rows, HD), F32),
            shape((ticks, key_count, stacked), F32),
        ],
        scalars=1,
    )

    low_rows = shape((rows, columns), BF16)
    low_scores = shape((near_count, key_count, stacked), BF16)
    low_grads = shape((near_count, stacked, HD), BF16)
    rows_operands = (segment_inputs, norm_gain, queries, inverse, masks, waiting_grads)
    query_grad_near, dscore_near, probs_near, coupled = call(
        functools.partial(first_near_rows_kernel, sizes),
        "first_near_rows",
        (*rows_operands, *own_set),
        [low_grads, low_scores, low_scores, shape((rows, HD), F32)],
    )
    input_grad_first, query_grad_far, dscore_far, probs_far = call(
        functools.partial(first_far_rows_kernel, sizes),
        "first_far_rows",
        (*rows_operands, *far_set, query_grad_near, coupled),
        [low_rows, low_grads, low_scores, low_scores],
    )
    arrived = lax.ppermute(
        input_grad_first, "pipe", [(i, (i - 1) % pipe_count) for i in range(pipe_count)]
    )
    gain_shape = shape((gain_count, HD), F32)
    pair_rows = 2 * block
    own_shape = shape((pair_rows, HD), F32)
    first_sums = (near_count, pair_rows, HD)
    gain_first, *sums_first = call(
        functools.partial(first_keys_kernel, sizes),
        "first_keys",
        (
            segment_inputs,
            queries,
            inverse,
            waiting_grads,
            query_grad_near,
            query_grad_far,
            dscore_near,
            dscore_far,
            probs_near,
            probs_far,
        ),
        [gain_shape, shape(first_sums, F32)] + [shape(first_sums, BF16)] * (cycle - 1),
    )
    sums_first = sums_first[:1] + [
        to_near(value, -step, 0) for step, value in enumerate(sums_first[1:], 1)
    ]
    (probs_second,) = call(
        functools.partial(second_probs_kernel, sizes),
        "second_probs",
        (masks, queries, *kv),
        [shape((tp_count, key_count, stacked), F32)],
    )
    message = shape((pair_rows + gain_count, HD), BF16)
    query_grad_second, gain_rows, own_second, *sends = call(
        functools.partial(second_keys_kernel, sizes),
        "second_keys",
        (
            segment_inputs,
            queries,
            inverse,
            arrived,
            output_grads,
            probs_second,
            gain_first,
            *kv,
        ),
        [shape((tp_count, stacked, HD), BF16), gain_shape, own_shape] + [message] * len(places),
        scratch=[pltpu.VMEM((gain_count, HD), F32)],
    )
    received = [to_near(value, -step, near) for value, (step, near) in zip(sends, places)]
    own_first, *sends_first = call(
        functools.partial(first_sum_kernel, sizes),
        "first_sum",
        sums_first,
        [own_shape] + [shape((pair_rows, HD), BF16)] * (near_count - 1),
    )
    received_first = [to_near(value, 0, near) for near, value in enumerate(sends_first, 1)]
    (input_grads,) = call(
        functools.partial(second_rows_kernel, sizes),
        "second_rows",
        (
            segment_inputs,
            norm_gain,
            inverse,
            arrived,
            output_grads,
            query_grad_second,
            input_grad_first,
        ),
        [shape((1, ticks, rows, columns), BF16)],
    )
    keep_shape = shape((block, HD), F32)
    keep_first, send_first = call(
        functools.partial(first_near_kernel, sizes),
        "first_near",
        (own_first, *received_first),
        [keep_shape, shape((block, HD), BF16)],
    )
    keep_second, gain_sum, send_second = call(
        functools.partial(second_near_kernel, sizes),
        "second_near",
        (own_second, gain_rows, *received),
        [keep_shape, gain_shape, shape((block + gain_count, HD), BF16)],
    )
    grads_shape = shape((1, ticks, block, HD), F32)
    key_grads, value_grads, gain_grads = call(
        functools.partial(finish_kernel, sizes),
        "finish",
        (keep_first, keep_second, to_far(send_first), to_far(send_second), gain_sum),
        [grads_shape, grads_shape, gain_shape],
    )
    return input_grads, key_grads, value_grads, gain_grads.reshape(1, columns)


def solution(mesh):
    in_specs = (
        P("pipe", None, ("ctx", "tp"), None),
        P("pipe", None, "ctx", "tp"),
        P("pipe", None, "ctx", "tp"),
        P("pipe", None),
        P("pipe", ("ctx", "tp"), None),
        P(None, ("ctx", "tp"), None),
        P(),
    )
    out_specs = (
        P("pipe", None, ("ctx", "tp"), None),
        P("pipe", None, "ctx", "tp"),
        P("pipe", None, "ctx", "tp"),
        P("pipe", None),
    )
    return jax.shard_map(
        on_device, mesh=mesh, in_specs=in_specs, out_specs=out_specs, check_vma=False
    )
```

```python
import functools

import jax
import jax.numpy as jnp
from jax import lax
from jax.experimental import pallas as pl
from jax.experimental.pallas import tpu as pltpu
from jax.sharding import PartitionSpec as P

HD = 128
EPSILON = 1e-05
FILL = -1e30
SCALE = HD ** (-0.5)
TICKS = 2
F32 = jnp.float32
BF16 = jnp.bfloat16

NT = (((1,), (1,)), ((), ()))
NN = (((1,), (0,)), ((), ()))
TN = (((0,), (0,)), ((), ()))


def dot(a, b, dims):
    return lax.dot_general(a, b, dims, preferred_element_type=F32)


def in_order(values, owners):
    total = None
    for owner in range(len(values)):
        term = jnp.where(owners[0] == owner, values[0], 0.0)
        for value, whose in zip(values[1:], owners[1:]):
            term = jnp.where(whose == owner, value, term)
        total = term if total is None else total + term
    return total


def pack_kernel(tp_count, half, both_ref, own_ref, other_ref):
    parity = lax.axis_index("tp") // (tp_count // 2)
    own_first = pl.multiple_of(parity * half, half)
    other_first = pl.multiple_of((1 - parity) * half, half)
    for kind in range(2):
        for tick in range(TICKS):
            own_ref[tick, kind] = both_ref[kind, tick, pl.ds(own_first, half), :]
            other_ref[tick, kind] = both_ref[kind, tick, pl.ds(other_first, half), :]


def norm_kernel(sizes, doc_ref, x_ref, gain_ref, query_ref, inverse_ref, mask_ref):
    rows, columns = sizes[0], sizes[5]
    for tick in range(TICKS):
        squares = jnp.zeros((rows, HD), F32)
        for first in range(0, columns, HD):
            part = x_ref[0, tick, :, first : first + HD].astype(F32)
            squares = squares + part * part
        mean = jnp.sum(squares, axis=1, keepdims=True) * (1.0 / columns)
        inverse = jnp.broadcast_to(lax.rsqrt(mean + EPSILON), (rows, HD))
        inverse_ref[tick] = inverse
        for first in range(0, columns, HD):
            here = slice(first, first + HD)
            normed = x_ref[0, tick, :, here].astype(F32) * inverse
            query_ref[tick, :, here] = (normed * gain_ref[:, here]).astype(BF16)
        mask_ref[tick] = jnp.where(visible_keys(sizes, tick, doc_ref), 0.0, FILL)


class Group:
    def __init__(self, sizes, turn):
        self.rows, self.group = sizes[0], sizes[4]
        width = self.group * HD
        self.head_group = lax.axis_index("tp") ^ turn
        self.first = pl.multiple_of(self.head_group * width, width)

    def head(self, index):
        return pl.ds(self.first + index * HD, HD)

    def stacked(self, load):
        return jnp.concatenate([load(self.head(index)) for index in range(self.group)], axis=0)

    def unstacked(self, value):
        return [value[index * self.rows : (index + 1) * self.rows] for index in range(self.group)]


def waiting_from(waiting_ref):
    return lambda where: waiting_ref[0, :, where]


def arriving_from(output_ref, chip_ref, link_ref):
    place = lax.axis_index("pipe")
    last = place == lax.axis_size("pipe") - 1
    even = place % 2 == 0

    def arriving(where):
        arrived = jnp.where(even, chip_ref[:, where], link_ref[:, where])
        return jnp.where(last, output_ref[0, :, where], arrived)

    return arriving


def visible_keys(sizes, tick, doc_ref):
    rows, half, cycle, tp_count, group, columns = sizes
    cycle_place = lax.axis_index("ctx")
    tp_place = lax.axis_index("tp")
    parity = tp_place // (tp_count // 2)
    stacked = group * rows

    def section_first(owner):
        return half * jnp.where(parity == 0, owner, 2 * cycle - 1 - owner)

    row_first = section_first(cycle_place) + (tp_place % (tp_count // 2)) * rows
    query_pos = row_first + (lax.broadcasted_iota(jnp.int32, (1, stacked), 1) & (rows - 1))
    key_place = lax.broadcasted_iota(jnp.int32, (cycle * half, 1), 0)
    key_pos = key_place + section_first(cycle_place)
    for turn in range(1, cycle):
        first = section_first((cycle_place - turn + cycle) % cycle)
        key_pos = jnp.where(key_place >= turn * half, key_place - turn * half + first, key_pos)
    micro = lax.axis_index("pipe") + tick
    closing = jnp.int32(0)
    query_start = jnp.zeros((1, stacked), jnp.int32)
    for doc in range(doc_ref.shape[1]):
        length = doc_ref[micro, doc]
        closing = closing + length
        query_start = query_start + jnp.where(closing <= query_pos, length, 0)
    return (key_pos <= query_pos) & (key_pos >= query_start)


def probabilities(mask, products):
    scores = SCALE * products + mask
    weights = jnp.exp(scores - jnp.max(scores, axis=0, keepdims=True))
    return weights * (1.0 / jnp.sum(weights, axis=0, keepdims=True))


def score_grads(probs, prob_grad):
    row_term = jnp.sum(probs * prob_grad, axis=0, keepdims=True)
    return (probs * (prob_grad - row_term)).astype(BF16)


class Keys:
    def __init__(self, sizes, tick, refs):
        self.near_count = sizes[3] // 2
        self.tick = tick
        self.refs = refs

    def __call__(self, near, kind):
        parts = [ref[self.tick, kind] for ref in self.refs[near :: self.near_count]]
        return jnp.concatenate(parts, axis=0)


def place_of(sizes, far, kind):
    half = sizes[1]
    return slice((far * 2 + kind) * half, (far * 2 + kind + 1) * half)


def put_key_grads(sizes, turn, parts, own_ref, message_refs):
    half, cycle, tp_count = sizes[1:4]
    near_count = tp_count // 2
    near, far = turn % near_count, turn // near_count
    for kind, part in enumerate(parts):
        here = place_of(sizes, far, kind)
        for step in range(cycle):
            piece = part[step * half : (step + 1) * half]
            if step == 0 and near == 0:
                own_ref[here, :] = piece
            else:
                message_refs[step * near_count + near - 1][here, :] = piece.astype(BF16)


def gain_terms(columns_of, query_grad, normed_of, gain_rows_ref):
    rows = []
    for index, low in enumerate(columns_of.unstacked(query_grad)):
        term = low.astype(F32) * normed_of(columns_of.head(index))
        rows.append(jnp.sum(term, axis=0, keepdims=True))
    group = columns_of.group
    place = pl.ds(pl.multiple_of(columns_of.head_group * group, group), group)
    gain_rows_ref[place, :] = jnp.concatenate(rows, axis=0)


def coupled_terms(columns_of, query_grad, normed_of, gain_ref, coupled):
    for index, low in enumerate(columns_of.unstacked(query_grad)):
        where = columns_of.head(index)
        coupled = coupled + low.astype(F32) * gain_ref[:, where] * normed_of(where)
    return coupled


def write_input_grads(sizes, coupled, query_grad_of, normed_of, gain_ref, inverse, arriving, write):
    coupling = jnp.sum(coupled, axis=1, keepdims=True) * (1.0 / sizes[5])
    for turn in range(sizes[3]):
        columns_of = Group(sizes, turn)
        for index, low in enumerate(columns_of.unstacked(query_grad_of(turn))):
            where = columns_of.head(index)
            scaled = low.astype(F32) * gain_ref[:, where]
            result = arriving(where).astype(F32) + inverse * (scaled - normed_of(where) * coupling)
            write(where, result.astype(BF16))


def normed_from(x_ref, tick, inverse):
    return lambda where: x_ref[0, tick, :, where].astype(F32) * inverse


def first_half(sizes, far, keys, mask, query_ref, arriving, dscore_ref, probs_ref):
    near_count = sizes[3] // 2
    nears = range(near_count)
    columns_of = [Group(sizes, far * near_count + near) for near in nears]
    scores, prob_grads = [], []
    for near in nears:
        query = columns_of[near].stacked(lambda where: query_ref[0, :, where])
        scores.append(dot(keys(near, 0), query, NT))
        prob_grads.append(dot(keys(near, 1), columns_of[near].stacked(arriving), NT))
    dscores = []
    for near in nears:
        probs = probabilities(mask, scores[near])
        dscores.append(score_grads(probs, prob_grads[near]))
        dscore_ref[near] = dscores[near]
        probs_ref[near] = probs.astype(BF16)
    return [(SCALE * dot(dscores[near], keys(near, 0), TN)).astype(BF16) for near in nears]


def first_near_rows_kernel(sizes, *refs):
    members = sizes[2] * sizes[3] // 2
    x_ref, gain_ref, query_ref, inverse_ref, mask_ref, waiting_ref = refs[:6]
    keys = Keys(sizes, 0, refs[6 : 6 + members])
    query_grad_ref, dscore_ref, probs_ref, coupled_ref = refs[6 + members :]
    query_grads = first_half(
        sizes,
        0,
        keys,
        mask_ref[0],
        query_ref,
        waiting_from(waiting_ref),
        dscore_ref,
        probs_ref,
    )
    normed_of = normed_from(x_ref, 0, inverse_ref[0])
    coupled = jnp.zeros((sizes[0], HD), F32)
    for near, query_grad in enumerate(query_grads):
        query_grad_ref[near] = query_grad
        coupled = coupled_terms(Group(sizes, near), query_grad, normed_of, gain_ref, coupled)
    coupled_ref[...] = coupled


def first_far_rows_kernel(sizes, *refs):
    near_count = sizes[3] // 2
    members = sizes[2] * near_count
    x_ref, gain_ref, query_ref, inverse_ref, mask_ref, waiting_ref = refs[:6]
    keys = Keys(sizes, 0, refs[6 : 6 + members])
    near_grad_ref, coupled_ref = refs[6 + members : 8 + members]
    input_grad_ref, query_grad_ref, dscore_ref, probs_ref = refs[8 + members :]
    arriving = waiting_from(waiting_ref)
    query_grads = first_half(
        sizes, 1, keys, mask_ref[0], query_ref, arriving, dscore_ref, probs_ref
    )
    normed_of = normed_from(x_ref, 0, inverse_ref[0])
    coupled = coupled_ref[...]
    for near, query_grad in enumerate(query_grads):
        query_grad_ref[near] = query_grad
        coupled = coupled_terms(
            Group(sizes, near_count + near), query_grad, normed_of, gain_ref, coupled
        )

    def query_grad_of(turn):
        return near_grad_ref[turn] if turn < near_count else query_grads[turn - near_count]

    def write(where, result):
        input_grad_ref[:, where] = result

    write_input_grads(
        sizes, coupled, query_grad_of, normed_of, gain_ref, inverse_ref[0], arriving, write
    )


def first_keys_kernel(sizes, *refs):
    half, cycle, tp_count = sizes[1:4]
    near_count = tp_count // 2
    x_ref, query_ref, inverse_ref, waiting_ref = refs[:4]
    query_grad_refs, dscore_refs, probs_refs = refs[4:6], refs[6:8], refs[8:10]
    gain_rows_ref, own_ref = refs[10:12]
    send_refs = refs[12:]
    arriving = waiting_from(waiting_ref)
    normed_of = normed_from(x_ref, 0, inverse_ref[0])
    for turn in range(tp_count):
        near, far = turn % near_count, turn // near_count
        columns_of = Group(sizes, turn)
        query = columns_of.stacked(lambda where: query_ref[0, :, where])
        grad = columns_of.stacked(arriving)
        parts = (
            SCALE * dot(dscore_refs[far][near], query, NN),
            dot(probs_refs[far][near], grad, NN),
        )
        for kind, part in enumerate(parts):
            here = place_of(sizes, far, kind)
            own_ref[near, here, :] = part[:half]
            for step, ref in enumerate(send_refs, 1):
                ref[near, here, :] = part[step * half : (step + 1) * half].astype(BF16)
        gain_terms(columns_of, query_grad_refs[far][near], normed_of, gain_rows_ref)


def both_sets(sizes, refs):
    near_count = sizes[3] // 2
    members = sizes[2] * near_count
    sets = [Keys(sizes, 1, refs[:members]), Keys(sizes, 1, refs[members:])]
    return lambda turn, kind: sets[turn // near_count](turn % near_count, kind)


def second_probs_kernel(sizes, *refs):
    turns = range(sizes[3])
    mask_ref, query_ref = refs[:2]
    keys, probs_ref = both_sets(sizes, refs[2:-1]), refs[-1]
    mask = mask_ref[1]
    scores = []
    for turn in turns:
        query = Group(sizes, turn).stacked(lambda where: query_ref[1, :, where])
        scores.append(dot(keys(turn, 0), query, NT))
    for turn in turns:
        probs_ref[turn] = probabilities(mask, scores[turn])


def second_keys_kernel(sizes, *refs):
    cycle, tp_count = sizes[2:4]
    turns = range(tp_count)
    kv_count = cycle * tp_count
    x_ref, query_ref, inverse_ref, output_ref, chip_ref, link_ref = refs[:6]
    probs_ref, before_ref, *refs = refs[6:]
    keys, refs = both_sets(sizes, refs[:kv_count]), refs[kv_count:]
    query_grad_ref, gain_rows_ref, own_ref = refs[:3]
    message_refs, gain_scratch = refs[3:-1], refs[-1]
    arriving = arriving_from(output_ref, chip_ref, link_ref)
    normed_of = normed_from(x_ref, 1, inverse_ref[1])
    columns_of = [Group(sizes, turn) for turn in turns]
    grads = [columns_of[turn].stacked(arriving) for turn in turns]
    prob_grads = [dot(keys(turn, 1), grads[turn], NT) for turn in turns]
    value_grads = [dot(probs_ref[turn].astype(BF16), grads[turn], NN) for turn in turns]
    dscores = [score_grads(probs_ref[turn], prob_grads[turn]) for turn in turns]
    query_grads = [
        (SCALE * dot(dscores[turn], keys(turn, 0), TN)).astype(BF16) for turn in turns
    ]
    for turn in turns:
        query = columns_of[turn].stacked(lambda where: query_ref[1, :, where])
        key_grad = SCALE * dot(dscores[turn], query, NN)
        put_key_grads(sizes, turn, (key_grad, value_grads[turn]), own_ref, message_refs)
    for turn in turns:
        query_grad_ref[turn] = query_grads[turn]
        gain_terms(columns_of[turn], query_grads[turn], normed_of, gain_scratch)
    gain_rows = gain_scratch[...] + before_ref[...]
    gain_rows_ref[...] = gain_rows
    gain_low = gain_rows.astype(BF16)
    for ref in message_refs:
        ref[own_ref.shape[0] :, :] = gain_low


def first_sum_kernel(sizes, *refs):
    cycle = sizes[2]
    parts, own_ref, message_refs = refs[:cycle], refs[cycle], refs[cycle + 1 :]
    for near in range(sizes[3] // 2):
        total = parts[0][near]
        for ref in parts[1:]:
            total = total + ref[near].astype(F32)
        if near == 0:
            own_ref[...] = total
        else:
            message_refs[near - 1][...] = total.astype(BF16)


def second_rows_kernel(sizes, *refs):
    x_ref, gain_ref, inverse_ref, output_ref, chip_ref, link_ref = refs[:6]
    query_grad_ref, first_ref, input_grads_ref = refs[6:]
    input_grads_ref[0, 0] = first_ref[...]
    inverse = inverse_ref[1]
    normed_of = normed_from(x_ref, 1, inverse)
    coupled = jnp.zeros((sizes[0], HD), F32)
    for turn in range(sizes[3]):
        coupled = coupled_terms(
            Group(sizes, turn), query_grad_ref[turn], normed_of, gain_ref, coupled
        )

    def write(where, result):
        input_grads_ref[0, 1, :, where] = result

    write_input_grads(
        sizes,
        coupled,
        lambda turn: query_grad_ref[turn],
        normed_of,
        gain_ref,
        inverse,
        arriving_from(output_ref, chip_ref, link_ref),
        write,
    )


def first_near_kernel(sizes, own_ref, *refs):
    block = 2 * sizes[1]
    keep_ref, send_ref = refs[-2:]
    total = own_ref[...]
    for ref in refs[:-2]:
        total = total + ref[...].astype(F32)
    keep_ref[...] = total[:block]
    send_ref[...] = total[block:].astype(BF16)


def second_near_kernel(sizes, *refs):
    rows, half, cycle, tp_count, group, columns = sizes
    near_count = tp_count // 2
    members = cycle * near_count
    own_ref, gain_ref = refs[:2]
    message_refs = refs[2 : 1 + members]
    keep_ref, gain_sum_ref, send_ref = refs[1 + members :]
    block = 2 * half
    total = own_ref[...]
    for ref in message_refs:
        total = total + ref[: 2 * block, :].astype(F32)
    keep_ref[...] = total[:block]
    send_ref[:block, :] = total[block:].astype(BF16)
    cycle_place = lax.axis_index("ctx")
    near_place = lax.axis_index("tp") % near_count
    values = [gain_ref[...].astype(BF16).astype(F32)]
    owners = [cycle_place * near_count + near_place]
    for place, ref in enumerate(message_refs, 1):
        step, near = place // near_count, place % near_count
        values.append(ref[2 * block :, :].astype(F32))
        owners.append(((cycle_place + step) % cycle) * near_count + (near_place ^ near))
    gain = in_order(values, owners)
    gain_sum_ref[...] = gain
    send_ref[block:, :] = gain.astype(BF16)


def finish_kernel(sizes, *refs):
    half = sizes[1]
    keep_refs, receive_refs, gain_ref = refs[:TICKS], refs[TICKS : 2 * TICKS], refs[2 * TICKS]
    key_ref, value_ref, gain_out_ref = refs[2 * TICKS + 1 :]
    parity = lax.axis_index("tp") // (sizes[3] // 2)
    block = 2 * half
    own_first = pl.multiple_of(parity * half, half)
    other_first = pl.multiple_of((1 - parity) * half, half)
    for tick in range(TICKS):
        for kind, out in enumerate((key_ref, value_ref)):
            here = slice(kind * half, (kind + 1) * half)
            out[0, tick, pl.ds(own_first, half), :] = keep_refs[tick][here, :]
            out[0, tick, pl.ds(other_first, half), :] = receive_refs[tick][here, :].astype(F32)
    own = gain_ref[...].astype(BF16).astype(F32)
    gain_out_ref[...] = own + receive_refs[TICKS - 1][block:, :].astype(F32)


def shape(dims, dtype):
    return jax.ShapeDtypeStruct(dims, dtype)


def on_device(segment_inputs, keys, values, norm_gain, waiting_grads, output_grads, doc_lengths):
    cycle = lax.axis_size("ctx")
    tp_count = lax.axis_size("tp")
    pipe_count = lax.axis_size("pipe")
    _, ticks, rows, columns = segment_inputs.shape
    half = keys.shape[2] // 2
    group = columns // (tp_count * HD)
    gain_count = columns // HD
    sizes = (rows, half, cycle, tp_count, group, columns)
    block = 2 * half
    key_count = cycle * half
    stacked = group * rows
    score_bytes = key_count * stacked * 4
    usual_limit = min(56 << 20, (12 << 20) + 20 * score_bytes)

    def call(kernel, name, operands, out_shape, scratch=(), scalars=0):
        in_specs = [pl.BlockSpec(memory_space=pltpu.SMEM)] * scalars
        in_specs += [pl.BlockSpec(memory_space=pltpu.VMEM)] * (len(operands) - scalars)
        return pl.pallas_call(
            kernel,
            out_shape=out_shape,
            in_specs=in_specs,
            out_specs=[pl.BlockSpec(memory_space=pltpu.VMEM)] * len(out_shape),
            scratch_shapes=scratch,
            compiler_params=pltpu.CompilerParams(vmem_limit_bytes=usual_limit),
            name=name,
        )(*operands)

    near_count = tp_count // 2

    def to_near(value, step, near):
        if step == 0:
            return lax.ppermute(value, "tp", [(i, i ^ near) for i in range(tp_count)])
        if near == 0:
            return lax.ppermute(value, "ctx", [(i, (i + step) % cycle) for i in range(cycle)])
        pairs = [
            (c * tp_count + t, ((c + step) % cycle) * tp_count + (t ^ near))
            for c in range(cycle)
            for t in range(tp_count)
        ]
        return lax.ppermute(value, ("ctx", "tp"), pairs)

    def to_far(value):
        return lax.ppermute(value, "tp", [(i, i ^ near_count) for i in range(tp_count)])

    sections = shape((ticks, 2, half, HD), BF16)
    own_kv, other_kv = call(
        functools.partial(pack_kernel, tp_count, half),
        "pack_kv",
        (jnp.stack([keys[0], values[0]]),),
        [sections, sections],
    )
    far_kv = to_far(other_kv)
    places = [(step, near) for step in range(cycle) for near in range(near_count)][1:]
    kv = [
        block if place == (0, 0) else to_near(block, *place)
        for block in (own_kv, far_kv)
        for place in [(0, 0)] + places
    ]
    own_set, far_set = kv[: len(kv) // 2], kv[len(kv) // 2 :]
    queries, inverse, masks = call(
        functools.partial(norm_kernel, sizes),
        "norm",
        (doc_lengths, segment_inputs, norm_gain),
        [
            shape((ticks, rows, columns), BF16),
            shape((ticks, rows, HD), F32),
            shape((ticks, key_count, stacked), F32),
        ],
        scalars=1,
    )

    low_rows = shape((rows, columns), BF16)
    low_scores = shape((near_count, key_count, stacked), BF16)
    low_grads = shape((near_count, stacked, HD), BF16)
    rows_operands = (segment_inputs, norm_gain, queries, inverse, masks, waiting_grads)
    query_grad_near, dscore_near, probs_near, coupled = call(
        functools.partial(first_near_rows_kernel, sizes),
        "first_near_rows",
        (*rows_operands, *own_set),
        [low_grads, low_scores, low_scores, shape((rows, HD), F32)],
    )
    input_grad_first, query_grad_far, dscore_far, probs_far = call(
        functools.partial(first_far_rows_kernel, sizes),
        "first_far_rows",
        (*rows_operands, *far_set, query_grad_near, coupled),
        [low_rows, low_grads, low_scores, low_scores],
    )
    over_link = lax.ppermute(
        input_grad_first, "pipe", [(i, i - 1) for i in range(2, pipe_count, 2)]
    )
    on_chip = lax.ppermute(input_grad_first, "pipe", [(i, i ^ 1) for i in range(pipe_count)])
    gain_shape = shape((gain_count, HD), F32)
    pair_rows = 2 * block
    own_shape = shape((pair_rows, HD), F32)
    first_sums = (near_count, pair_rows, HD)
    gain_first, *sums_first = call(
        functools.partial(first_keys_kernel, sizes),
        "first_keys",
        (
            segment_inputs,
            queries,
            inverse,
            waiting_grads,
            query_grad_near,
            query_grad_far,
            dscore_near,
            dscore_far,
            probs_near,
            probs_far,
        ),
        [gain_shape, shape(first_sums, F32)] + [shape(first_sums, BF16)] * (cycle - 1),
    )
    sums_first = sums_first[:1] + [
        to_near(value, -step, 0) for step, value in enumerate(sums_first[1:], 1)
    ]
    (probs_second,) = call(
        functools.partial(second_probs_kernel, sizes),
        "second_probs",
        (masks, queries, *kv),
        [shape((tp_count, key_count, stacked), F32)],
    )
    message = shape((pair_rows + gain_count, HD), BF16)
    query_grad_second, gain_rows, own_second, *sends = call(
        functools.partial(second_keys_kernel, sizes),
        "second_keys",
        (
            segment_inputs,
            queries,
            inverse,
            output_grads,
            on_chip,
            over_link,
            probs_second,
            gain_first,
            *kv,
        ),
        [shape((tp_count, stacked, HD), BF16), gain_shape, own_shape] + [message] * len(places),
        scratch=[pltpu.VMEM((gain_count, HD), F32)],
    )
    received = [to_near(value, -step, near) for value, (step, near) in zip(sends, places)]
    own_first, *sends_first = call(
        functools.partial(first_sum_kernel, sizes),
        "first_sum",
        sums_first,
        [own_shape] + [shape((pair_rows, HD), BF16)] * (near_count - 1),
    )
    received_first = [to_near(value, 0, near) for near, value in enumerate(sends_first, 1)]
    (input_grads,) = call(
        functools.partial(second_rows_kernel, sizes),
        "second_rows",
        (
            segment_inputs,
            norm_gain,
            inverse,
            output_grads,
            on_chip,
            over_link,
            query_grad_second,
            input_grad_first,
        ),
        [shape((1, ticks, rows, columns), BF16)],
    )
    keep_shape = shape((block, HD), F32)
    keep_first, send_first = call(
        functools.partial(first_near_kernel, sizes),
        "first_near",
        (own_first, *received_first),
        [keep_shape, shape((block, HD), BF16)],
    )
    keep_second, gain_sum, send_second = call(
        functools.partial(second_near_kernel, sizes),
        "second_near",
        (own_second, gain_rows, *received),
        [keep_shape, gain_shape, shape((block + gain_count, HD), BF16)],
    )
    grads_shape = shape((1, ticks, block, HD), F32)
    key_grads, value_grads, gain_grads = call(
        functools.partial(finish_kernel, sizes),
        "finish",
        (keep_first, keep_second, to_far(send_first), to_far(send_second), gain_sum),
        [grads_shape, grads_shape, gain_shape],
    )
    return input_grads, key_grads, value_grads, gain_grads.reshape(1, columns)


def solution(mesh):
    in_specs = (
        P("pipe", None, ("ctx", "tp"), None),
        P("pipe", None, "ctx", "tp"),
        P("pipe", None, "ctx", "tp"),
        P("pipe", None),
        P("pipe", ("ctx", "tp"), None),
        P(None, ("ctx", "tp"), None),
        P(),
    )
    out_specs = (
        P("pipe", None, ("ctx", "tp"), None),
        P("pipe", None, "ctx", "tp"),
        P("pipe", None, "ctx", "tp"),
        P("pipe", None),
    )
    return jax.shard_map(
        on_device, mesh=mesh, in_specs=in_specs, out_specs=out_specs, check_vma=False
    )
```

```python
import functools

import jax
import jax.numpy as jnp
from jax import lax
from jax.experimental import pallas as pl
from jax.experimental.pallas import tpu as pltpu
from jax.sharding import PartitionSpec as P

HD = 128
EPSILON = 1e-05
FILL = -1e30
SCALE = HD ** (-0.5)
TICKS = 2
F32 = jnp.float32
BF16 = jnp.bfloat16

NT = (((1,), (1,)), ((), ()))
NN = (((1,), (0,)), ((), ()))
TN = (((0,), (0,)), ((), ()))


def dot(a, b, dims):
    return lax.dot_general(a, b, dims, preferred_element_type=F32)


def in_order(values, owners):
    total = None
    for owner in range(len(values)):
        term = jnp.where(owners[0] == owner, values[0], 0.0)
        for value, whose in zip(values[1:], owners[1:]):
            term = jnp.where(whose == owner, value, term)
        total = term if total is None else total + term
    return total


def pack_kernel(tp_count, half, both_ref, own_ref, other_ref):
    parity = lax.axis_index("tp") // (tp_count // 2)
    own_first = pl.multiple_of(parity * half, half)
    other_first = pl.multiple_of((1 - parity) * half, half)
    for kind in range(2):
        for tick in range(TICKS):
            own_ref[tick, kind] = both_ref[kind, tick, pl.ds(own_first, half), :]
            other_ref[tick, kind] = both_ref[kind, tick, pl.ds(other_first, half), :]


def norm_kernel(sizes, doc_ref, x_ref, gain_ref, query_ref, inverse_ref, mask_ref):
    rows, columns = sizes[0], sizes[5]
    for tick in range(TICKS):
        squares = jnp.zeros((rows, HD), F32)
        for first in range(0, columns, HD):
            part = x_ref[0, tick, :, first : first + HD].astype(F32)
            squares = squares + part * part
        mean = jnp.sum(squares, axis=1, keepdims=True) * (1.0 / columns)
        inverse = jnp.broadcast_to(lax.rsqrt(mean + EPSILON), (rows, HD))
        inverse_ref[tick] = inverse
        for first in range(0, columns, HD):
            here = slice(first, first + HD)
            normed = x_ref[0, tick, :, here].astype(F32) * inverse
            query_ref[tick, :, here] = (normed * gain_ref[:, here]).astype(BF16)
        mask_ref[tick] = jnp.where(visible_keys(sizes, tick, doc_ref), 0.0, FILL)


class Group:
    def __init__(self, sizes, turn):
        self.rows, self.group = sizes[0], sizes[4]
        width = self.group * HD
        self.head_group = lax.axis_index("tp") ^ turn
        self.first = pl.multiple_of(self.head_group * width, width)

    def head(self, index):
        return pl.ds(self.first + index * HD, HD)

    def stacked(self, load):
        return jnp.concatenate([load(self.head(index)) for index in range(self.group)], axis=0)

    def unstacked(self, value):
        return [value[index * self.rows : (index + 1) * self.rows] for index in range(self.group)]


def waiting_from(waiting_ref):
    return lambda where: waiting_ref[0, :, where]


def arriving_from(output_ref, chip_ref, link_ref):
    place = lax.axis_index("pipe")
    last = place == lax.axis_size("pipe") - 1
    even = place % 2 == 0

    def arriving(where):
        arrived = jnp.where(even, chip_ref[:, where], link_ref[:, where])
        return jnp.where(last, output_ref[0, :, where], arrived)

    return arriving


def visible_keys(sizes, tick, doc_ref):
    rows, half, cycle, tp_count, group, columns = sizes
    cycle_place = lax.axis_index("ctx")
    tp_place = lax.axis_index("tp")
    parity = tp_place // (tp_count // 2)
    stacked = group * rows

    def section_first(owner):
        return half * jnp.where(parity == 0, owner, 2 * cycle - 1 - owner)

    row_first = section_first(cycle_place) + (tp_place % (tp_count // 2)) * rows
    query_pos = row_first + (lax.broadcasted_iota(jnp.int32, (1, stacked), 1) & (rows - 1))
    key_place = lax.broadcasted_iota(jnp.int32, (cycle * half, 1), 0)
    key_pos = key_place + section_first(cycle_place)
    for turn in range(1, cycle):
        first = section_first((cycle_place - turn + cycle) % cycle)
        key_pos = jnp.where(key_place >= turn * half, key_place - turn * half + first, key_pos)
    micro = lax.axis_index("pipe") + tick
    closing = jnp.int32(0)
    query_start = jnp.zeros((1, stacked), jnp.int32)
    for doc in range(doc_ref.shape[1]):
        length = doc_ref[micro, doc]
        closing = closing + length
        query_start = query_start + jnp.where(closing <= query_pos, length, 0)
    return (key_pos <= query_pos) & (key_pos >= query_start)


def probabilities(mask, products):
    scores = SCALE * products + mask
    weights = jnp.exp(scores - jnp.max(scores, axis=0, keepdims=True))
    return weights * (1.0 / jnp.sum(weights, axis=0, keepdims=True))


def score_grads(probs, prob_grad):
    row_term = jnp.sum(probs * prob_grad, axis=0, keepdims=True)
    return (probs * (prob_grad - row_term)).astype(BF16)


class Keys:
    def __init__(self, sizes, tick, refs):
        self.near_count = sizes[3] // 2
        self.tick = tick
        self.refs = refs

    def __call__(self, near, kind):
        parts = [ref[self.tick, kind] for ref in self.refs[near :: self.near_count]]
        return jnp.concatenate(parts, axis=0)


def place_of(sizes, far, kind):
    half = sizes[1]
    return slice((far * 2 + kind) * half, (far * 2 + kind + 1) * half)


def put_key_grads(sizes, turn, parts, own_ref, message_refs):
    half, cycle, tp_count = sizes[1:4]
    near_count = tp_count // 2
    near, far = turn % near_count, turn // near_count
    for kind, part in enumerate(parts):
        here = place_of(sizes, far, kind)
        for step in range(cycle):
            piece = part[step * half : (step + 1) * half]
            if step == 0 and near == 0:
                own_ref[here, :] = piece
            else:
                message_refs[step * near_count + near - 1][here, :] = piece.astype(BF16)


def gain_terms(columns_of, query_grad, normed_of, gain_rows_ref):
    rows = []
    for index, low in enumerate(columns_of.unstacked(query_grad)):
        term = low.astype(F32) * normed_of(columns_of.head(index))
        rows.append(jnp.sum(term, axis=0, keepdims=True))
    group = columns_of.group
    place = pl.ds(pl.multiple_of(columns_of.head_group * group, group), group)
    gain_rows_ref[place, :] = jnp.concatenate(rows, axis=0)


def coupled_terms(columns_of, query_grad, normed_of, gain_ref, coupled):
    for index, low in enumerate(columns_of.unstacked(query_grad)):
        where = columns_of.head(index)
        coupled = coupled + low.astype(F32) * gain_ref[:, where] * normed_of(where)
    return coupled


def write_input_grads(sizes, coupled, query_grad_of, normed_of, gain_ref, inverse, arriving, write):
    coupling = jnp.sum(coupled, axis=1, keepdims=True) * (1.0 / sizes[5])
    for turn in range(sizes[3]):
        columns_of = Group(sizes, turn)
        for index, low in enumerate(columns_of.unstacked(query_grad_of(turn))):
            where = columns_of.head(index)
            scaled = low.astype(F32) * gain_ref[:, where]
            result = arriving(where).astype(F32) + inverse * (scaled - normed_of(where) * coupling)
            write(where, result.astype(BF16))


def normed_from(x_ref, tick, inverse):
    return lambda where: x_ref[0, tick, :, where].astype(F32) * inverse


def first_half(sizes, far, keys, mask, query_ref, arriving, dscore_ref, probs_ref):
    near_count = sizes[3] // 2
    nears = range(near_count)
    columns_of = [Group(sizes, far * near_count + near) for near in nears]
    scores, prob_grads = [], []
    for near in nears:
        query = columns_of[near].stacked(lambda where: query_ref[0, :, where])
        scores.append(dot(keys(near, 0), query, NT))
        prob_grads.append(dot(keys(near, 1), columns_of[near].stacked(arriving), NT))
    dscores = []
    for near in nears:
        probs = probabilities(mask, scores[near])
        dscores.append(score_grads(probs, prob_grads[near]))
        dscore_ref[near] = dscores[near]
        probs_ref[near] = probs.astype(BF16)
    return [(SCALE * dot(dscores[near], keys(near, 0), TN)).astype(BF16) for near in nears]


def first_near_rows_kernel(sizes, *refs):
    members = sizes[2] * sizes[3] // 2
    x_ref, gain_ref, query_ref, inverse_ref, mask_ref, waiting_ref = refs[:6]
    keys = Keys(sizes, 0, refs[6 : 6 + members])
    query_grad_ref, dscore_ref, probs_ref, coupled_ref = refs[6 + members :]
    query_grads = first_half(
        sizes,
        0,
        keys,
        mask_ref[0],
        query_ref,
        waiting_from(waiting_ref),
        dscore_ref,
        probs_ref,
    )
    normed_of = normed_from(x_ref, 0, inverse_ref[0])
    coupled = jnp.zeros((sizes[0], HD), F32)
    for near, query_grad in enumerate(query_grads):
        query_grad_ref[near] = query_grad
        coupled = coupled_terms(Group(sizes, near), query_grad, normed_of, gain_ref, coupled)
    coupled_ref[...] = coupled


def first_far_rows_kernel(sizes, *refs):
    near_count = sizes[3] // 2
    members = sizes[2] * near_count
    x_ref, gain_ref, query_ref, inverse_ref, mask_ref, waiting_ref = refs[:6]
    keys = Keys(sizes, 0, refs[6 : 6 + members])
    near_grad_ref, coupled_ref = refs[6 + members : 8 + members]
    input_grad_ref, query_grad_ref, dscore_ref, probs_ref = refs[8 + members :]
    arriving = waiting_from(waiting_ref)
    query_grads = first_half(
        sizes, 1, keys, mask_ref[0], query_ref, arriving, dscore_ref, probs_ref
    )
    normed_of = normed_from(x_ref, 0, inverse_ref[0])
    coupled = coupled_ref[...]
    for near, query_grad in enumerate(query_grads):
        query_grad_ref[near] = query_grad
        coupled = coupled_terms(
            Group(sizes, near_count + near), query_grad, normed_of, gain_ref, coupled
        )

    def query_grad_of(turn):
        return near_grad_ref[turn] if turn < near_count else query_grads[turn - near_count]

    def write(where, result):
        input_grad_ref[:, where] = result

    write_input_grads(
        sizes, coupled, query_grad_of, normed_of, gain_ref, inverse_ref[0], arriving, write
    )


def first_keys_kernel(sizes, *refs):
    half, cycle, tp_count = sizes[1:4]
    near_count = tp_count // 2
    x_ref, query_ref, inverse_ref, waiting_ref = refs[:4]
    query_grad_refs, dscore_refs, probs_refs = refs[4:6], refs[6:8], refs[8:10]
    gain_rows_ref, own_ref = refs[10:12]
    send_refs = refs[12:]
    arriving = waiting_from(waiting_ref)
    normed_of = normed_from(x_ref, 0, inverse_ref[0])
    for turn in range(tp_count):
        near, far = turn % near_count, turn // near_count
        columns_of = Group(sizes, turn)
        query = columns_of.stacked(lambda where: query_ref[0, :, where])
        grad = columns_of.stacked(arriving)
        parts = (
            SCALE * dot(dscore_refs[far][near], query, NN),
            dot(probs_refs[far][near], grad, NN),
        )
        for kind, part in enumerate(parts):
            here = place_of(sizes, far, kind)
            own_ref[near, here, :] = part[:half]
            for step, ref in enumerate(send_refs, 1):
                ref[near, here, :] = part[step * half : (step + 1) * half].astype(BF16)
        gain_terms(columns_of, query_grad_refs[far][near], normed_of, gain_rows_ref)


def both_sets(sizes, refs):
    near_count = sizes[3] // 2
    members = sizes[2] * near_count
    sets = [Keys(sizes, 1, refs[:members]), Keys(sizes, 1, refs[members:])]
    return lambda turn, kind: sets[turn // near_count](turn % near_count, kind)


def second_probs_kernel(sizes, *refs):
    turns = range(sizes[3])
    mask_ref, query_ref = refs[:2]
    keys, probs_ref = both_sets(sizes, refs[2:-1]), refs[-1]
    mask = mask_ref[1]
    scores = []
    for turn in turns:
        query = Group(sizes, turn).stacked(lambda where: query_ref[1, :, where])
        scores.append(dot(keys(turn, 0), query, NT))
    for turn in turns:
        probs_ref[turn] = probabilities(mask, scores[turn])


def second_keys_kernel(sizes, *refs):
    cycle, tp_count = sizes[2:4]
    turns = range(tp_count)
    kv_count = cycle * tp_count
    x_ref, query_ref, inverse_ref, output_ref, chip_ref, link_ref = refs[:6]
    probs_ref, before_ref, *refs = refs[6:]
    keys, refs = both_sets(sizes, refs[:kv_count]), refs[kv_count:]
    query_grad_ref, gain_rows_ref, own_ref = refs[:3]
    message_refs, gain_scratch = refs[3:-1], refs[-1]
    arriving = arriving_from(output_ref, chip_ref, link_ref)
    normed_of = normed_from(x_ref, 1, inverse_ref[1])
    columns_of = [Group(sizes, turn) for turn in turns]
    grads = [columns_of[turn].stacked(arriving) for turn in turns]
    prob_grads = [dot(keys(turn, 1), grads[turn], NT) for turn in turns]
    value_grads = [dot(probs_ref[turn].astype(BF16), grads[turn], NN) for turn in turns]
    dscores = [score_grads(probs_ref[turn], prob_grads[turn]) for turn in turns]
    query_grads = [
        (SCALE * dot(dscores[turn], keys(turn, 0), TN)).astype(BF16) for turn in turns
    ]
    for turn in turns:
        query = columns_of[turn].stacked(lambda where: query_ref[1, :, where])
        key_grad = SCALE * dot(dscores[turn], query, NN)
        put_key_grads(sizes, turn, (key_grad, value_grads[turn]), own_ref, message_refs)
    for turn in turns:
        query_grad_ref[turn] = query_grads[turn]
        gain_terms(columns_of[turn], query_grads[turn], normed_of, gain_scratch)
    gain_rows = gain_scratch[...] + before_ref[...]
    gain_rows_ref[...] = gain_rows
    gain_low = gain_rows.astype(BF16)
    for ref in message_refs:
        ref[own_ref.shape[0] :, :] = gain_low


def first_sum_kernel(sizes, *refs):
    cycle = sizes[2]
    parts, own_ref, message_refs = refs[:cycle], refs[cycle], refs[cycle + 1 :]
    for near in range(sizes[3] // 2):
        total = parts[0][near]
        for ref in parts[1:]:
            total = total + ref[near].astype(F32)
        if near == 0:
            own_ref[...] = total
        else:
            message_refs[near - 1][...] = total.astype(BF16)


def second_rows_kernel(sizes, *refs):
    x_ref, gain_ref, inverse_ref, output_ref, chip_ref, link_ref = refs[:6]
    query_grad_ref, first_ref, input_grads_ref = refs[6:]
    input_grads_ref[0, 0] = first_ref[...]
    inverse = inverse_ref[1]
    normed_of = normed_from(x_ref, 1, inverse)
    coupled = jnp.zeros((sizes[0], HD), F32)
    for turn in range(sizes[3]):
        coupled = coupled_terms(
            Group(sizes, turn), query_grad_ref[turn], normed_of, gain_ref, coupled
        )

    def write(where, result):
        input_grads_ref[0, 1, :, where] = result

    write_input_grads(
        sizes,
        coupled,
        lambda turn: query_grad_ref[turn],
        normed_of,
        gain_ref,
        inverse,
        arriving_from(output_ref, chip_ref, link_ref),
        write,
    )


def near_sum_kernel(sizes, *refs):
    rows, half, cycle, tp_count, group, columns = sizes
    near_count = tp_count // 2
    members = cycle * near_count
    own_ref, gain_ref = refs[:2]
    message_refs, refs = refs[2 : 1 + members], refs[1 + members :]
    own_first_ref, first_refs, refs = refs[0], refs[1:near_count], refs[near_count:]
    keep_ref, gain_sum_ref, send_ref = refs
    block = 2 * half
    first, second = own_first_ref[...], own_ref[...]
    for ref in message_refs:
        second = second + ref[: 2 * block, :].astype(F32)
    for ref in first_refs:
        first = first + ref[...].astype(F32)
    for tick, total in enumerate((first, second)):
        here = slice(tick * block, (tick + 1) * block)
        keep_ref[here, :] = total[:block]
        send_ref[here, :] = total[block:].astype(BF16)
    cycle_place = lax.axis_index("ctx")
    near_place = lax.axis_index("tp") % near_count
    values = [gain_ref[...].astype(BF16).astype(F32)]
    owners = [cycle_place * near_count + near_place]
    for place, ref in enumerate(message_refs, 1):
        step, near = place // near_count, place % near_count
        values.append(ref[2 * block :, :].astype(F32))
        owners.append(((cycle_place + step) % cycle) * near_count + (near_place ^ near))
    gain = in_order(values, owners)
    gain_sum_ref[...] = gain
    send_ref[TICKS * block :, :] = gain.astype(BF16)


def finish_kernel(sizes, keep_ref, gain_ref, receive_ref, key_ref, value_ref, gain_out_ref):
    half = sizes[1]
    parity = lax.axis_index("tp") // (sizes[3] // 2)
    own_first = pl.multiple_of(parity * half, half)
    other_first = pl.multiple_of((1 - parity) * half, half)
    for tick in range(TICKS):
        for kind, out in enumerate((key_ref, value_ref)):
            begin = (tick * 2 + kind) * half
            here = slice(begin, begin + half)
            out[0, tick, pl.ds(own_first, half), :] = keep_ref[here, :]
            out[0, tick, pl.ds(other_first, half), :] = receive_ref[here, :].astype(F32)
    own = gain_ref[...].astype(BF16).astype(F32)
    gain_out_ref[...] = own + receive_ref[TICKS * 2 * half :, :].astype(F32)


def shape(dims, dtype):
    return jax.ShapeDtypeStruct(dims, dtype)


def on_device(segment_inputs, keys, values, norm_gain, waiting_grads, output_grads, doc_lengths):
    cycle = lax.axis_size("ctx")
    tp_count = lax.axis_size("tp")
    pipe_count = lax.axis_size("pipe")
    _, ticks, rows, columns = segment_inputs.shape
    half = keys.shape[2] // 2
    group = columns // (tp_count * HD)
    gain_count = columns // HD
    sizes = (rows, half, cycle, tp_count, group, columns)
    block = 2 * half
    key_count = cycle * half
    stacked = group * rows
    score_bytes = key_count * stacked * 4
    usual_limit = min(56 << 20, (12 << 20) + 20 * score_bytes)

    def call(kernel, name, operands, out_shape, scratch=(), scalars=0):
        in_specs = [pl.BlockSpec(memory_space=pltpu.SMEM)] * scalars
        in_specs += [pl.BlockSpec(memory_space=pltpu.VMEM)] * (len(operands) - scalars)
        return pl.pallas_call(
            kernel,
            out_shape=out_shape,
            in_specs=in_specs,
            out_specs=[pl.BlockSpec(memory_space=pltpu.VMEM)] * len(out_shape),
            scratch_shapes=scratch,
            compiler_params=pltpu.CompilerParams(vmem_limit_bytes=usual_limit),
            name=name,
        )(*operands)

    near_count = tp_count // 2

    def to_near(value, step, near):
        if step == 0:
            return lax.ppermute(value, "tp", [(i, i ^ near) for i in range(tp_count)])
        if near == 0:
            return lax.ppermute(value, "ctx", [(i, (i + step) % cycle) for i in range(cycle)])
        pairs = [
            (c * tp_count + t, ((c + step) % cycle) * tp_count + (t ^ near))
            for c in range(cycle)
            for t in range(tp_count)
        ]
        return lax.ppermute(value, ("ctx", "tp"), pairs)

    def to_far(value):
        return lax.ppermute(value, "tp", [(i, i ^ near_count) for i in range(tp_count)])

    sections = shape((ticks, 2, half, HD), BF16)
    own_kv, other_kv = call(
        functools.partial(pack_kernel, tp_count, half),
        "pack_kv",
        (jnp.stack([keys[0], values[0]]),),
        [sections, sections],
    )
    far_kv = to_far(other_kv)
    places = [(step, near) for step in range(cycle) for near in range(near_count)][1:]
    kv = [
        block if place == (0, 0) else to_near(block, *place)
        for block in (own_kv, far_kv)
        for place in [(0, 0)] + places
    ]
    own_set, far_set = kv[: len(kv) // 2], kv[len(kv) // 2 :]
    queries, inverse, masks = call(
        functools.partial(norm_kernel, sizes),
        "norm",
        (doc_lengths, segment_inputs, norm_gain),
        [
            shape((ticks, rows, columns), BF16),
            shape((ticks, rows, HD), F32),
            shape((ticks, key_count, stacked), F32),
        ],
        scalars=1,
    )

    low_rows = shape((rows, columns), BF16)
    low_scores = shape((near_count, key_count, stacked), BF16)
    low_grads = shape((near_count, stacked, HD), BF16)
    rows_operands = (segment_inputs, norm_gain, queries, inverse, masks, waiting_grads)
    query_grad_near, dscore_near, probs_near, coupled = call(
        functools.partial(first_near_rows_kernel, sizes),
        "first_near_rows",
        (*rows_operands, *own_set),
        [low_grads, low_scores, low_scores, shape((rows, HD), F32)],
    )
    input_grad_first, query_grad_far, dscore_far, probs_far = call(
        functools.partial(first_far_rows_kernel, sizes),
        "first_far_rows",
        (*rows_operands, *far_set, query_grad_near, coupled),
        [low_rows, low_grads, low_scores, low_scores],
    )
    over_link = lax.ppermute(
        input_grad_first, "pipe", [(i, i - 1) for i in range(2, pipe_count, 2)]
    )
    on_chip = lax.ppermute(input_grad_first, "pipe", [(i, i ^ 1) for i in range(pipe_count)])
    gain_shape = shape((gain_count, HD), F32)
    pair_rows = 2 * block
    own_shape = shape((pair_rows, HD), F32)
    first_sums = (near_count, pair_rows, HD)
    gain_first, *sums_first = call(
        functools.partial(first_keys_kernel, sizes),
        "first_keys",
        (
            segment_inputs,
            queries,
            inverse,
            waiting_grads,
            query_grad_near,
            query_grad_far,
            dscore_near,
            dscore_far,
            probs_near,
            probs_far,
        ),
        [gain_shape, shape(first_sums, F32)] + [shape(first_sums, BF16)] * (cycle - 1),
    )
    sums_first = sums_first[:1] + [
        to_near(value, -step, 0) for step, value in enumerate(sums_first[1:], 1)
    ]
    (probs_second,) = call(
        functools.partial(second_probs_kernel, sizes),
        "second_probs",
        (masks, queries, *kv),
        [shape((tp_count, key_count, stacked), F32)],
    )
    message = shape((pair_rows + gain_count, HD), BF16)
    query_grad_second, gain_rows, own_second, *sends = call(
        functools.partial(second_keys_kernel, sizes),
        "second_keys",
        (
            segment_inputs,
            queries,
            inverse,
            output_grads,
            on_chip,
            over_link,
            probs_second,
            gain_first,
            *kv,
        ),
        [shape((tp_count, stacked, HD), BF16), gain_shape, own_shape] + [message] * len(places),
        scratch=[pltpu.VMEM((gain_count, HD), F32)],
    )
    received = [to_near(value, -step, near) for value, (step, near) in zip(sends, places)]
    own_first, *sends_first = call(
        functools.partial(first_sum_kernel, sizes),
        "first_sum",
        sums_first,
        [own_shape] + [shape((pair_rows, HD), BF16)] * (near_count - 1),
    )
    received_first = [to_near(value, 0, near) for near, value in enumerate(sends_first, 1)]
    (input_grads,) = call(
        functools.partial(second_rows_kernel, sizes),
        "second_rows",
        (
            segment_inputs,
            norm_gain,
            inverse,
            output_grads,
            on_chip,
            over_link,
            query_grad_second,
            input_grad_first,
        ),
        [shape((1, ticks, rows, columns), BF16)],
    )
    keep, gain_sum, send = call(
        functools.partial(near_sum_kernel, sizes),
        "near_sum",
        (own_second, gain_rows, *received, own_first, *received_first),
        [
            shape((ticks * block, HD), F32),
            gain_shape,
            shape((ticks * block + gain_count, HD), BF16),
        ],
    )
    grads_shape = shape((1, ticks, block, HD), F32)
    key_grads, value_grads, gain_grads = call(
        functools.partial(finish_kernel, sizes),
        "finish",
        (keep, gain_sum, to_far(send)),
        [grads_shape, grads_shape, gain_shape],
    )
    return input_grads, key_grads, value_grads, gain_grads.reshape(1, columns)


def solution(mesh):
    in_specs = (
        P("pipe", None, ("ctx", "tp"), None),
        P("pipe", None, "ctx", "tp"),
        P("pipe", None, "ctx", "tp"),
        P("pipe", None),
        P("pipe", ("ctx", "tp"), None),
        P(None, ("ctx", "tp"), None),
        P(),
    )
    out_specs = (
        P("pipe", None, ("ctx", "tp"), None),
        P("pipe", None, "ctx", "tp"),
        P("pipe", None, "ctx", "tp"),
        P("pipe", None),
    )
    return jax.shard_map(
        on_device, mesh=mesh, in_specs=in_specs, out_specs=out_specs, check_vma=False
    )
```

```python
import functools

import jax
import jax.numpy as jnp
from jax import lax
from jax.experimental import pallas as pl
from jax.experimental.pallas import tpu as pltpu
from jax.sharding import PartitionSpec as P

HD = 128
EPSILON = 1e-05
FILL = -1e30
SCALE = HD ** (-0.5)
TICKS = 2
F32 = jnp.float32
BF16 = jnp.bfloat16

NT = (((1,), (1,)), ((), ()))
NN = (((1,), (0,)), ((), ()))
TN = (((0,), (0,)), ((), ()))


def dot(a, b, dims):
    return lax.dot_general(a, b, dims, preferred_element_type=F32)


def in_order(values, owners):
    total = None
    for owner in range(len(values)):
        term = jnp.where(owners[0] == owner, values[0], 0.0)
        for value, whose in zip(values[1:], owners[1:]):
            term = jnp.where(whose == owner, value, term)
        total = term if total is None else total + term
    return total


def pack_kernel(tp_count, half, both_ref, own_ref, other_ref):
    parity = lax.axis_index("tp") // (tp_count // 2)
    own_first = pl.multiple_of(parity * half, half)
    other_first = pl.multiple_of((1 - parity) * half, half)
    for kind in range(2):
        for tick in range(TICKS):
            own_ref[tick, kind] = both_ref[kind, tick, pl.ds(own_first, half), :]
            other_ref[tick, kind] = both_ref[kind, tick, pl.ds(other_first, half), :]


def norm_kernel(sizes, doc_ref, x_ref, gain_ref, query_ref, inverse_ref, mask_ref):
    rows, columns = sizes[0], sizes[5]
    for tick in range(TICKS):
        squares = jnp.zeros((rows, HD), F32)
        for first in range(0, columns, HD):
            part = x_ref[0, tick, :, first : first + HD].astype(F32)
            squares = squares + part * part
        mean = jnp.sum(squares, axis=1, keepdims=True) * (1.0 / columns)
        inverse = jnp.broadcast_to(lax.rsqrt(mean + EPSILON), (rows, HD))
        inverse_ref[tick] = inverse
        for first in range(0, columns, HD):
            here = slice(first, first + HD)
            normed = x_ref[0, tick, :, here].astype(F32) * inverse
            query_ref[tick, :, here] = (normed * gain_ref[:, here]).astype(BF16)
        mask_ref[tick] = jnp.where(visible_keys(sizes, tick, doc_ref), 0.0, FILL)


class Group:
    def __init__(self, sizes, turn):
        self.rows, self.group = sizes[0], sizes[4]
        width = self.group * HD
        self.head_group = lax.axis_index("tp") ^ turn
        self.first = pl.multiple_of(self.head_group * width, width)

    def head(self, index):
        return pl.ds(self.first + index * HD, HD)

    def stacked(self, load):
        return jnp.concatenate([load(self.head(index)) for index in range(self.group)], axis=0)

    def unstacked(self, value):
        return [value[index * self.rows : (index + 1) * self.rows] for index in range(self.group)]


def waiting_from(waiting_ref):
    return lambda where: waiting_ref[0, :, where]


def choose_arriving(output_ref, chip_ref, link_ref, target_ref):
    place = lax.axis_index("pipe")
    last = place == lax.axis_size("pipe") - 1
    even = place % 2 == 0

    @pl.when(last)
    def _():
        target_ref[...] = output_ref[0]

    @pl.when(jnp.logical_not(last) & even)
    def _():
        target_ref[...] = chip_ref[...]

    @pl.when(jnp.logical_not(last) & jnp.logical_not(even))
    def _():
        target_ref[...] = link_ref[...]


def visible_keys(sizes, tick, doc_ref):
    rows, half, cycle, tp_count, group, columns = sizes
    cycle_place = lax.axis_index("ctx")
    tp_place = lax.axis_index("tp")
    parity = tp_place // (tp_count // 2)
    stacked = group * rows

    def section_first(owner):
        return half * jnp.where(parity == 0, owner, 2 * cycle - 1 - owner)

    row_first = section_first(cycle_place) + (tp_place % (tp_count // 2)) * rows
    query_pos = row_first + (lax.broadcasted_iota(jnp.int32, (1, stacked), 1) & (rows - 1))
    key_place = lax.broadcasted_iota(jnp.int32, (cycle * half, 1), 0)
    key_pos = key_place + section_first(cycle_place)
    for turn in range(1, cycle):
        first = section_first((cycle_place - turn + cycle) % cycle)
        key_pos = jnp.where(key_place >= turn * half, key_place - turn * half + first, key_pos)
    micro = lax.axis_index("pipe") + tick
    closing = jnp.int32(0)
    query_start = jnp.zeros((1, stacked), jnp.int32)
    for doc in range(doc_ref.shape[1]):
        length = doc_ref[micro, doc]
        closing = closing + length
        query_start = query_start + jnp.where(closing <= query_pos, length, 0)
    return (key_pos <= query_pos) & (key_pos >= query_start)


def probabilities(mask, products):
    scores = SCALE * products + mask
    weights = jnp.exp(scores - jnp.max(scores, axis=0, keepdims=True))
    return weights * (1.0 / jnp.sum(weights, axis=0, keepdims=True))


def score_grads(probs, prob_grad):
    row_term = jnp.sum(probs * prob_grad, axis=0, keepdims=True)
    return (probs * (prob_grad - row_term)).astype(BF16)


class Keys:
    def __init__(self, sizes, tick, refs):
        self.near_count = sizes[3] // 2
        self.tick = tick
        self.refs = refs

    def __call__(self, near, kind):
        parts = [ref[self.tick, kind] for ref in self.refs[near :: self.near_count]]
        return jnp.concatenate(parts, axis=0)


def place_of(sizes, far, kind):
    half = sizes[1]
    return slice((far * 2 + kind) * half, (far * 2 + kind + 1) * half)


def put_key_grads(sizes, turn, parts, own_ref, message_refs):
    half, cycle, tp_count = sizes[1:4]
    near_count = tp_count // 2
    near, far = turn % near_count, turn // near_count
    for kind, part in enumerate(parts):
        here = place_of(sizes, far, kind)
        for step in range(cycle):
            piece = part[step * half : (step + 1) * half]
            if step == 0 and near == 0:
                own_ref[here, :] = piece
            else:
                message_refs[step * near_count + near - 1][here, :] = piece.astype(BF16)


def gain_terms(columns_of, query_grad, normed_of, gain_rows_ref):
    rows = []
    for index, low in enumerate(columns_of.unstacked(query_grad)):
        term = low.astype(F32) * normed_of(columns_of.head(index))
        rows.append(jnp.sum(term, axis=0, keepdims=True))
    group = columns_of.group
    place = pl.ds(pl.multiple_of(columns_of.head_group * group, group), group)
    gain_rows_ref[place, :] = jnp.concatenate(rows, axis=0)


def coupled_terms(columns_of, query_grad, normed_of, gain_ref, coupled):
    for index, low in enumerate(columns_of.unstacked(query_grad)):
        where = columns_of.head(index)
        coupled = coupled + low.astype(F32) * gain_ref[:, where] * normed_of(where)
    return coupled


def write_input_grads(sizes, coupled, query_grad_of, normed_of, gain_ref, inverse, arriving, write):
    coupling = jnp.sum(coupled, axis=1, keepdims=True) * (1.0 / sizes[5])
    for turn in range(sizes[3]):
        columns_of = Group(sizes, turn)
        for index, low in enumerate(columns_of.unstacked(query_grad_of(turn))):
            where = columns_of.head(index)
            scaled = low.astype(F32) * gain_ref[:, where]
            result = arriving(where).astype(F32) + inverse * (scaled - normed_of(where) * coupling)
            write(where, result.astype(BF16))


def normed_from(x_ref, tick, inverse):
    return lambda where: x_ref[0, tick, :, where].astype(F32) * inverse


def first_half(keys, mask, products, dscore_ref, probs_ref):
    dscores = []
    for near, (scores, prob_grads) in enumerate(products):
        probs = probabilities(mask, scores)
        dscores.append(score_grads(probs, prob_grads))
        dscore_ref[near] = dscores[near]
        probs_ref[near] = probs.astype(BF16)
    return [
        (SCALE * dot(dscore, keys(near, 0), TN)).astype(BF16)
        for near, dscore in enumerate(dscores)
    ]


def first_near_rows_kernel(sizes, *refs):
    near_count = sizes[3] // 2
    members = sizes[2] * near_count
    x_ref, gain_ref, query_ref, inverse_ref, mask_ref, waiting_ref = refs[:6]
    keys = Keys(sizes, 0, refs[6 : 6 + members])
    query_grad_ref, dscore_ref, probs_ref, coupled_ref, turned_ref = refs[6 + members :]
    loads = (lambda where: query_ref[0, :, where], waiting_from(waiting_ref))
    products = []
    for near in range(near_count):
        operands = [Group(sizes, near).stacked(load) for load in loads]
        products.append([dot(keys(near, kind), operands[kind], NT) for kind in range(2)])
    query_grads = first_half(keys, mask_ref[0], products, dscore_ref, probs_ref)
    normed_of = normed_from(x_ref, 0, inverse_ref[0])
    coupled = jnp.zeros((sizes[0], HD), F32)
    for near, query_grad in enumerate(query_grads):
        query_grad_ref[near] = query_grad
        coupled = coupled_terms(Group(sizes, near), query_grad, normed_of, gain_ref, coupled)
    coupled_ref[...] = coupled
    for near in range(near_count):
        columns_of = Group(sizes, near_count + near)
        for kind, load in enumerate(loads):
            turned_ref[near, kind] = columns_of.stacked(load).T


def first_far_rows_kernel(sizes, *refs):
    near_count = sizes[3] // 2
    members = sizes[2] * near_count
    x_ref, gain_ref, inverse_ref, mask_ref, waiting_ref = refs[:5]
    keys, refs = Keys(sizes, 0, refs[5 : 5 + members]), refs[5 + members :]
    near_grad_ref, coupled_ref, turned_ref = refs[:3]
    input_grad_ref, query_grad_ref, dscore_ref, probs_ref = refs[3:]
    products = [
        [dot(keys(near, kind), turned_ref[near, kind], NN) for kind in range(2)]
        for near in range(near_count)
    ]
    query_grads = first_half(keys, mask_ref[0], products, dscore_ref, probs_ref)
    normed_of = normed_from(x_ref, 0, inverse_ref[0])
    coupled = coupled_ref[...]
    for near, query_grad in enumerate(query_grads):
        query_grad_ref[near] = query_grad
        coupled = coupled_terms(
            Group(sizes, near_count + near), query_grad, normed_of, gain_ref, coupled
        )

    def query_grad_of(turn):
        return near_grad_ref[turn] if turn < near_count else query_grads[turn - near_count]

    def write(where, result):
        input_grad_ref[:, where] = result

    write_input_grads(
        sizes,
        coupled,
        query_grad_of,
        normed_of,
        gain_ref,
        inverse_ref[0],
        waiting_from(waiting_ref),
        write,
    )


def first_keys_kernel(sizes, *refs):
    half, cycle, tp_count = sizes[1:4]
    near_count = tp_count // 2
    x_ref, query_ref, inverse_ref, waiting_ref = refs[:4]
    query_grad_refs, dscore_refs, probs_refs = refs[4:6], refs[6:8], refs[8:10]
    gain_rows_ref, own_ref = refs[10:12]
    send_refs = refs[12:]
    arriving = waiting_from(waiting_ref)
    normed_of = normed_from(x_ref, 0, inverse_ref[0])
    for turn in range(tp_count):
        near, far = turn % near_count, turn // near_count
        columns_of = Group(sizes, turn)
        query = columns_of.stacked(lambda where: query_ref[0, :, where])
        grad = columns_of.stacked(arriving)
        parts = (
            SCALE * dot(dscore_refs[far][near], query, NN),
            dot(probs_refs[far][near], grad, NN),
        )
        for kind, part in enumerate(parts):
            here = place_of(sizes, far, kind)
            own_ref[near, here, :] = part[:half]
            for step, ref in enumerate(send_refs, 1):
                ref[near, here, :] = part[step * half : (step + 1) * half].astype(BF16)
        gain_terms(columns_of, query_grad_refs[far][near], normed_of, gain_rows_ref)


def both_sets(sizes, refs):
    near_count = sizes[3] // 2
    members = sizes[2] * near_count
    sets = [Keys(sizes, 1, refs[:members]), Keys(sizes, 1, refs[members:])]
    return lambda turn, kind: sets[turn // near_count](turn % near_count, kind)


def second_probs_kernel(sizes, *refs):
    turns = range(sizes[3])
    mask_ref, query_ref = refs[:2]
    keys, probs_ref = both_sets(sizes, refs[2:-1]), refs[-1]
    mask = mask_ref[1]
    scores = []
    for turn in turns:
        query = Group(sizes, turn).stacked(lambda where: query_ref[1, :, where])
        scores.append(dot(keys(turn, 0), query, NT))
    for turn in turns:
        probs_ref[turn] = probabilities(mask, scores[turn])


def second_keys_kernel(sizes, *refs):
    cycle, tp_count = sizes[2:4]
    turns = range(tp_count)
    kv_count = cycle * tp_count
    x_ref, query_ref, inverse_ref, output_ref, chip_ref, link_ref = refs[:6]
    probs_ref, before_ref, *refs = refs[6:]
    keys, refs = both_sets(sizes, refs[:kv_count]), refs[kv_count:]
    query_grad_ref, gain_rows_ref, own_ref, arriving_ref = refs[:4]
    message_refs, gain_scratch = refs[4:-1], refs[-1]
    choose_arriving(output_ref, chip_ref, link_ref, arriving_ref)

    def arriving(where):
        return arriving_ref[:, where]

    normed_of = normed_from(x_ref, 1, inverse_ref[1])
    columns_of = [Group(sizes, turn) for turn in turns]
    grads = [columns_of[turn].stacked(arriving) for turn in turns]
    prob_grads = [dot(keys(turn, 1), grads[turn], NT) for turn in turns]
    value_grads = [dot(probs_ref[turn].astype(BF16), grads[turn], NN) for turn in turns]
    dscores = [score_grads(probs_ref[turn], prob_grads[turn]) for turn in turns]
    query_grads = [
        (SCALE * dot(dscores[turn], keys(turn, 0), TN)).astype(BF16) for turn in turns
    ]
    for turn in turns:
        query = columns_of[turn].stacked(lambda where: query_ref[1, :, where])
        key_grad = SCALE * dot(dscores[turn], query, NN)
        put_key_grads(sizes, turn, (key_grad, value_grads[turn]), own_ref, message_refs)
    for turn in turns:
        query_grad_ref[turn] = query_grads[turn]
        gain_terms(columns_of[turn], query_grads[turn], normed_of, gain_scratch)
    gain_rows = gain_scratch[...] + before_ref[...]
    gain_rows_ref[...] = gain_rows
    gain_low = gain_rows.astype(BF16)
    for ref in message_refs:
        ref[own_ref.shape[0] :, :] = gain_low


def first_sum_kernel(sizes, *refs):
    cycle = sizes[2]
    parts, own_ref, message_refs = refs[:cycle], refs[cycle], refs[cycle + 1 :]
    for near in range(sizes[3] // 2):
        total = parts[0][near]
        for ref in parts[1:]:
            total = total + ref[near].astype(F32)
        if near == 0:
            own_ref[...] = total
        else:
            message_refs[near - 1][...] = total.astype(BF16)


def second_rows_kernel(sizes, *refs):
    x_ref, gain_ref, inverse_ref, arriving_ref, query_grad_ref, first_ref, input_grads_ref = refs
    input_grads_ref[0, 0] = first_ref[...]
    inverse = inverse_ref[1]
    normed_of = normed_from(x_ref, 1, inverse)
    coupled = jnp.zeros((sizes[0], HD), F32)
    for turn in range(sizes[3]):
        coupled = coupled_terms(
            Group(sizes, turn), query_grad_ref[turn], normed_of, gain_ref, coupled
        )

    def write(where, result):
        input_grads_ref[0, 1, :, where] = result

    write_input_grads(
        sizes,
        coupled,
        lambda turn: query_grad_ref[turn],
        normed_of,
        gain_ref,
        inverse,
        lambda where: arriving_ref[:, where],
        write,
    )


def near_sum_kernel(sizes, *refs):
    rows, half, cycle, tp_count, group, columns = sizes
    near_count = tp_count // 2
    members = cycle * near_count
    own_ref, gain_ref = refs[:2]
    message_refs, refs = refs[2 : 1 + members], refs[1 + members :]
    own_first_ref, first_refs, refs = refs[0], refs[1:near_count], refs[near_count:]
    keep_ref, gain_sum_ref, send_ref = refs
    block = 2 * half
    first, second = own_first_ref[...], own_ref[...]
    for ref in message_refs:
        second = second + ref[: 2 * block, :].astype(F32)
    for ref in first_refs:
        first = first + ref[...].astype(F32)
    for tick, total in enumerate((first, second)):
        here = slice(tick * block, (tick + 1) * block)
        keep_ref[here, :] = total[:block]
        send_ref[here, :] = total[block:].astype(BF16)
    cycle_place = lax.axis_index("ctx")
    near_place = lax.axis_index("tp") % near_count
    values = [gain_ref[...].astype(BF16).astype(F32)]
    owners = [cycle_place * near_count + near_place]
    for place, ref in enumerate(message_refs, 1):
        step, near = place // near_count, place % near_count
        values.append(ref[2 * block :, :].astype(F32))
        owners.append(((cycle_place + step) % cycle) * near_count + (near_place ^ near))
    gain = in_order(values, owners)
    gain_sum_ref[...] = gain
    send_ref[TICKS * block :, :] = gain.astype(BF16)


def finish_kernel(sizes, keep_ref, gain_ref, receive_ref, key_ref, value_ref, gain_out_ref):
    half = sizes[1]
    parity = lax.axis_index("tp") // (sizes[3] // 2)
    own_first = pl.multiple_of(parity * half, half)
    other_first = pl.multiple_of((1 - parity) * half, half)
    for tick in range(TICKS):
        for kind, out in enumerate((key_ref, value_ref)):
            begin = (tick * 2 + kind) * half
            here = slice(begin, begin + half)
            out[0, tick, pl.ds(own_first, half), :] = keep_ref[here, :]
            out[0, tick, pl.ds(other_first, half), :] = receive_ref[here, :].astype(F32)
    own = gain_ref[...].astype(BF16).astype(F32)
    gain_out_ref[...] = own + receive_ref[TICKS * 2 * half :, :].astype(F32)


def shape(dims, dtype):
    return jax.ShapeDtypeStruct(dims, dtype)


def on_device(segment_inputs, keys, values, norm_gain, waiting_grads, output_grads, doc_lengths):
    cycle = lax.axis_size("ctx")
    tp_count = lax.axis_size("tp")
    pipe_count = lax.axis_size("pipe")
    _, ticks, rows, columns = segment_inputs.shape
    half = keys.shape[2] // 2
    group = columns // (tp_count * HD)
    gain_count = columns // HD
    sizes = (rows, half, cycle, tp_count, group, columns)
    block = 2 * half
    key_count = cycle * half
    stacked = group * rows
    score_bytes = key_count * stacked * 4
    usual_limit = min(56 << 20, (12 << 20) + 20 * score_bytes)

    def call(kernel, name, operands, out_shape, scratch=(), scalars=0):
        in_specs = [pl.BlockSpec(memory_space=pltpu.SMEM)] * scalars
        in_specs += [pl.BlockSpec(memory_space=pltpu.VMEM)] * (len(operands) - scalars)
        return pl.pallas_call(
            kernel,
            out_shape=out_shape,
            in_specs=in_specs,
            out_specs=[pl.BlockSpec(memory_space=pltpu.VMEM)] * len(out_shape),
            scratch_shapes=scratch,
            compiler_params=pltpu.CompilerParams(vmem_limit_bytes=usual_limit),
            name=name,
        )(*operands)

    near_count = tp_count // 2

    def to_near(value, step, near):
        if step == 0:
            return lax.ppermute(value, "tp", [(i, i ^ near) for i in range(tp_count)])
        if near == 0:
            return lax.ppermute(value, "ctx", [(i, (i + step) % cycle) for i in range(cycle)])
        pairs = [
            (c * tp_count + t, ((c + step) % cycle) * tp_count + (t ^ near))
            for c in range(cycle)
            for t in range(tp_count)
        ]
        return lax.ppermute(value, ("ctx", "tp"), pairs)

    def to_far(value):
        return lax.ppermute(value, "tp", [(i, i ^ near_count) for i in range(tp_count)])

    sections = shape((ticks, 2, half, HD), BF16)
    own_kv, other_kv = call(
        functools.partial(pack_kernel, tp_count, half),
        "pack_kv",
        (jnp.stack([keys[0], values[0]]),),
        [sections, sections],
    )
    far_kv = to_far(other_kv)
    places = [(step, near) for step in range(cycle) for near in range(near_count)][1:]
    kv = [
        block if place == (0, 0) else to_near(block, *place)
        for block in (own_kv, far_kv)
        for place in [(0, 0)] + places
    ]
    own_set, far_set = kv[: len(kv) // 2], kv[len(kv) // 2 :]
    queries, inverse, masks = call(
        functools.partial(norm_kernel, sizes),
        "norm",
        (doc_lengths, segment_inputs, norm_gain),
        [
            shape((ticks, rows, columns), BF16),
            shape((ticks, rows, HD), F32),
            shape((ticks, key_count, stacked), F32),
        ],
        scalars=1,
    )

    low_rows = shape((rows, columns), BF16)
    low_scores = shape((near_count, key_count, stacked), BF16)
    low_grads = shape((near_count, stacked, HD), BF16)
    query_grad_near, dscore_near, probs_near, coupled, turned = call(
        functools.partial(first_near_rows_kernel, sizes),
        "first_near_rows",
        (segment_inputs, norm_gain, queries, inverse, masks, waiting_grads, *own_set),
        [
            low_grads,
            low_scores,
            low_scores,
            shape((rows, HD), F32),
            shape((near_count, 2, HD, stacked), BF16),
        ],
    )
    input_grad_first, query_grad_far, dscore_far, probs_far = call(
        functools.partial(first_far_rows_kernel, sizes),
        "first_far_rows",
        (
            segment_inputs,
            norm_gain,
            inverse,
            masks,
            waiting_grads,
            *far_set,
            query_grad_near,
            coupled,
            turned,
        ),
        [low_rows, low_grads, low_scores, low_scores],
    )
    over_link = lax.ppermute(
        input_grad_first, "pipe", [(i, i - 1) for i in range(2, pipe_count, 2)]
    )
    on_chip = lax.ppermute(input_grad_first, "pipe", [(i, i ^ 1) for i in range(pipe_count)])
    gain_shape = shape((gain_count, HD), F32)
    pair_rows = 2 * block
    own_shape = shape((pair_rows, HD), F32)
    first_sums = (near_count, pair_rows, HD)
    gain_first, *sums_first = call(
        functools.partial(first_keys_kernel, sizes),
        "first_keys",
        (
            segment_inputs,
            queries,
            inverse,
            waiting_grads,
            query_grad_near,
            query_grad_far,
            dscore_near,
            dscore_far,
            probs_near,
            probs_far,
        ),
        [gain_shape, shape(first_sums, F32)] + [shape(first_sums, BF16)] * (cycle - 1),
    )
    sums_first = sums_first[:1] + [
        to_near(value, -step, 0) for step, value in enumerate(sums_first[1:], 1)
    ]
    (probs_second,) = call(
        functools.partial(second_probs_kernel, sizes),
        "second_probs",
        (masks, queries, *kv),
        [shape((tp_count, key_count, stacked), F32)],
    )
    message = shape((pair_rows + gain_count, HD), BF16)
    query_grad_second, gain_rows, own_second, arriving, *sends = call(
        functools.partial(second_keys_kernel, sizes),
        "second_keys",
        (
            segment_inputs,
            queries,
            inverse,
            output_grads,
            on_chip,
            over_link,
            probs_second,
            gain_first,
            *kv,
        ),
        [shape((tp_count, stacked, HD), BF16), gain_shape, own_shape, low_rows]
        + [message] * len(places),
        scratch=[pltpu.VMEM((gain_count, HD), F32)],
    )
    received = [to_near(value, -step, near) for value, (step, near) in zip(sends, places)]
    own_first, *sends_first = call(
        functools.partial(first_sum_kernel, sizes),
        "first_sum",
        sums_first,
        [own_shape] + [shape((pair_rows, HD), BF16)] * (near_count - 1),
    )
    received_first = [to_near(value, 0, near) for near, value in enumerate(sends_first, 1)]
    (input_grads,) = call(
        functools.partial(second_rows_kernel, sizes),
        "second_rows",
        (
            segment_inputs,
            norm_gain,
            inverse,
            arriving,
            query_grad_second,
            input_grad_first,
        ),
        [shape((1, ticks, rows, columns), BF16)],
    )
    keep, gain_sum, send = call(
        functools.partial(near_sum_kernel, sizes),
        "near_sum",
        (own_second, gain_rows, *received, own_first, *received_first),
        [
            shape((ticks * block, HD), F32),
            gain_shape,
            shape((ticks * block + gain_count, HD), BF16),
        ],
    )
    grads_shape = shape((1, ticks, block, HD), F32)
    key_grads, value_grads, gain_grads = call(
        functools.partial(finish_kernel, sizes),
        "finish",
        (keep, gain_sum, to_far(send)),
        [grads_shape, grads_shape, gain_shape],
    )
    return input_grads, key_grads, value_grads, gain_grads.reshape(1, columns)


def solution(mesh):
    in_specs = (
        P("pipe", None, ("ctx", "tp"), None),
        P("pipe", None, "ctx", "tp"),
        P("pipe", None, "ctx", "tp"),
        P("pipe", None),
        P("pipe", ("ctx", "tp"), None),
        P(None, ("ctx", "tp"), None),
        P(),
    )
    out_specs = (
        P("pipe", None, ("ctx", "tp"), None),
        P("pipe", None, "ctx", "tp"),
        P("pipe", None, "ctx", "tp"),
        P("pipe", None),
    )
    return jax.shard_map(
        on_device, mesh=mesh, in_specs=in_specs, out_specs=out_specs, check_vma=False
    )
```

```python
import functools

import jax
import jax.numpy as jnp
from jax import lax
from jax.experimental import pallas as pl
from jax.experimental.pallas import tpu as pltpu
from jax.sharding import PartitionSpec as P

HD = 128
EPSILON = 1e-05
FILL = -1e30
SCALE = HD ** (-0.5)
TICKS = 2
F32 = jnp.float32
BF16 = jnp.bfloat16

NT = (((1,), (1,)), ((), ()))
NN = (((1,), (0,)), ((), ()))
TN = (((0,), (0,)), ((), ()))


def dot(a, b, dims):
    return lax.dot_general(a, b, dims, preferred_element_type=F32)


def in_order(values, owners):
    total = None
    for owner in range(len(values)):
        term = jnp.where(owners[0] == owner, values[0], 0.0)
        for value, whose in zip(values[1:], owners[1:]):
            term = jnp.where(whose == owner, value, term)
        total = term if total is None else total + term
    return total


def pack_kernel(tp_count, half, both_ref, own_ref, other_ref):
    parity = lax.axis_index("tp") // (tp_count // 2)
    own_first = pl.multiple_of(parity * half, half)
    other_first = pl.multiple_of((1 - parity) * half, half)
    for kind in range(2):
        for tick in range(TICKS):
            own_ref[tick, kind] = both_ref[kind, tick, pl.ds(own_first, half), :]
            other_ref[tick, kind] = both_ref[kind, tick, pl.ds(other_first, half), :]


def norm_kernel(sizes, doc_ref, x_ref, gain_ref, query_ref, inverse_ref, mask_ref):
    rows, columns = sizes[0], sizes[5]
    for tick in range(TICKS):
        squares = jnp.zeros((rows, HD), F32)
        for first in range(0, columns, HD):
            part = x_ref[0, tick, :, first : first + HD].astype(F32)
            squares = squares + part * part
        mean = jnp.sum(squares, axis=1, keepdims=True) * (1.0 / columns)
        inverse = jnp.broadcast_to(lax.rsqrt(mean + EPSILON), (rows, HD))
        inverse_ref[tick] = inverse
        for first in range(0, columns, HD):
            here = slice(first, first + HD)
            normed = x_ref[0, tick, :, here].astype(F32) * inverse
            query_ref[tick, :, here] = (normed * gain_ref[:, here]).astype(BF16)
        mask_ref[tick] = jnp.where(visible_keys(sizes, tick, doc_ref), 0.0, FILL)


class Group:
    def __init__(self, sizes, turn):
        self.rows, self.group = sizes[0], sizes[4]
        width = self.group * HD
        self.head_group = lax.axis_index("tp") ^ turn
        self.first = pl.multiple_of(self.head_group * width, width)

    def head(self, index):
        return pl.ds(self.first + index * HD, HD)

    def stacked(self, load):
        return jnp.concatenate([load(self.head(index)) for index in range(self.group)], axis=0)

    def unstacked(self, value):
        return [value[index * self.rows : (index + 1) * self.rows] for index in range(self.group)]


def waiting_from(waiting_ref):
    return lambda where: waiting_ref[0, :, where]


def choose_arriving(output_ref, chip_ref, link_ref, target_ref):
    place = lax.axis_index("pipe")
    last = place == lax.axis_size("pipe") - 1
    even = place % 2 == 0

    @pl.when(last)
    def _():
        target_ref[...] = output_ref[0]

    @pl.when(jnp.logical_not(last) & even)
    def _():
        target_ref[...] = chip_ref[...]

    @pl.when(jnp.logical_not(last) & jnp.logical_not(even))
    def _():
        target_ref[...] = link_ref[...]


def visible_keys(sizes, tick, doc_ref):
    rows, half, cycle, tp_count, group, columns = sizes
    cycle_place = lax.axis_index("ctx")
    tp_place = lax.axis_index("tp")
    parity = tp_place // (tp_count // 2)
    stacked = group * rows

    def section_first(owner):
        return half * jnp.where(parity == 0, owner, 2 * cycle - 1 - owner)

    row_first = section_first(cycle_place) + (tp_place % (tp_count // 2)) * rows
    query_pos = row_first + (lax.broadcasted_iota(jnp.int32, (1, stacked), 1) & (rows - 1))
    key_place = lax.broadcasted_iota(jnp.int32, (cycle * half, 1), 0)
    key_pos = key_place + section_first(cycle_place)
    for turn in range(1, cycle):
        first = section_first((cycle_place - turn + cycle) % cycle)
        key_pos = jnp.where(key_place >= turn * half, key_place - turn * half + first, key_pos)
    micro = lax.axis_index("pipe") + tick
    closing = jnp.int32(0)
    query_start = jnp.zeros((1, stacked), jnp.int32)
    for doc in range(doc_ref.shape[1]):
        length = doc_ref[micro, doc]
        closing = closing + length
        query_start = query_start + jnp.where(closing <= query_pos, length, 0)
    return (key_pos <= query_pos) & (key_pos >= query_start)


def probabilities(mask, products):
    scores = SCALE * products + mask
    weights = jnp.exp(scores - jnp.max(scores, axis=0, keepdims=True))
    return weights * (1.0 / jnp.sum(weights, axis=0, keepdims=True))


def score_grads(probs, prob_grad):
    row_term = jnp.sum(probs * prob_grad, axis=0, keepdims=True)
    return (probs * (prob_grad - row_term)).astype(BF16)


class Keys:
    def __init__(self, sizes, tick, refs):
        self.near_count = sizes[3] // 2
        self.tick = tick
        self.refs = refs

    def __call__(self, near, kind):
        parts = [ref[self.tick, kind] for ref in self.refs[near :: self.near_count]]
        return jnp.concatenate(parts, axis=0)


def place_of(sizes, far, kind):
    half = sizes[1]
    return slice((far * 2 + kind) * half, (far * 2 + kind + 1) * half)


def put_key_grads(sizes, turn, parts, own_ref, message_refs):
    half, cycle, tp_count = sizes[1:4]
    near_count = tp_count // 2
    near, far = turn % near_count, turn // near_count
    for kind, part in enumerate(parts):
        here = place_of(sizes, far, kind)
        for step in range(cycle):
            piece = part[step * half : (step + 1) * half]
            if step == 0 and near == 0:
                own_ref[here, :] = piece
            else:
                message_refs[step * near_count + near - 1][here, :] = piece.astype(BF16)


def gain_terms(columns_of, query_grad, normed_of, gain_rows_ref):
    rows = []
    for index, low in enumerate(columns_of.unstacked(query_grad)):
        term = low.astype(F32) * normed_of(columns_of.head(index))
        rows.append(jnp.sum(term, axis=0, keepdims=True))
    group = columns_of.group
    place = pl.ds(pl.multiple_of(columns_of.head_group * group, group), group)
    gain_rows_ref[place, :] = jnp.concatenate(rows, axis=0)


def coupled_terms(columns_of, query_grad, normed_of, gain_ref, coupled):
    for index, low in enumerate(columns_of.unstacked(query_grad)):
        where = columns_of.head(index)
        coupled = coupled + low.astype(F32) * gain_ref[:, where] * normed_of(where)
    return coupled


def write_input_grads(sizes, coupled, query_grad_of, normed_of, gain_ref, inverse, arriving, write):
    coupling = jnp.sum(coupled, axis=1, keepdims=True) * (1.0 / sizes[5])
    for turn in range(sizes[3]):
        columns_of = Group(sizes, turn)
        for index, low in enumerate(columns_of.unstacked(query_grad_of(turn))):
            where = columns_of.head(index)
            scaled = low.astype(F32) * gain_ref[:, where]
            result = arriving(where).astype(F32) + inverse * (scaled - normed_of(where) * coupling)
            write(where, result.astype(BF16))


def normed_from(x_ref, tick, inverse):
    return lambda where: x_ref[0, tick, :, where].astype(F32) * inverse


def first_half(keys, mask, products, dscore_ref, probs_ref):
    dscores = []
    for near, (scores, prob_grads) in enumerate(products):
        probs = probabilities(mask, scores)
        dscores.append(score_grads(probs, prob_grads))
        dscore_ref[near] = dscores[near]
        probs_ref[near] = probs.astype(BF16)
    return [
        (SCALE * dot(dscore, keys(near, 0), TN)).astype(BF16)
        for near, dscore in enumerate(dscores)
    ]


def first_near_rows_kernel(sizes, *refs):
    near_count = sizes[3] // 2
    members = sizes[2] * near_count
    x_ref, gain_ref, query_ref, inverse_ref, mask_ref, waiting_ref = refs[:6]
    keys = Keys(sizes, 0, refs[6 : 6 + members])
    query_grad_ref, dscore_ref, probs_ref, coupled_ref, turned_ref = refs[6 + members :]
    loads = (lambda where: query_ref[0, :, where], waiting_from(waiting_ref))
    products = []
    for near in range(near_count):
        operands = [Group(sizes, near).stacked(load) for load in loads]
        products.append([dot(keys(near, kind), operands[kind], NT) for kind in range(2)])
    query_grads = first_half(keys, mask_ref[0], products, dscore_ref, probs_ref)
    normed_of = normed_from(x_ref, 0, inverse_ref[0])
    coupled = jnp.zeros((sizes[0], HD), F32)
    for near, query_grad in enumerate(query_grads):
        query_grad_ref[near] = query_grad
        coupled = coupled_terms(Group(sizes, near), query_grad, normed_of, gain_ref, coupled)
    coupled_ref[...] = coupled
    for near in range(near_count):
        columns_of = Group(sizes, near_count + near)
        for kind, load in enumerate(loads):
            turned_ref[near, kind] = columns_of.stacked(load).T


def first_far_rows_kernel(sizes, *refs):
    near_count = sizes[3] // 2
    members = sizes[2] * near_count
    x_ref, gain_ref, inverse_ref, mask_ref, waiting_ref = refs[:5]
    keys, refs = Keys(sizes, 0, refs[5 : 5 + members]), refs[5 + members :]
    near_grad_ref, coupled_ref, turned_ref = refs[:3]
    input_grad_ref, query_grad_ref, dscore_ref, probs_ref = refs[3:]
    products = [
        [dot(keys(near, kind), turned_ref[near, kind], NN) for kind in range(2)]
        for near in range(near_count)
    ]
    query_grads = first_half(keys, mask_ref[0], products, dscore_ref, probs_ref)
    normed_of = normed_from(x_ref, 0, inverse_ref[0])
    coupled = coupled_ref[...]
    for near, query_grad in enumerate(query_grads):
        query_grad_ref[near] = query_grad
        coupled = coupled_terms(
            Group(sizes, near_count + near), query_grad, normed_of, gain_ref, coupled
        )

    def query_grad_of(turn):
        return near_grad_ref[turn] if turn < near_count else query_grads[turn - near_count]

    def write(where, result):
        input_grad_ref[:, where] = result

    write_input_grads(
        sizes,
        coupled,
        query_grad_of,
        normed_of,
        gain_ref,
        inverse_ref[0],
        waiting_from(waiting_ref),
        write,
    )


def first_keys_kernel(sizes, *refs):
    half, cycle, tp_count = sizes[1:4]
    near_count = tp_count // 2
    x_ref, query_ref, inverse_ref, waiting_ref = refs[:4]
    query_grad_refs, dscore_refs, probs_refs = refs[4:6], refs[6:8], refs[8:10]
    gain_rows_ref, own_ref = refs[10:12]
    send_refs = refs[12:]
    arriving = waiting_from(waiting_ref)
    normed_of = normed_from(x_ref, 0, inverse_ref[0])
    for turn in range(tp_count):
        near, far = turn % near_count, turn // near_count
        columns_of = Group(sizes, turn)
        query = columns_of.stacked(lambda where: query_ref[0, :, where])
        grad = columns_of.stacked(arriving)
        parts = (
            SCALE * dot(dscore_refs[far][near], query, NN),
            dot(probs_refs[far][near], grad, NN),
        )
        for kind, part in enumerate(parts):
            here = place_of(sizes, far, kind)
            own_ref[near, here, :] = part[:half]
            for step, ref in enumerate(send_refs, 1):
                ref[near, here, :] = part[step * half : (step + 1) * half].astype(BF16)
        gain_terms(columns_of, query_grad_refs[far][near], normed_of, gain_rows_ref)


def both_sets(sizes, refs):
    near_count = sizes[3] // 2
    members = sizes[2] * near_count
    sets = [Keys(sizes, 1, refs[:members]), Keys(sizes, 1, refs[members:])]
    return lambda turn, kind: sets[turn // near_count](turn % near_count, kind)


def second_probs_kernel(sizes, *refs):
    turns = range(sizes[3])
    mask_ref, query_ref = refs[:2]
    keys, probs_ref = both_sets(sizes, refs[2:-1]), refs[-1]
    mask = mask_ref[1]
    scores = []
    for turn in turns:
        query = Group(sizes, turn).stacked(lambda where: query_ref[1, :, where])
        scores.append(dot(keys(turn, 0), query, NT))
    for turn in turns:
        probs_ref[turn] = probabilities(mask, scores[turn])


def second_keys_kernel(sizes, *refs):
    cycle, tp_count = sizes[2:4]
    turns = range(tp_count)
    kv_count = cycle * tp_count
    x_ref, query_ref, inverse_ref, output_ref, chip_ref, link_ref = refs[:6]
    probs_ref, before_ref, *refs = refs[6:]
    keys, refs = both_sets(sizes, refs[:kv_count]), refs[kv_count:]
    query_grad_ref, gain_rows_ref, own_ref, arriving_ref = refs[:4]
    message_refs, gain_scratch = refs[4:-1], refs[-1]
    choose_arriving(output_ref, chip_ref, link_ref, arriving_ref)

    def arriving(where):
        return arriving_ref[:, where]

    normed_of = normed_from(x_ref, 1, inverse_ref[1])
    columns_of = [Group(sizes, turn) for turn in turns]
    grads = [columns_of[turn].stacked(arriving) for turn in turns]
    prob_grads = [dot(keys(turn, 1), grads[turn], NT) for turn in turns]
    value_grads = [dot(probs_ref[turn].astype(BF16), grads[turn], NN) for turn in turns]
    dscores = [score_grads(probs_ref[turn], prob_grads[turn]) for turn in turns]
    query_grads = [
        (SCALE * dot(dscores[turn], keys(turn, 0), TN)).astype(BF16) for turn in turns
    ]
    for turn in turns:
        query = columns_of[turn].stacked(lambda where: query_ref[1, :, where])
        key_grad = SCALE * dot(dscores[turn], query, NN)
        put_key_grads(sizes, turn, (key_grad, value_grads[turn]), own_ref, message_refs)
    for turn in turns:
        query_grad_ref[turn] = query_grads[turn]
        gain_terms(columns_of[turn], query_grads[turn], normed_of, gain_scratch)
    gain_rows = gain_scratch[...] + before_ref[...]
    gain_rows_ref[...] = gain_rows
    gain_low = gain_rows.astype(BF16)
    for ref in message_refs:
        ref[own_ref.shape[0] :, :] = gain_low


def first_sum_kernel(sizes, *refs):
    cycle = sizes[2]
    parts, own_ref, message_refs = refs[:cycle], refs[cycle], refs[cycle + 1 :]
    for near in range(sizes[3] // 2):
        total = parts[0][near]
        for ref in parts[1:]:
            total = total + ref[near].astype(F32)
        if near == 0:
            own_ref[...] = total
        else:
            message_refs[near - 1][...] = total.astype(BF16)


def second_rows_kernel(sizes, *refs):
    x_ref, gain_ref, inverse_ref, arriving_ref, query_grad_ref, first_ref, input_grads_ref = refs
    input_grads_ref[0, 0] = first_ref[...]
    inverse = inverse_ref[1]
    normed_of = normed_from(x_ref, 1, inverse)
    coupled = jnp.zeros((sizes[0], HD), F32)
    for turn in range(sizes[3]):
        coupled = coupled_terms(
            Group(sizes, turn), query_grad_ref[turn], normed_of, gain_ref, coupled
        )

    def write(where, result):
        input_grads_ref[0, 1, :, where] = result

    write_input_grads(
        sizes,
        coupled,
        lambda turn: query_grad_ref[turn],
        normed_of,
        gain_ref,
        inverse,
        lambda where: arriving_ref[:, where],
        write,
    )


def first_near_kernel(sizes, own_ref, *refs):
    block = 2 * sizes[1]
    keep_ref, send_ref = refs[-2:]
    total = own_ref[...]
    for ref in refs[:-2]:
        total = total + ref[...].astype(F32)
    keep_ref[...] = total[:block]
    send_ref[...] = total[block:].astype(BF16)


def second_near_kernel(sizes, *refs):
    rows, half, cycle, tp_count, group, columns = sizes
    near_count = tp_count // 2
    members = cycle * near_count
    own_ref, gain_ref = refs[:2]
    message_refs = refs[2 : 1 + members][::-1]
    keep_ref, gain_sum_ref, send_ref = refs[1 + members :]
    block = 2 * half
    total = own_ref[...]
    for ref in message_refs:
        total = total + ref[: 2 * block, :].astype(F32)
    keep_ref[...] = total[:block]
    send_ref[:block, :] = total[block:].astype(BF16)
    cycle_place = lax.axis_index("ctx")
    near_place = lax.axis_index("tp") % near_count
    values = [gain_ref[...].astype(BF16).astype(F32)]
    owners = [cycle_place * near_count + near_place]
    for place, ref in enumerate(message_refs, 1):
        step, near = place // near_count, place % near_count
        values.append(ref[2 * block :, :].astype(F32))
        owners.append(((cycle_place + step) % cycle) * near_count + (near_place ^ near))
    gain = in_order(values, owners)
    gain_sum_ref[...] = gain
    send_ref[block:, :] = gain.astype(BF16)


def finish_kernel(sizes, *refs):
    half = sizes[1]
    keep_refs, receive_refs, gain_ref = refs[:TICKS], refs[TICKS : 2 * TICKS], refs[2 * TICKS]
    key_ref, value_ref, gain_out_ref = refs[2 * TICKS + 1 :]
    parity = lax.axis_index("tp") // (sizes[3] // 2)
    block = 2 * half
    own_first = pl.multiple_of(parity * half, half)
    other_first = pl.multiple_of((1 - parity) * half, half)
    for tick in range(TICKS):
        for kind, out in enumerate((key_ref, value_ref)):
            here = slice(kind * half, (kind + 1) * half)
            out[0, tick, pl.ds(own_first, half), :] = keep_refs[tick][here, :]
            out[0, tick, pl.ds(other_first, half), :] = receive_refs[tick][here, :].astype(F32)
    own = gain_ref[...].astype(BF16).astype(F32)
    gain_out_ref[...] = own + receive_refs[TICKS - 1][block:, :].astype(F32)


def shape(dims, dtype):
    return jax.ShapeDtypeStruct(dims, dtype)


def on_device(segment_inputs, keys, values, norm_gain, waiting_grads, output_grads, doc_lengths):
    cycle = lax.axis_size("ctx")
    tp_count = lax.axis_size("tp")
    pipe_count = lax.axis_size("pipe")
    _, ticks, rows, columns = segment_inputs.shape
    half = keys.shape[2] // 2
    group = columns // (tp_count * HD)
    gain_count = columns // HD
    sizes = (rows, half, cycle, tp_count, group, columns)
    block = 2 * half
    key_count = cycle * half
    stacked = group * rows
    score_bytes = key_count * stacked * 4
    usual_limit = min(56 << 20, (12 << 20) + 20 * score_bytes)

    def call(kernel, name, operands, out_shape, scratch=(), scalars=0):
        in_specs = [pl.BlockSpec(memory_space=pltpu.SMEM)] * scalars
        in_specs += [pl.BlockSpec(memory_space=pltpu.VMEM)] * (len(operands) - scalars)
        return pl.pallas_call(
            kernel,
            out_shape=out_shape,
            in_specs=in_specs,
            out_specs=[pl.BlockSpec(memory_space=pltpu.VMEM)] * len(out_shape),
            scratch_shapes=scratch,
            compiler_params=pltpu.CompilerParams(vmem_limit_bytes=usual_limit),
            name=name,
        )(*operands)

    near_count = tp_count // 2

    def to_near(value, step, near):
        if step == 0:
            return lax.ppermute(value, "tp", [(i, i ^ near) for i in range(tp_count)])
        if near == 0:
            return lax.ppermute(value, "ctx", [(i, (i + step) % cycle) for i in range(cycle)])
        pairs = [
            (c * tp_count + t, ((c + step) % cycle) * tp_count + (t ^ near))
            for c in range(cycle)
            for t in range(tp_count)
        ]
        return lax.ppermute(value, ("ctx", "tp"), pairs)

    def to_far(value):
        return lax.ppermute(value, "tp", [(i, i ^ near_count) for i in range(tp_count)])

    sections = shape((ticks, 2, half, HD), BF16)
    own_kv, other_kv = call(
        functools.partial(pack_kernel, tp_count, half),
        "pack_kv",
        (jnp.stack([keys[0], values[0]]),),
        [sections, sections],
    )
    far_kv = to_far(other_kv)
    places = [(step, near) for step in range(cycle) for near in range(near_count)][1:]
    kv = [
        block if place == (0, 0) else to_near(block, *place)
        for block in (own_kv, far_kv)
        for place in [(0, 0)] + places
    ]
    own_set, far_set = kv[: len(kv) // 2], kv[len(kv) // 2 :]
    queries, inverse, masks = call(
        functools.partial(norm_kernel, sizes),
        "norm",
        (doc_lengths, segment_inputs, norm_gain),
        [
            shape((ticks, rows, columns), BF16),
            shape((ticks, rows, HD), F32),
            shape((ticks, key_count, stacked), F32),
        ],
        scalars=1,
    )

    low_rows = shape((rows, columns), BF16)
    low_scores = shape((near_count, key_count, stacked), BF16)
    low_grads = shape((near_count, stacked, HD), BF16)
    query_grad_near, dscore_near, probs_near, coupled, turned = call(
        functools.partial(first_near_rows_kernel, sizes),
        "first_near_rows",
        (segment_inputs, norm_gain, queries, inverse, masks, waiting_grads, *own_set),
        [
            low_grads,
            low_scores,
            low_scores,
            shape((rows, HD), F32),
            shape((near_count, 2, HD, stacked), BF16),
        ],
    )
    input_grad_first, query_grad_far, dscore_far, probs_far = call(
        functools.partial(first_far_rows_kernel, sizes),
        "first_far_rows",
        (
            segment_inputs,
            norm_gain,
            inverse,
            masks,
            waiting_grads,
            *far_set,
            query_grad_near,
            coupled,
            turned,
        ),
        [low_rows, low_grads, low_scores, low_scores],
    )
    over_link = lax.ppermute(
        input_grad_first, "pipe", [(i, i - 1) for i in range(2, pipe_count, 2)]
    )
    on_chip = lax.ppermute(input_grad_first, "pipe", [(i, i ^ 1) for i in range(pipe_count)])
    gain_shape = shape((gain_count, HD), F32)
    pair_rows = 2 * block
    own_shape = shape((pair_rows, HD), F32)
    first_sums = (near_count, pair_rows, HD)
    gain_first, *sums_first = call(
        functools.partial(first_keys_kernel, sizes),
        "first_keys",
        (
            segment_inputs,
            queries,
            inverse,
            waiting_grads,
            query_grad_near,
            query_grad_far,
            dscore_near,
            dscore_far,
            probs_near,
            probs_far,
        ),
        [gain_shape, shape(first_sums, F32)] + [shape(first_sums, BF16)] * (cycle - 1),
    )
    sums_first = sums_first[:1] + [
        to_near(value, -step, 0) for step, value in enumerate(sums_first[1:], 1)
    ]
    (probs_second,) = call(
        functools.partial(second_probs_kernel, sizes),
        "second_probs",
        (masks, queries, *kv),
        [shape((tp_count, key_count, stacked), F32)],
    )
    message = shape((pair_rows + gain_count, HD), BF16)
    query_grad_second, gain_rows, own_second, arriving, *sends = call(
        functools.partial(second_keys_kernel, sizes),
        "second_keys",
        (
            segment_inputs,
            queries,
            inverse,
            output_grads,
            on_chip,
            over_link,
            probs_second,
            gain_first,
            *kv,
        ),
        [shape((tp_count, stacked, HD), BF16), gain_shape, own_shape, low_rows]
        + [message] * len(places),
        scratch=[pltpu.VMEM((gain_count, HD), F32)],
    )
    received = [to_near(value, -step, near) for value, (step, near) in zip(sends, places)]
    own_first, *sends_first = call(
        functools.partial(first_sum_kernel, sizes),
        "first_sum",
        sums_first,
        [own_shape] + [shape((pair_rows, HD), BF16)] * (near_count - 1),
    )
    received_first = [to_near(value, 0, near) for near, value in enumerate(sends_first, 1)]
    (input_grads,) = call(
        functools.partial(second_rows_kernel, sizes),
        "second_rows",
        (
            segment_inputs,
            norm_gain,
            inverse,
            arriving,
            query_grad_second,
            input_grad_first,
        ),
        [shape((1, ticks, rows, columns), BF16)],
    )
    keep_shape = shape((block, HD), F32)
    keep_first, send_first = call(
        functools.partial(first_near_kernel, sizes),
        "first_near",
        (own_first, *received_first),
        [keep_shape, shape((block, HD), BF16)],
    )
    keep_second, gain_sum, send_second = call(
        functools.partial(second_near_kernel, sizes),
        "second_near",
        (own_second, gain_rows, *received[::-1]),
        [keep_shape, gain_shape, shape((block + gain_count, HD), BF16)],
    )
    grads_shape = shape((1, ticks, block, HD), F32)
    key_grads, value_grads, gain_grads = call(
        functools.partial(finish_kernel, sizes),
        "finish",
        (keep_first, keep_second, to_far(send_first), to_far(send_second), gain_sum),
        [grads_shape, grads_shape, gain_shape],
    )
    return input_grads, key_grads, value_grads, gain_grads.reshape(1, columns)


def solution(mesh):
    in_specs = (
        P("pipe", None, ("ctx", "tp"), None),
        P("pipe", None, "ctx", "tp"),
        P("pipe", None, "ctx", "tp"),
        P("pipe", None),
        P("pipe", ("ctx", "tp"), None),
        P(None, ("ctx", "tp"), None),
        P(),
    )
    out_specs = (
        P("pipe", None, ("ctx", "tp"), None),
        P("pipe", None, "ctx", "tp"),
        P("pipe", None, "ctx", "tp"),
        P("pipe", None),
    )
    return jax.shard_map(
        on_device, mesh=mesh, in_specs=in_specs, out_specs=out_specs, check_vma=False
    )
```

```python
import functools

import jax
import jax.numpy as jnp
from jax import lax
from jax.experimental import pallas as pl
from jax.experimental.pallas import tpu as pltpu
from jax.sharding import PartitionSpec as P

HD = 128
EPSILON = 1e-05
FILL = -1e30
SCALE = HD ** (-0.5)
TICKS = 2
F32 = jnp.float32
BF16 = jnp.bfloat16

NT = (((1,), (1,)), ((), ()))
NN = (((1,), (0,)), ((), ()))
TN = (((0,), (0,)), ((), ()))


def dot(a, b, dims):
    return lax.dot_general(a, b, dims, preferred_element_type=F32)


def in_order(values, owners):
    total = None
    for owner in range(len(values)):
        term = jnp.where(owners[0] == owner, values[0], 0.0)
        for value, whose in zip(values[1:], owners[1:]):
            term = jnp.where(whose == owner, value, term)
        total = term if total is None else total + term
    return total


def pack_kernel(tp_count, half, both_ref, own_ref, other_ref):
    parity = lax.axis_index("tp") // (tp_count // 2)
    own_first = pl.multiple_of(parity * half, half)
    other_first = pl.multiple_of((1 - parity) * half, half)
    for kind in range(2):
        for tick in range(TICKS):
            own_ref[tick, kind] = both_ref[kind, tick, pl.ds(own_first, half), :]
            other_ref[tick, kind] = both_ref[kind, tick, pl.ds(other_first, half), :]


def norm_kernel(sizes, doc_ref, x_ref, gain_ref, query_ref, inverse_ref, mask_ref):
    rows, columns = sizes[0], sizes[5]
    for tick in range(TICKS):
        squares = jnp.zeros((rows, HD), F32)
        for first in range(0, columns, HD):
            part = x_ref[0, tick, :, first : first + HD].astype(F32)
            squares = squares + part * part
        mean = jnp.sum(squares, axis=1, keepdims=True) * (1.0 / columns)
        inverse = jnp.broadcast_to(lax.rsqrt(mean + EPSILON), (rows, HD))
        inverse_ref[tick] = inverse
        for first in range(0, columns, HD):
            here = slice(first, first + HD)
            normed = x_ref[0, tick, :, here].astype(F32) * inverse
            query_ref[tick, :, here] = (normed * gain_ref[:, here]).astype(BF16)
        mask_ref[tick] = jnp.where(visible_keys(sizes, tick, doc_ref), 0.0, FILL)


class Group:
    def __init__(self, sizes, turn):
        self.rows, self.group = sizes[0], sizes[4]
        width = self.group * HD
        self.head_group = lax.axis_index("tp") ^ turn
        self.first = pl.multiple_of(self.head_group * width, width)

    def head(self, index):
        return pl.ds(self.first + index * HD, HD)

    def stacked(self, load):
        return jnp.concatenate([load(self.head(index)) for index in range(self.group)], axis=0)

    def unstacked(self, value):
        return [value[index * self.rows : (index + 1) * self.rows] for index in range(self.group)]


def waiting_from(waiting_ref):
    return lambda where: waiting_ref[0, :, where]


def choose_arriving(output_ref, chip_ref, link_ref, target_ref):
    place = lax.axis_index("pipe")
    last = place == lax.axis_size("pipe") - 1
    even = place % 2 == 0

    @pl.when(last)
    def _():
        target_ref[...] = output_ref[0]

    @pl.when(jnp.logical_not(last) & even)
    def _():
        target_ref[...] = chip_ref[...]

    @pl.when(jnp.logical_not(last) & jnp.logical_not(even))
    def _():
        target_ref[...] = link_ref[...]


def visible_keys(sizes, tick, doc_ref):
    rows, half, cycle, tp_count, group, columns = sizes
    cycle_place = lax.axis_index("ctx")
    tp_place = lax.axis_index("tp")
    parity = tp_place // (tp_count // 2)
    stacked = group * rows

    def section_first(owner):
        return half * jnp.where(parity == 0, owner, 2 * cycle - 1 - owner)

    row_first = section_first(cycle_place) + (tp_place % (tp_count // 2)) * rows
    query_pos = row_first + (lax.broadcasted_iota(jnp.int32, (1, stacked), 1) & (rows - 1))
    key_place = lax.broadcasted_iota(jnp.int32, (cycle * half, 1), 0)
    key_pos = key_place + section_first(cycle_place)
    for turn in range(1, cycle):
        first = section_first((cycle_place - turn + cycle) % cycle)
        key_pos = jnp.where(key_place >= turn * half, key_place - turn * half + first, key_pos)
    micro = lax.axis_index("pipe") + tick
    closing = jnp.int32(0)
    query_start = jnp.zeros((1, stacked), jnp.int32)
    for doc in range(doc_ref.shape[1]):
        length = doc_ref[micro, doc]
        closing = closing + length
        query_start = query_start + jnp.where(closing <= query_pos, length, 0)
    return (key_pos <= query_pos) & (key_pos >= query_start)


def probabilities(mask, products):
    scores = SCALE * products + mask
    weights = jnp.exp(scores - jnp.max(scores, axis=0, keepdims=True))
    return weights * (1.0 / jnp.sum(weights, axis=0, keepdims=True))


def score_grads(probs, prob_grad):
    row_term = jnp.sum(probs * prob_grad, axis=0, keepdims=True)
    return (probs * (prob_grad - row_term)).astype(BF16)


class Keys:
    def __init__(self, sizes, tick, refs):
        self.near_count = sizes[3] // 2
        self.tick = tick
        self.refs = refs

    def __call__(self, near, kind):
        parts = [ref[self.tick, kind] for ref in self.refs[near :: self.near_count]]
        return jnp.concatenate(parts, axis=0)


def place_of(sizes, far, kind):
    half = sizes[1]
    return slice((far * 2 + kind) * half, (far * 2 + kind + 1) * half)


def put_key_grads(sizes, turn, parts, own_ref, message_refs):
    half, cycle, tp_count = sizes[1:4]
    near_count = tp_count // 2
    near, far = turn % near_count, turn // near_count
    for kind, part in enumerate(parts):
        here = place_of(sizes, far, kind)
        for step in range(cycle):
            piece = part[step * half : (step + 1) * half]
            if step == 0 and near == 0:
                own_ref[here, :] = piece
            else:
                message_refs[step * near_count + near - 1][here, :] = piece.astype(BF16)


def gain_terms(columns_of, query_grad, normed_of, gain_rows_ref):
    rows = []
    for index, low in enumerate(columns_of.unstacked(query_grad)):
        term = low.astype(F32) * normed_of(columns_of.head(index))
        rows.append(jnp.sum(term, axis=0, keepdims=True))
    group = columns_of.group
    place = pl.ds(pl.multiple_of(columns_of.head_group * group, group), group)
    gain_rows_ref[place, :] = jnp.concatenate(rows, axis=0)


def coupled_terms(columns_of, query_grad, normed_of, gain_ref, coupled):
    for index, low in enumerate(columns_of.unstacked(query_grad)):
        where = columns_of.head(index)
        coupled = coupled + low.astype(F32) * gain_ref[:, where] * normed_of(where)
    return coupled


def write_input_grads(sizes, coupled, query_grad_of, normed_of, gain_ref, inverse, arriving, write):
    coupling = jnp.sum(coupled, axis=1, keepdims=True) * (1.0 / sizes[5])
    for turn in range(sizes[3]):
        columns_of = Group(sizes, turn)
        for index, low in enumerate(columns_of.unstacked(query_grad_of(turn))):
            where = columns_of.head(index)
            scaled = low.astype(F32) * gain_ref[:, where]
            result = arriving(where).astype(F32) + inverse * (scaled - normed_of(where) * coupling)
            write(where, result.astype(BF16))


def normed_from(x_ref, tick, inverse):
    return lambda where: x_ref[0, tick, :, where].astype(F32) * inverse


def first_half(keys, mask, products, dscore_ref, probs_ref):
    dscores = []
    for near, (scores, prob_grads) in enumerate(products):
        probs = probabilities(mask, scores)
        dscores.append(score_grads(probs, prob_grads))
        dscore_ref[near] = dscores[near]
        probs_ref[near] = probs.astype(BF16)
    return [
        (SCALE * dot(dscore, keys(near, 0), TN)).astype(BF16)
        for near, dscore in enumerate(dscores)
    ]


def first_near_rows_kernel(sizes, *refs):
    near_count = sizes[3] // 2
    members = sizes[2] * near_count
    x_ref, gain_ref, query_ref, inverse_ref, mask_ref, waiting_ref = refs[:6]
    keys = Keys(sizes, 0, refs[6 : 6 + members])
    query_grad_ref, dscore_ref, probs_ref, coupled_ref, turned_ref = refs[6 + members :]
    loads = (lambda where: query_ref[0, :, where], waiting_from(waiting_ref))
    products = []
    for near in range(near_count):
        operands = [Group(sizes, near).stacked(load) for load in loads]
        products.append([dot(keys(near, kind), operands[kind], NT) for kind in range(2)])
    query_grads = first_half(keys, mask_ref[0], products, dscore_ref, probs_ref)
    normed_of = normed_from(x_ref, 0, inverse_ref[0])
    coupled = jnp.zeros((sizes[0], HD), F32)
    for near, query_grad in enumerate(query_grads):
        query_grad_ref[near] = query_grad
        coupled = coupled_terms(Group(sizes, near), query_grad, normed_of, gain_ref, coupled)
    coupled_ref[...] = coupled
    for near in range(near_count):
        columns_of = Group(sizes, near_count + near)
        for kind, load in enumerate(loads):
            turned_ref[near, kind] = columns_of.stacked(load).T


def first_far_rows_kernel(sizes, *refs):
    near_count = sizes[3] // 2
    members = sizes[2] * near_count
    x_ref, gain_ref, inverse_ref, mask_ref, waiting_ref = refs[:5]
    keys, refs = Keys(sizes, 0, refs[5 : 5 + members]), refs[5 + members :]
    near_grad_ref, coupled_ref, turned_ref = refs[:3]
    input_grad_ref, query_grad_ref, dscore_ref, probs_ref = refs[3:]
    products = [
        [dot(keys(near, kind), turned_ref[near, kind], NN) for kind in range(2)]
        for near in range(near_count)
    ]
    query_grads = first_half(keys, mask_ref[0], products, dscore_ref, probs_ref)
    normed_of = normed_from(x_ref, 0, inverse_ref[0])
    coupled = coupled_ref[...]
    for near, query_grad in enumerate(query_grads):
        query_grad_ref[near] = query_grad
        coupled = coupled_terms(
            Group(sizes, near_count + near), query_grad, normed_of, gain_ref, coupled
        )

    def query_grad_of(turn):
        return near_grad_ref[turn] if turn < near_count else query_grads[turn - near_count]

    def write(where, result):
        input_grad_ref[:, where] = result

    write_input_grads(
        sizes,
        coupled,
        query_grad_of,
        normed_of,
        gain_ref,
        inverse_ref[0],
        waiting_from(waiting_ref),
        write,
    )


def first_keys_kernel(sizes, *refs):
    half, cycle, tp_count = sizes[1:4]
    near_count = tp_count // 2
    x_ref, query_ref, inverse_ref, waiting_ref = refs[:4]
    query_grad_refs, dscore_refs, probs_refs = refs[4:6], refs[6:8], refs[8:10]
    gain_rows_ref, own_ref = refs[10:12]
    send_refs = refs[12:]
    arriving = waiting_from(waiting_ref)
    normed_of = normed_from(x_ref, 0, inverse_ref[0])
    for turn in range(tp_count):
        near, far = turn % near_count, turn // near_count
        columns_of = Group(sizes, turn)
        query = columns_of.stacked(lambda where: query_ref[0, :, where])
        grad = columns_of.stacked(arriving)
        parts = (
            SCALE * dot(dscore_refs[far][near], query, NN),
            dot(probs_refs[far][near], grad, NN),
        )
        for kind, part in enumerate(parts):
            here = place_of(sizes, far, kind)
            own_ref[near, here, :] = part[:half]
            for step, ref in enumerate(send_refs, 1):
                ref[near, here, :] = part[step * half : (step + 1) * half].astype(BF16)
        gain_terms(columns_of, query_grad_refs[far][near], normed_of, gain_rows_ref)


def both_sets(sizes, refs):
    near_count = sizes[3] // 2
    members = sizes[2] * near_count
    sets = [Keys(sizes, 1, refs[:members]), Keys(sizes, 1, refs[members:])]
    return lambda turn, kind: sets[turn // near_count](turn % near_count, kind)


def second_probs_kernel(sizes, *refs):
    turns = range(sizes[3])
    mask_ref, query_ref = refs[:2]
    keys, probs_ref = both_sets(sizes, refs[2:-1]), refs[-1]
    mask = mask_ref[1]
    scores = []
    for turn in turns:
        query = Group(sizes, turn).stacked(lambda where: query_ref[1, :, where])
        scores.append(dot(keys(turn, 0), query, NT))
    for turn in turns:
        probs_ref[turn] = probabilities(mask, scores[turn])


def second_keys_kernel(sizes, *refs):
    cycle, tp_count = sizes[2:4]
    turns = range(tp_count)
    kv_count = cycle * tp_count
    x_ref, query_ref, inverse_ref, output_ref, chip_ref, link_ref = refs[:6]
    probs_ref, before_ref, *refs = refs[6:]
    keys, refs = both_sets(sizes, refs[:kv_count]), refs[kv_count:]
    query_grad_ref, gain_rows_ref, own_ref, arriving_ref = refs[:4]
    message_refs, gain_scratch = refs[4:-1], refs[-1]
    choose_arriving(output_ref, chip_ref, link_ref, arriving_ref)

    def arriving(where):
        return arriving_ref[:, where]

    normed_of = normed_from(x_ref, 1, inverse_ref[1])
    columns_of = [Group(sizes, turn) for turn in turns]
    grads = [columns_of[turn].stacked(arriving) for turn in turns]
    prob_grads = [dot(keys(turn, 1), grads[turn], NT) for turn in turns]
    value_grads = [dot(probs_ref[turn].astype(BF16), grads[turn], NN) for turn in turns]
    dscores = [score_grads(probs_ref[turn], prob_grads[turn]) for turn in turns]
    query_grads = [
        (SCALE * dot(dscores[turn], keys(turn, 0), TN)).astype(BF16) for turn in turns
    ]
    for turn in turns:
        query = columns_of[turn].stacked(lambda where: query_ref[1, :, where])
        key_grad = SCALE * dot(dscores[turn], query, NN)
        put_key_grads(sizes, turn, (key_grad, value_grads[turn]), own_ref, message_refs)
    for turn in turns:
        query_grad_ref[turn] = query_grads[turn]
        gain_terms(columns_of[turn], query_grads[turn], normed_of, gain_scratch)
    gain_rows = gain_scratch[...] + before_ref[...]
    gain_rows_ref[...] = gain_rows
    gain_low = gain_rows.astype(BF16)
    for ref in message_refs:
        ref[own_ref.shape[0] :, :] = gain_low


def first_sum_kernel(sizes, *refs):
    cycle = sizes[2]
    parts, own_ref, message_refs = refs[:cycle], refs[cycle], refs[cycle + 1 :]
    for near in range(sizes[3] // 2):
        total = parts[0][near]
        for ref in parts[1:]:
            total = total + ref[near].astype(F32)
        if near == 0:
            own_ref[...] = total
        else:
            message_refs[near - 1][...] = total.astype(BF16)


def second_rows_kernel(sizes, *refs):
    x_ref, gain_ref, inverse_ref, arriving_ref, query_grad_ref, first_ref, input_grads_ref = refs
    input_grads_ref[0, 0] = first_ref[...]
    inverse = inverse_ref[1]
    normed_of = normed_from(x_ref, 1, inverse)
    coupled = jnp.zeros((sizes[0], HD), F32)
    for turn in range(sizes[3]):
        coupled = coupled_terms(
            Group(sizes, turn), query_grad_ref[turn], normed_of, gain_ref, coupled
        )

    def write(where, result):
        input_grads_ref[0, 1, :, where] = result

    write_input_grads(
        sizes,
        coupled,
        lambda turn: query_grad_ref[turn],
        normed_of,
        gain_ref,
        inverse,
        lambda where: arriving_ref[:, where],
        write,
    )


def first_near_kernel(sizes, own_ref, *refs):
    block = 2 * sizes[1]
    keep_ref, send_ref = refs[-2:]
    total = own_ref[...]
    for ref in refs[:-2]:
        total = total + ref[...].astype(F32)
    keep_ref[...] = total[:block]
    send_ref[...] = total[block:].astype(BF16)


def second_near_kernel(sizes, *refs):
    rows, half, cycle, tp_count, group, columns = sizes
    near_count = tp_count // 2
    members = cycle * near_count
    own_ref, gain_ref = refs[:2]
    message_refs = refs[2 : 1 + members][::-1]
    keep_ref, gain_sum_ref, send_ref = refs[1 + members :]
    block = 2 * half
    total = own_ref[...]
    for ref in message_refs:
        total = total + ref[: 2 * block, :].astype(F32)
    keep_ref[...] = total[:block]
    send_ref[:block, :] = total[block:].astype(BF16)
    cycle_place = lax.axis_index("ctx")
    near_place = lax.axis_index("tp") % near_count
    values = [gain_ref[...].astype(BF16).astype(F32)]
    owners = [cycle_place * near_count + near_place]
    for place, ref in enumerate(message_refs, 1):
        step, near = place // near_count, place % near_count
        values.append(ref[2 * block :, :].astype(F32))
        owners.append(((cycle_place + step) % cycle) * near_count + (near_place ^ near))
    gain = in_order(values, owners)
    gain_sum_ref[...] = gain
    send_ref[block:, :] = gain.astype(BF16)


def finish_kernel(sizes, *refs):
    half = sizes[1]
    keep_refs, receive_refs = refs[:TICKS][::-1], refs[TICKS : 2 * TICKS][::-1]
    gain_ref = refs[2 * TICKS]
    key_ref, value_ref, gain_out_ref = refs[2 * TICKS + 1 :]
    parity = lax.axis_index("tp") // (sizes[3] // 2)
    block = 2 * half
    own_first = pl.multiple_of(parity * half, half)
    other_first = pl.multiple_of((1 - parity) * half, half)
    for tick in range(TICKS):
        for kind, out in enumerate((key_ref, value_ref)):
            here = slice(kind * half, (kind + 1) * half)
            out[0, tick, pl.ds(own_first, half), :] = keep_refs[tick][here, :]
            out[0, tick, pl.ds(other_first, half), :] = receive_refs[tick][here, :].astype(F32)
    own = gain_ref[...].astype(BF16).astype(F32)
    gain_out_ref[...] = own + receive_refs[TICKS - 1][block:, :].astype(F32)


def shape(dims, dtype):
    return jax.ShapeDtypeStruct(dims, dtype)


def on_device(segment_inputs, keys, values, norm_gain, waiting_grads, output_grads, doc_lengths):
    cycle = lax.axis_size("ctx")
    tp_count = lax.axis_size("tp")
    pipe_count = lax.axis_size("pipe")
    _, ticks, rows, columns = segment_inputs.shape
    half = keys.shape[2] // 2
    group = columns // (tp_count * HD)
    gain_count = columns // HD
    sizes = (rows, half, cycle, tp_count, group, columns)
    block = 2 * half
    key_count = cycle * half
    stacked = group * rows
    score_bytes = key_count * stacked * 4
    usual_limit = min(56 << 20, (12 << 20) + 20 * score_bytes)

    def call(kernel, name, operands, out_shape, scratch=(), scalars=0):
        in_specs = [pl.BlockSpec(memory_space=pltpu.SMEM)] * scalars
        in_specs += [pl.BlockSpec(memory_space=pltpu.VMEM)] * (len(operands) - scalars)
        return pl.pallas_call(
            kernel,
            out_shape=out_shape,
            in_specs=in_specs,
            out_specs=[pl.BlockSpec(memory_space=pltpu.VMEM)] * len(out_shape),
            scratch_shapes=scratch,
            compiler_params=pltpu.CompilerParams(vmem_limit_bytes=usual_limit),
            name=name,
        )(*operands)

    near_count = tp_count // 2

    def to_near(value, step, near):
        if step == 0:
            return lax.ppermute(value, "tp", [(i, i ^ near) for i in range(tp_count)])
        if near == 0:
            return lax.ppermute(value, "ctx", [(i, (i + step) % cycle) for i in range(cycle)])
        pairs = [
            (c * tp_count + t, ((c + step) % cycle) * tp_count + (t ^ near))
            for c in range(cycle)
            for t in range(tp_count)
        ]
        return lax.ppermute(value, ("ctx", "tp"), pairs)

    def to_far(value):
        return lax.ppermute(value, "tp", [(i, i ^ near_count) for i in range(tp_count)])

    sections = shape((ticks, 2, half, HD), BF16)
    own_kv, other_kv = call(
        functools.partial(pack_kernel, tp_count, half),
        "pack_kv",
        (jnp.stack([keys[0], values[0]]),),
        [sections, sections],
    )
    far_kv = to_far(other_kv)
    places = [(step, near) for step in range(cycle) for near in range(near_count)][1:]
    kv = [
        block if place == (0, 0) else to_near(block, *place)
        for block in (own_kv, far_kv)
        for place in [(0, 0)] + places
    ]
    own_set, far_set = kv[: len(kv) // 2], kv[len(kv) // 2 :]
    queries, inverse, masks = call(
        functools.partial(norm_kernel, sizes),
        "norm",
        (doc_lengths, segment_inputs, norm_gain),
        [
            shape((ticks, rows, columns), BF16),
            shape((ticks, rows, HD), F32),
            shape((ticks, key_count, stacked), F32),
        ],
        scalars=1,
    )

    low_rows = shape((rows, columns), BF16)
    low_scores = shape((near_count, key_count, stacked), BF16)
    low_grads = shape((near_count, stacked, HD), BF16)
    query_grad_near, dscore_near, probs_near, coupled, turned = call(
        functools.partial(first_near_rows_kernel, sizes),
        "first_near_rows",
        (segment_inputs, norm_gain, queries, inverse, masks, waiting_grads, *own_set),
        [
            low_grads,
            low_scores,
            low_scores,
            shape((rows, HD), F32),
            shape((near_count, 2, HD, stacked), BF16),
        ],
    )
    input_grad_first, query_grad_far, dscore_far, probs_far = call(
        functools.partial(first_far_rows_kernel, sizes),
        "first_far_rows",
        (
            segment_inputs,
            norm_gain,
            inverse,
            masks,
            waiting_grads,
            *far_set,
            query_grad_near,
            coupled,
            turned,
        ),
        [low_rows, low_grads, low_scores, low_scores],
    )
    over_link = lax.ppermute(
        input_grad_first, "pipe", [(i, i - 1) for i in range(2, pipe_count, 2)]
    )
    on_chip = lax.ppermute(input_grad_first, "pipe", [(i, i ^ 1) for i in range(pipe_count)])
    gain_shape = shape((gain_count, HD), F32)
    pair_rows = 2 * block
    own_shape = shape((pair_rows, HD), F32)
    first_sums = (near_count, pair_rows, HD)
    gain_first, *sums_first = call(
        functools.partial(first_keys_kernel, sizes),
        "first_keys",
        (
            segment_inputs,
            queries,
            inverse,
            waiting_grads,
            query_grad_near,
            query_grad_far,
            dscore_near,
            dscore_far,
            probs_near,
            probs_far,
        ),
        [gain_shape, shape(first_sums, F32)] + [shape(first_sums, BF16)] * (cycle - 1),
    )
    sums_first = sums_first[:1] + [
        to_near(value, -step, 0) for step, value in enumerate(sums_first[1:], 1)
    ]
    (probs_second,) = call(
        functools.partial(second_probs_kernel, sizes),
        "second_probs",
        (masks, queries, *kv),
        [shape((tp_count, key_count, stacked), F32)],
    )
    message = shape((pair_rows + gain_count, HD), BF16)
    query_grad_second, gain_rows, own_second, arriving, *sends = call(
        functools.partial(second_keys_kernel, sizes),
        "second_keys",
        (
            segment_inputs,
            queries,
            inverse,
            output_grads,
            on_chip,
            over_link,
            probs_second,
            gain_first,
            *kv,
        ),
        [shape((tp_count, stacked, HD), BF16), gain_shape, own_shape, low_rows]
        + [message] * len(places),
        scratch=[pltpu.VMEM((gain_count, HD), F32)],
    )
    received = [to_near(value, -step, near) for value, (step, near) in zip(sends, places)]
    own_first, *sends_first = call(
        functools.partial(first_sum_kernel, sizes),
        "first_sum",
        sums_first,
        [own_shape] + [shape((pair_rows, HD), BF16)] * (near_count - 1),
    )
    received_first = [to_near(value, 0, near) for near, value in enumerate(sends_first, 1)]
    (input_grads,) = call(
        functools.partial(second_rows_kernel, sizes),
        "second_rows",
        (
            segment_inputs,
            norm_gain,
            inverse,
            arriving,
            query_grad_second,
            input_grad_first,
        ),
        [shape((1, ticks, rows, columns), BF16)],
    )
    keep_shape = shape((block, HD), F32)
    keep_first, send_first = call(
        functools.partial(first_near_kernel, sizes),
        "first_near",
        (own_first, *received_first),
        [keep_shape, shape((block, HD), BF16)],
    )
    keep_second, gain_sum, send_second = call(
        functools.partial(second_near_kernel, sizes),
        "second_near",
        (own_second, gain_rows, *received[::-1]),
        [keep_shape, gain_shape, shape((block + gain_count, HD), BF16)],
    )
    grads_shape = shape((1, ticks, block, HD), F32)
    key_grads, value_grads, gain_grads = call(
        functools.partial(finish_kernel, sizes),
        "finish",
        (keep_second, keep_first, to_far(send_second), to_far(send_first), gain_sum),
        [grads_shape, grads_shape, gain_shape],
    )
    return input_grads, key_grads, value_grads, gain_grads.reshape(1, columns)


def solution(mesh):
    in_specs = (
        P("pipe", None, ("ctx", "tp"), None),
        P("pipe", None, "ctx", "tp"),
        P("pipe", None, "ctx", "tp"),
        P("pipe", None),
        P("pipe", ("ctx", "tp"), None),
        P(None, ("ctx", "tp"), None),
        P(),
    )
    out_specs = (
        P("pipe", None, ("ctx", "tp"), None),
        P("pipe", None, "ctx", "tp"),
        P("pipe", None, "ctx", "tp"),
        P("pipe", None),
    )
    return jax.shard_map(
        on_device, mesh=mesh, in_specs=in_specs, out_specs=out_specs, check_vma=False
    )
```

```python
import functools

import jax
import jax.numpy as jnp
from jax import lax
from jax.experimental import pallas as pl
from jax.experimental.pallas import tpu as pltpu
from jax.sharding import PartitionSpec as P

HD = 128
EPSILON = 1e-05
FILL = -1e30
SCALE = HD ** (-0.5)
TICKS = 2
F32 = jnp.float32
BF16 = jnp.bfloat16

NT = (((1,), (1,)), ((), ()))
NN = (((1,), (0,)), ((), ()))
TN = (((0,), (0,)), ((), ()))


def dot(a, b, dims):
    return lax.dot_general(a, b, dims, preferred_element_type=F32)


def in_order(values, owners):
    total = None
    for owner in range(len(values)):
        term = jnp.where(owners[0] == owner, values[0], 0.0)
        for value, whose in zip(values[1:], owners[1:]):
            term = jnp.where(whose == owner, value, term)
        total = term if total is None else total + term
    return total


def pack_kernel(tp_count, half, both_ref, own_ref, other_ref):
    parity = lax.axis_index("tp") // (tp_count // 2)
    own_first = pl.multiple_of(parity * half, half)
    other_first = pl.multiple_of((1 - parity) * half, half)
    for kind in range(2):
        for tick in range(TICKS):
            own_ref[tick, kind] = both_ref[kind, tick, pl.ds(own_first, half), :]
            other_ref[tick, kind] = both_ref[kind, tick, pl.ds(other_first, half), :]


def norm_kernel(sizes, doc_ref, x_ref, gain_ref, query_ref, inverse_ref, mask_ref):
    rows, columns = sizes[0], sizes[5]
    for tick in range(TICKS):
        squares = jnp.zeros((rows, HD), F32)
        for first in range(0, columns, HD):
            part = x_ref[0, tick, :, first : first + HD].astype(F32)
            squares = squares + part * part
        mean = jnp.sum(squares, axis=1, keepdims=True) * (1.0 / columns)
        inverse = jnp.broadcast_to(lax.rsqrt(mean + EPSILON), (rows, HD))
        inverse_ref[tick] = inverse
        for first in range(0, columns, HD):
            here = slice(first, first + HD)
            normed = x_ref[0, tick, :, here].astype(F32) * inverse
            query_ref[tick, :, here] = (normed * gain_ref[:, here]).astype(BF16)
        mask_ref[tick] = jnp.where(visible_keys(sizes, tick, doc_ref), 0.0, FILL)


class Group:
    def __init__(self, sizes, turn):
        self.rows, self.group = sizes[0], sizes[4]
        width = self.group * HD
        self.head_group = lax.axis_index("tp") ^ turn
        self.first = pl.multiple_of(self.head_group * width, width)

    def head(self, index):
        return pl.ds(self.first + index * HD, HD)

    def stacked(self, load):
        return jnp.concatenate([load(self.head(index)) for index in range(self.group)], axis=0)

    def unstacked(self, value):
        return [value[index * self.rows : (index + 1) * self.rows] for index in range(self.group)]


def waiting_from(waiting_ref):
    return lambda where: waiting_ref[0, :, where]


def choose_arriving(output_ref, chip_ref, link_ref, target_ref):
    place = lax.axis_index("pipe")
    last = place == lax.axis_size("pipe") - 1
    even = place % 2 == 0

    @pl.when(last)
    def _():
        target_ref[...] = output_ref[0]

    @pl.when(jnp.logical_not(last) & even)
    def _():
        target_ref[...] = chip_ref[...]

    @pl.when(jnp.logical_not(last) & jnp.logical_not(even))
    def _():
        target_ref[...] = link_ref[...]


def visible_keys(sizes, tick, doc_ref):
    rows, half, cycle, tp_count, group, columns = sizes
    cycle_place = lax.axis_index("ctx")
    tp_place = lax.axis_index("tp")
    parity = tp_place // (tp_count // 2)
    stacked = group * rows

    def section_first(owner):
        return half * jnp.where(parity == 0, owner, 2 * cycle - 1 - owner)

    row_first = section_first(cycle_place) + (tp_place % (tp_count // 2)) * rows
    query_pos = row_first + (lax.broadcasted_iota(jnp.int32, (1, stacked), 1) & (rows - 1))
    key_place = lax.broadcasted_iota(jnp.int32, (cycle * half, 1), 0)
    key_pos = key_place + section_first(cycle_place)
    for turn in range(1, cycle):
        first = section_first((cycle_place - turn + cycle) % cycle)
        key_pos = jnp.where(key_place >= turn * half, key_place - turn * half + first, key_pos)
    micro = lax.axis_index("pipe") + tick
    closing = jnp.int32(0)
    query_start = jnp.zeros((1, stacked), jnp.int32)
    for doc in range(doc_ref.shape[1]):
        length = doc_ref[micro, doc]
        closing = closing + length
        query_start = query_start + jnp.where(closing <= query_pos, length, 0)
    return (key_pos <= query_pos) & (key_pos >= query_start)


def probabilities(mask, products):
    scores = SCALE * products + mask
    weights = jnp.exp(scores - jnp.max(scores, axis=0, keepdims=True))
    return weights * (1.0 / jnp.sum(weights, axis=0, keepdims=True))


def score_grads(probs, prob_grad):
    row_term = jnp.sum(probs * prob_grad, axis=0, keepdims=True)
    return (probs * (prob_grad - row_term)).astype(BF16)


class Keys:
    def __init__(self, sizes, tick, refs):
        self.near_count = sizes[3] // 2
        self.tick = tick
        self.refs = refs

    def __call__(self, near, kind):
        parts = [ref[self.tick, kind] for ref in self.refs[near :: self.near_count]]
        return jnp.concatenate(parts, axis=0)


def place_of(sizes, far, kind):
    half = sizes[1]
    return slice((far * 2 + kind) * half, (far * 2 + kind + 1) * half)


def put_key_grads(sizes, turn, parts, own_ref, message_refs):
    half, cycle, tp_count = sizes[1:4]
    near_count = tp_count // 2
    near, far = turn % near_count, turn // near_count
    for kind, part in enumerate(parts):
        here = place_of(sizes, far, kind)
        for step in range(cycle):
            piece = part[step * half : (step + 1) * half]
            if step == 0 and near == 0:
                own_ref[here, :] = piece
            else:
                message_refs[step * near_count + near - 1][here, :] = piece.astype(BF16)


def gain_terms(columns_of, query_grad, normed_of, gain_rows_ref):
    rows = []
    for index, low in enumerate(columns_of.unstacked(query_grad)):
        term = low.astype(F32) * normed_of(columns_of.head(index))
        rows.append(jnp.sum(term, axis=0, keepdims=True))
    group = columns_of.group
    place = pl.ds(pl.multiple_of(columns_of.head_group * group, group), group)
    gain_rows_ref[place, :] = jnp.concatenate(rows, axis=0)


def coupled_terms(columns_of, query_grad, normed_of, gain_ref, coupled):
    for index, low in enumerate(columns_of.unstacked(query_grad)):
        where = columns_of.head(index)
        coupled = coupled + low.astype(F32) * gain_ref[:, where] * normed_of(where)
    return coupled


def write_input_grads(sizes, coupled, query_grad_of, normed_of, gain_ref, inverse, arriving, write):
    coupling = jnp.sum(coupled, axis=1, keepdims=True) * (1.0 / sizes[5])
    for turn in range(sizes[3]):
        columns_of = Group(sizes, turn)
        for index, low in enumerate(columns_of.unstacked(query_grad_of(turn))):
            where = columns_of.head(index)
            scaled = low.astype(F32) * gain_ref[:, where]
            result = arriving(where).astype(F32) + inverse * (scaled - normed_of(where) * coupling)
            write(where, result.astype(BF16))


def normed_from(x_ref, tick, inverse):
    return lambda where: x_ref[0, tick, :, where].astype(F32) * inverse


def first_half(keys, mask, products, dscore_ref, probs_ref):
    dscores = []
    for near, (scores, prob_grads) in enumerate(products):
        probs = probabilities(mask, scores)
        dscores.append(score_grads(probs, prob_grads))
        dscore_ref[near] = dscores[near]
        probs_ref[near] = probs.astype(BF16)
    return [
        (SCALE * dot(dscore, keys(near, 0), TN)).astype(BF16)
        for near, dscore in enumerate(dscores)
    ]


def first_near_rows_kernel(sizes, *refs):
    near_count = sizes[3] // 2
    members = sizes[2] * near_count
    x_ref, gain_ref, query_ref, inverse_ref, mask_ref, waiting_ref = refs[:6]
    keys = Keys(sizes, 0, refs[6 : 6 + members])
    query_grad_ref, dscore_ref, probs_ref, coupled_ref, turned_ref = refs[6 + members :]
    loads = (lambda where: query_ref[0, :, where], waiting_from(waiting_ref))
    products = []
    for near in range(near_count):
        operands = [Group(sizes, near).stacked(load) for load in loads]
        products.append([dot(keys(near, kind), operands[kind], NT) for kind in range(2)])
    query_grads = first_half(keys, mask_ref[0], products, dscore_ref, probs_ref)
    normed_of = normed_from(x_ref, 0, inverse_ref[0])
    coupled = jnp.zeros((sizes[0], HD), F32)
    for near, query_grad in enumerate(query_grads):
        query_grad_ref[near] = query_grad
        coupled = coupled_terms(Group(sizes, near), query_grad, normed_of, gain_ref, coupled)
    coupled_ref[...] = coupled
    for near in range(near_count):
        columns_of = Group(sizes, near_count + near)
        for kind, load in enumerate(loads):
            turned_ref[near, kind] = columns_of.stacked(load).T


def first_far_rows_kernel(sizes, *refs):
    near_count = sizes[3] // 2
    members = sizes[2] * near_count
    x_ref, gain_ref, inverse_ref, mask_ref, waiting_ref = refs[:5]
    keys, refs = Keys(sizes, 0, refs[5 : 5 + members]), refs[5 + members :]
    near_grad_ref, coupled_ref, turned_ref = refs[:3]
    input_grad_ref, query_grad_ref, dscore_ref, probs_ref = refs[3:]
    products = [
        [dot(keys(near, kind), turned_ref[near, kind], NN) for kind in range(2)]
        for near in range(near_count)
    ]
    query_grads = first_half(keys, mask_ref[0], products, dscore_ref, probs_ref)
    normed_of = normed_from(x_ref, 0, inverse_ref[0])
    coupled = coupled_ref[...]
    for near, query_grad in enumerate(query_grads):
        query_grad_ref[near] = query_grad
        coupled = coupled_terms(
            Group(sizes, near_count + near), query_grad, normed_of, gain_ref, coupled
        )

    def query_grad_of(turn):
        return near_grad_ref[turn] if turn < near_count else query_grads[turn - near_count]

    def write(where, result):
        input_grad_ref[:, where] = result

    write_input_grads(
        sizes,
        coupled,
        query_grad_of,
        normed_of,
        gain_ref,
        inverse_ref[0],
        waiting_from(waiting_ref),
        write,
    )


def first_keys_kernel(sizes, *refs):
    half, cycle, tp_count = sizes[1:4]
    near_count = tp_count // 2
    x_ref, query_ref, inverse_ref, waiting_ref = refs[:4]
    query_grad_refs, dscore_refs, probs_refs = refs[4:6], refs[6:8], refs[8:10]
    gain_rows_ref, own_ref = refs[10:12]
    send_refs = refs[12:]
    arriving = waiting_from(waiting_ref)
    normed_of = normed_from(x_ref, 0, inverse_ref[0])
    for turn in range(tp_count):
        near, far = turn % near_count, turn // near_count
        columns_of = Group(sizes, turn)
        query = columns_of.stacked(lambda where: query_ref[0, :, where])
        grad = columns_of.stacked(arriving)
        parts = (
            SCALE * dot(dscore_refs[far][near], query, NN),
            dot(probs_refs[far][near], grad, NN),
        )
        for kind, part in enumerate(parts):
            here = place_of(sizes, far, kind)
            for step in range(cycle):
                piece = part[step * half : (step + 1) * half]
                if near == 0:
                    own_ref[step, here, :] = piece
                else:
                    send_refs[near - 1][step, here, :] = piece.astype(BF16)
        gain_terms(columns_of, query_grad_refs[far][near], normed_of, gain_rows_ref)


def both_sets(sizes, refs):
    near_count = sizes[3] // 2
    members = sizes[2] * near_count
    sets = [Keys(sizes, 1, refs[:members]), Keys(sizes, 1, refs[members:])]
    return lambda turn, kind: sets[turn // near_count](turn % near_count, kind)


def second_probs_kernel(sizes, *refs):
    turns = range(sizes[3])
    mask_ref, query_ref = refs[:2]
    keys, probs_ref = both_sets(sizes, refs[2:-1]), refs[-1]
    mask = mask_ref[1]
    scores = []
    for turn in turns:
        query = Group(sizes, turn).stacked(lambda where: query_ref[1, :, where])
        scores.append(dot(keys(turn, 0), query, NT))
    for turn in turns:
        probs_ref[turn] = probabilities(mask, scores[turn])


def second_keys_kernel(sizes, *refs):
    cycle, tp_count = sizes[2:4]
    turns = range(tp_count)
    kv_count = cycle * tp_count
    x_ref, query_ref, inverse_ref, output_ref, chip_ref, link_ref = refs[:6]
    probs_ref, before_ref, *refs = refs[6:]
    keys, refs = both_sets(sizes, refs[:kv_count]), refs[kv_count:]
    query_grad_ref, gain_rows_ref, own_ref, arriving_ref = refs[:4]
    message_refs, gain_scratch = refs[4:-1], refs[-1]
    choose_arriving(output_ref, chip_ref, link_ref, arriving_ref)

    def arriving(where):
        return arriving_ref[:, where]

    normed_of = normed_from(x_ref, 1, inverse_ref[1])
    columns_of = [Group(sizes, turn) for turn in turns]
    grads = [columns_of[turn].stacked(arriving) for turn in turns]
    prob_grads = [dot(keys(turn, 1), grads[turn], NT) for turn in turns]
    value_grads = [dot(probs_ref[turn].astype(BF16), grads[turn], NN) for turn in turns]
    dscores = [score_grads(probs_ref[turn], prob_grads[turn]) for turn in turns]
    query_grads = [
        (SCALE * dot(dscores[turn], keys(turn, 0), TN)).astype(BF16) for turn in turns
    ]
    for turn in turns:
        query = columns_of[turn].stacked(lambda where: query_ref[1, :, where])
        key_grad = SCALE * dot(dscores[turn], query, NN)
        put_key_grads(sizes, turn, (key_grad, value_grads[turn]), own_ref, message_refs)
    for turn in turns:
        query_grad_ref[turn] = query_grads[turn]
        gain_terms(columns_of[turn], query_grads[turn], normed_of, gain_scratch)
    gain_rows = gain_scratch[...] + before_ref[...]
    gain_rows_ref[...] = gain_rows
    gain_low = gain_rows.astype(BF16)
    for ref in message_refs:
        ref[own_ref.shape[0] :, :] = gain_low


def first_sum_kernel(sizes, *refs):
    near_count = sizes[3] // 2
    parts, own_ref, message_refs = refs[:near_count], refs[near_count], refs[near_count + 1 :]
    for step in range(sizes[2]):
        total = parts[0][step]
        for ref in parts[1:]:
            total = total + ref[step].astype(F32)
        if step == 0:
            own_ref[...] = total
        else:
            message_refs[step - 1][...] = total.astype(BF16)


def second_rows_kernel(sizes, *refs):
    x_ref, gain_ref, inverse_ref, arriving_ref, query_grad_ref, first_ref, input_grads_ref = refs
    input_grads_ref[0, 0] = first_ref[...]
    inverse = inverse_ref[1]
    normed_of = normed_from(x_ref, 1, inverse)
    coupled = jnp.zeros((sizes[0], HD), F32)
    for turn in range(sizes[3]):
        coupled = coupled_terms(
            Group(sizes, turn), query_grad_ref[turn], normed_of, gain_ref, coupled
        )

    def write(where, result):
        input_grads_ref[0, 1, :, where] = result

    write_input_grads(
        sizes,
        coupled,
        lambda turn: query_grad_ref[turn],
        normed_of,
        gain_ref,
        inverse,
        lambda where: arriving_ref[:, where],
        write,
    )


def first_near_kernel(sizes, own_ref, *refs):
    block = 2 * sizes[1]
    keep_ref, send_ref = refs[-2:]
    total = own_ref[...]
    for ref in refs[:-2]:
        total = total + ref[...].astype(F32)
    keep_ref[...] = total[:block]
    send_ref[...] = total[block:].astype(BF16)


def second_near_kernel(sizes, *refs):
    rows, half, cycle, tp_count, group, columns = sizes
    near_count = tp_count // 2
    members = cycle * near_count
    own_ref, gain_ref = refs[:2]
    message_refs = refs[2 : 1 + members][::-1]
    keep_ref, gain_sum_ref, send_ref = refs[1 + members :]
    block = 2 * half
    total = own_ref[...]
    for ref in message_refs:
        total = total + ref[: 2 * block, :].astype(F32)
    keep_ref[...] = total[:block]
    send_ref[:block, :] = total[block:].astype(BF16)
    cycle_place = lax.axis_index("ctx")
    near_place = lax.axis_index("tp") % near_count
    values = [gain_ref[...].astype(BF16).astype(F32)]
    owners = [cycle_place * near_count + near_place]
    for place, ref in enumerate(message_refs, 1):
        step, near = place // near_count, place % near_count
        values.append(ref[2 * block :, :].astype(F32))
        owners.append(((cycle_place + step) % cycle) * near_count + (near_place ^ near))
    gain = in_order(values, owners)
    gain_sum_ref[...] = gain
    send_ref[block:, :] = gain.astype(BF16)


def finish_kernel(sizes, *refs):
    half = sizes[1]
    keep_refs, receive_refs = refs[:TICKS][::-1], refs[TICKS : 2 * TICKS][::-1]
    gain_ref = refs[2 * TICKS]
    key_ref, value_ref, gain_out_ref = refs[2 * TICKS + 1 :]
    parity = lax.axis_index("tp") // (sizes[3] // 2)
    block = 2 * half
    own_first = pl.multiple_of(parity * half, half)
    other_first = pl.multiple_of((1 - parity) * half, half)
    for tick in range(TICKS):
        for kind, out in enumerate((key_ref, value_ref)):
            here = slice(kind * half, (kind + 1) * half)
            out[0, tick, pl.ds(own_first, half), :] = keep_refs[tick][here, :]
            out[0, tick, pl.ds(other_first, half), :] = receive_refs[tick][here, :].astype(F32)
    own = gain_ref[...].astype(BF16).astype(F32)
    gain_out_ref[...] = own + receive_refs[TICKS - 1][block:, :].astype(F32)


def shape(dims, dtype):
    return jax.ShapeDtypeStruct(dims, dtype)


def on_device(segment_inputs, keys, values, norm_gain, waiting_grads, output_grads, doc_lengths):
    cycle = lax.axis_size("ctx")
    tp_count = lax.axis_size("tp")
    pipe_count = lax.axis_size("pipe")
    _, ticks, rows, columns = segment_inputs.shape
    half = keys.shape[2] // 2
    group = columns // (tp_count * HD)
    gain_count = columns // HD
    sizes = (rows, half, cycle, tp_count, group, columns)
    block = 2 * half
    key_count = cycle * half
    stacked = group * rows
    score_bytes = key_count * stacked * 4
    usual_limit = min(56 << 20, (12 << 20) + 20 * score_bytes)

    def call(kernel, name, operands, out_shape, scratch=(), scalars=0):
        in_specs = [pl.BlockSpec(memory_space=pltpu.SMEM)] * scalars
        in_specs += [pl.BlockSpec(memory_space=pltpu.VMEM)] * (len(operands) - scalars)
        return pl.pallas_call(
            kernel,
            out_shape=out_shape,
            in_specs=in_specs,
            out_specs=[pl.BlockSpec(memory_space=pltpu.VMEM)] * len(out_shape),
            scratch_shapes=scratch,
            compiler_params=pltpu.CompilerParams(vmem_limit_bytes=usual_limit),
            name=name,
        )(*operands)

    near_count = tp_count // 2

    def to_near(value, step, near):
        if step == 0:
            return lax.ppermute(value, "tp", [(i, i ^ near) for i in range(tp_count)])
        if near == 0:
            return lax.ppermute(value, "ctx", [(i, (i + step) % cycle) for i in range(cycle)])
        pairs = [
            (c * tp_count + t, ((c + step) % cycle) * tp_count + (t ^ near))
            for c in range(cycle)
            for t in range(tp_count)
        ]
        return lax.ppermute(value, ("ctx", "tp"), pairs)

    def to_far(value):
        return lax.ppermute(value, "tp", [(i, i ^ near_count) for i in range(tp_count)])

    sections = shape((ticks, 2, half, HD), BF16)
    own_kv, other_kv = call(
        functools.partial(pack_kernel, tp_count, half),
        "pack_kv",
        (jnp.stack([keys[0], values[0]]),),
        [sections, sections],
    )
    far_kv = to_far(other_kv)
    places = [(step, near) for step in range(cycle) for near in range(near_count)][1:]
    kv = [
        block if place == (0, 0) else to_near(block, *place)
        for block in (own_kv, far_kv)
        for place in [(0, 0)] + places
    ]
    own_set, far_set = kv[: len(kv) // 2], kv[len(kv) // 2 :]
    queries, inverse, masks = call(
        functools.partial(norm_kernel, sizes),
        "norm",
        (doc_lengths, segment_inputs, norm_gain),
        [
            shape((ticks, rows, columns), BF16),
            shape((ticks, rows, HD), F32),
            shape((ticks, key_count, stacked), F32),
        ],
        scalars=1,
    )

    low_rows = shape((rows, columns), BF16)
    low_scores = shape((near_count, key_count, stacked), BF16)
    low_grads = shape((near_count, stacked, HD), BF16)
    query_grad_near, dscore_near, probs_near, coupled, turned = call(
        functools.partial(first_near_rows_kernel, sizes),
        "first_near_rows",
        (segment_inputs, norm_gain, queries, inverse, masks, waiting_grads, *own_set),
        [
            low_grads,
            low_scores,
            low_scores,
            shape((rows, HD), F32),
            shape((near_count, 2, HD, stacked), BF16),
        ],
    )
    input_grad_first, query_grad_far, dscore_far, probs_far = call(
        functools.partial(first_far_rows_kernel, sizes),
        "first_far_rows",
        (
            segment_inputs,
            norm_gain,
            inverse,
            masks,
            waiting_grads,
            *far_set,
            query_grad_near,
            coupled,
            turned,
        ),
        [low_rows, low_grads, low_scores, low_scores],
    )
    over_link = lax.ppermute(
        input_grad_first, "pipe", [(i, i - 1) for i in range(2, pipe_count, 2)]
    )
    on_chip = lax.ppermute(input_grad_first, "pipe", [(i, i ^ 1) for i in range(pipe_count)])
    gain_shape = shape((gain_count, HD), F32)
    pair_rows = 2 * block
    own_shape = shape((pair_rows, HD), F32)
    first_sums = (cycle, pair_rows, HD)
    gain_first, *sums_first = call(
        functools.partial(first_keys_kernel, sizes),
        "first_keys",
        (
            segment_inputs,
            queries,
            inverse,
            waiting_grads,
            query_grad_near,
            query_grad_far,
            dscore_near,
            dscore_far,
            probs_near,
            probs_far,
        ),
        [gain_shape, shape(first_sums, F32)] + [shape(first_sums, BF16)] * (near_count - 1),
    )
    sums_first = sums_first[:1] + [
        to_near(value, 0, near) for near, value in enumerate(sums_first[1:], 1)
    ]
    (probs_second,) = call(
        functools.partial(second_probs_kernel, sizes),
        "second_probs",
        (masks, queries, *kv),
        [shape((tp_count, key_count, stacked), F32)],
    )
    message = shape((pair_rows + gain_count, HD), BF16)
    query_grad_second, gain_rows, own_second, arriving, *sends = call(
        functools.partial(second_keys_kernel, sizes),
        "second_keys",
        (
            segment_inputs,
            queries,
            inverse,
            output_grads,
            on_chip,
            over_link,
            probs_second,
            gain_first,
            *kv,
        ),
        [shape((tp_count, stacked, HD), BF16), gain_shape, own_shape, low_rows]
        + [message] * len(places),
        scratch=[pltpu.VMEM((gain_count, HD), F32)],
    )
    received = [to_near(value, -step, near) for value, (step, near) in zip(sends, places)]
    own_first, *sends_first = call(
        functools.partial(first_sum_kernel, sizes),
        "first_sum",
        sums_first,
        [own_shape] + [shape((pair_rows, HD), BF16)] * (cycle - 1),
    )
    received_first = [to_near(value, -step, 0) for step, value in enumerate(sends_first, 1)]
    (input_grads,) = call(
        functools.partial(second_rows_kernel, sizes),
        "second_rows",
        (
            segment_inputs,
            norm_gain,
            inverse,
            arriving,
            query_grad_second,
            input_grad_first,
        ),
        [shape((1, ticks, rows, columns), BF16)],
    )
    keep_shape = shape((block, HD), F32)
    keep_first, send_first = call(
        functools.partial(first_near_kernel, sizes),
        "first_near",
        (own_first, *received_first),
        [keep_shape, shape((block, HD), BF16)],
    )
    keep_second, gain_sum, send_second = call(
        functools.partial(second_near_kernel, sizes),
        "second_near",
        (own_second, gain_rows, *received[::-1]),
        [keep_shape, gain_shape, shape((block + gain_count, HD), BF16)],
    )
    grads_shape = shape((1, ticks, block, HD), F32)
    key_grads, value_grads, gain_grads = call(
        functools.partial(finish_kernel, sizes),
        "finish",
        (keep_second, keep_first, to_far(send_second), to_far(send_first), gain_sum),
        [grads_shape, grads_shape, gain_shape],
    )
    return input_grads, key_grads, value_grads, gain_grads.reshape(1, columns)


def solution(mesh):
    in_specs = (
        P("pipe", None, ("ctx", "tp"), None),
        P("pipe", None, "ctx", "tp"),
        P("pipe", None, "ctx", "tp"),
        P("pipe", None),
        P("pipe", ("ctx", "tp"), None),
        P(None, ("ctx", "tp"), None),
        P(),
    )
    out_specs = (
        P("pipe", None, ("ctx", "tp"), None),
        P("pipe", None, "ctx", "tp"),
        P("pipe", None, "ctx", "tp"),
        P("pipe", None),
    )
    return jax.shard_map(
        on_device, mesh=mesh, in_specs=in_specs, out_specs=out_specs, check_vma=False
    )
```

```python
import functools

import jax
import jax.numpy as jnp
from jax import lax
from jax.experimental import pallas as pl
from jax.experimental.pallas import tpu as pltpu
from jax.sharding import PartitionSpec as P

HD = 128
EPSILON = 1e-05
FILL = -1e30
SCALE = HD ** (-0.5)
TICKS = 2
F32 = jnp.float32
BF16 = jnp.bfloat16

NT = (((1,), (1,)), ((), ()))
NN = (((1,), (0,)), ((), ()))
TN = (((0,), (0,)), ((), ()))


def dot(a, b, dims):
    return lax.dot_general(a, b, dims, preferred_element_type=F32)


def in_order(values, owners):
    total = None
    for owner in range(len(values)):
        term = jnp.where(owners[0] == owner, values[0], 0.0)
        for value, whose in zip(values[1:], owners[1:]):
            term = jnp.where(whose == owner, value, term)
        total = term if total is None else total + term
    return total


def pack_kernel(tp_count, half, both_ref, own_ref, other_ref):
    parity = lax.axis_index("tp") // (tp_count // 2)
    own_first = pl.multiple_of(parity * half, half)
    other_first = pl.multiple_of((1 - parity) * half, half)
    for kind in range(2):
        for tick in range(TICKS):
            own_ref[tick, kind] = both_ref[kind, tick, pl.ds(own_first, half), :]
            other_ref[tick, kind] = both_ref[kind, tick, pl.ds(other_first, half), :]


def norm_kernel(sizes, doc_ref, x_ref, gain_ref, query_ref, inverse_ref, mask_ref):
    rows, columns = sizes[0], sizes[5]
    for tick in range(TICKS):
        squares = jnp.zeros((rows, HD), F32)
        for first in range(0, columns, HD):
            part = x_ref[0, tick, :, first : first + HD].astype(F32)
            squares = squares + part * part
        mean = jnp.sum(squares, axis=1, keepdims=True) * (1.0 / columns)
        inverse = jnp.broadcast_to(lax.rsqrt(mean + EPSILON), (rows, HD))
        inverse_ref[tick] = inverse
        for first in range(0, columns, HD):
            here = slice(first, first + HD)
            normed = x_ref[0, tick, :, here].astype(F32) * inverse
            query_ref[tick, :, here] = (normed * gain_ref[:, here]).astype(BF16)
        mask_ref[tick] = jnp.where(visible_keys(sizes, tick, doc_ref), 0.0, FILL)


class Group:
    def __init__(self, sizes, turn):
        self.rows, self.group = sizes[0], sizes[4]
        width = self.group * HD
        self.head_group = lax.axis_index("tp") ^ turn
        self.first = pl.multiple_of(self.head_group * width, width)

    def head(self, index):
        return pl.ds(self.first + index * HD, HD)

    def stacked(self, load):
        return jnp.concatenate([load(self.head(index)) for index in range(self.group)], axis=0)

    def unstacked(self, value):
        return [value[index * self.rows : (index + 1) * self.rows] for index in range(self.group)]


def waiting_from(waiting_ref):
    return lambda where: waiting_ref[0, :, where]


def choose_arriving(output_ref, chip_ref, link_ref, target_ref):
    place = lax.axis_index("pipe")
    last = place == lax.axis_size("pipe") - 1
    even = place % 2 == 0

    @pl.when(last)
    def _():
        target_ref[...] = output_ref[0]

    @pl.when(jnp.logical_not(last) & even)
    def _():
        target_ref[...] = chip_ref[...]

    @pl.when(jnp.logical_not(last) & jnp.logical_not(even))
    def _():
        target_ref[...] = link_ref[...]


def visible_keys(sizes, tick, doc_ref):
    rows, half, cycle, tp_count, group, columns = sizes
    cycle_place = lax.axis_index("ctx")
    tp_place = lax.axis_index("tp")
    parity = tp_place // (tp_count // 2)
    stacked = group * rows

    def section_first(owner):
        return half * jnp.where(parity == 0, owner, 2 * cycle - 1 - owner)

    row_first = section_first(cycle_place) + (tp_place % (tp_count // 2)) * rows
    query_pos = row_first + (lax.broadcasted_iota(jnp.int32, (1, stacked), 1) & (rows - 1))
    key_place = lax.broadcasted_iota(jnp.int32, (cycle * half, 1), 0)
    key_pos = key_place + section_first(cycle_place)
    for turn in range(1, cycle):
        first = section_first((cycle_place - turn + cycle) % cycle)
        key_pos = jnp.where(key_place >= turn * half, key_place - turn * half + first, key_pos)
    micro = lax.axis_index("pipe") + tick
    closing = jnp.int32(0)
    query_start = jnp.zeros((1, stacked), jnp.int32)
    for doc in range(doc_ref.shape[1]):
        length = doc_ref[micro, doc]
        closing = closing + length
        query_start = query_start + jnp.where(closing <= query_pos, length, 0)
    return (key_pos <= query_pos) & (key_pos >= query_start)


def probabilities(mask, products):
    scores = SCALE * products + mask
    weights = jnp.exp(scores - jnp.max(scores, axis=0, keepdims=True))
    return weights * (1.0 / jnp.sum(weights, axis=0, keepdims=True))


def score_grads(probs, prob_grad):
    row_term = jnp.sum(probs * prob_grad, axis=0, keepdims=True)
    return (probs * (prob_grad - row_term)).astype(BF16)


class Keys:
    def __init__(self, sizes, tick, refs):
        self.near_count = sizes[3] // 2
        self.tick = tick
        self.refs = [refs[0], *refs[1:][::-1]]

    def __call__(self, near, kind):
        parts = [ref[self.tick, kind] for ref in self.refs[near :: self.near_count]]
        return jnp.concatenate(parts, axis=0)


def place_of(sizes, far, kind):
    half = sizes[1]
    return slice((far * 2 + kind) * half, (far * 2 + kind + 1) * half)


def put_key_grads(sizes, turn, parts, own_ref, message_refs):
    half, cycle, tp_count = sizes[1:4]
    near_count = tp_count // 2
    near, far = turn % near_count, turn // near_count
    for kind, part in enumerate(parts):
        here = place_of(sizes, far, kind)
        for step in range(cycle):
            piece = part[step * half : (step + 1) * half]
            if step == 0 and near == 0:
                own_ref[here, :] = piece
            else:
                message_refs[step * near_count + near - 1][here, :] = piece.astype(BF16)


def gain_terms(columns_of, query_grad, normed_of, gain_rows_ref):
    rows = []
    for index, low in enumerate(columns_of.unstacked(query_grad)):
        term = low.astype(F32) * normed_of(columns_of.head(index))
        rows.append(jnp.sum(term, axis=0, keepdims=True))
    group = columns_of.group
    place = pl.ds(pl.multiple_of(columns_of.head_group * group, group), group)
    gain_rows_ref[place, :] = jnp.concatenate(rows, axis=0)


def coupled_terms(columns_of, query_grad, normed_of, gain_ref, coupled):
    for index, low in enumerate(columns_of.unstacked(query_grad)):
        where = columns_of.head(index)
        coupled = coupled + low.astype(F32) * gain_ref[:, where] * normed_of(where)
    return coupled


def write_input_grads(sizes, coupled, query_grad_of, normed_of, gain_ref, inverse, arriving, write):
    coupling = jnp.sum(coupled, axis=1, keepdims=True) * (1.0 / sizes[5])
    for turn in range(sizes[3]):
        columns_of = Group(sizes, turn)
        for index, low in enumerate(columns_of.unstacked(query_grad_of(turn))):
            where = columns_of.head(index)
            scaled = low.astype(F32) * gain_ref[:, where]
            result = arriving(where).astype(F32) + inverse * (scaled - normed_of(where) * coupling)
            write(where, result.astype(BF16))


def normed_from(x_ref, tick, inverse):
    return lambda where: x_ref[0, tick, :, where].astype(F32) * inverse


def first_half(keys, mask, products, dscore_ref, probs_ref):
    dscores = []
    for near, (scores, prob_grads) in enumerate(products):
        probs = probabilities(mask, scores)
        dscores.append(score_grads(probs, prob_grads))
        dscore_ref[near] = dscores[near]
        probs_ref[near] = probs.astype(BF16)
    return [
        (SCALE * dot(dscore, keys(near, 0), TN)).astype(BF16)
        for near, dscore in enumerate(dscores)
    ]


def first_near_rows_kernel(sizes, *refs):
    near_count = sizes[3] // 2
    members = sizes[2] * near_count
    x_ref, gain_ref, query_ref, inverse_ref, mask_ref, waiting_ref = refs[:6]
    keys = Keys(sizes, 0, refs[6 : 6 + members])
    query_grad_ref, dscore_ref, probs_ref, coupled_ref, turned_ref = refs[6 + members : 11 + members]
    base_ref, pull_ref, rate_ref, weight_ref = refs[11 + members :]
    loads = (lambda where: query_ref[0, :, where], waiting_from(waiting_ref))
    products = []
    for near in range(near_count):
        operands = [Group(sizes, near).stacked(load) for load in loads]
        products.append([dot(keys(near, kind), operands[kind], NT) for kind in range(2)])
    query_grads = first_half(keys, mask_ref[0], products, dscore_ref, probs_ref)
    normed_of = normed_from(x_ref, 0, inverse_ref[0])
    coupled = jnp.zeros((sizes[0], HD), F32)
    for near, query_grad in enumerate(query_grads):
        query_grad_ref[near] = query_grad
        coupled = coupled_terms(Group(sizes, near), query_grad, normed_of, gain_ref, coupled)
    coupled_ref[...] = coupled
    inverse = inverse_ref[0]
    for near in range(near_count):
        columns_of = Group(sizes, near)
        for index, low in enumerate(columns_of.unstacked(query_grads[near])):
            where = columns_of.head(index)
            scaled = low.astype(F32) * gain_ref[:, where]
            base_ref[:, where] = loads[1](where).astype(F32) + inverse * scaled
            pull_ref[:, where] = inverse * normed_of(where)
        columns_of = Group(sizes, near_count + near)
        for kind, load in enumerate(loads):
            turned_ref[near, kind] = columns_of.stacked(load).T
        for index in range(columns_of.group):
            where = columns_of.head(index)
            normed = normed_of(where)
            pull_ref[:, where] = inverse * normed
            rate_ref[:, where] = inverse * gain_ref[:, where]
            weight_ref[:, where] = normed * gain_ref[:, where]


def first_far_rows_kernel(sizes, *refs):
    near_count = sizes[3] // 2
    members = sizes[2] * near_count
    mask_ref, waiting_ref = refs[:2]
    keys, refs = Keys(sizes, 0, refs[2 : 2 + members]), refs[2 + members :]
    coupled_ref, turned_ref, base_ref, pull_ref, rate_ref, weight_ref = refs[:6]
    input_grad_ref, query_grad_ref, dscore_ref, probs_ref = refs[6:]
    products = [
        [dot(keys(near, kind), turned_ref[near, kind], NN) for kind in range(2)]
        for near in range(near_count)
    ]
    query_grads = first_half(keys, mask_ref[0], products, dscore_ref, probs_ref)
    coupled = coupled_ref[...]
    groups = [Group(sizes, turn) for turn in range(2 * near_count)]
    for near, query_grad in enumerate(query_grads):
        query_grad_ref[near] = query_grad
        columns_of = groups[near_count + near]
        for index, low in enumerate(columns_of.unstacked(query_grad)):
            coupled = coupled + low.astype(F32) * weight_ref[:, columns_of.head(index)]
    coupling = jnp.sum(coupled, axis=1, keepdims=True) * (1.0 / sizes[5])
    for near, query_grad in enumerate(query_grads):
        for index in range(groups[near].group):
            where = groups[near].head(index)
            input_grad_ref[:, where] = (base_ref[:, where] - pull_ref[:, where] * coupling).astype(
                BF16
            )
        columns_of = groups[near_count + near]
        for index, low in enumerate(columns_of.unstacked(query_grad)):
            where = columns_of.head(index)
            base = waiting_ref[0, :, where].astype(F32) + low.astype(F32) * rate_ref[:, where]
            input_grad_ref[:, where] = (base - pull_ref[:, where] * coupling).astype(BF16)


def first_keys_kernel(sizes, *refs):
    half, cycle, tp_count = sizes[1:4]
    near_count = tp_count // 2
    x_ref, query_ref, inverse_ref, waiting_ref = refs[:4]
    query_grad_refs, dscore_refs, probs_refs = refs[4:6], refs[6:8], refs[8:10]
    gain_rows_ref, own_ref = refs[10:12]
    send_refs = refs[12:]
    arriving = waiting_from(waiting_ref)
    normed_of = normed_from(x_ref, 0, inverse_ref[0])
    for turn in range(tp_count):
        near, far = turn % near_count, turn // near_count
        columns_of = Group(sizes, turn)
        query = columns_of.stacked(lambda where: query_ref[0, :, where])
        grad = columns_of.stacked(arriving)
        parts = (
            SCALE * dot(dscore_refs[far][near], query, NN),
            dot(probs_refs[far][near], grad, NN),
        )
        for kind, part in enumerate(parts):
            here = place_of(sizes, far, kind)
            own_ref[near, here, :] = part[:half]
            for step, ref in enumerate(send_refs, 1):
                ref[near, here, :] = part[step * half : (step + 1) * half].astype(BF16)
        gain_terms(columns_of, query_grad_refs[far][near], normed_of, gain_rows_ref)


def both_sets(sizes, refs):
    near_count = sizes[3] // 2
    members = sizes[2] * near_count
    sets = [Keys(sizes, 1, refs[:members]), Keys(sizes, 1, refs[members:])]
    return lambda turn, kind: sets[turn // near_count](turn % near_count, kind)


def second_probs_kernel(sizes, *refs):
    turns = range(sizes[3])
    mask_ref, query_ref = refs[:2]
    keys, probs_ref = both_sets(sizes, refs[2:-1]), refs[-1]
    mask = mask_ref[1]
    scores = []
    for turn in turns:
        query = Group(sizes, turn).stacked(lambda where: query_ref[1, :, where])
        scores.append(dot(keys(turn, 0), query, NT))
    for turn in turns:
        probs_ref[turn] = probabilities(mask, scores[turn])


def second_keys_kernel(sizes, *refs):
    cycle, tp_count = sizes[2:4]
    turns = range(tp_count)
    kv_count = cycle * tp_count
    x_ref, query_ref, inverse_ref, output_ref, link_ref, chip_ref = refs[:6]
    probs_ref, before_ref, *refs = refs[6:]
    keys, refs = both_sets(sizes, refs[:kv_count]), refs[kv_count:]
    query_grad_ref, gain_rows_ref, own_ref, arriving_ref = refs[:4]
    message_refs, gain_scratch = refs[4:-1], refs[-1]
    choose_arriving(output_ref, chip_ref, link_ref, arriving_ref)

    def arriving(where):
        return arriving_ref[:, where]

    normed_of = normed_from(x_ref, 1, inverse_ref[1])
    columns_of = [Group(sizes, turn) for turn in turns]
    grads = [columns_of[turn].stacked(arriving) for turn in turns]
    prob_grads = [dot(keys(turn, 1), grads[turn], NT) for turn in turns]
    value_grads = [dot(probs_ref[turn].astype(BF16), grads[turn], NN) for turn in turns]
    dscores = [score_grads(probs_ref[turn], prob_grads[turn]) for turn in turns]
    query_grads = [
        (SCALE * dot(dscores[turn], keys(turn, 0), TN)).astype(BF16) for turn in turns
    ]
    for turn in turns:
        query = columns_of[turn].stacked(lambda where: query_ref[1, :, where])
        key_grad = SCALE * dot(dscores[turn], query, NN)
        put_key_grads(sizes, turn, (key_grad, value_grads[turn]), own_ref, message_refs)
    for turn in turns:
        query_grad_ref[turn] = query_grads[turn]
        gain_terms(columns_of[turn], query_grads[turn], normed_of, gain_scratch)
    gain_rows = gain_scratch[...] + before_ref[...]
    gain_rows_ref[...] = gain_rows
    gain_low = gain_rows.astype(BF16)
    for ref in message_refs:
        ref[own_ref.shape[0] :, :] = gain_low


def first_sum_kernel(sizes, *refs):
    cycle = sizes[2]
    parts, own_ref, message_refs = refs[:cycle], refs[cycle], refs[cycle + 1 :]
    for near in range(sizes[3] // 2):
        total = parts[0][near]
        for ref in parts[1:]:
            total = total + ref[near].astype(F32)
        if near == 0:
            own_ref[...] = total
        else:
            message_refs[near - 1][...] = total.astype(BF16)


def second_rows_kernel(sizes, *refs):
    x_ref, gain_ref, inverse_ref, arriving_ref, query_grad_ref, first_ref, input_grads_ref = refs
    input_grads_ref[0, 0] = first_ref[...]
    inverse = inverse_ref[1]
    normed_of = normed_from(x_ref, 1, inverse)
    coupled = jnp.zeros((sizes[0], HD), F32)
    for turn in range(sizes[3]):
        coupled = coupled_terms(
            Group(sizes, turn), query_grad_ref[turn], normed_of, gain_ref, coupled
        )

    def write(where, result):
        input_grads_ref[0, 1, :, where] = result

    write_input_grads(
        sizes,
        coupled,
        lambda turn: query_grad_ref[turn],
        normed_of,
        gain_ref,
        inverse,
        lambda where: arriving_ref[:, where],
        write,
    )


def first_near_kernel(sizes, own_ref, *refs):
    block = 2 * sizes[1]
    keep_ref, send_ref = refs[-2:]
    total = own_ref[...]
    for ref in refs[:-2]:
        total = total + ref[...].astype(F32)
    keep_ref[...] = total[:block]
    send_ref[...] = total[block:].astype(BF16)


def second_near_kernel(sizes, *refs):
    rows, half, cycle, tp_count, group, columns = sizes
    near_count = tp_count // 2
    members = cycle * near_count
    own_ref, gain_ref = refs[:2]
    message_refs = refs[2 : 1 + members][::-1]
    keep_ref, gain_sum_ref, send_ref = refs[1 + members :]
    block = 2 * half
    total = own_ref[...]
    for ref in message_refs:
        total = total + ref[: 2 * block, :].astype(F32)
    keep_ref[...] = total[:block]
    send_ref[:block, :] = total[block:].astype(BF16)
    cycle_place = lax.axis_index("ctx")
    near_place = lax.axis_index("tp") % near_count
    values = [gain_ref[...].astype(BF16).astype(F32)]
    owners = [cycle_place * near_count + near_place]
    for place, ref in enumerate(message_refs, 1):
        step, near = place // near_count, place % near_count
        values.append(ref[2 * block :, :].astype(F32))
        owners.append(((cycle_place + step) % cycle) * near_count + (near_place ^ near))
    gain = in_order(values, owners)
    gain_sum_ref[...] = gain
    send_ref[block:, :] = gain.astype(BF16)


def finish_kernel(sizes, *refs):
    half = sizes[1]
    keep_refs, receive_refs, gain_ref = refs[:TICKS], refs[TICKS : 2 * TICKS], refs[2 * TICKS]
    key_ref, value_ref, gain_out_ref = refs[2 * TICKS + 1 :]
    parity = lax.axis_index("tp") // (sizes[3] // 2)
    block = 2 * half
    own_first = pl.multiple_of(parity * half, half)
    other_first = pl.multiple_of((1 - parity) * half, half)
    for tick in range(TICKS):
        for kind, out in enumerate((key_ref, value_ref)):
            here = slice(kind * half, (kind + 1) * half)
            out[0, tick, pl.ds(own_first, half), :] = keep_refs[tick][here, :]
            out[0, tick, pl.ds(other_first, half), :] = receive_refs[tick][here, :].astype(F32)
    own = gain_ref[...].astype(BF16).astype(F32)
    gain_out_ref[...] = own + receive_refs[TICKS - 1][block:, :].astype(F32)


def shape(dims, dtype):
    return jax.ShapeDtypeStruct(dims, dtype)


def on_device(segment_inputs, keys, values, norm_gain, waiting_grads, output_grads, doc_lengths):
    cycle = lax.axis_size("ctx")
    tp_count = lax.axis_size("tp")
    pipe_count = lax.axis_size("pipe")
    _, ticks, rows, columns = segment_inputs.shape
    half = keys.shape[2] // 2
    group = columns // (tp_count * HD)
    gain_count = columns // HD
    sizes = (rows, half, cycle, tp_count, group, columns)
    block = 2 * half
    key_count = cycle * half
    stacked = group * rows
    score_bytes = key_count * stacked * 4
    usual_limit = min(56 << 20, (12 << 20) + 20 * score_bytes)

    def call(kernel, name, operands, out_shape, scratch=(), scalars=0):
        in_specs = [pl.BlockSpec(memory_space=pltpu.SMEM)] * scalars
        in_specs += [pl.BlockSpec(memory_space=pltpu.VMEM)] * (len(operands) - scalars)
        return pl.pallas_call(
            kernel,
            out_shape=out_shape,
            in_specs=in_specs,
            out_specs=[pl.BlockSpec(memory_space=pltpu.VMEM)] * len(out_shape),
            scratch_shapes=scratch,
            compiler_params=pltpu.CompilerParams(vmem_limit_bytes=usual_limit),
            name=name,
        )(*operands)

    near_count = tp_count // 2

    def to_near(value, step, near):
        if step == 0:
            return lax.ppermute(value, "tp", [(i, i ^ near) for i in range(tp_count)])
        if near == 0:
            return lax.ppermute(value, "ctx", [(i, (i + step) % cycle) for i in range(cycle)])
        pairs = [
            (c * tp_count + t, ((c + step) % cycle) * tp_count + (t ^ near))
            for c in range(cycle)
            for t in range(tp_count)
        ]
        return lax.ppermute(value, ("ctx", "tp"), pairs)

    def to_far(value):
        return lax.ppermute(value, "tp", [(i, i ^ near_count) for i in range(tp_count)])

    sections = shape((ticks, 2, half, HD), BF16)
    own_kv, other_kv = call(
        functools.partial(pack_kernel, tp_count, half),
        "pack_kv",
        (jnp.stack([keys[0], values[0]]),),
        [sections, sections],
    )
    far_kv = to_far(other_kv)
    places = [(step, near) for step in range(cycle) for near in range(near_count)][1:]
    kv = [
        block if place == (0, 0) else to_near(block, *place)
        for block in (own_kv, far_kv)
        for place in [(0, 0)] + places[::-1]
    ]
    own_set, far_set = kv[: len(kv) // 2], kv[len(kv) // 2 :]
    queries, inverse, masks = call(
        functools.partial(norm_kernel, sizes),
        "norm",
        (doc_lengths, segment_inputs, norm_gain),
        [
            shape((ticks, rows, columns), BF16),
            shape((ticks, rows, HD), F32),
            shape((ticks, key_count, stacked), F32),
        ],
        scalars=1,
    )

    low_rows = shape((rows, columns), BF16)
    low_scores = shape((near_count, key_count, stacked), BF16)
    low_grads = shape((near_count, stacked, HD), BF16)
    query_grad_near, dscore_near, probs_near, coupled, turned, *factors = call(
        functools.partial(first_near_rows_kernel, sizes),
        "first_near_rows",
        (segment_inputs, norm_gain, queries, inverse, masks, waiting_grads, *own_set),
        [
            low_grads,
            low_scores,
            low_scores,
            shape((rows, HD), F32),
            shape((near_count, 2, HD, stacked), BF16),
        ]
        + [shape((rows, columns), F32)] * 4,
    )
    input_grad_first, query_grad_far, dscore_far, probs_far = call(
        functools.partial(first_far_rows_kernel, sizes),
        "first_far_rows",
        (
            masks,
            waiting_grads,
            *far_set,
            coupled,
            turned,
            *factors,
        ),
        [low_rows, low_grads, low_scores, low_scores],
    )
    over_link = lax.ppermute(
        input_grad_first, "pipe", [(i, i - 1) for i in range(2, pipe_count, 2)]
    )
    on_chip = lax.ppermute(input_grad_first, "pipe", [(i, i ^ 1) for i in range(pipe_count)])
    gain_shape = shape((gain_count, HD), F32)
    pair_rows = 2 * block
    own_shape = shape((pair_rows, HD), F32)
    first_sums = (near_count, pair_rows, HD)
    gain_first, *sums_first = call(
        functools.partial(first_keys_kernel, sizes),
        "first_keys",
        (
            segment_inputs,
            queries,
            inverse,
            waiting_grads,
            query_grad_near,
            query_grad_far,
            dscore_near,
            dscore_far,
            probs_near,
            probs_far,
        ),
        [gain_shape, shape(first_sums, F32)] + [shape(first_sums, BF16)] * (cycle - 1),
    )
    sums_first = sums_first[:1] + [
        to_near(value, -step, 0) for step, value in enumerate(sums_first[1:], 1)
    ]
    (probs_second,) = call(
        functools.partial(second_probs_kernel, sizes),
        "second_probs",
        (masks, queries, *kv),
        [shape((tp_count, key_count, stacked), F32)],
    )
    message = shape((pair_rows + gain_count, HD), BF16)
    query_grad_second, gain_rows, own_second, arriving, *sends = call(
        functools.partial(second_keys_kernel, sizes),
        "second_keys",
        (
            segment_inputs,
            queries,
            inverse,
            output_grads,
            over_link,
            on_chip,
            probs_second,
            gain_first,
            *kv,
        ),
        [shape((tp_count, stacked, HD), BF16), gain_shape, own_shape, low_rows]
        + [message] * len(places),
        scratch=[pltpu.VMEM((gain_count, HD), F32)],
    )
    received = [to_near(value, -step, near) for value, (step, near) in zip(sends, places)]
    own_first, *sends_first = call(
        functools.partial(first_sum_kernel, sizes),
        "first_sum",
        sums_first,
        [own_shape] + [shape((pair_rows, HD), BF16)] * (near_count - 1),
    )
    received_first = [to_near(value, 0, near) for near, value in enumerate(sends_first, 1)]
    (input_grads,) = call(
        functools.partial(second_rows_kernel, sizes),
        "second_rows",
        (
            segment_inputs,
            norm_gain,
            inverse,
            arriving,
            query_grad_second,
            input_grad_first,
        ),
        [shape((1, ticks, rows, columns), BF16)],
    )
    keep_shape = shape((block, HD), F32)
    keep_first, send_first = call(
        functools.partial(first_near_kernel, sizes),
        "first_near",
        (own_first, *received_first),
        [keep_shape, shape((block, HD), BF16)],
    )
    keep_second, gain_sum, send_second = call(
        functools.partial(second_near_kernel, sizes),
        "second_near",
        (own_second, gain_rows, *received[::-1]),
        [keep_shape, gain_shape, shape((block + gain_count, HD), BF16)],
    )
    grads_shape = shape((1, ticks, block, HD), F32)
    key_grads, value_grads, gain_grads = call(
        functools.partial(finish_kernel, sizes),
        "finish",
        (keep_first, keep_second, to_far(send_first), to_far(send_second), gain_sum),
        [grads_shape, grads_shape, gain_shape],
    )
    return input_grads, key_grads, value_grads, gain_grads.reshape(1, columns)


def solution(mesh):
    in_specs = (
        P("pipe", None, ("ctx", "tp"), None),
        P("pipe", None, "ctx", "tp"),
        P("pipe", None, "ctx", "tp"),
        P("pipe", None),
        P("pipe", ("ctx", "tp"), None),
        P(None, ("ctx", "tp"), None),
        P(),
    )
    out_specs = (
        P("pipe", None, ("ctx", "tp"), None),
        P("pipe", None, "ctx", "tp"),
        P("pipe", None, "ctx", "tp"),
        P("pipe", None),
    )
    return jax.shard_map(
        on_device, mesh=mesh, in_specs=in_specs, out_specs=out_specs, check_vma=False
    )
```

```python
import functools

import jax
import jax.numpy as jnp
from jax import lax
from jax.experimental import pallas as pl
from jax.experimental.pallas import tpu as pltpu
from jax.sharding import PartitionSpec as P

HD = 128
EPSILON = 1e-05
FILL = -1e30
SCALE = HD ** (-0.5)
TICKS = 2
F32 = jnp.float32
BF16 = jnp.bfloat16

NT = (((1,), (1,)), ((), ()))
NN = (((1,), (0,)), ((), ()))
TN = (((0,), (0,)), ((), ()))


def dot(a, b, dims):
    return lax.dot_general(a, b, dims, preferred_element_type=F32)


def in_order(values, owners):
    total = None
    for owner in range(len(values)):
        term = jnp.where(owners[0] == owner, values[0], 0.0)
        for value, whose in zip(values[1:], owners[1:]):
            term = jnp.where(whose == owner, value, term)
        total = term if total is None else total + term
    return total


def pack_kernel(tp_count, half, both_ref, own_ref, other_ref):
    parity = lax.axis_index("tp") // (tp_count // 2)
    own_first = pl.multiple_of(parity * half, half)
    other_first = pl.multiple_of((1 - parity) * half, half)
    for kind in range(2):
        for tick in range(TICKS):
            own_ref[tick, kind] = both_ref[kind, tick, pl.ds(own_first, half), :]
            other_ref[tick, kind] = both_ref[kind, tick, pl.ds(other_first, half), :]


def norm_kernel(sizes, doc_ref, x_ref, gain_ref, query_ref, inverse_ref, mask_ref):
    rows, columns = sizes[0], sizes[5]
    for tick in range(TICKS):
        squares = jnp.zeros((rows, HD), F32)
        for first in range(0, columns, HD):
            part = x_ref[0, tick, :, first : first + HD].astype(F32)
            squares = squares + part * part
        mean = jnp.sum(squares, axis=1, keepdims=True) * (1.0 / columns)
        inverse = jnp.broadcast_to(lax.rsqrt(mean + EPSILON), (rows, HD))
        inverse_ref[tick] = inverse
        for first in range(0, columns, HD):
            here = slice(first, first + HD)
            normed = x_ref[0, tick, :, here].astype(F32) * inverse
            query_ref[tick, :, here] = (normed * gain_ref[:, here]).astype(BF16)
        mask_ref[tick] = jnp.where(visible_keys(sizes, tick, doc_ref), 0.0, FILL)


class Group:
    def __init__(self, sizes, turn):
        self.rows, self.group = sizes[0], sizes[4]
        width = self.group * HD
        self.head_group = lax.axis_index("tp") ^ turn
        self.first = pl.multiple_of(self.head_group * width, width)

    def head(self, index):
        return pl.ds(self.first + index * HD, HD)

    def stacked(self, load):
        return jnp.concatenate([load(self.head(index)) for index in range(self.group)], axis=0)

    def unstacked(self, value):
        return [value[index * self.rows : (index + 1) * self.rows] for index in range(self.group)]


def waiting_from(waiting_ref):
    return lambda where: waiting_ref[0, :, where]


def choose_arriving(output_ref, chip_ref, link_ref, target_ref):
    place = lax.axis_index("pipe")
    last = place == lax.axis_size("pipe") - 1
    even = place % 2 == 0

    @pl.when(last)
    def _():
        target_ref[...] = output_ref[0]

    @pl.when(jnp.logical_not(last) & even)
    def _():
        target_ref[...] = chip_ref[...]

    @pl.when(jnp.logical_not(last) & jnp.logical_not(even))
    def _():
        target_ref[...] = link_ref[...]


def visible_keys(sizes, tick, doc_ref):
    rows, half, cycle, tp_count, group, columns = sizes
    cycle_place = lax.axis_index("ctx")
    tp_place = lax.axis_index("tp")
    parity = tp_place // (tp_count // 2)
    stacked = group * rows

    def section_first(owner):
        return half * jnp.where(parity == 0, owner, 2 * cycle - 1 - owner)

    row_first = section_first(cycle_place) + (tp_place % (tp_count // 2)) * rows
    query_pos = row_first + (lax.broadcasted_iota(jnp.int32, (1, stacked), 1) & (rows - 1))
    key_place = lax.broadcasted_iota(jnp.int32, (cycle * half, 1), 0)
    key_pos = key_place + section_first(cycle_place)
    for turn in range(1, cycle):
        first = section_first((cycle_place - turn + cycle) % cycle)
        key_pos = jnp.where(key_place >= turn * half, key_place - turn * half + first, key_pos)
    micro = lax.axis_index("pipe") + tick
    closing = jnp.int32(0)
    query_start = jnp.zeros((1, stacked), jnp.int32)
    for doc in range(doc_ref.shape[1]):
        length = doc_ref[micro, doc]
        closing = closing + length
        query_start = query_start + jnp.where(closing <= query_pos, length, 0)
    return (key_pos <= query_pos) & (key_pos >= query_start)


def probabilities(mask, products):
    scores = SCALE * products + mask
    weights = jnp.exp(scores - jnp.max(scores, axis=0, keepdims=True))
    return weights * (1.0 / jnp.sum(weights, axis=0, keepdims=True))


def score_grads(probs, prob_grad):
    row_term = jnp.sum(probs * prob_grad, axis=0, keepdims=True)
    return (probs * (prob_grad - row_term)).astype(BF16)


class Keys:
    def __init__(self, sizes, tick, refs):
        self.near_count = sizes[3] // 2
        self.tick = tick
        self.refs = refs

    def __call__(self, near, kind):
        parts = [ref[self.tick, kind] for ref in self.refs[near :: self.near_count]]
        return jnp.concatenate(parts, axis=0)


def place_of(sizes, far, kind):
    half = sizes[1]
    return slice((far * 2 + kind) * half, (far * 2 + kind + 1) * half)


def put_key_grads(sizes, turn, parts, own_ref, message_refs):
    half, cycle, tp_count = sizes[1:4]
    near_count = tp_count // 2
    near, far = turn % near_count, turn // near_count
    for kind, part in enumerate(parts):
        here = place_of(sizes, far, kind)
        for step in range(cycle):
            piece = part[step * half : (step + 1) * half]
            if step == 0 and near == 0:
                own_ref[here, :] = piece
            else:
                message_refs[step * near_count + near - 1][here, :] = piece.astype(BF16)


def gain_terms(columns_of, query_grad, normed_of, gain_rows_ref):
    rows = []
    for index, low in enumerate(columns_of.unstacked(query_grad)):
        term = low.astype(F32) * normed_of(columns_of.head(index))
        rows.append(jnp.sum(term, axis=0, keepdims=True))
    group = columns_of.group
    place = pl.ds(pl.multiple_of(columns_of.head_group * group, group), group)
    gain_rows_ref[place, :] = jnp.concatenate(rows, axis=0)


def coupled_terms(columns_of, query_grad, normed_of, gain_ref, coupled):
    for index, low in enumerate(columns_of.unstacked(query_grad)):
        where = columns_of.head(index)
        coupled = coupled + low.astype(F32) * gain_ref[:, where] * normed_of(where)
    return coupled


def write_input_grads(sizes, coupled, query_grad_of, normed_of, gain_ref, inverse, arriving, write):
    coupling = jnp.sum(coupled, axis=1, keepdims=True) * (1.0 / sizes[5])
    for turn in range(sizes[3]):
        columns_of = Group(sizes, turn)
        for index, low in enumerate(columns_of.unstacked(query_grad_of(turn))):
            where = columns_of.head(index)
            scaled = low.astype(F32) * gain_ref[:, where]
            result = arriving(where).astype(F32) + inverse * (scaled - normed_of(where) * coupling)
            write(where, result.astype(BF16))


def normed_from(x_ref, tick, inverse):
    return lambda where: x_ref[0, tick, :, where].astype(F32) * inverse


def first_half(keys, mask, products, dscore_ref, probs_ref):
    dscores = []
    for near, (scores, prob_grads) in enumerate(products):
        probs = probabilities(mask, scores)
        dscores.append(score_grads(probs, prob_grads))
        dscore_ref[near] = dscores[near]
        probs_ref[near] = probs.astype(BF16)
    return [
        (SCALE * dot(dscore, keys(near, 0), TN)).astype(BF16)
        for near, dscore in enumerate(dscores)
    ]


def first_near_rows_kernel(sizes, *refs):
    near_count = sizes[3] // 2
    members = sizes[2] * near_count
    x_ref, gain_ref, query_ref, inverse_ref, mask_ref, waiting_ref = refs[:6]
    keys = Keys(sizes, 0, refs[6 : 6 + members])
    query_grad_ref, dscore_ref, probs_ref, coupled_ref, turned_ref = refs[6 + members :]
    loads = (lambda where: query_ref[0, :, where], waiting_from(waiting_ref))
    products = []
    for near in range(near_count):
        operands = [Group(sizes, near).stacked(load) for load in loads]
        products.append([dot(keys(near, kind), operands[kind], NT) for kind in range(2)])
    query_grads = first_half(keys, mask_ref[0], products, dscore_ref, probs_ref)
    normed_of = normed_from(x_ref, 0, inverse_ref[0])
    coupled = jnp.zeros((sizes[0], HD), F32)
    for near, query_grad in enumerate(query_grads):
        query_grad_ref[near] = query_grad
        coupled = coupled_terms(Group(sizes, near), query_grad, normed_of, gain_ref, coupled)
    coupled_ref[...] = coupled
    for near in range(near_count):
        columns_of = Group(sizes, near_count + near)
        for kind, load in enumerate(loads):
            turned_ref[near, kind] = columns_of.stacked(load).T


def first_far_rows_kernel(sizes, *refs):
    near_count = sizes[3] // 2
    members = sizes[2] * near_count
    x_ref, gain_ref, inverse_ref, mask_ref, waiting_ref = refs[:5]
    keys, refs = Keys(sizes, 0, refs[5 : 5 + members]), refs[5 + members :]
    near_grad_ref, coupled_ref, turned_ref = refs[:3]
    input_grad_ref, query_grad_ref, dscore_ref, probs_ref = refs[3:]
    products = [
        [dot(keys(near, kind), turned_ref[near, kind], NN) for kind in range(2)]
        for near in range(near_count)
    ]
    query_grads = first_half(keys, mask_ref[0], products, dscore_ref, probs_ref)
    normed_of = normed_from(x_ref, 0, inverse_ref[0])
    coupled = coupled_ref[...]
    for near, query_grad in enumerate(query_grads):
        query_grad_ref[near] = query_grad
        coupled = coupled_terms(
            Group(sizes, near_count + near), query_grad, normed_of, gain_ref, coupled
        )

    def query_grad_of(turn):
        return near_grad_ref[turn] if turn < near_count else query_grads[turn - near_count]

    def write(where, result):
        input_grad_ref[:, where] = result

    write_input_grads(
        sizes,
        coupled,
        query_grad_of,
        normed_of,
        gain_ref,
        inverse_ref[0],
        waiting_from(waiting_ref),
        write,
    )


def first_keys_kernel(sizes, *refs):
    half, cycle, tp_count = sizes[1:4]
    near_count = tp_count // 2
    x_ref, query_ref, inverse_ref, waiting_ref = refs[:4]
    query_grad_refs, dscore_refs, probs_refs = refs[4:6], refs[6:8], refs[8:10]
    gain_rows_ref, own_ref = refs[10:12]
    send_refs = refs[12:]
    arriving = waiting_from(waiting_ref)
    normed_of = normed_from(x_ref, 0, inverse_ref[0])
    for turn in range(tp_count):
        near, far = turn % near_count, turn // near_count
        columns_of = Group(sizes, turn)
        query = columns_of.stacked(lambda where: query_ref[0, :, where])
        grad = columns_of.stacked(arriving)
        parts = (
            SCALE * dot(dscore_refs[far][near], query, NN),
            dot(probs_refs[far][near], grad, NN),
        )
        for kind, part in enumerate(parts):
            here = place_of(sizes, far, kind)
            own_ref[near, here, :] = part[:half]
            for step, ref in enumerate(send_refs, 1):
                ref[near, here, :] = part[step * half : (step + 1) * half].astype(BF16)
        gain_terms(columns_of, query_grad_refs[far][near], normed_of, gain_rows_ref)


def both_sets(sizes, refs):
    near_count = sizes[3] // 2
    members = sizes[2] * near_count
    sets = [Keys(sizes, 1, refs[:members]), Keys(sizes, 1, refs[members:])]
    return lambda turn, kind: sets[turn // near_count](turn % near_count, kind)


def second_probs_kernel(sizes, *refs):
    turns = range(sizes[3])
    mask_ref, query_ref, x_ref, inverse_ref = refs[:4]
    keys, (probs_ref, low_ref, normed_ref) = both_sets(sizes, refs[4:-3]), refs[-3:]
    mask = mask_ref[1]
    scores = []
    for turn in turns:
        query = Group(sizes, turn).stacked(lambda where: query_ref[1, :, where])
        scores.append(dot(keys(turn, 0), query, NT))
    for turn in turns:
        probs = probabilities(mask, scores[turn])
        probs_ref[turn] = probs
        low_ref[turn] = probs.astype(BF16)
    inverse = inverse_ref[1]
    for first in range(0, sizes[5], HD):
        here = slice(first, first + HD)
        normed_ref[:, here] = x_ref[0, 1, :, here].astype(F32) * inverse


def second_keys_kernel(sizes, *refs):
    cycle, tp_count = sizes[2:4]
    turns = range(tp_count)
    kv_count = cycle * tp_count
    normed_ref, query_ref, low_ref, output_ref, chip_ref, link_ref = refs[:6]
    probs_ref, before_ref, *refs = refs[6:]
    keys, refs = both_sets(sizes, refs[:kv_count]), refs[kv_count:]
    query_grad_ref, gain_rows_ref, own_ref, arriving_ref = refs[:4]
    message_refs, gain_scratch = refs[4:-1], refs[-1]
    choose_arriving(output_ref, chip_ref, link_ref, arriving_ref)

    def arriving(where):
        return arriving_ref[:, where]

    columns_of = [Group(sizes, turn) for turn in turns]
    grads = [columns_of[turn].stacked(arriving) for turn in turns]
    prob_grads = [dot(keys(turn, 1), grads[turn], NT) for turn in turns]
    value_grads = [dot(low_ref[turn], grads[turn], NN) for turn in turns]
    dscores = [score_grads(probs_ref[turn], prob_grads[turn]) for turn in turns]
    query_grads = [
        (SCALE * dot(dscores[turn], keys(turn, 0), TN)).astype(BF16) for turn in turns
    ]
    for turn in turns:
        query = columns_of[turn].stacked(lambda where: query_ref[1, :, where])
        key_grad = SCALE * dot(dscores[turn], query, NN)
        put_key_grads(sizes, turn, (key_grad, value_grads[turn]), own_ref, message_refs)
    for turn in turns:
        query_grad_ref[turn] = query_grads[turn]
        gain_terms(
            columns_of[turn], query_grads[turn], lambda where: normed_ref[:, where], gain_scratch
        )
    gain_rows = gain_scratch[...] + before_ref[...]
    gain_rows_ref[...] = gain_rows
    gain_low = gain_rows.astype(BF16)
    for ref in message_refs:
        ref[own_ref.shape[0] :, :] = gain_low


def first_sum_kernel(sizes, *refs):
    cycle = sizes[2]
    parts, own_ref, message_refs = refs[:cycle], refs[cycle], refs[cycle + 1 :]
    for near in range(sizes[3] // 2):
        total = parts[0][near]
        for ref in parts[1:]:
            total = total + ref[near].astype(F32)
        if near == 0:
            own_ref[...] = total
        else:
            message_refs[near - 1][...] = total.astype(BF16)


def second_rows_kernel(sizes, *refs):
    x_ref, gain_ref, inverse_ref, arriving_ref, query_grad_ref, first_ref, input_grads_ref = refs
    input_grads_ref[0, 0] = first_ref[...]
    inverse = inverse_ref[1]
    normed_of = normed_from(x_ref, 1, inverse)
    coupled = jnp.zeros((sizes[0], HD), F32)
    for turn in range(sizes[3]):
        coupled = coupled_terms(
            Group(sizes, turn), query_grad_ref[turn], normed_of, gain_ref, coupled
        )

    def write(where, result):
        input_grads_ref[0, 1, :, where] = result

    write_input_grads(
        sizes,
        coupled,
        lambda turn: query_grad_ref[turn],
        normed_of,
        gain_ref,
        inverse,
        lambda where: arriving_ref[:, where],
        write,
    )


def first_near_kernel(sizes, own_ref, *refs):
    block = 2 * sizes[1]
    keep_ref, send_ref = refs[-2:]
    total = own_ref[...]
    for ref in refs[:-2]:
        total = total + ref[...].astype(F32)
    keep_ref[...] = total[:block]
    send_ref[...] = total[block:].astype(BF16)


def second_near_kernel(sizes, *refs):
    rows, half, cycle, tp_count, group, columns = sizes
    near_count = tp_count // 2
    members = cycle * near_count
    own_ref, gain_ref = refs[:2]
    message_refs = refs[2 : 1 + members][::-1]
    keep_ref, gain_sum_ref, send_ref = refs[1 + members :]
    block = 2 * half
    total = own_ref[...]
    for ref in message_refs:
        total = total + ref[: 2 * block, :].astype(F32)
    keep_ref[...] = total[:block]
    send_ref[:block, :] = total[block:].astype(BF16)
    cycle_place = lax.axis_index("ctx")
    near_place = lax.axis_index("tp") % near_count
    values = [gain_ref[...].astype(BF16).astype(F32)]
    owners = [cycle_place * near_count + near_place]
    for place, ref in enumerate(message_refs, 1):
        step, near = place // near_count, place % near_count
        values.append(ref[2 * block :, :].astype(F32))
        owners.append(((cycle_place + step) % cycle) * near_count + (near_place ^ near))
    gain = in_order(values, owners)
    gain_sum_ref[...] = gain
    send_ref[block:, :] = gain.astype(BF16)


def finish_kernel(sizes, *refs):
    half = sizes[1]
    keep_refs, receive_refs, gain_ref = refs[:TICKS], refs[TICKS : 2 * TICKS], refs[2 * TICKS]
    key_ref, value_ref, gain_out_ref = refs[2 * TICKS + 1 :]
    parity = lax.axis_index("tp") // (sizes[3] // 2)
    block = 2 * half
    own_first = pl.multiple_of(parity * half, half)
    other_first = pl.multiple_of((1 - parity) * half, half)
    for tick in range(TICKS):
        for kind, out in enumerate((key_ref, value_ref)):
            here = slice(kind * half, (kind + 1) * half)
            out[0, tick, pl.ds(own_first, half), :] = keep_refs[tick][here, :]
            out[0, tick, pl.ds(other_first, half), :] = receive_refs[tick][here, :].astype(F32)
    own = gain_ref[...].astype(BF16).astype(F32)
    gain_out_ref[...] = own + receive_refs[TICKS - 1][block:, :].astype(F32)


def shape(dims, dtype):
    return jax.ShapeDtypeStruct(dims, dtype)


def on_device(segment_inputs, keys, values, norm_gain, waiting_grads, output_grads, doc_lengths):
    cycle = lax.axis_size("ctx")
    tp_count = lax.axis_size("tp")
    pipe_count = lax.axis_size("pipe")
    _, ticks, rows, columns = segment_inputs.shape
    half = keys.shape[2] // 2
    group = columns // (tp_count * HD)
    gain_count = columns // HD
    sizes = (rows, half, cycle, tp_count, group, columns)
    block = 2 * half
    key_count = cycle * half
    stacked = group * rows
    score_bytes = key_count * stacked * 4
    usual_limit = min(56 << 20, (12 << 20) + 20 * score_bytes)

    def call(kernel, name, operands, out_shape, scratch=(), scalars=0):
        in_specs = [pl.BlockSpec(memory_space=pltpu.SMEM)] * scalars
        in_specs += [pl.BlockSpec(memory_space=pltpu.VMEM)] * (len(operands) - scalars)
        return pl.pallas_call(
            kernel,
            out_shape=out_shape,
            in_specs=in_specs,
            out_specs=[pl.BlockSpec(memory_space=pltpu.VMEM)] * len(out_shape),
            scratch_shapes=scratch,
            compiler_params=pltpu.CompilerParams(vmem_limit_bytes=usual_limit),
            name=name,
        )(*operands)

    near_count = tp_count // 2

    def to_near(value, step, near):
        if step == 0:
            return lax.ppermute(value, "tp", [(i, i ^ near) for i in range(tp_count)])
        if near == 0:
            return lax.ppermute(value, "ctx", [(i, (i + step) % cycle) for i in range(cycle)])
        pairs = [
            (c * tp_count + t, ((c + step) % cycle) * tp_count + (t ^ near))
            for c in range(cycle)
            for t in range(tp_count)
        ]
        return lax.ppermute(value, ("ctx", "tp"), pairs)

    def to_far(value):
        return lax.ppermute(value, "tp", [(i, i ^ near_count) for i in range(tp_count)])

    sections = shape((ticks, 2, half, HD), BF16)
    own_kv, other_kv = call(
        functools.partial(pack_kernel, tp_count, half),
        "pack_kv",
        (jnp.stack([keys[0], values[0]]),),
        [sections, sections],
    )
    far_kv = to_far(other_kv)
    places = [(step, near) for step in range(cycle) for near in range(near_count)][1:]
    kv = [
        block if place == (0, 0) else to_near(block, *place)
        for block in (own_kv, far_kv)
        for place in [(0, 0)] + places
    ]
    own_set, far_set = kv[: len(kv) // 2], kv[len(kv) // 2 :]
    queries, inverse, masks = call(
        functools.partial(norm_kernel, sizes),
        "norm",
        (doc_lengths, segment_inputs, norm_gain),
        [
            shape((ticks, rows, columns), BF16),
            shape((ticks, rows, HD), F32),
            shape((ticks, key_count, stacked), F32),
        ],
        scalars=1,
    )

    low_rows = shape((rows, columns), BF16)
    low_scores = shape((near_count, key_count, stacked), BF16)
    low_grads = shape((near_count, stacked, HD), BF16)
    query_grad_near, dscore_near, probs_near, coupled, turned = call(
        functools.partial(first_near_rows_kernel, sizes),
        "first_near_rows",
        (segment_inputs, norm_gain, queries, inverse, masks, waiting_grads, *own_set),
        [
            low_grads,
            low_scores,
            low_scores,
            shape((rows, HD), F32),
            shape((near_count, 2, HD, stacked), BF16),
        ],
    )
    input_grad_first, query_grad_far, dscore_far, probs_far = call(
        functools.partial(first_far_rows_kernel, sizes),
        "first_far_rows",
        (
            segment_inputs,
            norm_gain,
            inverse,
            masks,
            waiting_grads,
            *far_set,
            query_grad_near,
            coupled,
            turned,
        ),
        [low_rows, low_grads, low_scores, low_scores],
    )
    over_link = lax.ppermute(
        input_grad_first, "pipe", [(i, i - 1) for i in range(2, pipe_count, 2)]
    )
    on_chip = lax.ppermute(input_grad_first, "pipe", [(i, i ^ 1) for i in range(pipe_count)])
    gain_shape = shape((gain_count, HD), F32)
    pair_rows = 2 * block
    own_shape = shape((pair_rows, HD), F32)
    first_sums = (near_count, pair_rows, HD)
    gain_first, *sums_first = call(
        functools.partial(first_keys_kernel, sizes),
        "first_keys",
        (
            segment_inputs,
            queries,
            inverse,
            waiting_grads,
            query_grad_near,
            query_grad_far,
            dscore_near,
            dscore_far,
            probs_near,
            probs_far,
        ),
        [gain_shape, shape(first_sums, F32)] + [shape(first_sums, BF16)] * (cycle - 1),
    )
    sums_first = sums_first[:1] + [
        to_near(value, -step, 0) for step, value in enumerate(sums_first[1:], 1)
    ]
    probs_second, probs_low, normed_second = call(
        functools.partial(second_probs_kernel, sizes),
        "second_probs",
        (masks, queries, segment_inputs, inverse, *kv),
        [
            shape((tp_count, key_count, stacked), F32),
            shape((tp_count, key_count, stacked), BF16),
            shape((rows, columns), F32),
        ],
    )
    message = shape((pair_rows + gain_count, HD), BF16)
    query_grad_second, gain_rows, own_second, arriving, *sends = call(
        functools.partial(second_keys_kernel, sizes),
        "second_keys",
        (
            normed_second,
            queries,
            probs_low,
            output_grads,
            on_chip,
            over_link,
            probs_second,
            gain_first,
            *kv,
        ),
        [shape((tp_count, stacked, HD), BF16), gain_shape, own_shape, low_rows]
        + [message] * len(places),
        scratch=[pltpu.VMEM((gain_count, HD), F32)],
    )
    received = [to_near(value, -step, near) for value, (step, near) in zip(sends, places)]
    own_first, *sends_first = call(
        functools.partial(first_sum_kernel, sizes),
        "first_sum",
        sums_first,
        [own_shape] + [shape((pair_rows, HD), BF16)] * (near_count - 1),
    )
    received_first = [to_near(value, 0, near) for near, value in enumerate(sends_first, 1)]
    (input_grads,) = call(
        functools.partial(second_rows_kernel, sizes),
        "second_rows",
        (
            segment_inputs,
            norm_gain,
            inverse,
            arriving,
            query_grad_second,
            input_grad_first,
        ),
        [shape((1, ticks, rows, columns), BF16)],
    )
    keep_shape = shape((block, HD), F32)
    keep_first, send_first = call(
        functools.partial(first_near_kernel, sizes),
        "first_near",
        (own_first, *received_first),
        [keep_shape, shape((block, HD), BF16)],
    )
    keep_second, gain_sum, send_second = call(
        functools.partial(second_near_kernel, sizes),
        "second_near",
        (own_second, gain_rows, *received[::-1]),
        [keep_shape, gain_shape, shape((block + gain_count, HD), BF16)],
    )
    grads_shape = shape((1, ticks, block, HD), F32)
    key_grads, value_grads, gain_grads = call(
        functools.partial(finish_kernel, sizes),
        "finish",
        (keep_first, keep_second, to_far(send_first), to_far(send_second), gain_sum),
        [grads_shape, grads_shape, gain_shape],
    )
    return input_grads, key_grads, value_grads, gain_grads.reshape(1, columns)


def solution(mesh):
    in_specs = (
        P("pipe", None, ("ctx", "tp"), None),
        P("pipe", None, "ctx", "tp"),
        P("pipe", None, "ctx", "tp"),
        P("pipe", None),
        P("pipe", ("ctx", "tp"), None),
        P(None, ("ctx", "tp"), None),
        P(),
    )
    out_specs = (
        P("pipe", None, ("ctx", "tp"), None),
        P("pipe", None, "ctx", "tp"),
        P("pipe", None, "ctx", "tp"),
        P("pipe", None),
    )
    return jax.shard_map(
        on_device, mesh=mesh, in_specs=in_specs, out_specs=out_specs, check_vma=False
    )
```

```python
import functools

import jax
import jax.numpy as jnp
from jax import lax
from jax.experimental import pallas as pl
from jax.experimental.pallas import tpu as pltpu
from jax.sharding import PartitionSpec as P

HD = 128
EPSILON = 1e-05
FILL = -1e30
SCALE = HD ** (-0.5)
TICKS = 2
F32 = jnp.float32
BF16 = jnp.bfloat16

NT = (((1,), (1,)), ((), ()))
NN = (((1,), (0,)), ((), ()))
TN = (((0,), (0,)), ((), ()))


def dot(a, b, dims):
    return lax.dot_general(a, b, dims, preferred_element_type=F32)


def in_order(values, owners):
    total = None
    for owner in range(len(values)):
        term = jnp.where(owners[0] == owner, values[0], 0.0)
        for value, whose in zip(values[1:], owners[1:]):
            term = jnp.where(whose == owner, value, term)
        total = term if total is None else total + term
    return total


def pack_kernel(tp_count, half, both_ref, own_ref, other_ref):
    parity = lax.axis_index("tp") // (tp_count // 2)
    own_first = pl.multiple_of(parity * half, half)
    other_first = pl.multiple_of((1 - parity) * half, half)
    for kind in range(2):
        for tick in range(TICKS):
            own_ref[tick, kind] = both_ref[kind, tick, pl.ds(own_first, half), :]
            other_ref[tick, kind] = both_ref[kind, tick, pl.ds(other_first, half), :]


def norm_kernel(sizes, doc_ref, x_ref, gain_ref, query_ref, inverse_ref, mask_ref):
    rows, columns = sizes[0], sizes[5]
    for tick in range(TICKS):
        squares = jnp.zeros((rows, HD), F32)
        for first in range(0, columns, HD):
            part = x_ref[0, tick, :, first : first + HD].astype(F32)
            squares = squares + part * part
        mean = jnp.sum(squares, axis=1, keepdims=True) * (1.0 / columns)
        inverse = jnp.broadcast_to(lax.rsqrt(mean + EPSILON), (rows, HD))
        inverse_ref[tick] = inverse
        for first in range(0, columns, HD):
            here = slice(first, first + HD)
            normed = x_ref[0, tick, :, here].astype(F32) * inverse
            query_ref[tick, :, here] = (normed * gain_ref[:, here]).astype(BF16)
        mask_ref[tick] = jnp.where(visible_keys(sizes, tick, doc_ref), 0.0, FILL)


class Group:
    def __init__(self, sizes, turn):
        self.rows, self.group = sizes[0], sizes[4]
        width = self.group * HD
        self.head_group = lax.axis_index("tp") ^ turn
        self.first = pl.multiple_of(self.head_group * width, width)

    def head(self, index):
        return pl.ds(self.first + index * HD, HD)

    def stacked(self, load):
        return jnp.concatenate([load(self.head(index)) for index in range(self.group)], axis=0)

    def unstacked(self, value):
        return [value[index * self.rows : (index + 1) * self.rows] for index in range(self.group)]


def waiting_from(waiting_ref):
    return lambda where: waiting_ref[0, :, where]


def choose_arriving(output_ref, chip_ref, link_ref, target_ref):
    place = lax.axis_index("pipe")
    last = place == lax.axis_size("pipe") - 1
    even = place % 2 == 0

    @pl.when(last)
    def _():
        target_ref[...] = output_ref[0]

    @pl.when(jnp.logical_not(last) & even)
    def _():
        target_ref[...] = chip_ref[...]

    @pl.when(jnp.logical_not(last) & jnp.logical_not(even))
    def _():
        target_ref[...] = link_ref[...]


def visible_keys(sizes, tick, doc_ref):
    rows, half, cycle, tp_count, group, columns = sizes
    cycle_place = lax.axis_index("ctx")
    tp_place = lax.axis_index("tp")
    parity = tp_place // (tp_count // 2)
    stacked = group * rows

    def section_first(owner):
        return half * jnp.where(parity == 0, owner, 2 * cycle - 1 - owner)

    row_first = section_first(cycle_place) + (tp_place % (tp_count // 2)) * rows
    query_pos = row_first + (lax.broadcasted_iota(jnp.int32, (1, stacked), 1) & (rows - 1))
    key_place = lax.broadcasted_iota(jnp.int32, (cycle * half, 1), 0)
    key_pos = key_place + section_first(cycle_place)
    for turn in range(1, cycle):
        first = section_first((cycle_place - turn + cycle) % cycle)
        key_pos = jnp.where(key_place >= turn * half, key_place - turn * half + first, key_pos)
    micro = lax.axis_index("pipe") + tick
    closing = jnp.int32(0)
    query_start = jnp.zeros((1, stacked), jnp.int32)
    for doc in range(doc_ref.shape[1]):
        length = doc_ref[micro, doc]
        closing = closing + length
        query_start = query_start + jnp.where(closing <= query_pos, length, 0)
    return (key_pos <= query_pos) & (key_pos >= query_start)


def probabilities(mask, products):
    scores = SCALE * products + mask
    weights = jnp.exp(scores - jnp.max(scores, axis=0, keepdims=True))
    return weights * (1.0 / jnp.sum(weights, axis=0, keepdims=True))


def score_grads(probs, prob_grad):
    row_term = jnp.sum(probs * prob_grad, axis=0, keepdims=True)
    return (probs * (prob_grad - row_term)).astype(BF16)


class Keys:
    def __init__(self, sizes, tick, refs):
        self.near_count = sizes[3] // 2
        self.tick = tick
        self.refs = [refs[0], *refs[1:][::-1]]

    def __call__(self, near, kind):
        parts = [ref[self.tick, kind] for ref in self.refs[near :: self.near_count]]
        return jnp.concatenate(parts, axis=0)


def place_of(sizes, far, kind):
    half = sizes[1]
    return slice((far * 2 + kind) * half, (far * 2 + kind + 1) * half)


def put_key_grads(sizes, turn, parts, own_ref, message_refs):
    half, cycle, tp_count = sizes[1:4]
    near_count = tp_count // 2
    near, far = turn % near_count, turn // near_count
    for kind, part in enumerate(parts):
        here = place_of(sizes, far, kind)
        for step in range(cycle):
            piece = part[step * half : (step + 1) * half]
            if step == 0 and near == 0:
                own_ref[here, :] = piece
            else:
                message_refs[step * near_count + near - 1][here, :] = piece.astype(BF16)


def gain_terms(columns_of, query_grad, normed_of, gain_rows_ref):
    rows = []
    for index, low in enumerate(columns_of.unstacked(query_grad)):
        term = low.astype(F32) * normed_of(columns_of.head(index))
        rows.append(jnp.sum(term, axis=0, keepdims=True))
    group = columns_of.group
    place = pl.ds(pl.multiple_of(columns_of.head_group * group, group), group)
    gain_rows_ref[place, :] = jnp.concatenate(rows, axis=0)


def coupled_terms(columns_of, query_grad, normed_of, gain_ref, coupled):
    for index, low in enumerate(columns_of.unstacked(query_grad)):
        where = columns_of.head(index)
        coupled = coupled + low.astype(F32) * gain_ref[:, where] * normed_of(where)
    return coupled


def write_input_grads(sizes, coupled, query_grad_of, normed_of, gain_ref, inverse, arriving, write):
    coupling = jnp.sum(coupled, axis=1, keepdims=True) * (1.0 / sizes[5])
    for turn in range(sizes[3]):
        columns_of = Group(sizes, turn)
        for index, low in enumerate(columns_of.unstacked(query_grad_of(turn))):
            where = columns_of.head(index)
            scaled = low.astype(F32) * gain_ref[:, where]
            result = arriving(where).astype(F32) + inverse * (scaled - normed_of(where) * coupling)
            write(where, result.astype(BF16))


def normed_from(x_ref, tick, inverse):
    return lambda where: x_ref[0, tick, :, where].astype(F32) * inverse


def first_half(keys, mask, products, dscore_ref, probs_ref):
    dscores = []
    for near, (scores, prob_grads) in enumerate(products):
        probs = probabilities(mask, scores)
        dscores.append(score_grads(probs, prob_grads))
        dscore_ref[near] = dscores[near]
        probs_ref[near] = probs.astype(BF16)
    return [
        (SCALE * dot(dscore, keys(near, 0), TN)).astype(BF16)
        for near, dscore in enumerate(dscores)
    ]


def first_near_rows_kernel(sizes, *refs):
    near_count = sizes[3] // 2
    members = sizes[2] * near_count
    x_ref, gain_ref, query_ref, inverse_ref, mask_ref, waiting_ref = refs[:6]
    keys = Keys(sizes, 0, refs[6 : 6 + members])
    query_grad_ref, dscore_ref, probs_ref, coupled_ref, turned_ref = refs[6 + members : 11 + members]
    base_ref, pull_ref, rate_ref, weight_ref = refs[11 + members :]
    loads = (lambda where: query_ref[0, :, where], waiting_from(waiting_ref))
    products = []
    for near in range(near_count):
        operands = [Group(sizes, near).stacked(load) for load in loads]
        products.append([dot(keys(near, kind), operands[kind], NT) for kind in range(2)])
    query_grads = first_half(keys, mask_ref[0], products, dscore_ref, probs_ref)
    normed_of = normed_from(x_ref, 0, inverse_ref[0])
    coupled = jnp.zeros((sizes[0], HD), F32)
    for near, query_grad in enumerate(query_grads):
        query_grad_ref[near] = query_grad
        coupled = coupled_terms(Group(sizes, near), query_grad, normed_of, gain_ref, coupled)
    coupled_ref[...] = coupled
    inverse = inverse_ref[0]
    for near in range(near_count):
        columns_of = Group(sizes, near)
        for index, low in enumerate(columns_of.unstacked(query_grads[near])):
            where = columns_of.head(index)
            scaled = low.astype(F32) * gain_ref[:, where]
            base_ref[:, where] = loads[1](where).astype(F32) + inverse * scaled
            pull_ref[:, where] = inverse * normed_of(where)
        columns_of = Group(sizes, near_count + near)
        for kind, load in enumerate(loads):
            turned_ref[near, kind] = columns_of.stacked(load).T
        for index in range(columns_of.group):
            where = columns_of.head(index)
            normed = normed_of(where)
            pull_ref[:, where] = inverse * normed
            rate_ref[:, where] = inverse * gain_ref[:, where]
            weight_ref[:, where] = normed * gain_ref[:, where]


def first_far_rows_kernel(sizes, *refs):
    near_count = sizes[3] // 2
    members = sizes[2] * near_count
    mask_ref, waiting_ref = refs[:2]
    keys, refs = Keys(sizes, 0, refs[2 : 2 + members]), refs[2 + members :]
    coupled_ref, turned_ref, base_ref, pull_ref, rate_ref, weight_ref = refs[:6]
    input_grad_ref, query_grad_ref, dscore_ref, probs_ref = refs[6:]
    products = [
        [dot(keys(near, kind), turned_ref[near, kind], NN) for kind in range(2)]
        for near in range(near_count)
    ]
    query_grads = first_half(keys, mask_ref[0], products, dscore_ref, probs_ref)
    coupled = coupled_ref[...]
    groups = [Group(sizes, turn) for turn in range(2 * near_count)]
    for near, query_grad in enumerate(query_grads):
        query_grad_ref[near] = query_grad
        columns_of = groups[near_count + near]
        for index, low in enumerate(columns_of.unstacked(query_grad)):
            coupled = coupled + low.astype(F32) * weight_ref[:, columns_of.head(index)]
    coupling = jnp.sum(coupled, axis=1, keepdims=True) * (1.0 / sizes[5])
    for near, query_grad in enumerate(query_grads):
        for index in range(groups[near].group):
            where = groups[near].head(index)
            input_grad_ref[:, where] = (base_ref[:, where] - pull_ref[:, where] * coupling).astype(
                BF16
            )
        columns_of = groups[near_count + near]
        for index, low in enumerate(columns_of.unstacked(query_grad)):
            where = columns_of.head(index)
            base = waiting_ref[0, :, where].astype(F32) + low.astype(F32) * rate_ref[:, where]
            input_grad_ref[:, where] = (base - pull_ref[:, where] * coupling).astype(BF16)


def first_keys_kernel(sizes, *refs):
    half, cycle, tp_count = sizes[1:4]
    near_count = tp_count // 2
    x_ref, query_ref, inverse_ref, waiting_ref = refs[:4]
    query_grad_refs, dscore_refs, probs_refs = refs[4:6], refs[6:8], refs[8:10]
    gain_rows_ref, own_ref = refs[10:12]
    send_refs = refs[12:]
    arriving = waiting_from(waiting_ref)
    normed_of = normed_from(x_ref, 0, inverse_ref[0])
    for turn in range(tp_count):
        near, far = turn % near_count, turn // near_count
        columns_of = Group(sizes, turn)
        query = columns_of.stacked(lambda where: query_ref[0, :, where])
        grad = columns_of.stacked(arriving)
        parts = (
            SCALE * dot(dscore_refs[far][near], query, NN),
            dot(probs_refs[far][near], grad, NN),
        )
        for kind, part in enumerate(parts):
            here = place_of(sizes, far, kind)
            own_ref[near, here, :] = part[:half]
            for step, ref in enumerate(send_refs, 1):
                ref[near, here, :] = part[step * half : (step + 1) * half].astype(BF16)
        gain_terms(columns_of, query_grad_refs[far][near], normed_of, gain_rows_ref)


def both_sets(sizes, refs):
    near_count = sizes[3] // 2
    members = sizes[2] * near_count
    sets = [Keys(sizes, 1, refs[:members]), Keys(sizes, 1, refs[members:])]
    return lambda turn, kind: sets[turn // near_count](turn % near_count, kind)


def second_probs_kernel(sizes, *refs):
    turns = range(sizes[3])
    mask_ref, query_ref, x_ref, inverse_ref = refs[:4]
    keys, (probs_ref, low_ref, normed_ref) = both_sets(sizes, refs[4:-3]), refs[-3:]
    mask = mask_ref[1]
    scores = []
    for turn in turns:
        query = Group(sizes, turn).stacked(lambda where: query_ref[1, :, where])
        scores.append(dot(keys(turn, 0), query, NT))
    for turn in turns:
        probs = probabilities(mask, scores[turn])
        probs_ref[turn] = probs
        low_ref[turn] = probs.astype(BF16)
    inverse = inverse_ref[1]
    for first in range(0, sizes[5], HD):
        here = slice(first, first + HD)
        normed_ref[:, here] = x_ref[0, 1, :, here].astype(F32) * inverse


def second_keys_kernel(sizes, *refs):
    cycle, tp_count = sizes[2:4]
    turns = range(tp_count)
    kv_count = cycle * tp_count
    normed_ref, query_ref, low_ref, output_ref, link_ref, chip_ref = refs[:6]
    probs_ref, before_ref, *refs = refs[6:]
    keys, refs = both_sets(sizes, refs[:kv_count]), refs[kv_count:]
    query_grad_ref, gain_rows_ref, own_ref, arriving_ref = refs[:4]
    message_refs, gain_scratch = refs[4:-1], refs[-1]
    choose_arriving(output_ref, chip_ref, link_ref, arriving_ref)

    def arriving(where):
        return arriving_ref[:, where]

    columns_of = [Group(sizes, turn) for turn in turns]
    grads = [columns_of[turn].stacked(arriving) for turn in turns]
    prob_grads = [dot(keys(turn, 1), grads[turn], NT) for turn in turns]
    value_grads = [dot(low_ref[turn], grads[turn], NN) for turn in turns]
    dscores = [score_grads(probs_ref[turn], prob_grads[turn]) for turn in turns]
    query_grads = [
        (SCALE * dot(dscores[turn], keys(turn, 0), TN)).astype(BF16) for turn in turns
    ]
    for turn in turns:
        query = columns_of[turn].stacked(lambda where: query_ref[1, :, where])
        key_grad = SCALE * dot(dscores[turn], query, NN)
        put_key_grads(sizes, turn, (key_grad, value_grads[turn]), own_ref, message_refs)
    for turn in turns:
        query_grad_ref[turn] = query_grads[turn]
        gain_terms(
            columns_of[turn], query_grads[turn], lambda where: normed_ref[:, where], gain_scratch
        )
    gain_rows = gain_scratch[...] + before_ref[...]
    gain_rows_ref[...] = gain_rows
    gain_low = gain_rows.astype(BF16)
    for ref in message_refs:
        ref[own_ref.shape[0] :, :] = gain_low


def first_sum_kernel(sizes, *refs):
    cycle = sizes[2]
    parts, own_ref, message_refs = refs[:cycle], refs[cycle], refs[cycle + 1 :]
    for near in range(sizes[3] // 2):
        total = parts[0][near]
        for ref in parts[1:]:
            total = total + ref[near].astype(F32)
        if near == 0:
            own_ref[...] = total
        else:
            message_refs[near - 1][...] = total.astype(BF16)


def second_rows_kernel(sizes, *refs):
    x_ref, gain_ref, inverse_ref, arriving_ref, query_grad_ref, first_ref, input_grads_ref = refs
    input_grads_ref[0, 0] = first_ref[...]
    inverse = inverse_ref[1]
    normed_of = normed_from(x_ref, 1, inverse)
    coupled = jnp.zeros((sizes[0], HD), F32)
    for turn in range(sizes[3]):
        coupled = coupled_terms(
            Group(sizes, turn), query_grad_ref[turn], normed_of, gain_ref, coupled
        )

    def write(where, result):
        input_grads_ref[0, 1, :, where] = result

    write_input_grads(
        sizes,
        coupled,
        lambda turn: query_grad_ref[turn],
        normed_of,
        gain_ref,
        inverse,
        lambda where: arriving_ref[:, where],
        write,
    )


def first_near_kernel(sizes, own_ref, *refs):
    block = 2 * sizes[1]
    keep_ref, send_ref = refs[-2:]
    total = own_ref[...]
    for ref in refs[:-2]:
        total = total + ref[...].astype(F32)
    keep_ref[...] = total[:block]
    send_ref[...] = total[block:].astype(BF16)


def second_near_kernel(sizes, *refs):
    rows, half, cycle, tp_count, group, columns = sizes
    near_count = tp_count // 2
    members = cycle * near_count
    own_ref, gain_ref = refs[:2]
    message_refs = refs[2 : 1 + members][::-1]
    keep_ref, gain_sum_ref, send_ref = refs[1 + members :]
    block = 2 * half
    total = own_ref[...]
    for ref in message_refs:
        total = total + ref[: 2 * block, :].astype(F32)
    keep_ref[...] = total[:block]
    send_ref[:block, :] = total[block:].astype(BF16)
    cycle_place = lax.axis_index("ctx")
    near_place = lax.axis_index("tp") % near_count
    values = [gain_ref[...].astype(BF16).astype(F32)]
    owners = [cycle_place * near_count + near_place]
    for place, ref in enumerate(message_refs, 1):
        step, near = place // near_count, place % near_count
        values.append(ref[2 * block :, :].astype(F32))
        owners.append(((cycle_place + step) % cycle) * near_count + (near_place ^ near))
    gain = in_order(values, owners)
    gain_sum_ref[...] = gain
    send_ref[block:, :] = gain.astype(BF16)


def finish_kernel(sizes, *refs):
    half = sizes[1]
    keep_refs, receive_refs, gain_ref = refs[:TICKS], refs[TICKS : 2 * TICKS], refs[2 * TICKS]
    key_ref, value_ref, gain_out_ref = refs[2 * TICKS + 1 :]
    parity = lax.axis_index("tp") // (sizes[3] // 2)
    block = 2 * half
    own_first = pl.multiple_of(parity * half, half)
    other_first = pl.multiple_of((1 - parity) * half, half)
    for tick in range(TICKS):
        for kind, out in enumerate((key_ref, value_ref)):
            here = slice(kind * half, (kind + 1) * half)
            out[0, tick, pl.ds(own_first, half), :] = keep_refs[tick][here, :]
            out[0, tick, pl.ds(other_first, half), :] = receive_refs[tick][here, :].astype(F32)
    own = gain_ref[...].astype(BF16).astype(F32)
    gain_out_ref[...] = own + receive_refs[TICKS - 1][block:, :].astype(F32)


def shape(dims, dtype):
    return jax.ShapeDtypeStruct(dims, dtype)


def on_device(segment_inputs, keys, values, norm_gain, waiting_grads, output_grads, doc_lengths):
    cycle = lax.axis_size("ctx")
    tp_count = lax.axis_size("tp")
    pipe_count = lax.axis_size("pipe")
    _, ticks, rows, columns = segment_inputs.shape
    half = keys.shape[2] // 2
    group = columns // (tp_count * HD)
    gain_count = columns // HD
    sizes = (rows, half, cycle, tp_count, group, columns)
    block = 2 * half
    key_count = cycle * half
    stacked = group * rows
    score_bytes = key_count * stacked * 4
    usual_limit = min(56 << 20, (12 << 20) + 20 * score_bytes)

    def call(kernel, name, operands, out_shape, scratch=(), scalars=0):
        in_specs = [pl.BlockSpec(memory_space=pltpu.SMEM)] * scalars
        in_specs += [pl.BlockSpec(memory_space=pltpu.VMEM)] * (len(operands) - scalars)
        return pl.pallas_call(
            kernel,
            out_shape=out_shape,
            in_specs=in_specs,
            out_specs=[pl.BlockSpec(memory_space=pltpu.VMEM)] * len(out_shape),
            scratch_shapes=scratch,
            compiler_params=pltpu.CompilerParams(vmem_limit_bytes=usual_limit),
            name=name,
        )(*operands)

    near_count = tp_count // 2

    def to_near(value, step, near):
        if step == 0:
            return lax.ppermute(value, "tp", [(i, i ^ near) for i in range(tp_count)])
        if near == 0:
            return lax.ppermute(value, "ctx", [(i, (i + step) % cycle) for i in range(cycle)])
        pairs = [
            (c * tp_count + t, ((c + step) % cycle) * tp_count + (t ^ near))
            for c in range(cycle)
            for t in range(tp_count)
        ]
        return lax.ppermute(value, ("ctx", "tp"), pairs)

    def to_far(value):
        return lax.ppermute(value, "tp", [(i, i ^ near_count) for i in range(tp_count)])

    sections = shape((ticks, 2, half, HD), BF16)
    own_kv, other_kv = call(
        functools.partial(pack_kernel, tp_count, half),
        "pack_kv",
        (jnp.stack([keys[0], values[0]]),),
        [sections, sections],
    )
    far_kv = to_far(other_kv)
    places = [(step, near) for step in range(cycle) for near in range(near_count)][1:]
    kv = [
        block if place == (0, 0) else to_near(block, *place)
        for block in (own_kv, far_kv)
        for place in [(0, 0)] + places[::-1]
    ]
    own_set, far_set = kv[: len(kv) // 2], kv[len(kv) // 2 :]
    queries, inverse, masks = call(
        functools.partial(norm_kernel, sizes),
        "norm",
        (doc_lengths, segment_inputs, norm_gain),
        [
            shape((ticks, rows, columns), BF16),
            shape((ticks, rows, HD), F32),
            shape((ticks, key_count, stacked), F32),
        ],
        scalars=1,
    )

    low_rows = shape((rows, columns), BF16)
    low_scores = shape((near_count, key_count, stacked), BF16)
    low_grads = shape((near_count, stacked, HD), BF16)
    query_grad_near, dscore_near, probs_near, coupled, turned, *factors = call(
        functools.partial(first_near_rows_kernel, sizes),
        "first_near_rows",
        (segment_inputs, norm_gain, queries, inverse, masks, waiting_grads, *own_set),
        [
            low_grads,
            low_scores,
            low_scores,
            shape((rows, HD), F32),
            shape((near_count, 2, HD, stacked), BF16),
        ]
        + [shape((rows, columns), F32)] * 4,
    )
    input_grad_first, query_grad_far, dscore_far, probs_far = call(
        functools.partial(first_far_rows_kernel, sizes),
        "first_far_rows",
        (
            masks,
            waiting_grads,
            *far_set,
            coupled,
            turned,
            *factors,
        ),
        [low_rows, low_grads, low_scores, low_scores],
    )
    over_link = lax.ppermute(
        input_grad_first, "pipe", [(i, i - 1) for i in range(2, pipe_count, 2)]
    )
    on_chip = lax.ppermute(input_grad_first, "pipe", [(i, i ^ 1) for i in range(pipe_count)])
    gain_shape = shape((gain_count, HD), F32)
    pair_rows = 2 * block
    own_shape = shape((pair_rows, HD), F32)
    first_sums = (near_count, pair_rows, HD)
    gain_first, *sums_first = call(
        functools.partial(first_keys_kernel, sizes),
        "first_keys",
        (
            segment_inputs,
            queries,
            inverse,
            waiting_grads,
            query_grad_near,
            query_grad_far,
            dscore_near,
            dscore_far,
            probs_near,
            probs_far,
        ),
        [gain_shape, shape(first_sums, F32)] + [shape(first_sums, BF16)] * (cycle - 1),
    )
    sums_first = sums_first[:1] + [
        to_near(value, -step, 0) for step, value in enumerate(sums_first[1:], 1)
    ]
    probs_second, probs_low, normed_second = call(
        functools.partial(second_probs_kernel, sizes),
        "second_probs",
        (masks, queries, segment_inputs, inverse, *kv),
        [
            shape((tp_count, key_count, stacked), F32),
            shape((tp_count, key_count, stacked), BF16),
            shape((rows, columns), F32),
        ],
    )
    message = shape((pair_rows + gain_count, HD), BF16)
    query_grad_second, gain_rows, own_second, arriving, *sends = call(
        functools.partial(second_keys_kernel, sizes),
        "second_keys",
        (
            normed_second,
            queries,
            probs_low,
            output_grads,
            over_link,
            on_chip,
            probs_second,
            gain_first,
            *kv,
        ),
        [shape((tp_count, stacked, HD), BF16), gain_shape, own_shape, low_rows]
        + [message] * len(places),
        scratch=[pltpu.VMEM((gain_count, HD), F32)],
    )
    received = [to_near(value, -step, near) for value, (step, near) in zip(sends, places)]
    own_first, *sends_first = call(
        functools.partial(first_sum_kernel, sizes),
        "first_sum",
        sums_first,
        [own_shape] + [shape((pair_rows, HD), BF16)] * (near_count - 1),
    )
    received_first = [to_near(value, 0, near) for near, value in enumerate(sends_first, 1)]
    (input_grads,) = call(
        functools.partial(second_rows_kernel, sizes),
        "second_rows",
        (
            segment_inputs,
            norm_gain,
            inverse,
            arriving,
            query_grad_second,
            input_grad_first,
        ),
        [shape((1, ticks, rows, columns), BF16)],
    )
    keep_shape = shape((block, HD), F32)
    keep_first, send_first = call(
        functools.partial(first_near_kernel, sizes),
        "first_near",
        (own_first, *received_first),
        [keep_shape, shape((block, HD), BF16)],
    )
    keep_second, gain_sum, send_second = call(
        functools.partial(second_near_kernel, sizes),
        "second_near",
        (own_second, gain_rows, *received[::-1]),
        [keep_shape, gain_shape, shape((block + gain_count, HD), BF16)],
    )
    grads_shape = shape((1, ticks, block, HD), F32)
    key_grads, value_grads, gain_grads = call(
        functools.partial(finish_kernel, sizes),
        "finish",
        (keep_first, keep_second, to_far(send_first), to_far(send_second), gain_sum),
        [grads_shape, grads_shape, gain_shape],
    )
    return input_grads, key_grads, value_grads, gain_grads.reshape(1, columns)


def solution(mesh):
    in_specs = (
        P("pipe", None, ("ctx", "tp"), None),
        P("pipe", None, "ctx", "tp"),
        P("pipe", None, "ctx", "tp"),
        P("pipe", None),
        P("pipe", ("ctx", "tp"), None),
        P(None, ("ctx", "tp"), None),
        P(),
    )
    out_specs = (
        P("pipe", None, ("ctx", "tp"), None),
        P("pipe", None, "ctx", "tp"),
        P("pipe", None, "ctx", "tp"),
        P("pipe", None),
    )
    return jax.shard_map(
        on_device, mesh=mesh, in_specs=in_specs, out_specs=out_specs, check_vma=False
    )
```
